256 devices in a mesh: tile: 64 (over z, y, core), chan: 4 (over x).
Axes of the slice: x: 4, y: 4, z: 8, core: 2. Of those that a mesh axis runs over, the one named last changes fastest.
Arguments:
- features: bfloat16 [128, 262144], P('chan', 'tile'), may hold values from -6 to 6
- conv1_weight: bfloat16 [9, 128, 128], P(None, 'chan'), may hold values from -0.1875 to 0.1875
- down_weight: bfloat16 [4, 128, 128], P(None, 'chan'), may hold values from -0.25 to 0.25
- conv2_weight: bfloat16 [9, 128, 128], P(None, 'chan'), may hold values from -0.1875 to 0.1875
- up_weight: bfloat16 [128, 128], P('chan'), may hold values from -0.5 to 0.5
- out_grad: bfloat16 [128, 262144], P('chan', 'tile'), may hold values from -6 to 6
- adjacency: int32 [64, 8, 2], replicated, may hold values from -1 to 63, as said below
Outputs:
- output: bfloat16 [128, 262144], P('chan', 'tile')
- grad_conv1: float32 [9, 128, 128], P(None, 'chan')
- grad_down: float32 [4, 128, 128], P(None, 'chan')
- grad_conv2: float32 [9, 128, 128], P(None, 'chan')
- grad_up: float32 [128, 128], P('chan')
The draws below stay inside these ranges and needn't reach their ends.
Inputs may be any that keep to these rules, and one draw needn't show every extreme that they name: adjacency[t, k, 0] is the tile beside side k of tile t (sides north, east, south, west, then corners north-east, south-east, south-west, north-west); it is -1 only at corners, where no single tile meets; adjacency[t, k, 1] is the number of counterclockwise quarter turns, 0 to 3, of that neighbour as seen from tile t.
All inputs are finite; a program needn't handle non-finite values.
Results may differ from the reference program's by a relative error of at most 0.0073.
Values may be sent and summed in bfloat16 or wider, within the bound.
A program may use at most 128 MiB of HBM per device.

```python
import jax
import jax.numpy as jnp
import numpy as np
from jax import lax

C = 128
SIDE = 64
TILES = 64
CELLS = 262144


def face_step(face, row, col, side, grid, faces):
    if side == 0:
        if row > 0:
            return (face, row - 1, col, 0)
        return ((face - 1) % faces, grid - 1 - col, grid - 1, 3)
    if side == 1:
        if col < grid - 1:
            return (face, row, col + 1, 0)
        return ((face + 1) % faces, 0, grid - 1 - row, 1)
    if side == 2:
        if row < grid - 1:
            return (face, row + 1, col, 0)
        return ((face + 1) % faces, grid - 1 - col, 0, 3)
    if col > 0:
        return (face, row, col - 1, 0)
    return ((face - 1) % faces, grid - 1, grid - 1 - row, 1)


def corner_walk(face, row, col, first_side, second_side, grid, faces):
    face_one, row_one, col_one, turn_one = face_step(face, row, col, first_side, grid, faces)
    face_two, row_two, col_two, turn_two = face_step(face_one, row_one, col_one, (second_side + turn_one) % 4, grid, faces)
    return (face_two, row_two, col_two, (turn_one + turn_two) % 4)


def base_table(tile_total):
    grid = 1
    while 4 * (2 * grid) * (2 * grid) <= tile_total:
        grid = grid * 2
    faces = tile_total // (grid * grid)
    table = np.zeros((tile_total, 8, 2), np.int32)
    corner_sides = ((0, 1), (2, 1), (2, 3), (0, 3))
    for face in range(faces):
        for row in range(grid):
            for col in range(grid):
                tile_id = face * grid * grid + row * grid + col
                for side in range(4):
                    other_face, other_row, other_col, turn = face_step(face, row, col, side, grid, faces)
                    table[tile_id, side, 0] = other_face * grid * grid + other_row * grid + other_col
                    table[tile_id, side, 1] = turn
                for corner in range(4):
                    first_side, second_side = corner_sides[corner]
                    path_one = corner_walk(face, row, col, first_side, second_side, grid, faces)
                    path_two = corner_walk(face, row, col, second_side, first_side, grid, faces)
                    other_id = path_one[0] * grid * grid + path_one[1] * grid + path_one[2]
                    if path_one == path_two and other_id != tile_id:
                        table[tile_id, 4 + corner, 0] = other_id
                        table[tile_id, 4 + corner, 1] = path_one[3]
                    else:
                        table[tile_id, 4 + corner, 0] = -1
                        table[tile_id, 4 + corner, 1] = 0
    return table


def draw_adjacency(key, part):
    key = jax.random.fold_in(key, 7)
    table = jnp.asarray(base_table(TILES))
    renamed = jax.random.permutation(key, TILES).astype(jnp.int32)
    initial = jnp.argsort(renamed).astype(jnp.int32)
    moved = table[initial]
    partners = moved[:, :, 0]
    partners = jnp.where(partners >= 0, renamed[jnp.clip(partners, 0, TILES - 1)], -1)
    return jnp.stack([partners, moved[:, :, 1]], axis=2).astype(jnp.int32)


def steps_of(stream_key, dims, split, least, top_value):
    gain, own = 1.0, jax.random.fold_in(stream_key, 6)
    for dim, blocks in split:
        heights = jnp.exp(jax.random.uniform(jax.random.fold_in(own, dim), (blocks,), jnp.float32, least / len(split), top_value / len(split)))
        gain = gain * jnp.repeat(heights, dims[dim] // blocks).reshape([-1 if axis == dim else 1 for axis in range(len(dims))])
    return gain


def bell_draw(stream_key, shape, scale, limit, pieces=(), kind=jnp.bfloat16):
    factor_of = steps_of(stream_key, shape, pieces, -0.22, 0.18) if pieces else 1.0
    drawn = jax.random.normal(stream_key, shape, jnp.float32) * scale * factor_of
    return jnp.minimum(jnp.maximum(drawn, -limit), limit).astype(kind)


def setup_inputs(seed: int = 0) -> dict:
    key_of = jax.random.split(jax.random.key(seed), 8)
    return {
        "features": bell_draw(key_of[0], (C, CELLS), 1.0, 6.0, ((0, 4), (1, 64))),
        "conv1_weight": bell_draw(key_of[1], (9, C, C), (9 * C) ** -0.5, 0.1875, ((1, 4),)),
        "down_weight": bell_draw(key_of[2], (4, C, C), (4 * C) ** -0.5, 0.25, ((1, 4),)),
        "conv2_weight": bell_draw(key_of[3], (9, C, C), (9 * C) ** -0.5, 0.1875, ((1, 4),)),
        "up_weight": bell_draw(key_of[4], (C, C), C ** -0.5, 0.5, ((0, 4),)),
        "out_grad": bell_draw(key_of[5], (C, CELLS), 1.0, 6.0, ((0, 4), (1, 64))),
        "adjacency": draw_adjacency(jax.random.fold_in(key_of[7], 71), 0),
    }


side_turns = (0, 1, 2, 3, 0, 2, 2, 0)

def turned(values, quarter):
    return jnp.rot90(values, quarter, axes=(1, 2))

def build_rims(center, width):
    side_len = center.shape[1]
    return jnp.stack([center[:, side_len - width:, :], turned(center[:, :, :width], 1), turned(center[:, :width, :], 2), turned(center[:, :, side_len - width:], 3)])

def pad_block(center, picked, width):
    side_len = center.shape[1]
    north_rows = picked[0]
    east_cols = turned(picked[1], -1)
    south_rows = turned(picked[2], -2)
    west_cols = turned(picked[3], -3)
    north_east = picked[4][:, :, :width]
    south_east = turned(picked[5], -2)[:, :, :width]
    south_west = turned(picked[6], -2)[:, :, side_len - width:]
    north_west = picked[7][:, :, side_len - width:]
    top_band = jnp.concatenate([north_west, north_rows, north_east], axis=2)
    middle = jnp.concatenate([west_cols, center, east_cols], axis=2)
    low_band = jnp.concatenate([south_west, south_rows, south_east], axis=2)
    return jnp.concatenate([top_band, middle, low_band], axis=1)

def choose_rims(partners, rim_slots, current, incoming, first_row):
    row_count = incoming.shape[0]
    relative = partners - first_row
    inside = (relative >= 0) & (relative < row_count)
    clipped = jnp.clip(relative, 0, row_count - 1)
    selected = incoming[clipped, rim_slots]
    return jnp.where(inside[:, None, None, None], selected, current)

def conv_taps(weights, padded, dilation, rows, cols):
    summed = jnp.zeros((weights.shape[1], rows * cols), jnp.float32)
    for row_tap in range(3):
        for col_tap in range(3):
            window = padded[:, row_tap * dilation:row_tap * dilation + rows, col_tap * dilation:col_tap * dilation + cols].reshape(padded.shape[0], rows * cols)
            summed = summed + jnp.dot(weights[3 * row_tap + col_tap], window, preferred_element_type=jnp.float32)
    return summed

def conv_grads(cotangent, padded, dilation, rows, cols):
    result = []
    for row_tap in range(3):
        for col_tap in range(3):
            window = padded[:, row_tap * dilation:row_tap * dilation + rows, col_tap * dilation:col_tap * dilation + cols].reshape(padded.shape[0], rows * cols)
            result.append(lax.dot_general(cotangent, window, (((1,), (1,)), ((), ())), preferred_element_type=jnp.float32))
    return jnp.stack(result)

def conv_back_terms(weight_cols, cotangent, dilation, rows, cols):
    summed = jnp.zeros((weight_cols.shape[2], rows + 2 * dilation, cols + 2 * dilation), jnp.float32)
    for row_tap in range(3):
        for col_tap in range(3):
            term = lax.dot_general(weight_cols[3 * row_tap + col_tap], cotangent, (((0,), (0,)), ((), ())), preferred_element_type=jnp.float32).reshape(weight_cols.shape[2], rows, cols)
            summed = summed + jnp.pad(term, ((0, 0), (row_tap * dilation, 2 * dilation - row_tap * dilation), (col_tap * dilation, 2 * dilation - col_tap * dilation)))
    return summed

def quarter_parts(values, rows, cols):
    blocks = values.reshape(values.shape[0], rows, 2, cols, 2)
    return [blocks[:, :, row_tap, :, col_tap].reshape(values.shape[0], rows * cols) for row_tap in range(2) for col_tap in range(2)]

def down_conv(weights, values, rows, cols):
    parts_list = quarter_parts(values, rows, cols)
    summed = jnp.dot(weights[0], parts_list[0], preferred_element_type=jnp.float32)
    for quarter in range(1, 4):
        summed = summed + jnp.dot(weights[quarter], parts_list[quarter], preferred_element_type=jnp.float32)
    return summed

def down_grads(cotangent, values, rows, cols):
    parts_list = quarter_parts(values, rows, cols)
    return jnp.stack([lax.dot_general(cotangent, piece_part, (((1,), (1,)), ((), ())), preferred_element_type=jnp.float32) for piece_part in parts_list])

def down_back(weight_cols, cotangent, rows, cols):
    stacked = jnp.stack([lax.dot_general(weight_cols[quarter], cotangent, (((0,), (0,)), ((), ())), preferred_element_type=jnp.float32) for quarter in range(4)])
    chans = weight_cols.shape[2]
    return stacked.reshape(2, 2, chans, rows, cols).transpose(2, 3, 0, 4, 1).reshape(chans, 4 * rows * cols)

def up_copy(values, rows, cols):
    chans = values.shape[0]
    grown = jnp.broadcast_to(values.reshape(chans, rows, 1, cols, 1), (chans, rows, 2, cols, 2))
    return grown.reshape(chans, 4 * rows * cols)

def pool_cells(cotangent, rows, cols):
    chans = cotangent.shape[0]
    return cotangent.astype(jnp.float32).reshape(chans, rows, 2, cols, 2).sum(axis=(2, 4)).reshape(chans, rows * cols)

def gelu_back(preact, cotangent):
    return jax.vjp(jax.nn.gelu, preact)[1](cotangent)[0]

def pad_transpose(cotangent, chans, half_len):
    zero_center = jnp.zeros((chans, half_len, half_len), jnp.float32)
    zero_picked = jnp.zeros((8, chans, 1, half_len), jnp.float32)

    def padding(center, picked):
        return pad_block(center, picked, 1)
    _, pullback = jax.vjp(padding, zero_center, zero_picked)
    return pullback(cotangent)

def rims_transpose(returned, chans, half_len):
    zero_center = jnp.zeros((chans, half_len, half_len), jnp.float32)

    def rimming(center):
        return build_rims(center, 1)
    _, pullback = jax.vjp(rimming, zero_center)
    return pullback(returned)[0]

def reference(features, conv1_weight, down_weight, conv2_weight, up_weight, out_grad, adjacency):
    side_len = SIDE
    half_len = side_len // 2
    tiles_x = features.reshape(C, TILES, side_len, side_len).transpose(1, 0, 2, 3)
    tiles_g = out_grad.reshape(C, TILES, side_len * side_len).transpose(1, 0, 2)
    partners = adjacency[:, :, 0]
    rim_slots = (adjacency[:, :, 1] + jnp.array(side_turns, jnp.int32)) % 4

    def fine_rims_of(center):
        return build_rims(center, 2)
    fine_rims = jax.vmap(fine_rims_of)(tiles_x)

    def padded_fine(tile_index):
        empty = jnp.zeros((8,) + fine_rims.shape[2:], fine_rims.dtype)
        picked = choose_rims(partners[tile_index], rim_slots[tile_index], empty, fine_rims, 0)
        return pad_block(tiles_x[tile_index], picked, 2)

    def forward_fine(tile_index):
        fine_all = padded_fine(tile_index)
        pre_one = conv_taps(conv1_weight, fine_all, 2, side_len, side_len)
        act_one = jax.nn.gelu(pre_one).astype(jnp.bfloat16)
        pre_two = down_conv(down_weight, act_one, half_len, half_len)
        act_two = jax.nn.gelu(pre_two).astype(jnp.bfloat16)
        return (pre_one, act_one, pre_two, act_two)
    tile_ids = jnp.arange(TILES, dtype=jnp.int32)
    pre_one, act_one, pre_two, act_two = lax.map(forward_fine, tile_ids)

    def coarse_rims_of(center):
        return build_rims(center, 1)
    coarse_rims = jax.vmap(coarse_rims_of)(act_two.reshape(TILES, C, half_len, half_len))

    def coarse_step(carry, tile_index):
        grad_conv2, grad_up = carry
        center = act_two[tile_index].reshape(C, half_len, half_len)
        empty = jnp.zeros((8,) + coarse_rims.shape[2:], coarse_rims.dtype)
        picked = choose_rims(partners[tile_index], rim_slots[tile_index], empty, coarse_rims, 0)
        coarse_all = pad_block(center, picked, 1)
        pre_three = conv_taps(conv2_weight, coarse_all, 1, half_len, half_len)
        coarse = jax.nn.gelu(pre_three).astype(jnp.bfloat16)
        lifted = jnp.dot(up_weight, coarse, preferred_element_type=jnp.float32)
        output = (act_one[tile_index].astype(jnp.float32) + up_copy(lifted, half_len, half_len)).astype(jnp.bfloat16)
        pooled = pool_cells(tiles_g[tile_index], half_len, half_len).astype(jnp.bfloat16)
        grad_up = grad_up + lax.dot_general(pooled, coarse, (((1,), (1,)), ((), ())), preferred_element_type=jnp.float32)
        back_up = lax.dot_general(up_weight, pooled, (((0,), (0,)), ((), ())), preferred_element_type=jnp.float32)
        grad_three = gelu_back(pre_three, back_up).astype(jnp.bfloat16)
        grad_conv2 = grad_conv2 + conv_grads(grad_three, coarse_all, 1, half_len, half_len)
        coarse_back = conv_back_terms(conv2_weight, grad_three, 1, half_len, half_len)
        grad_center, grad_picked = pad_transpose(coarse_back, C, half_len)
        return ((grad_conv2, grad_up), (output, grad_center, grad_picked))
    start_coarse = (jnp.zeros((9, C, C), jnp.float32), jnp.zeros((C, C), jnp.float32))
    (grad_conv2, grad_up), (outputs, grad_center, grad_picked) = lax.scan(coarse_step, start_coarse, tile_ids)
    has_partner = (partners >= 0).astype(jnp.float32)
    masked = (grad_picked * has_partner[:, :, None, None, None]).reshape(TILES * 8, C, 1, half_len)
    buffer = jnp.zeros((TILES, 4, C, 1, half_len), jnp.float32).at[jnp.clip(partners, 0, TILES - 1).reshape(-1), rim_slots.reshape(-1)].add(masked)

    def fine_step(carry, tile_index):
        grad_conv1, grad_down = carry
        grad_more = rims_transpose(buffer[tile_index], C, half_len)
        grad_act_two = (grad_center[tile_index] + grad_more).reshape(C, half_len * half_len)
        grad_two = gelu_back(pre_two[tile_index], grad_act_two).astype(jnp.bfloat16)
        grad_down = grad_down + down_grads(grad_two, act_one[tile_index], half_len, half_len)
        grad_act_one = tiles_g[tile_index].astype(jnp.float32) + down_back(down_weight, grad_two, half_len, half_len)
        grad_one = gelu_back(pre_one[tile_index], grad_act_one).astype(jnp.bfloat16)
        grad_conv1 = grad_conv1 + conv_grads(grad_one, padded_fine(tile_index), 2, side_len, side_len)
        return ((grad_conv1, grad_down), 0)
    start_fine = (jnp.zeros((9, C, C), jnp.float32), jnp.zeros((4, C, C), jnp.float32))
    (grad_conv1, grad_down), _ = lax.scan(fine_step, start_fine, tile_ids)
    grad_scale = CELLS ** (-0.5)
    output = outputs.transpose(1, 0, 2).reshape(C, CELLS)
    return (output, grad_conv1 * grad_scale, grad_down * grad_scale, grad_conv2 * grad_scale, grad_up * grad_scale)
```

```python
import functools

import jax
import jax.numpy as jnp
import numpy as np
from jax import lax
from jax.experimental import pallas as pl
from jax.experimental.pallas import tpu as pltpu
from jax.sharding import PartitionSpec as P

BF = jnp.bfloat16
F32 = jnp.float32
MESH = pl.DeviceIdType.MESH
TURNS = (0, 1, 2, 3, 0, 2, 2, 0)
VM = pl.BlockSpec(memory_space=pltpu.VMEM)
SM = pl.BlockSpec(memory_space=pltpu.SMEM)
ANY = pl.BlockSpec(memory_space=pl.ANY)
LIMIT = 56 * 1024 * 1024


def fine_perm():
    out = np.zeros((3, 128, 128), np.float32)
    for b in range(3):
        for rr in range(2):
            for par in range(2):
                for k in range(32):
                    col = 2 * (k - 1 + b) + par
                    if 0 <= col < 64:
                        out[b, rr * 64 + par * 32 + k, rr * 64 + col] = 1
    return out


def corner_maps():
    out = np.zeros((4, 128, 128), np.float32)
    for i in range(2):
        for j in range(2):
            out[0, i * 64 + j, 2 * i + j] = 1
            out[1, (1 - i) * 64 + 63 - j, 4 + 2 * i + j] = 1
            out[2, (1 - i) * 64 + 1 - j, 8 + 2 * i + j] = 1
            out[3, i * 64 + 62 + j, 12 + 2 * i + j] = 1
    return out


def fine_rim_maps():
    sel = np.zeros((4, 128, 640), np.float32)
    for q in range(4):
        for r in range(20):
            ir = 16 * q - 2 + r
            for par in range(2):
                if 0 <= ir < 64:
                    west = 384 + par * 64 + 63 - ir
                    east = 128 + (1 - par) * 64 + ir
                elif ir < 0:
                    west = 512 + 12 + 2 * (ir + 2) + par
                    east = 512 + 0 + 2 * (ir + 2) + par
                else:
                    west = 512 + 8 + 2 * (ir - 64) + par
                    east = 512 + 4 + 2 * (ir - 64) + par
                sel[q, r * 2 + par, west] = 1
                sel[q, 64 + r * 2 + par, east] = 1
    place = np.zeros((2, 1280, 128), np.float32)
    for r in range(20):
        for par in range(2):
            place[0, r * 64 + par * 32, r * 2 + par] = 1
            place[1, r * 64 + par * 32 + 31, 64 + r * 2 + par] = 1
    return sel, place


def coarse_rim_out():
    out = np.zeros((4, 256, 128), np.float32)
    for i in range(32):
        for s, (r, k) in enumerate(((31, i), (i, 0), (0, 31 - i), (31 - i, 31))):
            out[r // 8, (r % 8) * 32 + k, s * 32 + i] = 1
    return out


def coarse_rim_in():
    out = np.zeros((4, 960, 256), np.float32)
    for k in range(32):
        out[0, k, k] = 1
        out[3, 9 * 32 + k, 64 + 31 - k] = 1
    for q in range(4):
        for r in range(10):
            row = 8 * q - 1 + r
            if row < 0:
                west, east = 131, 128
            elif row >= 32:
                west, east = 130, 129
            else:
                west, east = 96 + 31 - row, 32 + row
            out[q, 320 + r * 32, west] = 1
            out[q, 640 + r * 32 + 31, east] = 1
    return out


def nt(a, b):
    return lax.dot_general(a, b, (((1,), (1,)), ((), ())), preferred_element_type=F32)


def tn(a, b):
    return lax.dot_general(a, b, (((0,), (0,)), ((), ())), preferred_element_type=F32)


def nn(a, b):
    return lax.dot_general(a, b, (((1,), (0,)), ((), ())), preferred_element_type=F32)


ROOT = 0.7978845608028654


def gelu(v):
    return 0.5 * v * (1.0 + jnp.tanh(ROOT * (v + 0.044715 * (v * v * v))))


def gelu_slope(v):
    t = jnp.tanh(ROOT * (v + 0.044715 * (v * v * v)))
    return 0.5 * (1.0 + t) + 0.5 * v * (1.0 - t * t) * (ROOT * (1.0 + 3 * 0.044715 * (v * v)))


def place_of():
    tile = lax.axis_index("tile")
    return tile, tile // 8, lax.rem(tile, 8), lax.axis_index("chan")


def x_peer(d):
    tile, _, _, x = place_of()
    return (tile, lax.rem(x + d, 4))


def z_peer(d):
    _, z, g, x = place_of()
    return (lax.rem(z + d, 8) * 8 + g, x)


def g_peer(d):
    _, z, g, x = place_of()
    return (z * 8 + lax.rem(g + d, 8), x)


def core_peer():
    tile, _, g, x = place_of()
    return (tile + 1 - 2 * lax.rem(g, 2), x)


def y_peer(d):
    _, z, g, x = place_of()
    return (z * 8 + lax.rem(g + 2 * d, 8), x)


def greet(peers):
    barrier = pltpu.get_barrier_semaphore()
    for peer in peers:
        pl.semaphore_signal(barrier, inc=1, device_id=peer, device_id_type=MESH)
    pl.semaphore_wait(barrier, len(peers))


def push(src, dst, ssem, rsem, peer):
    copy = pltpu.make_async_remote_copy(
        src_ref=src, dst_ref=dst, send_sem=ssem, recv_sem=rsem, device_id=peer, device_id_type=MESH
    )
    copy.start()
    return copy


def strips_kernel(table, feat, ograd, rims, w1, wd, w2, up, cmap,
                  f_out, g_out, w1_out, wd_out, w2_out, up_out, d_out,
                  held, slots, landed, lsem, xs, xr, zs, zr, gs, gr, ds, dr):
    tile, z, g, x = place_of()
    greet([x_peer(d) for d in (1, 2, 3)] + [z_peer(d) for d in range(1, 8)] + [g_peer(d) for d in range(1, 8)])
    mine = pl.ds(pl.multiple_of(x * 32, 32), 32)

    def pieces(j):
        start = pl.multiple_of(jnp.clip(j * 1024 - 128, 0, 2816), 128)
        lane = pl.multiple_of(j * 1024, 1024)
        return (
            (feat.at[:, pl.ds(start, 1280)], f_out.at[mine, :]),
            (w1, w1_out.at[:, mine, :]),
            (wd, wd_out.at[:, mine, :]),
            (ograd.at[:, pl.ds(lane, 1024)], g_out.at[mine, :]),
            (w2, w2_out.at[:, mine, :]),
            (up, up_out.at[mine, :]),
        )

    zc = [push(rims, held.at[pl.ds(z * 4, 4)], zs.at[d], zr.at[d], z_peer(d)) for d in range(1, 8)]
    own = pltpu.make_async_copy(rims, held.at[pl.ds(z * 4, 4)], lsem.at[6])
    own.start()
    xc, lc = [], []
    for n in range(6):
        for d in (1, 3, 2):
            src, dst = pieces(lax.rem(x + d, 4))[n]
            xc.append(push(src, dst, xs.at[n, d], xr.at[n, d], x_peer(d)))
        src, dst = pieces(x)[n]
        copy = pltpu.make_async_copy(src, dst, lsem.at[n])
        copy.start()
        lc.append(copy)
    own.wait()
    for c in zc:
        c.wait()
    gc = []
    for d in (1, 2, 3, 4, 5, 6, 7, 0):
        j = lax.rem(g + d, 8)
        corner = jnp.zeros((32, 128), F32)
        for k in range(8):
            v = table[j * 8 + k]
            block = held[jnp.maximum(v, 0)]
            block = jnp.where(v >= 0, block, jnp.zeros_like(block))
            if k < 4:
                slots[d, :, k * 128:(k + 1) * 128] = block
            else:
                corner = corner + nn(block, cmap[k - 4])
        slots[d, :, 512:640] = corner.astype(BF)
        if d:
            gc.append(push(slots.at[d], landed.at[d], gs.at[d], gr.at[d], g_peer(d)))
    for c in gc:
        c.wait()
    total = slots[0].astype(F32)
    for d in range(1, 8):
        total = total + landed[d].astype(F32)
    d_out[mine, :] = total.astype(BF)
    dc = [push(d_out.at[mine, :], d_out.at[mine, :], ds.at[d], dr.at[d], x_peer(d)) for d in (1, 3, 2)]
    for c in lc:
        c.wait()
    for c in xc:
        c.wait()
    for c in dc:
        c.wait()


def strips_call(table, feat, ograd, rims, w1, wd, w2, up, cmap):
    dma = pltpu.SemaphoreType.DMA
    return pl.pallas_call(
        strips_kernel,
        out_shape=(
            jax.ShapeDtypeStruct((128, 1280), BF),
            jax.ShapeDtypeStruct((128, 1024), BF),
            jax.ShapeDtypeStruct((9, 128, 128), BF),
            jax.ShapeDtypeStruct((4, 128, 128), BF),
            jax.ShapeDtypeStruct((9, 128, 128), BF),
            jax.ShapeDtypeStruct((128, 128), BF),
            jax.ShapeDtypeStruct((128, 640), BF),
        ),
        in_specs=[SM, ANY, ANY, VM, VM, VM, VM, VM, VM],
        out_specs=[VM] * 7,
        scratch_shapes=[
            pltpu.VMEM((32, 32, 128), BF),
            pltpu.VMEM((8, 32, 640), BF),
            pltpu.VMEM((8, 32, 640), BF),
            dma((7,)), dma((6, 4)), dma((6, 4)), dma((8,)), dma((8,)), dma((8,)), dma((8,)), dma((4,)), dma((4,)),
        ],
        compiler_params=pltpu.CompilerParams(collective_id=0, has_side_effects=True, vmem_limit_bytes=LIMIT),
    )(table, feat, ograd, rims, w1, wd, w2, up, cmap)


def taps_of(blocks, step, start, count):
    return jnp.concatenate(
        [blocks[b, pl.ds(a * step + start, count), :] for a in range(3) for b in range(3)], axis=1
    )


def side_by_side(weights, count):
    return jnp.concatenate([weights[t] for t in range(count)], axis=1)


def quarters(act):
    parts = act.reshape(8, 2, 2, 32, 128)
    return jnp.concatenate(
        [parts[:, a, b].reshape(256, 128) for a in range(2) for b in range(2)], axis=1
    )


def fine_kernel(f_ref, d_ref, w1, wd, perm, sel, place, rimout,
                cb, z1_ref, act1_ref, z2_ref, act2_ref, rq_ref):
    q = lax.axis_index("chan")
    shift = jnp.where(q == 0, -1, jnp.where(q == 3, 1, 0))
    perms = perm[...].reshape(384, 128)
    rim_rows = nt(sel[q], d_ref[...]).astype(BF)
    flip = (
        lax.broadcasted_iota(jnp.int32, (128, 128), 0) + lax.broadcasted_iota(jnp.int32, (128, 128), 1) == 127
    ).astype(F32).astype(BF)
    for n in range(10):
        at = jnp.clip(n + shift, 0, 9)
        block = f_ref[:, pl.ds(pl.multiple_of(at * 128, 128), 128)]
        if n == 0:
            block = jnp.where(q == 0, d_ref[:, 0:128], block)
        if n == 9:
            block = jnp.where(q == 3, nn(d_ref[:, 256:384], flip).astype(BF), block)
        turned = nt(perms, block)
        rows = pl.ds(n * 128, 128)
        cb[0, rows, :] = (turned[0:128] + nn(place[0, rows, :], rim_rows)).astype(BF)
        cb[1, rows, :] = turned[128:256].astype(BF)
        cb[2, rows, :] = (turned[256:384] + nn(place[1, rows, :], rim_rows)).astype(BF)
    w1c = side_by_side(w1, 9)
    for n in range(4):
        rows = pl.ds(n * 256, 256)
        pre = nt(taps_of(cb, 128, n * 256, 256), w1c)
        z1_ref[rows, :] = pre
        act1_ref[rows, :] = gelu(pre).astype(BF)
    pre = nt(quarters(act1_ref[...]), side_by_side(wd, 4))
    z2_ref[...] = pre
    act = gelu(pre).astype(BF)
    act2_ref[...] = act
    rq_ref[...] = tn(act, rimout[q]).astype(BF)


def fine_call(*args):
    return pl.pallas_call(
        fine_kernel,
        out_shape=(
            jax.ShapeDtypeStruct((3, 1280, 128), BF),
            jax.ShapeDtypeStruct((1024, 128), F32),
            jax.ShapeDtypeStruct((1024, 128), BF),
            jax.ShapeDtypeStruct((256, 128), F32),
            jax.ShapeDtypeStruct((256, 128), BF),
            jax.ShapeDtypeStruct((128, 128), BF),
        ),
        in_specs=[VM] * 8,
        out_specs=[VM] * 6,
        compiler_params=pltpu.CompilerParams(vmem_limit_bytes=LIMIT),
    )(*args)


def wanted(target, j):
    rows = lax.broadcasted_iota(jnp.int32, (1024, 256), 0)
    return jnp.where(rows == target[pl.ds(j, 1), :], 1.0, 0.0).astype(BF)


def coarse_rims_kernel(target, rq, act2, d_out, top, bottom,
                       xbuf, held, slots, landed, xs, xr, hs, hr, zs, zr, gs, gr, ds, dr):
    tile, z, g, x = place_of()
    greet([x_peer(d) for d in (1, 2, 3)] + [z_peer(d) for d in range(1, 8)] + [g_peer(d) for d in range(1, 8)])
    mine = pl.ds(pl.multiple_of(x * 32, 32), 32)
    xc = []
    for d in (1, 3, 2):
        theirs = pl.ds(pl.multiple_of(lax.rem(x + d, 4) * 32, 32), 32)
        xc.append(push(rq.at[theirs, :], xbuf.at[d], xs.at[d], xr.at[d], x_peer(d)))
    hc = [
        push(act2.at[pl.ds(224, 32), :], top, hs.at[0], hr.at[0], x_peer(1)),
        push(act2.at[pl.ds(0, 32), :], bottom, hs.at[1], hr.at[1], x_peer(3)),
    ]
    total = rq[mine, :].astype(F32)
    for c in xc:
        c.wait()
    for d in (1, 2, 3):
        total = total + xbuf[d].astype(F32)
    held[z] = total.astype(BF)
    zc = [push(held.at[z], held.at[z], zs.at[d], zr.at[d], z_peer(d)) for d in range(1, 8)]
    for c in zc:
        c.wait()
    every = jnp.concatenate([held[n] for n in range(8)], axis=1)
    gc = []
    for d in (1, 2, 3, 4, 5, 6, 7, 0):
        j = lax.rem(g + d, 8)
        slots[d] = nn(every, wanted(target, j)).astype(BF)
        if d:
            gc.append(push(slots.at[d], landed.at[d], gs.at[d], gr.at[d], g_peer(d)))
    for c in gc:
        c.wait()
    total = slots[0].astype(F32)
    for d in range(1, 8):
        total = total + landed[d].astype(F32)
    d_out[mine, :] = total.astype(BF)
    dc = [push(d_out.at[mine, :], d_out.at[mine, :], ds.at[d], dr.at[d], x_peer(d)) for d in (1, 3, 2)]
    for c in hc:
        c.wait()
    for c in dc:
        c.wait()


def coarse_rims_call(target, rq, act2):
    dma = pltpu.SemaphoreType.DMA
    return pl.pallas_call(
        coarse_rims_kernel,
        out_shape=(
            jax.ShapeDtypeStruct((128, 256), BF),
            jax.ShapeDtypeStruct((32, 128), BF),
            jax.ShapeDtypeStruct((32, 128), BF),
        ),
        in_specs=[VM] * 3,
        out_specs=[VM] * 3,
        scratch_shapes=[
            pltpu.VMEM((4, 32, 128), BF),
            pltpu.VMEM((8, 32, 128), BF),
            pltpu.VMEM((8, 32, 256), BF),
            pltpu.VMEM((8, 32, 256), BF),
            dma((4,)), dma((4,)), dma((2,)), dma((2,)), dma((8,)), dma((8,)), dma((8,)), dma((8,)), dma((4,)), dma((4,)),
        ],
        compiler_params=pltpu.CompilerParams(collective_id=1, has_side_effects=True, vmem_limit_bytes=LIMIT),
    )(target, rq, act2)


def coarse_kernel(act2, d_ref, top, bottom, w2, up, og, act1, perm, rimin,
                  out_ref, ogt, center, first, last, dq, grads):
    q = lax.axis_index("chan")
    sel = rimin[q]
    rim = nt(sel, d_ref[...])
    upper = jnp.where(q == 0, 0.0, top[...].astype(F32))
    lower = jnp.where(q == 3, 0.0, bottom[...].astype(F32))
    rows = jnp.concatenate([upper, act2[...].astype(F32), lower], axis=0) + rim[0:320]
    col = lax.rem(lax.broadcasted_iota(jnp.int32, (320, 128), 0), 32)
    west = jnp.where(col == 0, 0.0, pltpu.roll(rows, 1, 0)) + rim[320:640]
    east = jnp.where(col == 31, 0.0, pltpu.roll(rows, 319, 0)) + rim[640:960]
    blocks = [v.astype(BF) for v in (west, rows, east)]
    taps = jnp.concatenate([blocks[b][a * 32:a * 32 + 256] for a in range(3) for b in range(3)], axis=1)
    pre = nt(taps, side_by_side(w2, 9))
    coarse = gelu(pre).astype(BF)
    lifted = nt(coarse, up[...])
    flat = perm[1]
    for n in range(8):
        turned = nt(flat, og[:, n * 128:(n + 1) * 128])
        ogt[n * 128:(n + 1) * 128, :] = turned.astype(BF)
        row = lifted[n * 32:(n + 1) * 32]
        summed = act1[n * 128:(n + 1) * 128, :].astype(F32) + jnp.concatenate([row] * 4, axis=0)
        out_ref[:, n * 128:(n + 1) * 128] = tn(summed.astype(BF), flat).astype(BF)
    cells = ogt[...].astype(F32).reshape(8, 4, 32, 128)
    pooled = (cells[:, 0] + cells[:, 1] + cells[:, 2] + cells[:, 3]).reshape(256, 128).astype(BF)
    grads[:, 1152:1280] = tn(pooled, coarse)
    gz3 = (gelu_slope(pre) * nn(pooled, up[...])).astype(BF)
    grads[:, 0:1152] = tn(gz3, taps)
    none32, none64 = jnp.zeros((32, 128), F32), jnp.zeros((64, 128), F32)
    back = []
    for b in range(3):
        v0, v1, v2 = (nn(gz3, w2[3 * a + b]) for a in range(3))
        back.append(
            jnp.concatenate([v0, none64], axis=0)
            + jnp.concatenate([none32, v1, none32], axis=0)
            + jnp.concatenate([none64, v2], axis=0)
        )
    mid = (
        back[1]
        + jnp.where(col == 31, 0.0, pltpu.roll(back[0], 319, 0))
        + jnp.where(col == 0, 0.0, pltpu.roll(back[2], 1, 0))
    )
    center[...] = mid[32:288]
    first[...] = mid[0:32]
    last[...] = mid[288:320]
    cat = jnp.concatenate([mid.astype(BF), back[0].astype(BF), back[2].astype(BF)], axis=0)
    dq[...] = tn(cat, sel).astype(BF)


def coarse_call(*args):
    return pl.pallas_call(
        coarse_kernel,
        out_shape=(
            jax.ShapeDtypeStruct((128, 1024), BF),
            jax.ShapeDtypeStruct((1024, 128), BF),
            jax.ShapeDtypeStruct((256, 128), F32),
            jax.ShapeDtypeStruct((32, 128), F32),
            jax.ShapeDtypeStruct((32, 128), F32),
            jax.ShapeDtypeStruct((128, 256), BF),
            jax.ShapeDtypeStruct((128, 1280), F32),
        ),
        in_specs=[VM] * 10,
        out_specs=[VM] * 7,
        compiler_params=pltpu.CompilerParams(vmem_limit_bytes=LIMIT),
    )(*args)


def back_rims_kernel(target, dq, first, last, strip, t_out, top, bottom, out,
                     xbuf, held, slots, landed, osem, xs, xr, hs, hr, zs, zr, gs, gr, ds, dr, os, orr):
    tile, z, g, x = place_of()
    greet([x_peer(d) for d in (1, 2, 3)] + [z_peer(d) for d in range(1, 8)] + [g_peer(d) for d in range(1, 8)])
    mine = pl.ds(pl.multiple_of(x * 32, 32), 32)
    xc = []
    for d in (1, 3, 2):
        theirs = pl.ds(pl.multiple_of(lax.rem(x + d, 4) * 32, 32), 32)
        xc.append(push(dq.at[theirs, :], xbuf.at[d], xs.at[d], xr.at[d], x_peer(d)))
    hc = [
        push(last, top, hs.at[0], hr.at[0], x_peer(1)),
        push(first, bottom, hs.at[1], hr.at[1], x_peer(3)),
    ]
    lanes = pl.ds(pl.multiple_of(x * 1024, 1024), 1024)
    oc = []
    for d in (1, 3, 2):
        theirs = pl.ds(pl.multiple_of(lax.rem(x + d, 4) * 32, 32), 32)
        oc.append(push(strip.at[theirs, :], out.at[:, lanes], os.at[d], orr.at[d], x_peer(d)))
    own = pltpu.make_async_copy(strip.at[mine, :], out.at[:, lanes], osem)
    own.start()
    total = dq[mine, :].astype(F32)
    for c in xc:
        c.wait()
    for d in (1, 2, 3):
        total = total + xbuf[d].astype(F32)
    held[g] = total.astype(BF)
    gc = [push(held.at[g], held.at[g], gs.at[d], gr.at[d], g_peer(d)) for d in range(1, 8)]
    for c in gc:
        c.wait()
    total = nt(held[0], wanted(target, 0))
    for j in range(1, 8):
        total = total + nt(held[j], wanted(target, j))
    for n in range(8):
        slots[n] = total[:, n * 128:(n + 1) * 128]
    zc = [push(slots.at[lax.rem(z + d, 8)], landed.at[d], zs.at[d], zr.at[d], z_peer(d)) for d in range(1, 8)]
    for c in zc:
        c.wait()
    total = slots[z]
    for d in range(1, 8):
        total = total + landed[d]
    t_out[mine, :] = total
    dc = [push(t_out.at[mine, :], t_out.at[mine, :], ds.at[d], dr.at[d], x_peer(d)) for d in (1, 3, 2)]
    for c in hc:
        c.wait()
    for c in oc:
        c.wait()
    own.wait()
    for c in dc:
        c.wait()


def back_rims_call(target, dq, first, last, strip):
    dma = pltpu.SemaphoreType.DMA
    return pl.pallas_call(
        back_rims_kernel,
        out_shape=(
            jax.ShapeDtypeStruct((128, 128), F32),
            jax.ShapeDtypeStruct((32, 128), F32),
            jax.ShapeDtypeStruct((32, 128), F32),
            jax.ShapeDtypeStruct((32, 4096), BF),
        ),
        in_specs=[VM] * 5,
        out_specs=[VM] * 4,
        scratch_shapes=[
            pltpu.VMEM((4, 32, 256), BF),
            pltpu.VMEM((8, 32, 256), BF),
            pltpu.VMEM((8, 32, 128), F32),
            pltpu.VMEM((8, 32, 128), F32),
            dma, dma((4,)), dma((4,)), dma((2,)), dma((2,)), dma((8,)), dma((8,)), dma((8,)), dma((8,)),
            dma((4,)), dma((4,)), dma((4,)), dma((4,)),
        ],
        compiler_params=pltpu.CompilerParams(collective_id=2, has_side_effects=True, vmem_limit_bytes=LIMIT),
    )(target, dq, first, last, strip)


def fine_back_kernel(center, t_ref, top, bottom, z2, z1, act1, ogt, cb, wd, rimout, grads):
    q = lax.axis_index("chan")
    rim = t_ref[...]
    high = rim.astype(BF)
    low = (rim - high.astype(F32)).astype(BF)
    sel = rimout[q]
    upper = jnp.where(q == 0, 0.0, top[...])
    lower = jnp.where(q == 3, 0.0, bottom[...])
    middle = jnp.zeros((192, 128), F32)
    ga2 = center[...] + jnp.concatenate([upper, middle, lower], axis=0) + nt(sel, high) + nt(sel, low)
    gz2 = (gelu_slope(z2[...]) * ga2).astype(BF)
    grads[:, 1152:1664] = tn(gz2, quarters(act1[...]))
    fine = [nn(gz2, wd[t]).reshape(8, 1, 32, 128) for t in range(4)]
    spread = jnp.concatenate(fine, axis=1).reshape(1024, 128)
    gz1 = (gelu_slope(z1[...]) * (ogt[...].astype(F32) + spread)).astype(BF)
    for a in range(3):
        for b in range(3):
            t = 3 * a + b
            grads[:, t * 128:(t + 1) * 128] = tn(gz1, cb[b, a * 128:a * 128 + 1024, :])


def fine_back_call(*args):
    return pl.pallas_call(
        fine_back_kernel,
        out_shape=jax.ShapeDtypeStruct((128, 1664), F32),
        in_specs=[VM] * 11,
        out_specs=VM,
        compiler_params=pltpu.CompilerParams(vmem_limit_bytes=LIMIT),
    )(*args)


WIDE = 3072


def sums_kernel(fine, coarse, g1_out, gd_out, g2_out, gu_out,
                cout, cin, xout, xin, zout, zin, yin, full, final,
                cs, cr, xs, xr, zs, zr, ys, yr, as_, ar, fs, fr, scale):
    tile, z, g, x = place_of()
    y, core = g // 2, lax.rem(g, 2)
    greet(
        [core_peer()] + [x_peer(d) for d in (1, 2, 3)]
        + [z_peer(d) for d in range(1, 8)] + [y_peer(d) for d in (1, 2, 3)]
    )
    other = 1 - core
    cout[:, :, 0:1664] = fine[:, pl.ds(other, 1)].reshape(4, 16, 1664).astype(BF)
    cout[:, :, 1664:2944] = coarse[:, pl.ds(other, 1)].reshape(4, 16, 1280).astype(BF)
    cout[:, :, 2944:3072] = jnp.zeros((4, 16, 128), BF)
    cc = push(cout, cin, cs, cr, core_peer())
    cc.wait()
    xout[:, :, 0:1664] = (fine[:, pl.ds(core, 1)].reshape(4, 16, 1664) + cin[:, :, 0:1664].astype(F32)).astype(BF)
    xout[:, :, 1664:2944] = (coarse[:, pl.ds(core, 1)].reshape(4, 16, 1280) + cin[:, :, 1664:2944].astype(F32)).astype(BF)
    xout[:, :, 2944:3072] = jnp.zeros((4, 16, 128), BF)
    xc = [push(xout.at[lax.rem(x + d, 4)], xin.at[d], xs.at[d], xr.at[d], x_peer(d)) for d in (1, 3, 2)]
    for c in xc:
        c.wait()
    total = xout[x].astype(F32)
    for d in (1, 2, 3):
        total = total + xin[d].astype(F32)
    for n in range(8):
        zout[n] = total[:, n * 384:(n + 1) * 384].astype(BF)
    zc = [push(zout.at[lax.rem(z + d, 8)], zin.at[d], zs.at[d], zr.at[d], z_peer(d)) for d in range(1, 8)]
    for c in zc:
        c.wait()
    total = zout[z].astype(F32)
    for d in range(1, 8):
        total = total + zin[d].astype(F32)
    yin[y] = total
    yc = [push(yin.at[y], yin.at[y], ys.at[d], yr.at[d], y_peer(d)) for d in (1, 3, 2)]
    for c in yc:
        c.wait()
    full[z] = (((yin[0] + yin[1]) + (yin[2] + yin[3])) * scale).astype(BF)
    ac = [push(full.at[z], full.at[z], as_.at[d], ar.at[d], z_peer(d)) for d in range(1, 8)]
    for c in ac:
        c.wait()
    for n in range(8):
        final[pl.ds(core, 1), :, n * 384:(n + 1) * 384] = full[n].reshape(1, 16, 384)
    fc = push(final.at[core], final.at[core], fs, fr, core_peer())
    fc.wait()
    for c in range(2):
        rows = pl.ds(c * 16, 16)
        for t in range(23):
            block = final[c, :, t * 128:(t + 1) * 128].astype(F32)
            if t < 9:
                g1_out[t, rows, :] = block
            elif t < 13:
                gd_out[t - 9, rows, :] = block
            elif t < 22:
                g2_out[t - 13, rows, :] = block
            else:
                gu_out[rows, :] = block


def sums_call(fine, coarse, scale):
    dma = pltpu.SemaphoreType.DMA
    return pl.pallas_call(
        functools.partial(sums_kernel, scale=scale),
        out_shape=(
            jax.ShapeDtypeStruct((9, 32, 128), F32),
            jax.ShapeDtypeStruct((4, 32, 128), F32),
            jax.ShapeDtypeStruct((9, 32, 128), F32),
            jax.ShapeDtypeStruct((32, 128), F32),
        ),
        in_specs=[VM] * 2,
        out_specs=[VM] * 4,
        scratch_shapes=[
            pltpu.VMEM((4, 16, WIDE), BF),
            pltpu.VMEM((4, 16, WIDE), BF),
            pltpu.VMEM((4, 16, WIDE), BF),
            pltpu.VMEM((4, 16, WIDE), BF),
            pltpu.VMEM((8, 16, 384), BF),
            pltpu.VMEM((8, 16, 384), BF),
            pltpu.VMEM((4, 16, 384), F32),
            pltpu.VMEM((8, 16, 384), BF),
            pltpu.VMEM((2, 16, WIDE), BF),
            dma, dma, dma((4,)), dma((4,)), dma((8,)), dma((8,)), dma((4,)), dma((4,)), dma((8,)), dma((8,)), dma, dma,
        ],
        compiler_params=pltpu.CompilerParams(collective_id=3, has_side_effects=True, vmem_limit_bytes=LIMIT),
    )(fine, coarse)


def build_rims(center, width):
    side_len = center.shape[1]
    turned = functools.partial(jnp.rot90, axes=(1, 2))
    return jnp.stack(
        [
            center[:, side_len - width:, :],
            turned(center[:, :, :width], 1),
            turned(center[:, :width, :], 2),
            turned(center[:, :, side_len - width:], 3),
        ]
    )


def per_device(features, conv1_weight, down_weight, conv2_weight, up_weight, out_grad, adjacency):
    tile = lax.axis_index("tile")
    z, g = tile // 8, tile % 8
    rows = lax.dynamic_slice_in_dim(adjacency, z * 8, 8, 0)
    partner = rows[:, :, 0]
    slot = (rows[:, :, 1] + jnp.array(TURNS, jnp.int32)) % 4
    owned = (partner >= 0) & (partner % 8 == g)
    from_z = partner // 8
    table = jnp.where(owned, from_z * 4 + slot, -1).reshape(64)
    base = from_z * 128 + slot * 32
    sides = jnp.where(owned[:, :4, None], base[:, :4, None] + jnp.arange(32, dtype=jnp.int32), -1).reshape(8, 128)
    corners = jnp.where(owned[:, 4:], base[:, 4:] + jnp.array((0, 31, 0, 31), jnp.int32), -1)
    target = jnp.concatenate([sides, corners, jnp.full((8, 124), -1, jnp.int32)], axis=1)

    as_map = lambda m: jnp.asarray(m, BF)
    perm = as_map(fine_perm())
    fine_sel, fine_place = (as_map(m) for m in fine_rim_maps())
    rim_out, rim_in = as_map(coarse_rim_out()), as_map(coarse_rim_in())

    rims = build_rims(features.reshape(32, 64, 64), 2).reshape(4, 32, 128)
    strip, og, w1, wd, w2, up, picked = strips_call(
        table, features, out_grad, rims, conv1_weight, down_weight, conv2_weight, up_weight, as_map(corner_maps())
    )
    cb, z1, act1, z2, act2, rq = fine_call(strip, picked, w1, wd, perm, fine_sel, fine_place, rim_out)
    picked2, top, bottom = coarse_rims_call(target, rq, act2)
    out_strip, ogt, center, first, last, dq, grads_b = coarse_call(
        act2, picked2, top, bottom, w2, up, og, act1, perm, rim_in
    )
    back, top_back, bottom_back, output = back_rims_call(target, dq, first, last, out_strip)
    grads_a = fine_back_call(center, back, top_back, bottom_back, z2, z1, act1, ogt, cb, wd, rim_out)
    g1, gd, g2, gu = sums_call(
        grads_a.reshape(4, 2, 16, 1664), grads_b.reshape(4, 2, 16, 1280), 262144 ** -0.5
    )
    return output, g1, gd, g2, gu


def solution(mesh):
    weights = P(None, "chan", None)
    return jax.shard_map(
        per_device,
        mesh=mesh,
        in_specs=(P("chan", "tile"), weights, weights, weights, P("chan", None), P("chan", "tile"), P()),
        out_specs=(P("chan", "tile"), weights, weights, weights, P("chan", None)),
        check_vma=False,
    )
```

```python
import functools

import jax
import jax.numpy as jnp
import numpy as np
from jax import lax
from jax.experimental import pallas as pl
from jax.experimental.pallas import tpu as pltpu
from jax.sharding import PartitionSpec as P

BF = jnp.bfloat16
F32 = jnp.float32
MESH = pl.DeviceIdType.MESH
TURNS = (0, 1, 2, 3, 0, 2, 2, 0)
VM = pl.BlockSpec(memory_space=pltpu.VMEM)
SM = pl.BlockSpec(memory_space=pltpu.SMEM)
ANY = pl.BlockSpec(memory_space=pl.ANY)
LIMIT = 56 * 1024 * 1024


def fine_perm():
    out = np.zeros((3, 128, 128), np.float32)
    for b in range(3):
        for rr in range(2):
            for par in range(2):
                for k in range(32):
                    col = 2 * (k - 1 + b) + par
                    if 0 <= col < 64:
                        out[b, rr * 64 + par * 32 + k, rr * 64 + col] = 1
    return out


def corner_maps():
    out = np.zeros((4, 128, 128), np.float32)
    for i in range(2):
        for j in range(2):
            out[0, i * 64 + j, 2 * i + j] = 1
            out[1, (1 - i) * 64 + 63 - j, 4 + 2 * i + j] = 1
            out[2, (1 - i) * 64 + 1 - j, 8 + 2 * i + j] = 1
            out[3, i * 64 + 62 + j, 12 + 2 * i + j] = 1
    return out


def fine_rim_maps():
    sel = np.zeros((4, 128, 640), np.float32)
    for q in range(4):
        for r in range(20):
            ir = 16 * q - 2 + r
            for par in range(2):
                if 0 <= ir < 64:
                    west = 384 + par * 64 + 63 - ir
                    east = 128 + (1 - par) * 64 + ir
                elif ir < 0:
                    west = 512 + 12 + 2 * (ir + 2) + par
                    east = 512 + 0 + 2 * (ir + 2) + par
                else:
                    west = 512 + 8 + 2 * (ir - 64) + par
                    east = 512 + 4 + 2 * (ir - 64) + par
                sel[q, r * 2 + par, west] = 1
                sel[q, 64 + r * 2 + par, east] = 1
    place = np.zeros((2, 1280, 128), np.float32)
    for r in range(20):
        for par in range(2):
            place[0, r * 64 + par * 32, r * 2 + par] = 1
            place[1, r * 64 + par * 32 + 31, 64 + r * 2 + par] = 1
    return sel, place


def fine_rim_out():
    pick = np.zeros((1024, 128), np.float32)
    for r in range(16):
        for kind, col in enumerate((0, 1, 62, 63)):
            pick[r * 64 + col, kind * 16 + r] = 1
    put = np.zeros((4, 128, 256), np.float32)
    for s in range(4):
        for r16 in range(16):
            r = 16 * s + r16
            for kind, lane in enumerate((64 + r, r, 128 + 63 - r, 192 + 63 - r)):
                put[s, kind * 16 + r16, lane] = 1
    return pick, put


def coarse_rim_out():
    out = np.zeros((4, 256, 128), np.float32)
    for i in range(32):
        for s, (r, k) in enumerate(((31, i), (i, 0), (0, 31 - i), (31 - i, 31))):
            out[r // 8, (r % 8) * 32 + k, s * 32 + i] = 1
    return out


def coarse_rim_in():
    out = np.zeros((4, 960, 256), np.float32)
    for k in range(32):
        out[0, k, k] = 1
        out[3, 9 * 32 + k, 64 + 31 - k] = 1
    for q in range(4):
        for r in range(10):
            row = 8 * q - 1 + r
            if row < 0:
                west, east = 131, 128
            elif row >= 32:
                west, east = 130, 129
            else:
                west, east = 96 + 31 - row, 32 + row
            out[q, 320 + r * 32, west] = 1
            out[q, 640 + r * 32 + 31, east] = 1
    return out


def nt(a, b):
    return lax.dot_general(a, b, (((1,), (1,)), ((), ())), preferred_element_type=F32)


def tn(a, b):
    return lax.dot_general(a, b, (((0,), (0,)), ((), ())), preferred_element_type=F32)


def nn(a, b):
    return lax.dot_general(a, b, (((1,), (0,)), ((), ())), preferred_element_type=F32)


ROOT = 0.7978845608028654


def gelu(v):
    return 0.5 * v * (1.0 + jnp.tanh(ROOT * (v + 0.044715 * (v * v * v))))


def gelu_slope(v):
    t = jnp.tanh(ROOT * (v + 0.044715 * (v * v * v)))
    return 0.5 * (1.0 + t) + 0.5 * v * (1.0 - t * t) * (ROOT * (1.0 + 3 * 0.044715 * (v * v)))


def place_of():
    tile = lax.axis_index("tile")
    return tile, tile // 8, lax.rem(tile, 8), lax.axis_index("chan")


def x_peer(d):
    tile, _, _, x = place_of()
    return (tile, lax.rem(x + d, 4))


def z_peer(d):
    _, z, g, x = place_of()
    return (lax.rem(z + d, 8) * 8 + g, x)


def g_peer(d):
    _, z, g, x = place_of()
    return (z * 8 + lax.rem(g + d, 8), x)


def core_peer():
    tile, _, g, x = place_of()
    return (tile + 1 - 2 * lax.rem(g, 2), x)


def xy_peer(dx, dy):
    _, z, g, x = place_of()
    return (z * 8 + lax.rem(g + 2 * dy, 8), lax.rem(x + dx, 4))


def greet(peers):
    barrier = pltpu.get_barrier_semaphore()
    for peer in peers:
        pl.semaphore_signal(barrier, inc=1, device_id=peer, device_id_type=MESH)
    pl.semaphore_wait(barrier, len(peers))


def push(src, dst, ssem, rsem, peer):
    copy = pltpu.make_async_remote_copy(
        src_ref=src, dst_ref=dst, send_sem=ssem, recv_sem=rsem, device_id=peer, device_id_type=MESH
    )
    copy.start()
    return copy


AW, BW = 2048, 1536
XD = (1, 3, 2)
ZD = (4, 3, 5, 2, 6, 1, 7)
GD = (4, 3, 5, 2, 6, 1, 7)
XYD = [(dx, dy) for dx in range(4) for dy in range(4) if dx or dy]


def side_by_side(weights, count):
    return jnp.concatenate([weights[t] for t in range(count)], axis=1)


def quarters(act):
    parts = act.reshape(8, 2, 2, 32, 128)
    return jnp.concatenate(
        [parts[:, a, b].reshape(256, 128) for a in range(2) for b in range(2)], axis=1
    )


def flip_map():
    rows = lax.broadcasted_iota(jnp.int32, (128, 128), 0)
    cols = lax.broadcasted_iota(jnp.int32, (128, 128), 1)
    return jnp.where(rows + cols == 127, 1.0, 0.0).astype(BF)


def level_kernel(*refs):
    names = INPUTS + ("out", "final") + tuple(n for n, _ in SCRATCH)
    r = dict(zip(names, refs))
    tile, z, g, x = place_of()
    y, core = g // 2, lax.rem(g, 2)
    q = x
    adj = r["adj"]
    mine = pl.ds(pl.multiple_of(x * 32, 32), 32)

    def rows_of(n):
        return pl.ds(pl.multiple_of(n * 32, 32), 32)

    def local(n, src, dst):
        copy = pltpu.make_async_copy(src, dst, r["lsem"].at[n])
        copy.start()
        return copy

    own_feat = local(0, r["feat"], r["fv"])
    own = {
        "pick": local(1, r["pick"], r["v_pick"]),
        "put": local(2, r["put"], r["v_put"]),
        "perm": local(3, r["perm"], r["v_perm"]),
        "cmap": local(4, r["cmap"], r["v_cmap"]),
        "fsel": local(5, r["fsel"].at[q], r["v_fsel"]),
        "place": local(6, r["place"], r["v_place"]),
        "rout": local(7, r["rout"].at[q], r["v_rout"]),
        "rin": local(8, r["rin"].at[q], r["v_rin"]),
    }
    greet(
        [x_peer(d) for d in XD] + [z_peer(d) for d in ZD] + [g_peer(d) for d in GD]
        + [xy_peer(dx, dy) for dx, dy in XYD if dx and dy]
    )

    def piece(n, j):
        if n == 0:
            start = pl.multiple_of(jnp.clip(j * 1024 - 128, 0, 2816), 128)
            return r["feat"].at[:, pl.ds(start, 1280)], r["strip"].at[mine, :]
        if n == 3:
            return r["ograd"].at[:, pl.ds(pl.multiple_of(j * 1024, 1024), 1024)], r["og"].at[mine, :]
        if n == 5:
            return r["up"], r["v_up"].at[mine, :]
        name = {1: "w1", 2: "wd", 4: "w2"}[n]
        return r[name], r["v_" + name].at[:, mine, :]

    bulk = [[] for _ in range(6)]

    def send_bulk(n):
        for d in XD:
            src, dst = piece(n, lax.rem(x + d, 4))
            bulk[n].append(push(src, dst, r["bs"].at[n, d], r["br"].at[n, d], x_peer(d)))
        src, dst = piece(n, x)
        bulk[n].append(local(9 + n, src, dst))

    def take_bulk(n):
        for c in bulk[n]:
            c.wait()

    def spread(kind, dirs, peer, src, dst):
        return [push(src(d), dst(d), r[kind + "s"].at[d], r[kind + "r"].at[d], peer(d)) for d in dirs]

    def settle(copies):
        for c in copies:
            c.wait()

    send_bulk(0)
    send_bulk(1)

    own["pick"].wait()
    own["put"].wait()
    own_feat.wait()
    fv, held = r["fv"], r["held"]
    stacked = jnp.concatenate([fv[:, s * 1024:(s + 1) * 1024] for s in range(4)], axis=0)
    cols = nn(stacked, r["v_pick"][...]).astype(BF)
    both = nn(cols[0:32], r["v_put"][0])
    for s in range(1, 4):
        both = both + nn(cols[32 * s:32 * s + 32], r["v_put"][s])
    flip = flip_map()
    held[z * 4] = fv[:, 3968:4096]
    held[z * 4 + 1] = both[:, 0:128].astype(BF)
    held[z * 4 + 2] = nn(fv[:, 0:128], flip).astype(BF)
    held[z * 4 + 3] = both[:, 128:256].astype(BF)
    here = held.at[pl.ds(z * 4, 4)]
    c_z = spread("z1", ZD, z_peer, lambda d: here, lambda d: here)
    for n in range(2, 6):
        send_bulk(n)

    def entry(j, k):
        at = ((z * 8 + j) * 8 + k) * 2
        p = adj[at]
        s = lax.rem(adj[at + 1] + TURNS[k], 4)
        owned = jnp.logical_and(p >= 0, lax.rem(p, 8) == g)
        return owned, p // 8, s

    lane = lax.broadcasted_iota(jnp.int32, (1, 256), 1)
    depth = lax.broadcasted_iota(jnp.int32, (1024, 256), 0)
    for j in range(8):
        target = jnp.full((1, 256), -1, jnp.int32)
        for k in range(8):
            owned, zp, s = entry(j, k)
            base = jnp.where(owned, zp * 128 + s * 32, -4096)
            if k < 4:
                here_k = jnp.logical_and(lane >= 32 * k, lane < 32 * k + 32)
                target = jnp.where(here_k, base + lane - 32 * k, target)
            else:
                target = jnp.where(lane == 124 + k, base + (0, 31, 0, 31)[k - 4], target)
        r["maps"][j] = jnp.where(depth == target, 1.0, 0.0).astype(BF)

    own["perm"].wait()
    take_bulk(0)
    perm, cb, strip = r["v_perm"], r["cb"], r["strip"]
    perms = perm[...].reshape(384, 128)
    shift = jnp.where(q == 0, -1, jnp.where(q == 3, 1, 0))

    def strip_block(n):
        at = jnp.clip(n + shift, 0, 9)
        return strip[:, pl.ds(pl.multiple_of(at * 128, 128), 128)]

    for n in range(1, 9):
        turned = nt(perms, strip_block(n))
        for b in range(3):
            cb[b, n * 128:(n + 1) * 128, :] = turned[b * 128:(b + 1) * 128].astype(BF)

    own["cmap"].wait()
    settle(c_z)
    slots, landed = r["slots"], r["landed"]
    c_g = []
    for d in GD + (0,):
        j = lax.rem(g + d, 8)
        corner = jnp.zeros((32, 128), F32)
        for k in range(8):
            owned, zp, s = entry(j, k)
            block = held[jnp.where(owned, zp * 4 + s, 0)]
            block = jnp.where(owned, block, jnp.zeros_like(block))
            if k < 4:
                slots[d, :, k * 128:(k + 1) * 128] = block
            else:
                corner = corner + nn(block, r["v_cmap"][k - 4])
        slots[d, :, 512:640] = corner.astype(BF)
        if d:
            c_g += spread("g1", (d,), g_peer, lambda d: slots.at[d], lambda d: landed.at[d])
    settle(c_g)
    total = slots[0].astype(F32)
    for d in range(1, 8):
        total = total + landed[d].astype(F32)
    picked = r["picked"]
    picked[mine, :] = total.astype(BF)
    part = picked.at[mine, :]
    c_x = spread("x1", XD, x_peer, lambda d: part, lambda d: part)
    own["fsel"].wait()
    own["place"].wait()
    take_bulk(1)
    take_bulk(2)
    w1c = side_by_side(r["v_w1"], 9)
    settle(c_x)

    rim_rows = nt(r["v_fsel"][...], picked[...]).astype(BF)
    for n in (0, 9):
        block = strip_block(n)
        if n == 0:
            block = jnp.where(q == 0, picked[:, 0:128], block)
        else:
            block = jnp.where(q == 3, nn(picked[:, 256:384], flip).astype(BF), block)
        turned = nt(perms, block)
        for b in range(3):
            cb[b, n * 128:(n + 1) * 128, :] = turned[b * 128:(b + 1) * 128].astype(BF)
    for b in (0, 2):
        cb[b] = (cb[b].astype(F32) + nn(r["v_place"][b // 2], rim_rows)).astype(BF)
    z1, act1 = r["z1"], r["act1"]
    for n in range(4):
        taps = jnp.concatenate(
            [cb[b, a * 128 + n * 256:a * 128 + n * 256 + 256, :] for a in range(3) for b in range(3)], axis=1
        )
        pre = nt(taps, w1c)
        z1[n * 256:(n + 1) * 256, :] = pre
        act1[n * 256:(n + 1) * 256, :] = gelu(pre).astype(BF)
    pre = nt(quarters(act1[...]), side_by_side(r["v_wd"], 4))
    r["z2"][...] = pre
    act2 = gelu(pre).astype(BF)
    r["act2"][...] = act2
    own["rout"].wait()
    rq = r["rq"]
    rq[...] = tn(act2, r["v_rout"][...]).astype(BF)

    c_x = spread("x2", XD, x_peer, lambda d: rq.at[rows_of(lax.rem(x + d, 4)), :], lambda d: r["x2in"].at[d])
    c_h = [
        push(r["act2"].at[pl.ds(224, 32), :], r["h_top"], r["hs"].at[0], r["hr"].at[0], x_peer(1)),
        push(r["act2"].at[pl.ds(0, 32), :], r["h_bot"], r["hs"].at[1], r["hr"].at[1], x_peer(3)),
    ]
    total = rq[mine, :].astype(F32)
    settle(c_x)
    for d in XD:
        total = total + r["x2in"][d].astype(F32)
    held2 = r["held2"]
    held2[z] = total.astype(BF)
    c_z = spread("z2", ZD, z_peer, lambda d: held2.at[z], lambda d: held2.at[z])

    take_bulk(3)
    take_bulk(5)
    og, ogt, up = r["og"], r["ogt"], r["v_up"]
    flat = perm[1]
    for n in range(8):
        ogt[n * 128:(n + 1) * 128, :] = nt(flat, og[:, n * 128:(n + 1) * 128]).astype(BF)
    cells = ogt[...].astype(F32).reshape(8, 4, 32, 128)
    pooled = (cells[:, 0] + cells[:, 1] + cells[:, 2] + cells[:, 3]).reshape(256, 128).astype(BF)
    back_up = nn(pooled, up[...])

    settle(c_z)
    every = jnp.concatenate([held2[n] for n in range(8)], axis=1)
    slots2, landed2 = r["slots2"], r["landed2"]
    c_g = []
    for d in GD + (0,):
        slots2[d] = nn(every, r["maps"][lax.rem(g + d, 8)]).astype(BF)
        if d:
            c_g += spread("g2", (d,), g_peer, lambda d: slots2.at[d], lambda d: landed2.at[d])
    settle(c_g)
    total = slots2[0].astype(F32)
    for d in range(1, 8):
        total = total + landed2[d].astype(F32)
    picked2 = r["picked2"]
    picked2[mine, :] = total.astype(BF)
    part2 = picked2.at[mine, :]
    c_x = spread("x3", XD, x_peer, lambda d: part2, lambda d: part2)
    own["rin"].wait()
    take_bulk(4)
    settle(c_h)
    settle(c_x)

    sel = r["v_rin"][...]
    rim = nt(sel, picked2[...])
    upper = jnp.where(q == 0, 0.0, r["h_top"][...].astype(F32))
    lower = jnp.where(q == 3, 0.0, r["h_bot"][...].astype(F32))
    rows = jnp.concatenate([upper, act2.astype(F32), lower], axis=0) + rim[0:320]
    col = lax.rem(lax.broadcasted_iota(jnp.int32, (320, 128), 0), 32)
    west = jnp.where(col == 0, 0.0, pltpu.roll(rows, 1, 0)) + rim[320:640]
    east = jnp.where(col == 31, 0.0, pltpu.roll(rows, 319, 0)) + rim[640:960]
    blocks = [v.astype(BF) for v in (west, rows, east)]
    taps2 = jnp.concatenate([blocks[b][a * 32:a * 32 + 256] for a in range(3) for b in range(3)], axis=1)
    w2 = r["v_w2"]
    pre = nt(taps2, side_by_side(w2, 9))
    gz3 = (gelu_slope(pre) * back_up).astype(BF)
    none32, none64 = jnp.zeros((32, 128), F32), jnp.zeros((64, 128), F32)
    back = []
    for b in range(3):
        v0, v1, v2 = (nn(gz3, w2[3 * a + b]) for a in range(3))
        back.append(
            jnp.concatenate([v0, none64], axis=0)
            + jnp.concatenate([none32, v1, none32], axis=0)
            + jnp.concatenate([none64, v2], axis=0)
        )
    mid = (
        back[1]
        + jnp.where(col == 31, 0.0, pltpu.roll(back[0], 319, 0))
        + jnp.where(col == 0, 0.0, pltpu.roll(back[2], 1, 0))
    )
    cat = jnp.concatenate([mid.astype(BF), back[0].astype(BF), back[2].astype(BF)], axis=0)
    dq = r["dq"]
    dq[...] = tn(cat, sel).astype(BF)
    c_x = spread("x4", XD, x_peer, lambda d: dq.at[rows_of(lax.rem(x + d, 4)), :], lambda d: r["x4in"].at[d])
    r["first"][...] = mid[0:32]
    r["last"][...] = mid[288:320]
    c_h = [
        push(r["last"], r["b_top"], r["hs"].at[2], r["hr"].at[2], x_peer(1)),
        push(r["first"], r["b_bot"], r["hs"].at[3], r["hr"].at[3], x_peer(3)),
    ]

    other = 1 - core

    def halves(name, wide, parts):
        outs, ins = r[name + "c"], r[name + "ci"]
        for n in range(4):
            rows_n = pl.ds(pl.multiple_of(n * 32 + other * 16, 16), 16)
            at = 0
            for ref in parts:
                width = ref.shape[1]
                outs[n, :, at:at + width] = ref[rows_n, :].astype(BF)
                at += width
            outs[n, :, at:wide] = jnp.zeros((16, wide - at), BF)
        return [push(outs, ins, r[name + "cs"], r[name + "cr"], core_peer())]

    def shares(name, wide, parts):
        outs, ins = r[name + "o"], r[name + "i"]
        share = wide // 4
        for n in range(4):
            rows_n = pl.ds(pl.multiple_of(n * 32 + core * 16, 16), 16)
            own_n = jnp.concatenate(
                [ref[rows_n, :] for ref in parts]
                + [jnp.zeros((16, wide - sum(ref.shape[1] for ref in parts)), F32)],
                axis=1,
            )
            summed = (own_n + r[name + "ci"][n].astype(F32)).astype(BF)
            for m in range(4):
                outs[n, m] = summed[:, m * share:(m + 1) * share]
        sent = []
        for dx, dy in XYD:
            at = dx * 4 + dy
            sent.append(
                push(
                    outs.at[lax.rem(x + dx, 4), lax.rem(y + dy, 4)], ins.at[at],
                    r["gs_" + name].at[at], r["gr_" + name].at[at], xy_peer(dx, dy),
                )
            )
        return sent

    def along_z(name):
        total = r[name + "o"][x, y].astype(F32)
        for n in range(1, 16):
            total = total + r[name + "i"][n].astype(F32)
        zall = r[name + "z"]
        zall[z] = total.astype(BF)
        return spread(name + "z", ZD, z_peer, lambda d: zall.at[z], lambda d: zall.at[z])

    def whole(name):
        zall = r[name + "z"]
        total = zall[0].astype(F32)
        for n in range(1, 8):
            total = total + zall[n].astype(F32)
        return total.astype(BF)

    coarse = gelu(pre).astype(BF)
    r["gb_u"][...] = tn(pooled, coarse)
    r["gb_w"][...] = tn(gz3, taps2)
    parts_b = (r["gb_w"], r["gb_u"])
    c_bc = halves("b", BW, parts_b)
    settle(c_x)
    total = dq[mine, :].astype(F32)
    for d in XD:
        total = total + r["x4in"][d].astype(F32)
    held3 = r["held3"]
    held3[g] = total.astype(BF)
    c_g = spread("g3", GD, g_peer, lambda d: held3.at[g], lambda d: held3.at[g])

    settle(c_bc)
    c_b = shares("b", BW, parts_b)
    lifted = nt(coarse, up[...])
    out, ostrip = r["out"], r["ostrip"]
    for n in range(8):
        row = lifted[n * 32:(n + 1) * 32]
        summed = act1[n * 128:(n + 1) * 128, :].astype(F32) + jnp.concatenate([row] * 4, axis=0)
        ostrip[:, n * 128:(n + 1) * 128] = tn(summed.astype(BF), flat).astype(BF)

    settle(c_g)
    total = nt(held3[0], r["maps"][0])
    for j in range(1, 8):
        total = total + nt(held3[j], r["maps"][j])
    slots3, landed3 = r["slots3"], r["landed3"]
    for n in range(8):
        slots3[n] = total[:, n * 128:(n + 1) * 128].astype(BF)
    c_z = spread("z3", ZD, z_peer, lambda d: slots3.at[lax.rem(z + d, 8)], lambda d: landed3.at[d])
    lanes = pl.ds(pl.multiple_of(x * 1024, 1024), 1024)
    c_o = spread("o", XD, x_peer, lambda d: ostrip.at[rows_of(lax.rem(x + d, 4)), :], lambda d: out.at[:, lanes])
    c_o.append(local(15, ostrip.at[mine, :], out.at[:, lanes]))
    slope2 = gelu_slope(r["z2"][...])
    settle(c_z)
    total = slots3[z].astype(F32)
    for d in ZD:
        total = total + landed3[d].astype(F32)
    back_rim = r["back_rim"]
    back_rim[mine, :] = total.astype(BF)
    part3 = back_rim.at[mine, :]
    c_x = spread("x5", XD, x_peer, lambda d: part3, lambda d: part3)
    settle(c_b)
    c_bz = along_z("b")
    settle(c_h)
    upper = jnp.where(q == 0, 0.0, r["b_top"][...])
    lower = jnp.where(q == 3, 0.0, r["b_bot"][...])
    ga2 = mid[32:288] + jnp.concatenate([upper, jnp.zeros((192, 128), F32), lower], axis=0)
    settle(c_x)

    gz2 = (slope2 * (ga2 + nt(r["v_rout"][...], back_rim[...]))).astype(BF)
    wd = r["v_wd"]
    fine = [nn(gz2, wd[t]).reshape(8, 1, 32, 128) for t in range(4)]
    grown = jnp.concatenate(fine, axis=1).reshape(1024, 128)
    gz1 = (gelu_slope(z1[...]) * (ogt[...].astype(F32) + grown)).astype(BF)
    for a in range(3):
        for b in range(3):
            t = 3 * a + b
            r["ga_w"][:, t * 128:(t + 1) * 128] = tn(gz1, cb[b, a * 128:a * 128 + 1024, :])
    r["ga_d"][...] = tn(gz2, quarters(act1[...]))
    parts_a = (r["ga_w"], r["ga_d"])
    settle(halves("a", AW, parts_a))
    settle(shares("a", AW, parts_a))
    c_az = along_z("a")
    final, yall = r["final"], r["yall"]
    settle(c_bz)
    yall[y, :, 512:896] = whole("b")
    settle(c_o)
    settle(c_az)
    yall[y, :, 0:512] = whole("a")
    part4 = yall.at[y]
    settle(spread("y", XD, lambda d: xy_peer(0, d), lambda d: part4, lambda d: part4))
    final[core] = yall[...]
    settle([push(yall, final.at[core], r["fs"], r["fr"], core_peer())])


INPUTS = (
    "adj", "feat", "ograd", "w1", "wd", "w2", "up",
    "pick", "put", "perm", "cmap", "fsel", "place", "rout", "rin",
)


def buf(*shape, kind=BF):
    return pltpu.VMEM(shape, kind)


def sems(*shape):
    return pltpu.SemaphoreType.DMA(shape)


SCRATCH = [
    ("lsem", sems(16)), ("bs", sems(6, 4)), ("br", sems(6, 4)), ("hs", sems(4)), ("hr", sems(4)),
    ("fv", buf(32, 4096)), ("v_pick", buf(1024, 128)), ("v_put", buf(4, 128, 256)), ("v_perm", buf(3, 128, 128)),
    ("v_cmap", buf(4, 128, 128)), ("v_fsel", buf(128, 640)), ("v_place", buf(2, 1280, 128)),
    ("v_rout", buf(256, 128)), ("v_rin", buf(960, 256)),
    ("strip", buf(128, 1280)), ("og", buf(128, 1024)), ("v_w1", buf(9, 128, 128)), ("v_wd", buf(4, 128, 128)),
    ("v_w2", buf(9, 128, 128)), ("v_up", buf(128, 128)),
    ("held", buf(32, 32, 128)), ("slots", buf(8, 32, 640)), ("landed", buf(8, 32, 640)), ("picked", buf(128, 640)),
    ("maps", buf(8, 1024, 256)), ("cb", buf(3, 1280, 128)), ("z1", buf(1024, 128, kind=F32)), ("act1", buf(1024, 128)),
    ("z2", buf(256, 128, kind=F32)), ("act2", buf(256, 128)), ("rq", buf(128, 128)), ("x2in", buf(4, 32, 128)),
    ("h_top", buf(32, 128)), ("h_bot", buf(32, 128)), ("held2", buf(8, 32, 128)), ("ogt", buf(1024, 128)),
    ("slots2", buf(8, 32, 256)), ("landed2", buf(8, 32, 256)), ("picked2", buf(128, 256)),
    ("dq", buf(128, 256)), ("x4in", buf(4, 32, 256)),
    ("first", buf(32, 128, kind=F32)), ("last", buf(32, 128, kind=F32)),
    ("b_top", buf(32, 128, kind=F32)), ("b_bot", buf(32, 128, kind=F32)),
    ("held3", buf(8, 32, 256)), ("ostrip", buf(128, 1024)), ("slots3", buf(8, 32, 128)), ("landed3", buf(8, 32, 128)),
    ("back_rim", buf(128, 128)),
    ("gb_u", buf(128, 128, kind=F32)), ("gb_w", buf(128, 1152, kind=F32)),
    ("ga_d", buf(128, 512, kind=F32)), ("ga_w", buf(128, 1152, kind=F32)),
    ("bc", buf(4, 16, BW)), ("bci", buf(4, 16, BW)), ("bo", buf(4, 4, 16, BW // 4)), ("bi", buf(16, 16, BW // 4)),
    ("bz", buf(8, 16, BW // 4)), ("bcs", pltpu.SemaphoreType.DMA), ("bcr", pltpu.SemaphoreType.DMA),
    ("ac", buf(4, 16, AW)), ("aci", buf(4, 16, AW)), ("ao", buf(4, 4, 16, AW // 4)), ("ai", buf(16, 16, AW // 4)),
    ("az", buf(8, 16, AW // 4)), ("acs", pltpu.SemaphoreType.DMA), ("acr", pltpu.SemaphoreType.DMA),
    ("gs_b", sems(16)), ("gr_b", sems(16)), ("gs_a", sems(16)), ("gr_a", sems(16)),
    ("yall", buf(4, 16, 896)), ("fs", pltpu.SemaphoreType.DMA), ("fr", pltpu.SemaphoreType.DMA),
] + [
    (kind + way, sems(8))
    for kind in ("z1", "z2", "z3", "g1", "g2", "g3", "x1", "x2", "x3", "x4", "x5", "o", "y", "bz", "az")
    for way in ("s", "r")
]


def level_call(*args):
    return pl.pallas_call(
        level_kernel,
        out_shape=(jax.ShapeDtypeStruct((32, 4096), BF), jax.ShapeDtypeStruct((2, 4, 16, 896), BF)),
        in_specs=[SM] + [ANY] * 14,
        out_specs=[VM] * 2,
        scratch_shapes=[s for _, s in SCRATCH],
        compiler_params=pltpu.CompilerParams(collective_id=0, has_side_effects=True, vmem_limit_bytes=LIMIT),
    )(*args)


def result_kernel(out_in, final, out, g1, gd, g2, gu, *, scale):
    out[...] = out_in[...]
    for c in range(2):
        rows = pl.ds(c * 16, 16)
        for t in range(13):
            block = final[c, t // 4, :, (t % 4) * 128:(t % 4 + 1) * 128].astype(F32) * scale
            if t < 9:
                g1[t, rows, :] = block
            else:
                gd[t - 9, rows, :] = block
        for t in range(10):
            at = 512 + (t % 3) * 128
            block = final[c, t // 3, :, at:at + 128].astype(F32) * scale
            if t < 9:
                g2[t, rows, :] = block
            else:
                gu[rows, :] = block


def result_call(out_in, final, scale):
    return pl.pallas_call(
        functools.partial(result_kernel, scale=scale),
        out_shape=(
            jax.ShapeDtypeStruct((32, 4096), BF),
            jax.ShapeDtypeStruct((9, 32, 128), F32),
            jax.ShapeDtypeStruct((4, 32, 128), F32),
            jax.ShapeDtypeStruct((9, 32, 128), F32),
            jax.ShapeDtypeStruct((32, 128), F32),
        ),
        in_specs=[VM] * 2,
        out_specs=[VM] * 5,
        compiler_params=pltpu.CompilerParams(vmem_limit_bytes=16 * 1024 * 1024),
    )(out_in, final)


def per_device(features, conv1_weight, down_weight, conv2_weight, up_weight, out_grad, adjacency):
    pick, put = fine_rim_out()
    fine_sel, fine_place = fine_rim_maps()
    maps = [
        jnp.asarray(m, BF)
        for m in (pick, put, fine_perm(), corner_maps(), fine_sel, fine_place, coarse_rim_out(), coarse_rim_in())
    ]
    out, final = level_call(
        adjacency.reshape(1024), features, out_grad, conv1_weight, down_weight, conv2_weight, up_weight, *maps
    )
    return result_call(out, final, 262144 ** -0.5)


def solution(mesh):
    weights = P(None, "chan", None)
    return jax.shard_map(
        per_device,
        mesh=mesh,
        in_specs=(P("chan", "tile"), weights, weights, weights, P("chan", None), P("chan", "tile"), P()),
        out_specs=(P("chan", "tile"), weights, weights, weights, P("chan", None)),
        check_vma=False,
    )
```

```python
import functools

import jax
import jax.numpy as jnp
import numpy as np
from jax import lax
from jax.experimental import pallas as pl
from jax.experimental.pallas import tpu as pltpu
from jax.sharding import PartitionSpec as P

BF = jnp.bfloat16
F32 = jnp.float32
MESH = pl.DeviceIdType.MESH
TURNS = (0, 1, 2, 3, 0, 2, 2, 0)
VM = pl.BlockSpec(memory_space=pltpu.VMEM)
ANY = pl.BlockSpec(memory_space=pl.ANY)
LIMIT = 56 * 1024 * 1024


def fine_perm():
    out = np.zeros((3, 128, 128), np.float32)
    for b in range(3):
        for rr in range(2):
            for par in range(2):
                for k in range(32):
                    col = 2 * (k - 1 + b) + par
                    if 0 <= col < 64:
                        out[b, rr * 64 + par * 32 + k, rr * 64 + col] = 1
    return out


def corner_maps():
    out = np.zeros((4, 128, 128), np.float32)
    for i in range(2):
        for j in range(2):
            out[0, i * 64 + j, 2 * i + j] = 1
            out[1, (1 - i) * 64 + 63 - j, 4 + 2 * i + j] = 1
            out[2, (1 - i) * 64 + 1 - j, 8 + 2 * i + j] = 1
            out[3, i * 64 + 62 + j, 12 + 2 * i + j] = 1
    return out


def fine_rim_maps():
    sel = np.zeros((4, 128, 640), np.float32)
    for q in range(4):
        for r in range(20):
            ir = 16 * q - 2 + r
            for par in range(2):
                if 0 <= ir < 64:
                    west = 384 + par * 64 + 63 - ir
                    east = 128 + (1 - par) * 64 + ir
                elif ir < 0:
                    west = 512 + 12 + 2 * (ir + 2) + par
                    east = 512 + 0 + 2 * (ir + 2) + par
                else:
                    west = 512 + 8 + 2 * (ir - 64) + par
                    east = 512 + 4 + 2 * (ir - 64) + par
                sel[q, r * 2 + par, west] = 1
                sel[q, 64 + r * 2 + par, east] = 1
    place = np.zeros((2, 1280, 128), np.float32)
    for r in range(20):
        for par in range(2):
            place[0, r * 64 + par * 32, r * 2 + par] = 1
            place[1, r * 64 + par * 32 + 31, 64 + r * 2 + par] = 1
    return sel, place


def fine_rim_out():
    pick = np.zeros((1024, 128), np.float32)
    for r in range(16):
        for kind, col in enumerate((0, 1, 62, 63)):
            pick[r * 64 + col, kind * 16 + r] = 1
    put = np.zeros((4, 128, 256), np.float32)
    for s in range(4):
        for r16 in range(16):
            r = 16 * s + r16
            for kind, lane in enumerate((64 + r, r, 128 + 63 - r, 192 + 63 - r)):
                put[s, kind * 16 + r16, lane] = 1
    return pick, put


def coarse_rim_out():
    out = np.zeros((4, 256, 128), np.float32)
    for i in range(32):
        for s, (r, k) in enumerate(((31, i), (i, 0), (0, 31 - i), (31 - i, 31))):
            out[r // 8, (r % 8) * 32 + k, s * 32 + i] = 1
    return out


def coarse_rim_in():
    out = np.zeros((4, 960, 256), np.float32)
    for k in range(32):
        out[0, k, k] = 1
        out[3, 9 * 32 + k, 64 + 31 - k] = 1
    for q in range(4):
        for r in range(10):
            row = 8 * q - 1 + r
            if row < 0:
                west, east = 255, 128
            elif row >= 32:
                west, east = 192, 191
            else:
                west, east = 96 + 31 - row, 32 + row
            out[q, 320 + r * 32, west] = 1
            out[q, 640 + r * 32 + 31, east] = 1
    return out


def nt(a, b):
    return lax.dot_general(a, b, (((1,), (1,)), ((), ())), preferred_element_type=F32)


def tn(a, b):
    return lax.dot_general(a, b, (((0,), (0,)), ((), ())), preferred_element_type=F32)


def nn(a, b):
    return lax.dot_general(a, b, (((1,), (0,)), ((), ())), preferred_element_type=F32)


ROOT = 0.7978845608028654


def gelu(v):
    return 0.5 * v * (1.0 + jnp.tanh(ROOT * (v + 0.044715 * (v * v * v))))


def gelu_slope(v):
    t = jnp.tanh(ROOT * (v + 0.044715 * (v * v * v)))
    return 0.5 * (1.0 + t) + 0.5 * v * (1.0 - t * t) * (ROOT * (1.0 + 3 * 0.044715 * (v * v)))


def place_of():
    tile = lax.axis_index("tile")
    return tile, tile // 8, lax.rem(tile, 8), lax.axis_index("chan")


def x_peer(d):
    tile, _, _, x = place_of()
    return (tile, lax.rem(x + d, 4))


def z_peer(d):
    _, z, g, x = place_of()
    return (lax.rem(z + d, 8) * 8 + g, x)


def g_peer(d):
    _, z, g, x = place_of()
    return (z * 8 + lax.rem(g + d, 8), x)


def core_peer():
    tile, _, g, x = place_of()
    return (tile + 1 - 2 * lax.rem(g, 2), x)


def xy_peer(dx, dy):
    _, z, g, x = place_of()
    return (z * 8 + lax.rem(g + 2 * dy, 8), lax.rem(x + dx, 4))


AW, BW = 2048, 1536
XD = (1, 3, 2)
ZD = (4, 3, 5, 2, 6, 1, 7)
GD = (4, 3, 5, 2, 6, 1, 7)
XYD = [(dx, dy) for dx in range(4) for dy in range(4) if dx or dy]
EDGE = (0, 31, 0, 31)


def side_by_side(weights, count):
    return jnp.concatenate([weights[t] for t in range(count)], axis=1)


def quarters(act):
    parts = act.reshape(8, 2, 2, 32, 128)
    return jnp.concatenate(
        [parts[:, a, b].reshape(256, 128) for a in range(2) for b in range(2)], axis=1
    )


def flip_map():
    rows = lax.broadcasted_iota(jnp.int32, (128, 128), 0)
    cols = lax.broadcasted_iota(jnp.int32, (128, 128), 1)
    return jnp.where(rows + cols == 127, 1.0, 0.0).astype(BF)


def level_kernel(*refs):
    names = INPUTS + ("out", "final") + tuple(n for n, _ in SCRATCH)
    r = dict(zip(names, refs))
    tile, z, g, x = place_of()
    y, core = g // 2, lax.rem(g, 2)
    q = x
    mine = pl.ds(pl.multiple_of(x * 32, 32), 32)
    rounds = []

    def rows_of(n):
        return pl.ds(pl.multiple_of(n * 32, 32), 32)

    def local(n, src, dst):
        copy = pltpu.make_async_copy(src, dst, r["lsem"].at[n])
        copy.start()
        return copy

    def begin(whole):
        rounds.append(whole)
        return len(rounds) - 1

    def push(n, src, dst, peer):
        pltpu.make_async_remote_copy(
            src_ref=src, dst_ref=dst, send_sem=r["ss"].at[n], recv_sem=r["rs"].at[n],
            device_id=peer, device_id_type=MESH,
        ).start()

    def spread(whole, dirs, peer, src, dst):
        n = begin(whole)
        for d in dirs:
            push(n, src(d), dst(d), peer(d))
        return n

    def settle(n):
        pltpu.make_async_copy(rounds[n], rounds[n], r["rs"].at[n]).wait()

    barrier = pltpu.get_barrier_semaphore()
    peers = [x_peer(d) for d in XD] + [z_peer(d) for d in ZD] + [g_peer(d) for d in GD]
    peers += [xy_peer(dx, dy) for dx, dy in XYD if dx and dy]
    for peer in peers:
        pl.semaphore_signal(barrier, inc=1, device_id=peer, device_id_type=MESH)

    own_feat = local(0, r["feat"], r["fv"])
    own = {
        "pick": local(1, r["pick"], r["v_pick"]),
        "put": local(2, r["put"], r["v_put"]),
        "adj": local(3, r["adj"], r["s_adj"]),
        "cmap": local(4, r["cmap"], r["v_cmap"]),
        "perm": local(5, r["perm"], r["v_perm"]),
        "fsel": local(6, r["fsel"], r["v_fsel"]),
        "place": local(7, r["place"], r["v_place"]),
        "rout": local(8, r["rout"].at[q], r["v_rout"]),
        "rin": local(9, r["rin"].at[q], r["v_rin"]),
    }
    adj = r["s_adj"]

    own["pick"].wait()
    own["put"].wait()
    own_feat.wait()
    fv, held = r["fv"], (r["held0"], r["held1"])
    stacked = jnp.concatenate([fv[:, s * 1024:(s + 1) * 1024] for s in range(4)], axis=0)
    cols = nn(stacked, r["v_pick"][...]).astype(BF)
    both = nn(cols[0:32], r["v_put"][0])
    for s in range(1, 4):
        both = both + nn(cols[32 * s:32 * s + 32], r["v_put"][s])
    flip = flip_map()
    rims = (
        fv[:, 3968:4096],
        both[:, 0:128].astype(BF),
        nn(fv[:, 0:128], flip).astype(BF),
        both[:, 128:256].astype(BF),
    )
    for s in range(4):
        held[0][z * 4 + s] = rims[s][0:16]
        held[1][g * 4 + s] = rims[s][16:32]
    pl.semaphore_wait(barrier, len(peers))
    ways = ((z, ZD, z_peer), (g, GD, g_peer))
    first = []
    for h in range(2):
        at, dirs, peer = ways[h]
        part = held[h].at[pl.ds(at * 4, 4)]
        first.append(spread(held[h].at[pl.ds(0, 28)], dirs, peer, lambda d: part, lambda d: part))

    def piece(n, j):
        if n == 0:
            start = pl.multiple_of(jnp.clip(j * 1024 - 128, 0, 2816), 128)
            return r["feat"].at[:, pl.ds(start, 1280)], r["strip"].at[mine, :]
        if n == 3:
            return r["ograd"].at[:, pl.ds(pl.multiple_of(j * 1024, 1024), 1024)], r["og"].at[mine, :]
        if n == 5:
            return r["up"], r["v_up"].at[mine, :]
        name = {1: "w1", 2: "wd", 4: "w2"}[n]
        return r[name], r["v_" + name].at[:, mine, :]

    bulk = {}

    def send_bulk(n):
        three = pl.ds(0, 96)
        into = r[("strip", "v_w1", "v_wd", "og", "v_w2", "v_up")[n]]
        whole = into.at[:, three, :] if n in (1, 2, 4) else into.at[three, :]
        m = begin(whole)
        for d in XD:
            src, dst = piece(n, lax.rem(x + d, 4))
            push(m, src, dst, x_peer(d))
        src, dst = piece(n, x)
        bulk[n] = (m, local(10 + n, src, dst))

    def take_bulk(n):
        m, copy = bulk[n]
        copy.wait()
        settle(m)

    for n in range(3):
        send_bulk(n)

    own["adj"].wait()

    def entry(t, k, h=0):
        p = adj[2 * k, t]
        s = lax.rem(adj[2 * k + 1, t] + TURNS[k], 4)
        if h:
            return jnp.logical_and(p >= 0, p // 8 == z), lax.rem(p, 8), s
        return jnp.logical_and(p >= 0, lax.rem(p, 8) == g), p // 8, s

    own["perm"].wait()
    take_bulk(0)
    perm, cb, strip = r["v_perm"], r["cb"], r["strip"]
    perms = perm[...].reshape(384, 128)
    shift = jnp.where(q == 0, -1, jnp.where(q == 3, 1, 0))

    def strip_block(n):
        at = jnp.clip(n + shift, 0, 9)
        return strip[:, pl.ds(pl.multiple_of(at * 128, 128), 128)]

    for n in range(1, 9):
        turned = nt(perms, strip_block(n))
        for b in range(3):
            cb[b, n * 128:(n + 1) * 128, :] = turned[b * 128:(b + 1) * 128].astype(BF)

    own["cmap"].wait()
    slots, landed = r["slots"], r["landed"]
    second = []
    for h in (1, 0):
        settle(first[h])
        _, dirs, peer = ways[1 - h]
        order = dirs + (0,)
        m = begin(landed.at[h, pl.ds(1, 7)])
        second.append(m)
        corners = [[] for _ in range(4)]
        for d in order:
            t = z * 8 + lax.rem(g + d, 8) if h == 0 else lax.rem(z + d, 8) * 8 + g
            for k in range(8):
                owned, n, s = entry(t, k, h)
                block = held[h][jnp.where(owned, n * 4 + s, 0)]
                block = jnp.where(owned, block, jnp.zeros_like(block))
                if k < 4:
                    slots[h, d, :, k * 128:(k + 1) * 128] = block
                else:
                    corners[k - 4].append(block)
        corner = nn(jnp.concatenate(corners[0], axis=0), r["v_cmap"][0])
        for k in range(1, 4):
            corner = corner + nn(jnp.concatenate(corners[k], axis=0), r["v_cmap"][k])
        for n, d in enumerate(order):
            slots[h, d, :, 512:640] = corner[16 * n:16 * n + 16].astype(BF)
            if d:
                push(m, slots.at[h, d], landed.at[h, d], peer(d))
    halves_of = []
    for m, h in zip(second, (1, 0)):
        settle(m)
        total = slots[h, 0].astype(F32)
        for d in range(1, 8):
            total = total + landed[h, d].astype(F32)
        halves_of.append(total)
    total = jnp.concatenate([halves_of[1], halves_of[0]], axis=0).astype(BF)

    own["fsel"].wait()
    picked, pout = r["picked"], r["pout"]
    ends = (total[:, 0:128], None, None, nn(total[:, 256:384], flip).astype(BF))
    for j in range(4):
        pout[j, :, 0:128] = nt(total, r["v_fsel"][j]).astype(BF)
        pout[j, :, 128:256] = jnp.zeros((32, 128), BF) if ends[j] is None else ends[j]
    c_x = spread(
        picked.at[pl.ds(0, 96), :], XD, x_peer, lambda d: pout.at[lax.rem(x + d, 4)], lambda d: picked.at[mine, :]
    )
    picked[mine, :] = pout[x]
    for n in range(3, 6):
        send_bulk(n)
    own["place"].wait()
    take_bulk(1)
    take_bulk(2)
    w1c = side_by_side(r["v_w1"], 9)
    settle(c_x)

    for n in (0, 9):
        block = jnp.where(q == n // 3, picked[:, 128:256], strip_block(n))
        turned = nt(perms, block)
        for b in range(3):
            cb[b, n * 128:(n + 1) * 128, :] = turned[b * 128:(b + 1) * 128].astype(BF)
    sides = picked[:, 0:128]
    for b in (0, 2):
        cb[b] = (cb[b].astype(F32) + nt(r["v_place"][b // 2], sides)).astype(BF)
    z1, act1 = r["z1"], r["act1"]
    for n in range(4):
        taps = jnp.concatenate(
            [cb[b, a * 128 + n * 256:a * 128 + n * 256 + 256, :] for a in range(3) for b in range(3)], axis=1
        )
        pre = nt(taps, w1c)
        z1[n * 256:(n + 1) * 256, :] = pre
        act1[n * 256:(n + 1) * 256, :] = gelu(pre).astype(BF)
    pre = nt(quarters(act1[...]), side_by_side(r["v_wd"], 4))
    r["z2"][...] = pre
    act2 = gelu(pre).astype(BF)
    r["act2"][...] = act2
    own["rout"].wait()
    rq = r["rq"]
    rq[...] = tn(act2, r["v_rout"][...]).astype(BF)

    x2in, halo = r["x2in"], r["halo"]
    c_x = spread(
        x2in.at[pl.ds(1, 3)], XD, x_peer, lambda d: rq.at[rows_of(lax.rem(x + d, 4)), :], lambda d: x2in.at[d]
    )
    c_h = begin(halo)
    push(c_h, r["act2"].at[pl.ds(224, 32), :], halo.at[0], x_peer(1))
    push(c_h, r["act2"].at[pl.ds(0, 32), :], halo.at[1], x_peer(3))
    total = rq[mine, :].astype(F32)
    settle(c_x)
    for d in XD:
        total = total + x2in[d].astype(F32)
    held2 = r["held2"]
    held2[z] = total.astype(BF)
    c_z = spread(held2.at[pl.ds(0, 7)], ZD, z_peer, lambda d: held2.at[z], lambda d: held2.at[z])

    take_bulk(3)
    take_bulk(5)
    og, ogt, up = r["og"], r["ogt"], r["v_up"]
    flat = perm[1]
    for n in range(8):
        ogt[n * 128:(n + 1) * 128, :] = nt(flat, og[:, n * 128:(n + 1) * 128]).astype(BF)
    cells = ogt[...].astype(F32).reshape(8, 4, 32, 128)
    pooled = (cells[:, 0] + cells[:, 1] + cells[:, 2] + cells[:, 3]).reshape(256, 128).astype(BF)
    back_up = nn(pooled, up[...])

    settle(c_z)
    rolled = r["rolled"]
    for n in range(8):
        block = held2[n].astype(F32)
        rolled[n * 4] = held2[n]
        for m in range(1, 4):
            rolled[n * 4 + m] = pltpu.roll(block, 32 * m, 1).astype(BF)
    lane = lax.broadcasted_iota(jnp.int32, (32, 128), 1)
    slots2, landed2 = r["slots2"], r["landed2"]
    c_g = begin(landed2.at[pl.ds(1, 7)])
    for d in GD + (0,):
        t = z * 8 + lax.rem(g + d, 8)
        both = [jnp.zeros((32, 128), F32), jnp.zeros((32, 128), F32)]
        for k in range(8):
            owned, n, s = entry(t, k)
            block = rolled[jnp.where(owned, n * 4 + lax.rem(k + 4 - s, 4), 0)].astype(F32)
            block = jnp.where(owned, block, 0.0)
            if k < 4:
                both[0] = jnp.where(lane // 32 == k, block, both[0])
            else:
                both[1] = jnp.where(lane == 32 * (k - 4) + EDGE[k - 4], block, both[1])
        slots2[d, :, 0:128] = both[0].astype(BF)
        slots2[d, :, 128:256] = both[1].astype(BF)
        if d:
            push(c_g, slots2.at[d], landed2.at[d], g_peer(d))
    settle(c_g)
    total = slots2[0].astype(F32)
    for d in range(1, 8):
        total = total + landed2[d].astype(F32)
    picked2 = r["picked2"]
    picked2[mine, :] = total.astype(BF)
    part2 = picked2.at[mine, :]
    c_x = spread(picked2.at[pl.ds(0, 96), :], XD, x_peer, lambda d: part2, lambda d: part2)
    own["rin"].wait()
    take_bulk(4)
    settle(c_h)
    settle(c_x)

    sel = r["v_rin"][...]
    rim = nt(sel, picked2[...])
    upper = jnp.where(q == 0, 0.0, halo[0].astype(F32))
    lower = jnp.where(q == 3, 0.0, halo[1].astype(F32))
    rows = jnp.concatenate([upper, act2.astype(F32), lower], axis=0) + rim[0:320]
    col = lax.rem(lax.broadcasted_iota(jnp.int32, (320, 128), 0), 32)
    west = jnp.where(col == 0, 0.0, pltpu.roll(rows, 1, 0)) + rim[320:640]
    east = jnp.where(col == 31, 0.0, pltpu.roll(rows, 319, 0)) + rim[640:960]
    blocks = [v.astype(BF) for v in (west, rows, east)]
    taps2 = jnp.concatenate([blocks[b][a * 32:a * 32 + 256] for a in range(3) for b in range(3)], axis=1)
    w2 = r["v_w2"]
    pre = nt(taps2, side_by_side(w2, 9))
    gz3 = (gelu_slope(pre) * back_up).astype(BF)
    none32, none64 = jnp.zeros((32, 128), F32), jnp.zeros((64, 128), F32)
    back = []
    for b in range(3):
        v0, v1, v2 = (nn(gz3, w2[3 * a + b]) for a in range(3))
        back.append(
            jnp.concatenate([v0, none64], axis=0)
            + jnp.concatenate([none32, v1, none32], axis=0)
            + jnp.concatenate([none64, v2], axis=0)
        )
    mid = (
        back[1]
        + jnp.where(col == 31, 0.0, pltpu.roll(back[0], 319, 0))
        + jnp.where(col == 0, 0.0, pltpu.roll(back[2], 1, 0))
    )
    cat = jnp.concatenate([mid.astype(BF), back[0].astype(BF), back[2].astype(BF)], axis=0)
    dq = r["dq"]
    dq[...] = tn(cat, sel).astype(BF)
    x4in, hout, hin = r["x4in"], r["hout"], r["hin"]
    c_x = spread(
        x4in.at[pl.ds(1, 3)], XD, x_peer, lambda d: dq.at[rows_of(lax.rem(x + d, 4)), :], lambda d: x4in.at[d]
    )
    hout[0] = mid[288:320]
    hout[1] = mid[0:32]
    c_h = begin(hin)
    push(c_h, hout.at[0], hin.at[0], x_peer(1))
    push(c_h, hout.at[1], hin.at[1], x_peer(3))

    other = 1 - core

    def halves(name, wide, parts):
        outs, ins = r[name + "c"], r[name + "ci"]
        for n in range(4):
            rows_n = pl.ds(pl.multiple_of(n * 32 + other * 16, 16), 16)
            at = 0
            for ref in parts:
                width = ref.shape[1]
                outs[n, :, at:at + width] = ref[rows_n, :].astype(BF)
                at += width
            outs[n, :, at:wide] = jnp.zeros((16, wide - at), BF)
        n = begin(ins)
        push(n, outs, ins, core_peer())
        return n

    def shares(name, wide, parts):
        outs, ins = r[name + "o"], r[name + "i"]
        share = wide // 4
        for n in range(4):
            rows_n = pl.ds(pl.multiple_of(n * 32 + core * 16, 16), 16)
            own_n = jnp.concatenate(
                [ref[rows_n, :] for ref in parts]
                + [jnp.zeros((16, wide - sum(ref.shape[1] for ref in parts)), F32)],
                axis=1,
            )
            summed = (own_n + r[name + "ci"][n].astype(F32)).astype(BF)
            for m in range(4):
                outs[n, m] = summed[:, m * share:(m + 1) * share]
        m = begin(ins.at[pl.ds(1, 15)])
        for dx, dy in XYD:
            push(m, outs.at[lax.rem(x + dx, 4), lax.rem(y + dy, 4)], ins.at[dx * 4 + dy], xy_peer(dx, dy))
        return m

    def along_z(name):
        total = r[name + "o"][x, y].astype(F32)
        for n in range(1, 16):
            total = total + r[name + "i"][n].astype(F32)
        zall = r[name + "z"]
        zall[z] = total.astype(BF)
        return spread(zall.at[pl.ds(0, 7)], ZD, z_peer, lambda d: zall.at[z], lambda d: zall.at[z])

    def whole(name):
        zall = r[name + "z"]
        total = zall[0].astype(F32)
        for n in range(1, 8):
            total = total + zall[n].astype(F32)
        return total.astype(BF)

    coarse = gelu(pre).astype(BF)
    r["gb_u"][...] = tn(pooled, coarse)
    r["gb_w"][...] = tn(gz3, taps2)
    parts_b = (r["gb_w"], r["gb_u"])
    c_bc = halves("b", BW, parts_b)
    settle(c_x)
    total = dq[mine, :].astype(F32)
    for d in XD:
        total = total + x4in[d].astype(F32)
    held3 = r["held3"]
    held3[g] = total.astype(BF)
    c_g = spread(held3.at[pl.ds(0, 7)], GD, g_peer, lambda d: held3.at[g], lambda d: held3.at[g])

    settle(c_bc)
    c_b = shares("b", BW, parts_b)
    lifted = nt(coarse, up[...])
    out, ostrip = r["out"], r["ostrip"]
    for n in range(8):
        row = lifted[n * 32:(n + 1) * 32]
        summed = act1[n * 128:(n + 1) * 128, :].astype(F32) + jnp.concatenate([row] * 4, axis=0)
        ostrip[:, n * 128:(n + 1) * 128] = tn(summed.astype(BF), flat).astype(BF)

    settle(c_g)
    rolled3 = r["rolled3"]
    for j in range(8):
        for h in range(2):
            block = held3[j, :, 128 * h:128 * h + 128]
            rolled3[j * 8 + h * 4] = block
            for m in range(1, 4):
                rolled3[j * 8 + h * 4 + m] = pltpu.roll(block.astype(F32), 32 * m, 1).astype(BF)
    sums = [jnp.zeros((32, 128), F32) for _ in range(8)]
    for j in range(8):
        for k in range(8):
            owned, n, s = entry(z * 8 + j, k)
            block = rolled3[j * 8 + (k // 4) * 4 + lax.rem(s + 4 - k % 4, 4)].astype(F32)
            if k < 4:
                block = jnp.where(lane // 32 == s, block, 0.0)
            else:
                block = jnp.where(lane == 32 * s + EDGE[k - 4], block, 0.0)
            n = jnp.where(owned, n, -1)
            for m in range(8):
                sums[m] = sums[m] + jnp.where(n == m, block, 0.0)
    slots3, landed3 = r["slots3"], r["landed3"]
    for n in range(8):
        slots3[n] = sums[n].astype(BF)
    c_z = spread(
        landed3.at[pl.ds(1, 7)], ZD, z_peer, lambda d: slots3.at[lax.rem(z + d, 8)], lambda d: landed3.at[d]
    )
    slope2 = gelu_slope(r["z2"][...])
    settle(c_z)
    total = slots3[z].astype(F32)
    for d in ZD:
        total = total + landed3[d].astype(F32)
    back_rim = r["back_rim"]
    back_rim[mine, :] = total.astype(BF)
    part3 = back_rim.at[mine, :]
    c_x = spread(back_rim.at[pl.ds(0, 96), :], XD, x_peer, lambda d: part3, lambda d: part3)
    lanes = pl.ds(pl.multiple_of(x * 1024, 1024), 1024)
    c_o = spread(
        out.at[:, pl.ds(0, 3072)], XD, x_peer,
        lambda d: ostrip.at[rows_of(lax.rem(x + d, 4)), :], lambda d: out.at[:, lanes],
    )
    own_out = local(16, ostrip.at[mine, :], out.at[:, lanes])
    settle(c_b)
    c_bz = along_z("b")
    settle(c_h)
    upper = jnp.where(q == 0, 0.0, hin[0])
    lower = jnp.where(q == 3, 0.0, hin[1])
    ga2 = mid[32:288] + jnp.concatenate([upper, jnp.zeros((192, 128), F32), lower], axis=0)
    settle(c_x)

    gz2 = (slope2 * (ga2 + nt(r["v_rout"][...], back_rim[...]))).astype(BF)
    wd = r["v_wd"]
    fine = [nn(gz2, wd[t]).reshape(8, 1, 32, 128) for t in range(4)]
    grown = jnp.concatenate(fine, axis=1).reshape(1024, 128)
    gz1 = (gelu_slope(z1[...]) * (ogt[...].astype(F32) + grown)).astype(BF)
    for a in range(3):
        for b in range(3):
            t = 3 * a + b
            r["ga_w"][:, t * 128:(t + 1) * 128] = tn(gz1, cb[b, a * 128:a * 128 + 1024, :])
    r["ga_d"][...] = tn(gz2, quarters(act1[...]))
    parts_a = (r["ga_w"], r["ga_d"])
    settle(halves("a", AW, parts_a))
    settle(shares("a", AW, parts_a))
    c_az = along_z("a")
    final, yall = r["final"], r["yall"]
    settle(c_bz)
    yall[y, :, 512:896] = whole("b")
    settle(c_o)
    settle(c_az)
    yall[y, :, 0:512] = whole("a")
    part4 = yall.at[y]
    settle(spread(yall.at[pl.ds(0, 3)], XD, lambda d: xy_peer(0, d), lambda d: part4, lambda d: part4))
    final[core] = yall[...]
    n = begin(yall)
    push(n, yall, final.at[core], core_peer())
    settle(n)
    own_out.wait()
    for n, whole in enumerate(rounds):
        pltpu.make_async_copy(whole, whole, r["ss"].at[n]).wait()


INPUTS = (
    "adj", "feat", "ograd", "w1", "wd", "w2", "up",
    "pick", "put", "perm", "cmap", "fsel", "place", "rout", "rin",
)


def buf(*shape, kind=BF):
    return pltpu.VMEM(shape, kind)


def sems(*shape):
    return pltpu.SemaphoreType.DMA(shape)


SCRATCH = [
    ("lsem", sems(17)), ("ss", sems(30)), ("rs", sems(30)), ("s_adj", pltpu.SMEM((16, 64), jnp.int32)),
    ("fv", buf(32, 4096)), ("v_pick", buf(1024, 128)), ("v_put", buf(4, 128, 256)), ("v_perm", buf(3, 128, 128)),
    ("v_cmap", buf(4, 128, 128)), ("v_fsel", buf(4, 128, 640)), ("v_place", buf(2, 1280, 128)),
    ("v_rout", buf(256, 128)), ("v_rin", buf(960, 256)),
    ("strip", buf(128, 1280)), ("og", buf(128, 1024)), ("v_w1", buf(9, 128, 128)), ("v_wd", buf(4, 128, 128)),
    ("v_w2", buf(9, 128, 128)), ("v_up", buf(128, 128)),
    ("held0", buf(32, 16, 128)), ("held1", buf(32, 16, 128)), ("slots", buf(2, 8, 16, 640)), ("landed", buf(2, 8, 16, 640)),
    ("pout", buf(4, 32, 256)), ("picked", buf(128, 256)),
    ("cb", buf(3, 1280, 128)), ("z1", buf(1024, 128, kind=F32)), ("act1", buf(1024, 128)),
    ("z2", buf(256, 128, kind=F32)), ("act2", buf(256, 128)), ("rq", buf(128, 128)), ("x2in", buf(4, 32, 128)),
    ("halo", buf(2, 32, 128)), ("held2", buf(8, 32, 128)), ("rolled", buf(32, 32, 128)), ("ogt", buf(1024, 128)),
    ("slots2", buf(8, 32, 256)), ("landed2", buf(8, 32, 256)), ("picked2", buf(128, 256)),
    ("dq", buf(128, 256)), ("x4in", buf(4, 32, 256)),
    ("hout", buf(2, 32, 128, kind=F32)), ("hin", buf(2, 32, 128, kind=F32)),
    ("held3", buf(8, 32, 256)), ("rolled3", buf(64, 32, 128)), ("ostrip", buf(128, 1024)),
    ("slots3", buf(8, 32, 128)), ("landed3", buf(8, 32, 128)), ("back_rim", buf(128, 128)),
    ("gb_u", buf(128, 128, kind=F32)), ("gb_w", buf(128, 1152, kind=F32)),
    ("ga_d", buf(128, 512, kind=F32)), ("ga_w", buf(128, 1152, kind=F32)),
    ("bc", buf(4, 16, BW)), ("bci", buf(4, 16, BW)), ("bo", buf(4, 4, 16, BW // 4)), ("bi", buf(16, 16, BW // 4)),
    ("bz", buf(8, 16, BW // 4)),
    ("ac", buf(4, 16, AW)), ("aci", buf(4, 16, AW)), ("ao", buf(4, 4, 16, AW // 4)), ("ai", buf(16, 16, AW // 4)),
    ("az", buf(8, 16, AW // 4)),
    ("yall", buf(4, 16, 896)),
]


def level_call(*args):
    return pl.pallas_call(
        level_kernel,
        out_shape=(jax.ShapeDtypeStruct((32, 4096), BF), jax.ShapeDtypeStruct((2, 4, 16, 896), BF)),
        in_specs=[ANY] * 15,
        out_specs=[VM] * 2,
        scratch_shapes=[s for _, s in SCRATCH],
        compiler_params=pltpu.CompilerParams(collective_id=0, has_side_effects=True, vmem_limit_bytes=LIMIT),
    )(*args)


def result_kernel(out_in, final, out, g1, gd, g2, gu, *, scale):
    out[...] = out_in[...]
    for c in range(2):
        rows = pl.ds(c * 16, 16)
        for t in range(13):
            block = final[c, t // 4, :, (t % 4) * 128:(t % 4 + 1) * 128].astype(F32) * scale
            if t < 9:
                g1[t, rows, :] = block
            else:
                gd[t - 9, rows, :] = block
        for t in range(10):
            at = 512 + (t % 3) * 128
            block = final[c, t // 3, :, at:at + 128].astype(F32) * scale
            if t < 9:
                g2[t, rows, :] = block
            else:
                gu[rows, :] = block


def result_call(out_in, final, scale):
    return pl.pallas_call(
        functools.partial(result_kernel, scale=scale),
        out_shape=(
            jax.ShapeDtypeStruct((32, 4096), BF),
            jax.ShapeDtypeStruct((9, 32, 128), F32),
            jax.ShapeDtypeStruct((4, 32, 128), F32),
            jax.ShapeDtypeStruct((9, 32, 128), F32),
            jax.ShapeDtypeStruct((32, 128), F32),
        ),
        in_specs=[VM] * 2,
        out_specs=[VM] * 5,
        compiler_params=pltpu.CompilerParams(vmem_limit_bytes=16 * 1024 * 1024),
    )(out_in, final)


def per_device(features, conv1_weight, down_weight, conv2_weight, up_weight, out_grad, adjacency):
    pick, put = fine_rim_out()
    fine_sel, fine_place = fine_rim_maps()
    maps = [
        jnp.asarray(m, BF)
        for m in (pick, put, fine_perm(), corner_maps(), fine_sel, fine_place, coarse_rim_out(), coarse_rim_in())
    ]
    out, final = level_call(
        adjacency.transpose(1, 2, 0).reshape(16, 64), features, out_grad, conv1_weight, down_weight, conv2_weight, up_weight, *maps
    )
    return result_call(out, final, 262144 ** -0.5)


def solution(mesh):
    weights = P(None, "chan", None)
    return jax.shard_map(
        per_device,
        mesh=mesh,
        in_specs=(P("chan", "tile"), weights, weights, weights, P("chan", None), P("chan", "tile"), P()),
        out_specs=(P("chan", "tile"), weights, weights, weights, P("chan", None)),
        check_vma=False,
    )
```

```python
import functools

import jax
import jax.numpy as jnp
import numpy as np
from jax import lax
from jax.experimental import pallas as pl
from jax.experimental.pallas import tpu as pltpu
from jax.sharding import PartitionSpec as P

BF = jnp.bfloat16
F32 = jnp.float32
MESH = pl.DeviceIdType.MESH
TURNS = (0, 1, 2, 3, 0, 2, 2, 0)
VM = pl.BlockSpec(memory_space=pltpu.VMEM)
ANY = pl.BlockSpec(memory_space=pl.ANY)
LIMIT = 56 * 1024 * 1024


def fine_perm():
    out = np.zeros((3, 128, 128), np.float32)
    for b in range(3):
        for rr in range(2):
            for par in range(2):
                for k in range(32):
                    col = 2 * (k - 1 + b) + par
                    if 0 <= col < 64:
                        out[b, rr * 64 + par * 32 + k, rr * 64 + col] = 1
    return out


def corner_maps():
    out = np.zeros((4, 128, 128), np.float32)
    for i in range(2):
        for j in range(2):
            out[0, i * 64 + j, 2 * i + j] = 1
            out[1, (1 - i) * 64 + 63 - j, 4 + 2 * i + j] = 1
            out[2, (1 - i) * 64 + 1 - j, 8 + 2 * i + j] = 1
            out[3, i * 64 + 62 + j, 12 + 2 * i + j] = 1
    return out


def fine_rim_maps():
    sel = np.zeros((4, 128, 640), np.float32)
    for q in range(4):
        for r in range(20):
            ir = 16 * q - 2 + r
            for par in range(2):
                if 0 <= ir < 64:
                    west = 384 + par * 64 + 63 - ir
                    east = 128 + (1 - par) * 64 + ir
                elif ir < 0:
                    west = 512 + 12 + 2 * (ir + 2) + par
                    east = 512 + 0 + 2 * (ir + 2) + par
                else:
                    west = 512 + 8 + 2 * (ir - 64) + par
                    east = 512 + 4 + 2 * (ir - 64) + par
                sel[q, r * 2 + par, west] = 1
                sel[q, 64 + r * 2 + par, east] = 1
    place = np.zeros((2, 1280, 128), np.float32)
    for r in range(20):
        for par in range(2):
            place[0, r * 64 + par * 32, r * 2 + par] = 1
            place[1, r * 64 + par * 32 + 31, 64 + r * 2 + par] = 1
    return sel, place


def fine_rim_out():
    pick = np.zeros((1024, 128), np.float32)
    for r in range(16):
        for kind, col in enumerate((0, 1, 62, 63)):
            pick[r * 64 + col, kind * 16 + r] = 1
    put = np.zeros((4, 128, 256), np.float32)
    for s in range(4):
        for r16 in range(16):
            r = 16 * s + r16
            for kind, lane in enumerate((64 + r, r, 128 + 63 - r, 192 + 63 - r)):
                put[s, kind * 16 + r16, lane] = 1
    return pick, put


def coarse_rim_out():
    out = np.zeros((4, 256, 128), np.float32)
    for i in range(32):
        for s, (r, k) in enumerate(((31, i), (i, 0), (0, 31 - i), (31 - i, 31))):
            out[r // 8, (r % 8) * 32 + k, s * 32 + i] = 1
    return out


def coarse_rim_in():
    out = np.zeros((4, 960, 256), np.float32)
    for k in range(32):
        out[0, k, k] = 1
        out[3, 9 * 32 + k, 64 + 31 - k] = 1
    for q in range(4):
        for r in range(10):
            row = 8 * q - 1 + r
            if row < 0:
                west, east = 255, 128
            elif row >= 32:
                west, east = 192, 191
            else:
                west, east = 96 + 31 - row, 32 + row
            out[q, 320 + r * 32, west] = 1
            out[q, 640 + r * 32 + 31, east] = 1
    return out


def nt(a, b):
    return lax.dot_general(a, b, (((1,), (1,)), ((), ())), preferred_element_type=F32)


def tn(a, b):
    return lax.dot_general(a, b, (((0,), (0,)), ((), ())), preferred_element_type=F32)


def nn(a, b):
    return lax.dot_general(a, b, (((1,), (0,)), ((), ())), preferred_element_type=F32)


ROOT = 0.7978845608028654


def gelu(v):
    return 0.5 * v * (1.0 + jnp.tanh(ROOT * (v + 0.044715 * (v * v * v))))


def gelu_slope(v):
    t = jnp.tanh(ROOT * (v + 0.044715 * (v * v * v)))
    return 0.5 * (1.0 + t) + 0.5 * v * (1.0 - t * t) * (ROOT * (1.0 + 3 * 0.044715 * (v * v)))


def place_of():
    tile = lax.axis_index("tile")
    return tile, tile // 8, lax.rem(tile, 8), lax.axis_index("chan")


def x_peer(d):
    tile, _, _, x = place_of()
    return (tile, lax.rem(x + d, 4))


def z_peer(d):
    _, z, g, x = place_of()
    return (lax.rem(z + d, 8) * 8 + g, x)


def g_peer(d):
    _, z, g, x = place_of()
    return (z * 8 + lax.rem(g + d, 8), x)


def core_peer():
    tile, _, g, x = place_of()
    return (tile + 1 - 2 * lax.rem(g, 2), x)


def xy_peer(dx, dy):
    _, z, g, x = place_of()
    return (z * 8 + lax.rem(g + 2 * dy, 8), lax.rem(x + dx, 4))


AW, BW = 2048, 1536
XD = (1, 3, 2)
ZD = (4, 3, 5, 2, 6, 1, 7)
GD = (4, 3, 5, 2, 6, 1, 7)
XYD = [(dx, dy) for dx in range(4) for dy in range(4) if dx or dy]
EDGE = (0, 31, 0, 31)


def side_by_side(weights, count):
    return jnp.concatenate([weights[t] for t in range(count)], axis=1)


def quarters(act):
    parts = act.reshape(8, 2, 2, 32, 128)
    return jnp.concatenate(
        [parts[:, a, b].reshape(256, 128) for a in range(2) for b in range(2)], axis=1
    )


def flip_map():
    rows = lax.broadcasted_iota(jnp.int32, (128, 128), 0)
    cols = lax.broadcasted_iota(jnp.int32, (128, 128), 1)
    return jnp.where(rows + cols == 127, 1.0, 0.0).astype(BF)


def level_kernel(*refs):
    names = INPUTS + ("out", "final_a", "final_b") + tuple(n for n, _ in SCRATCH)
    r = dict(zip(names, refs))
    tile, z, g, x = place_of()
    y, core = g // 2, lax.rem(g, 2)
    q = x
    mine = pl.ds(pl.multiple_of(x * 32, 32), 32)
    rounds = []

    def rows_of(n):
        return pl.ds(pl.multiple_of(n * 32, 32), 32)

    def local(n, src, dst):
        copy = pltpu.make_async_copy(src, dst, r["lsem"].at[n])
        copy.start()
        return copy

    def begin(whole):
        rounds.append(whole)
        return len(rounds) - 1

    def push(n, src, dst, peer):
        pltpu.make_async_remote_copy(
            src_ref=src, dst_ref=dst, send_sem=r["ss"].at[n], recv_sem=r["rs"].at[n],
            device_id=peer, device_id_type=MESH,
        ).start()

    def spread(whole, dirs, peer, src, dst):
        n = begin(whole)
        for d in dirs:
            push(n, src(d), dst(d), peer(d))
        return n

    def settle(n):
        pltpu.make_async_copy(rounds[n], rounds[n], r["rs"].at[n]).wait()

    barrier = pltpu.get_barrier_semaphore()
    peers = [x_peer(d) for d in XD] + [z_peer(d) for d in ZD] + [g_peer(d) for d in GD]
    peers += [xy_peer(dx, dy) for dx, dy in XYD if dx and dy]
    for peer in peers:
        pl.semaphore_signal(barrier, inc=1, device_id=peer, device_id_type=MESH)

    own_feat = local(0, r["feat"], r["fv"])
    own = {
        "pick": local(1, r["pick"], r["v_pick"]),
        "put": local(2, r["put"], r["v_put"]),
        "adj": local(3, r["adj"], r["s_adj"]),
        "cmap": local(4, r["cmap"], r["v_cmap"]),
        "perm": local(5, r["perm"], r["v_perm"]),
        "fsel": local(6, r["fsel"], r["v_fsel"]),
        "place": local(7, r["place"], r["v_place"]),
        "rout": local(8, r["rout"].at[q], r["v_rout"]),
        "rin": local(9, r["rin"].at[q], r["v_rin"]),
    }
    adj = r["s_adj"]

    own["pick"].wait()
    own["put"].wait()
    own_feat.wait()
    fv, held = r["fv"], (r["held0"], r["held1"])
    stacked = jnp.concatenate([fv[:, s * 1024:(s + 1) * 1024] for s in range(4)], axis=0)
    cols = nn(stacked, r["v_pick"][...]).astype(BF)
    both = nn(cols[0:32], r["v_put"][0])
    for s in range(1, 4):
        both = both + nn(cols[32 * s:32 * s + 32], r["v_put"][s])
    flip = flip_map()
    rims = (
        fv[:, 3968:4096],
        both[:, 0:128].astype(BF),
        nn(fv[:, 0:128], flip).astype(BF),
        both[:, 128:256].astype(BF),
    )
    for s in range(4):
        held[0][z * 4 + s] = rims[s][0:16]
        held[1][g * 4 + s] = rims[s][16:32]
    pl.semaphore_wait(barrier, len(peers))
    ways = ((z, ZD, z_peer), (g, GD, g_peer))
    first = []
    for h in range(2):
        at, dirs, peer = ways[h]
        part = held[h].at[pl.ds(at * 4, 4)]
        first.append(spread(held[h].at[pl.ds(0, 28)], dirs, peer, lambda d: part, lambda d: part))

    def piece(n, j):
        if n == 0:
            start = pl.multiple_of(jnp.clip(j * 1024 - 128, 0, 2816), 128)
            return r["feat"].at[:, pl.ds(start, 1280)], r["strip"].at[mine, :]
        if n == 3:
            return r["ograd"].at[:, pl.ds(pl.multiple_of(j * 1024, 1024), 1024)], r["og"].at[mine, :]
        if n == 5:
            return r["up"], r["v_up"].at[mine, :]
        name = {1: "w1", 2: "wd", 4: "w2"}[n]
        return r[name], r["v_" + name].at[:, mine, :]

    bulk = {}

    def send_bulk(n):
        three = pl.ds(0, 96)
        into = r[("strip", "v_w1", "v_wd", "og", "v_w2", "v_up")[n]]
        whole = into.at[:, three, :] if n in (1, 2, 4) else into.at[three, :]
        m = begin(whole)
        for d in XD:
            src, dst = piece(n, lax.rem(x + d, 4))
            push(m, src, dst, x_peer(d))
        src, dst = piece(n, x)
        bulk[n] = (m, local(10 + n, src, dst))

    def take_bulk(n):
        m, copy = bulk[n]
        copy.wait()
        settle(m)

    for n in range(4):
        send_bulk(n)

    own["adj"].wait()

    def entry(t, k, h=0):
        p = adj[2 * k, t]
        s = lax.rem(adj[2 * k + 1, t] + TURNS[k], 4)
        if h:
            return jnp.logical_and(p >= 0, p // 8 == z), lax.rem(p, 8), s
        return jnp.logical_and(p >= 0, lax.rem(p, 8) == g), p // 8, s

    own["cmap"].wait()
    slots, landed = r["slots"], r["landed"]
    second = []
    for h in (1, 0):
        settle(first[h])
        _, dirs, peer = ways[1 - h]
        order = dirs + (0,)
        m = begin(landed.at[h, pl.ds(1, 7)])
        second.append(m)
        corners = [[] for _ in range(4)]
        for d in order:
            t = z * 8 + lax.rem(g + d, 8) if h == 0 else lax.rem(z + d, 8) * 8 + g
            for k in range(8):
                owned, n, s = entry(t, k, h)
                block = held[h][jnp.where(owned, n * 4 + s, 0)]
                block = jnp.where(owned, block, jnp.zeros_like(block))
                if k < 4:
                    slots[h, d, :, k * 128:(k + 1) * 128] = block
                else:
                    corners[k - 4].append(block)
        corner = nn(jnp.concatenate(corners[0], axis=0), r["v_cmap"][0])
        for k in range(1, 4):
            corner = corner + nn(jnp.concatenate(corners[k], axis=0), r["v_cmap"][k])
        for n, d in enumerate(order):
            slots[h, d, :, 512:640] = corner[16 * n:16 * n + 16].astype(BF)
            if d:
                push(m, slots.at[h, d], landed.at[h, d], peer(d))
    own["perm"].wait()
    take_bulk(0)
    perm, cb, strip = r["v_perm"], r["cb"], r["strip"]
    perms = perm[...].reshape(384, 128)
    shift = jnp.where(q == 0, -1, jnp.where(q == 3, 1, 0))

    def strip_block(n):
        at = jnp.clip(n + shift, 0, 9)
        return strip[:, pl.ds(pl.multiple_of(at * 128, 128), 128)]

    for n in range(1, 9):
        turned = nt(perms, strip_block(n))
        for b in range(3):
            cb[b, n * 128:(n + 1) * 128, :] = turned[b * 128:(b + 1) * 128].astype(BF)

    halves_of = []
    for m, h in zip(second, (1, 0)):
        settle(m)
        total = slots[h, 0].astype(F32)
        for d in range(1, 8):
            total = total + landed[h, d].astype(F32)
        halves_of.append(total)
    total = jnp.concatenate([halves_of[1], halves_of[0]], axis=0).astype(BF)

    own["fsel"].wait()
    picked, pout = r["picked"], r["pout"]
    ends = (total[:, 0:128], None, None, nn(total[:, 256:384], flip).astype(BF))
    for j in range(4):
        pout[j, :, 0:128] = nt(total, r["v_fsel"][j]).astype(BF)
        pout[j, :, 128:256] = jnp.zeros((32, 128), BF) if ends[j] is None else ends[j]
    c_x = spread(
        picked.at[pl.ds(0, 96), :], XD, x_peer, lambda d: pout.at[lax.rem(x + d, 4)], lambda d: picked.at[mine, :]
    )
    picked[mine, :] = pout[x]
    for n in (5, 4):
        send_bulk(n)
    own["place"].wait()
    take_bulk(1)
    take_bulk(2)
    w1c = side_by_side(r["v_w1"], 9)
    settle(c_x)

    for n in (0, 9):
        block = jnp.where(q == n // 3, picked[:, 128:256], strip_block(n))
        turned = nt(perms, block)
        for b in range(3):
            cb[b, n * 128:(n + 1) * 128, :] = turned[b * 128:(b + 1) * 128].astype(BF)
    sides = picked[:, 0:128]
    for b in (0, 2):
        cb[b] = (cb[b].astype(F32) + nt(r["v_place"][b // 2], sides)).astype(BF)
    z1, act1 = r["z1"], r["act1"]
    for n in range(4):
        taps = jnp.concatenate(
            [cb[b, a * 128 + n * 256:a * 128 + n * 256 + 256, :] for a in range(3) for b in range(3)], axis=1
        )
        pre = nt(taps, w1c)
        z1[n * 256:(n + 1) * 256, :] = pre
        act1[n * 256:(n + 1) * 256, :] = gelu(pre).astype(BF)
    pre = nt(quarters(act1[...]), side_by_side(r["v_wd"], 4))
    r["z2"][...] = pre
    act2 = gelu(pre).astype(BF)
    r["act2"][...] = act2
    own["rout"].wait()
    rq = r["rq"]
    rq[...] = tn(act2, r["v_rout"][...]).astype(BF)

    x2in, halo = r["x2in"], r["halo"]
    c_x = spread(
        x2in.at[pl.ds(1, 3)], XD, x_peer, lambda d: rq.at[rows_of(lax.rem(x + d, 4)), :], lambda d: x2in.at[d]
    )
    c_h = begin(halo)
    push(c_h, r["act2"].at[pl.ds(224, 32), :], halo.at[0], x_peer(1))
    push(c_h, r["act2"].at[pl.ds(0, 32), :], halo.at[1], x_peer(3))
    total = rq[mine, :].astype(F32)
    settle(c_x)
    for d in XD:
        total = total + x2in[d].astype(F32)
    held2 = r["held2"]
    held2[z] = total.astype(BF)
    c_z = spread(held2.at[pl.ds(0, 7)], ZD, z_peer, lambda d: held2.at[z], lambda d: held2.at[z])

    take_bulk(3)
    take_bulk(5)
    og, ogt, up = r["og"], r["ogt"], r["v_up"]
    flat = perm[1]
    for n in range(8):
        ogt[n * 128:(n + 1) * 128, :] = nt(flat, og[:, n * 128:(n + 1) * 128]).astype(BF)
    cells = ogt[...].astype(F32).reshape(8, 4, 32, 128)
    pooled = (cells[:, 0] + cells[:, 1] + cells[:, 2] + cells[:, 3]).reshape(256, 128).astype(BF)
    back_up = nn(pooled, up[...])

    settle(c_z)
    rolled = r["rolled"]
    for n in range(8):
        block = held2[n].astype(F32)
        rolled[n * 4] = held2[n]
        for m in range(1, 4):
            rolled[n * 4 + m] = pltpu.roll(block, 32 * m, 1).astype(BF)
    lane = lax.broadcasted_iota(jnp.int32, (32, 128), 1)
    slots2, landed2 = r["slots2"], r["landed2"]
    c_g = begin(landed2.at[pl.ds(1, 7)])
    for d in GD + (0,):
        t = z * 8 + lax.rem(g + d, 8)
        both = [jnp.zeros((32, 128), F32), jnp.zeros((32, 128), F32)]
        for k in range(8):
            owned, n, s = entry(t, k)
            block = rolled[jnp.where(owned, n * 4 + lax.rem(k + 4 - s, 4), 0)].astype(F32)
            block = jnp.where(owned, block, 0.0)
            if k < 4:
                both[0] = jnp.where(lane // 32 == k, block, both[0])
            else:
                both[1] = jnp.where(lane == 32 * (k - 4) + EDGE[k - 4], block, both[1])
        slots2[d, :, 0:128] = both[0].astype(BF)
        slots2[d, :, 128:256] = both[1].astype(BF)
        if d:
            push(c_g, slots2.at[d], landed2.at[d], g_peer(d))
    settle(c_g)
    total = slots2[0].astype(F32)
    for d in range(1, 8):
        total = total + landed2[d].astype(F32)
    picked2 = r["picked2"]
    picked2[mine, :] = total.astype(BF)
    part2 = picked2.at[mine, :]
    c_x = spread(picked2.at[pl.ds(0, 96), :], XD, x_peer, lambda d: part2, lambda d: part2)
    own["rin"].wait()
    take_bulk(4)
    settle(c_h)
    settle(c_x)

    sel = r["v_rin"][...]
    rim = nt(sel, picked2[...])
    upper = jnp.where(q == 0, 0.0, halo[0].astype(F32))
    lower = jnp.where(q == 3, 0.0, halo[1].astype(F32))
    rows = jnp.concatenate([upper, act2.astype(F32), lower], axis=0) + rim[0:320]
    col = lax.rem(lax.broadcasted_iota(jnp.int32, (320, 128), 0), 32)
    west = jnp.where(col == 0, 0.0, pltpu.roll(rows, 1, 0)) + rim[320:640]
    east = jnp.where(col == 31, 0.0, pltpu.roll(rows, 319, 0)) + rim[640:960]
    blocks = [v.astype(BF) for v in (west, rows, east)]
    taps2 = jnp.concatenate([blocks[b][a * 32:a * 32 + 256] for a in range(3) for b in range(3)], axis=1)
    w2 = r["v_w2"]
    pre = nt(taps2, side_by_side(w2, 9))
    gz3 = (gelu_slope(pre) * back_up).astype(BF)
    none32, none64 = jnp.zeros((32, 128), F32), jnp.zeros((64, 128), F32)
    back = []
    for b in range(3):
        v0, v1, v2 = (nn(gz3, w2[3 * a + b]) for a in range(3))
        back.append(
            jnp.concatenate([v0, none64], axis=0)
            + jnp.concatenate([none32, v1, none32], axis=0)
            + jnp.concatenate([none64, v2], axis=0)
        )
    mid = (
        back[1]
        + jnp.where(col == 31, 0.0, pltpu.roll(back[0], 319, 0))
        + jnp.where(col == 0, 0.0, pltpu.roll(back[2], 1, 0))
    )
    cat = jnp.concatenate([mid.astype(BF), back[0].astype(BF), back[2].astype(BF)], axis=0)
    dq = r["dq"]
    dq[...] = tn(cat, sel).astype(BF)
    x4in, hout, hin = r["x4in"], r["hout"], r["hin"]
    c_x = spread(
        x4in.at[pl.ds(1, 3)], XD, x_peer, lambda d: dq.at[rows_of(lax.rem(x + d, 4)), :], lambda d: x4in.at[d]
    )
    hout[0] = mid[288:320]
    hout[1] = mid[0:32]
    c_h = begin(hin)
    push(c_h, hout.at[0], hin.at[0], x_peer(1))
    push(c_h, hout.at[1], hin.at[1], x_peer(3))

    other = 1 - core

    def halves(name, wide, parts):
        outs, ins = r[name + "c"], r[name + "ci"]
        for n in range(4):
            rows_n = pl.ds(pl.multiple_of(n * 32 + other * 16, 16), 16)
            at = 0
            for ref in parts:
                width = ref.shape[1]
                outs[n, :, at:at + width] = ref[rows_n, :].astype(BF)
                at += width
            outs[n, :, at:wide] = jnp.zeros((16, wide - at), BF)
        n = begin(ins)
        push(n, outs, ins, core_peer())
        return n

    def shares(name, wide, parts):
        outs, ins = r[name + "o"], r[name + "i"]
        share = wide // 4
        for n in range(4):
            rows_n = pl.ds(pl.multiple_of(n * 32 + core * 16, 16), 16)
            own_n = jnp.concatenate(
                [ref[rows_n, :] for ref in parts]
                + [jnp.zeros((16, wide - sum(ref.shape[1] for ref in parts)), F32)],
                axis=1,
            )
            summed = (own_n + r[name + "ci"][n].astype(F32)).astype(BF)
            for m in range(4):
                outs[n, m] = summed[:, m * share:(m + 1) * share]
        m = begin(ins.at[pl.ds(1, 15)])
        for dx, dy in XYD:
            push(m, outs.at[lax.rem(x + dx, 4), lax.rem(y + dy, 4)], ins.at[dx * 4 + dy], xy_peer(dx, dy))
        return m

    def along_z(name):
        total = r[name + "o"][x, y].astype(F32)
        for n in range(1, 16):
            total = total + r[name + "i"][n].astype(F32)
        zall = r[name + "z"]
        zall[z] = total.astype(BF)
        return spread(zall.at[pl.ds(0, 7)], ZD, z_peer, lambda d: zall.at[z], lambda d: zall.at[z])

    def whole(name):
        zall = r[name + "z"]
        total = zall[0].astype(F32)
        for n in range(1, 8):
            total = total + zall[n].astype(F32)
        return total.astype(BF)

    coarse = gelu(pre).astype(BF)
    lifted = nt(coarse, up[...])
    out, ostrip = r["out"], r["ostrip"]
    for n in range(8):
        row = lifted[n * 32:(n + 1) * 32]
        summed = act1[n * 128:(n + 1) * 128, :].astype(F32) + jnp.concatenate([row] * 4, axis=0)
        ostrip[:, n * 128:(n + 1) * 128] = tn(summed.astype(BF), flat).astype(BF)

    settle(c_x)
    total = dq[mine, :].astype(F32)
    for d in XD:
        total = total + x4in[d].astype(F32)
    held3 = r["held3"]
    held3[g] = total.astype(BF)
    c_g = spread(held3.at[pl.ds(0, 7)], GD, g_peer, lambda d: held3.at[g], lambda d: held3.at[g])
    lanes = pl.ds(pl.multiple_of(x * 1024, 1024), 1024)
    c_o = spread(
        out.at[:, pl.ds(0, 3072)], XD, x_peer,
        lambda d: ostrip.at[rows_of(lax.rem(x + d, 4)), :], lambda d: out.at[:, lanes],
    )
    own_out = local(16, ostrip.at[mine, :], out.at[:, lanes])

    r["gb_u"][...] = tn(pooled, coarse)
    r["gb_w"][...] = tn(gz3, taps2)
    parts_b = (r["gb_w"], r["gb_u"])
    c_bc = halves("b", BW, parts_b)
    settle(c_g)
    rolled3 = r["rolled3"]
    for j in range(8):
        for h in range(2):
            block = held3[j, :, 128 * h:128 * h + 128]
            rolled3[j * 8 + h * 4] = block
            for m in range(1, 4):
                rolled3[j * 8 + h * 4 + m] = pltpu.roll(block.astype(F32), 32 * m, 1).astype(BF)
    sums = [jnp.zeros((32, 128), F32) for _ in range(8)]
    for j in range(8):
        for k in range(8):
            owned, n, s = entry(z * 8 + j, k)
            block = rolled3[j * 8 + (k // 4) * 4 + lax.rem(s + 4 - k % 4, 4)].astype(F32)
            if k < 4:
                block = jnp.where(lane // 32 == s, block, 0.0)
            else:
                block = jnp.where(lane == 32 * s + EDGE[k - 4], block, 0.0)
            n = jnp.where(owned, n, -1)
            for m in range(8):
                sums[m] = sums[m] + jnp.where(n == m, block, 0.0)
    slots3, landed3 = r["slots3"], r["landed3"]
    for n in range(8):
        slots3[n] = sums[n].astype(BF)
    c_z = spread(
        landed3.at[pl.ds(1, 7)], ZD, z_peer, lambda d: slots3.at[lax.rem(z + d, 8)], lambda d: landed3.at[d]
    )
    settle(c_bc)
    c_b = shares("b", BW, parts_b)
    slope2 = gelu_slope(r["z2"][...])
    settle(c_z)
    total = slots3[z].astype(F32)
    for d in ZD:
        total = total + landed3[d].astype(F32)
    back_rim = r["back_rim"]
    back_rim[mine, :] = total.astype(BF)
    part3 = back_rim.at[mine, :]
    c_x = spread(back_rim.at[pl.ds(0, 96), :], XD, x_peer, lambda d: part3, lambda d: part3)
    settle(c_b)
    c_bz = along_z("b")
    settle(c_h)
    upper = jnp.where(q == 0, 0.0, hin[0])
    lower = jnp.where(q == 3, 0.0, hin[1])
    ga2 = mid[32:288] + jnp.concatenate([upper, jnp.zeros((192, 128), F32), lower], axis=0)
    settle(c_x)

    gz2 = (slope2 * (ga2 + nt(r["v_rout"][...], back_rim[...]))).astype(BF)
    wd = r["v_wd"]
    fine = [nn(gz2, wd[t]).reshape(8, 1, 32, 128) for t in range(4)]
    grown = jnp.concatenate(fine, axis=1).reshape(1024, 128)
    gz1 = (gelu_slope(z1[...]) * (ogt[...].astype(F32) + grown)).astype(BF)
    for a in range(3):
        for b in range(3):
            t = 3 * a + b
            r["ga_w"][:, t * 128:(t + 1) * 128] = tn(gz1, cb[b, a * 128:a * 128 + 1024, :])
    r["ga_d"][...] = tn(gz2, quarters(act1[...]))
    parts_a = (r["ga_w"], r["ga_d"])
    c_ac = halves("a", AW, parts_a)

    def along_y(name, n):
        settle(n)
        yall = r[name + "y"]
        yall[y] = whole(name)
        return spread(yall.at[pl.ds(0, 3)], XD, lambda d: xy_peer(0, d), lambda d: yall.at[y], lambda d: yall.at[y])

    def to_core(name, n):
        settle(n)
        yall, final = r[name + "y"], r["final_" + name]
        m = begin(yall)
        push(m, yall, final.at[core], core_peer())
        final[core] = yall[...]
        return m

    c_by = along_y("b", c_bz)
    settle(c_ac)
    c_a = shares("a", AW, parts_a)
    c_bf = to_core("b", c_by)
    settle(c_a)
    c_az = along_z("a")
    settle(c_bf)
    settle(c_o)
    settle(to_core("a", along_y("a", c_az)))
    own_out.wait()
    for n, whole in enumerate(rounds):
        pltpu.make_async_copy(whole, whole, r["ss"].at[n]).wait()


INPUTS = (
    "adj", "feat", "ograd", "w1", "wd", "w2", "up",
    "pick", "put", "perm", "cmap", "fsel", "place", "rout", "rin",
)


def buf(*shape, kind=BF):
    return pltpu.VMEM(shape, kind)


def sems(*shape):
    return pltpu.SemaphoreType.DMA(shape)


SCRATCH = [
    ("lsem", sems(17)), ("ss", sems(32)), ("rs", sems(32)), ("s_adj", pltpu.SMEM((16, 64), jnp.int32)),
    ("fv", buf(32, 4096)), ("v_pick", buf(1024, 128)), ("v_put", buf(4, 128, 256)), ("v_perm", buf(3, 128, 128)),
    ("v_cmap", buf(4, 128, 128)), ("v_fsel", buf(4, 128, 640)), ("v_place", buf(2, 1280, 128)),
    ("v_rout", buf(256, 128)), ("v_rin", buf(960, 256)),
    ("strip", buf(128, 1280)), ("og", buf(128, 1024)), ("v_w1", buf(9, 128, 128)), ("v_wd", buf(4, 128, 128)),
    ("v_w2", buf(9, 128, 128)), ("v_up", buf(128, 128)),
    ("held0", buf(32, 16, 128)), ("held1", buf(32, 16, 128)), ("slots", buf(2, 8, 16, 640)), ("landed", buf(2, 8, 16, 640)),
    ("pout", buf(4, 32, 256)), ("picked", buf(128, 256)),
    ("cb", buf(3, 1280, 128)), ("z1", buf(1024, 128, kind=F32)), ("act1", buf(1024, 128)),
    ("z2", buf(256, 128, kind=F32)), ("act2", buf(256, 128)), ("rq", buf(128, 128)), ("x2in", buf(4, 32, 128)),
    ("halo", buf(2, 32, 128)), ("held2", buf(8, 32, 128)), ("rolled", buf(32, 32, 128)), ("ogt", buf(1024, 128)),
    ("slots2", buf(8, 32, 256)), ("landed2", buf(8, 32, 256)), ("picked2", buf(128, 256)),
    ("dq", buf(128, 256)), ("x4in", buf(4, 32, 256)),
    ("hout", buf(2, 32, 128, kind=F32)), ("hin", buf(2, 32, 128, kind=F32)),
    ("held3", buf(8, 32, 256)), ("rolled3", buf(64, 32, 128)), ("ostrip", buf(128, 1024)),
    ("slots3", buf(8, 32, 128)), ("landed3", buf(8, 32, 128)), ("back_rim", buf(128, 128)),
    ("gb_u", buf(128, 128, kind=F32)), ("gb_w", buf(128, 1152, kind=F32)),
    ("ga_d", buf(128, 512, kind=F32)), ("ga_w", buf(128, 1152, kind=F32)),
    ("bc", buf(4, 16, BW)), ("bci", buf(4, 16, BW)), ("bo", buf(4, 4, 16, BW // 4)), ("bi", buf(16, 16, BW // 4)),
    ("bz", buf(8, 16, BW // 4)),
    ("ac", buf(4, 16, AW)), ("aci", buf(4, 16, AW)), ("ao", buf(4, 4, 16, AW // 4)), ("ai", buf(16, 16, AW // 4)),
    ("az", buf(8, 16, AW // 4)),
    ("ay", buf(4, 16, AW // 4)), ("by", buf(4, 16, BW // 4)),
]


def level_call(*args):
    return pl.pallas_call(
        level_kernel,
        out_shape=(pltpu.VMEM((32, 4096), BF), pltpu.VMEM((2, 4, 16, AW // 4), BF), pltpu.VMEM((2, 4, 16, BW // 4), BF)),
        in_specs=[ANY] * 15,
        out_specs=[VM] * 3,
        scratch_shapes=[s for _, s in SCRATCH],
        compiler_params=pltpu.CompilerParams(collective_id=0, has_side_effects=True, vmem_limit_bytes=LIMIT),
    )(*args)


def result_kernel(out_in, final_a, final_b, out, g1, gd, g2, gu, *, scale):
    out[...] = out_in[...]
    for c in range(2):
        rows = pl.ds(c * 16, 16)
        for t in range(13):
            block = final_a[c, t // 4, :, (t % 4) * 128:(t % 4 + 1) * 128].astype(F32) * scale
            if t < 9:
                g1[t, rows, :] = block
            else:
                gd[t - 9, rows, :] = block
        for t in range(10):
            at = (t % 3) * 128
            block = final_b[c, t // 3, :, at:at + 128].astype(F32) * scale
            if t < 9:
                g2[t, rows, :] = block
            else:
                gu[rows, :] = block


def result_call(out_in, final_a, final_b, scale):
    return pl.pallas_call(
        functools.partial(result_kernel, scale=scale),
        out_shape=(
            jax.ShapeDtypeStruct((32, 4096), BF),
            jax.ShapeDtypeStruct((9, 32, 128), F32),
            jax.ShapeDtypeStruct((4, 32, 128), F32),
            jax.ShapeDtypeStruct((9, 32, 128), F32),
            jax.ShapeDtypeStruct((32, 128), F32),
        ),
        in_specs=[VM] * 3,
        out_specs=[VM] * 5,
        compiler_params=pltpu.CompilerParams(vmem_limit_bytes=16 * 1024 * 1024),
    )(out_in, final_a, final_b)


def per_device(features, conv1_weight, down_weight, conv2_weight, up_weight, out_grad, adjacency):
    pick, put = fine_rim_out()
    fine_sel, fine_place = fine_rim_maps()
    maps = [
        jnp.asarray(m, BF)
        for m in (pick, put, fine_perm(), corner_maps(), fine_sel, fine_place, coarse_rim_out(), coarse_rim_in())
    ]
    out, final_a, final_b = level_call(
        adjacency.transpose(1, 2, 0).reshape(16, 64), features, out_grad, conv1_weight, down_weight, conv2_weight, up_weight, *maps
    )
    return result_call(out, final_a, final_b, 262144 ** -0.5)


def solution(mesh):
    weights = P(None, "chan", None)
    return jax.shard_map(
        per_device,
        mesh=mesh,
        in_specs=(P("chan", "tile"), weights, weights, weights, P("chan", None), P("chan", "tile"), P()),
        out_specs=(P("chan", "tile"), weights, weights, weights, P("chan", None)),
        check_vma=False,
    )
```

```python
import functools

import jax
import jax.numpy as jnp
import numpy as np
from jax import lax
from jax.experimental import pallas as pl
from jax.experimental.pallas import tpu as pltpu
from jax.sharding import PartitionSpec as P

BF = jnp.bfloat16
F32 = jnp.float32
MESH = pl.DeviceIdType.MESH
TURNS = (0, 1, 2, 3, 0, 2, 2, 0)
VM = pl.BlockSpec(memory_space=pltpu.VMEM)
ANY = pl.BlockSpec(memory_space=pl.ANY)
LIMIT = 56 * 1024 * 1024


def fine_perm():
    out = np.zeros((3, 128, 128), np.float32)
    for b in range(3):
        for rr in range(2):
            for par in range(2):
                for k in range(32):
                    col = 2 * (k - 1 + b) + par
                    if 0 <= col < 64:
                        out[b, rr * 64 + par * 32 + k, rr * 64 + col] = 1
    return out


def corner_maps():
    out = np.zeros((4, 128, 128), np.float32)
    for i in range(2):
        for j in range(2):
            out[0, i * 64 + j, 2 * i + j] = 1
            out[1, (1 - i) * 64 + 63 - j, 4 + 2 * i + j] = 1
            out[2, (1 - i) * 64 + 1 - j, 8 + 2 * i + j] = 1
            out[3, i * 64 + 62 + j, 12 + 2 * i + j] = 1
    return out


def fine_rim_maps():
    sel = np.zeros((4, 128, 640), np.float32)
    for q in range(4):
        for r in range(20):
            ir = 16 * q - 2 + r
            for par in range(2):
                if 0 <= ir < 64:
                    west = 384 + par * 64 + 63 - ir
                    east = 128 + (1 - par) * 64 + ir
                elif ir < 0:
                    west = 512 + 12 + 2 * (ir + 2) + par
                    east = 512 + 0 + 2 * (ir + 2) + par
                else:
                    west = 512 + 8 + 2 * (ir - 64) + par
                    east = 512 + 4 + 2 * (ir - 64) + par
                sel[q, r * 2 + par, west] = 1
                sel[q, 64 + r * 2 + par, east] = 1
    place = np.zeros((2, 1280, 128), np.float32)
    for r in range(20):
        for par in range(2):
            place[0, r * 64 + par * 32, r * 2 + par] = 1
            place[1, r * 64 + par * 32 + 31, 64 + r * 2 + par] = 1
    return sel, place


def fine_rim_out():
    pick = np.zeros((1024, 128), np.float32)
    for r in range(16):
        for kind, col in enumerate((0, 1, 62, 63)):
            pick[r * 64 + col, kind * 16 + r] = 1
    put = np.zeros((4, 128, 256), np.float32)
    for s in range(4):
        for r16 in range(16):
            r = 16 * s + r16
            for kind, lane in enumerate((64 + r, r, 128 + 63 - r, 192 + 63 - r)):
                put[s, kind * 16 + r16, lane] = 1
    return pick, put


def coarse_rim_out():
    out = np.zeros((4, 256, 128), np.float32)
    for i in range(32):
        for s, (r, k) in enumerate(((31, i), (i, 0), (0, 31 - i), (31 - i, 31))):
            out[r // 8, (r % 8) * 32 + k, s * 32 + i] = 1
    return out


def coarse_rim_in():
    out = np.zeros((4, 960, 256), np.float32)
    for k in range(32):
        out[0, k, k] = 1
        out[3, 9 * 32 + k, 64 + 31 - k] = 1
    for q in range(4):
        for r in range(10):
            row = 8 * q - 1 + r
            if row < 0:
                west, east = 255, 128
            elif row >= 32:
                west, east = 192, 191
            else:
                west, east = 96 + 31 - row, 32 + row
            out[q, 320 + r * 32, west] = 1
            out[q, 640 + r * 32 + 31, east] = 1
    return out


def nt(a, b):
    return lax.dot_general(a, b, (((1,), (1,)), ((), ())), preferred_element_type=F32)


def tn(a, b):
    return lax.dot_general(a, b, (((0,), (0,)), ((), ())), preferred_element_type=F32)


def nn(a, b):
    return lax.dot_general(a, b, (((1,), (0,)), ((), ())), preferred_element_type=F32)


ROOT = 0.7978845608028654


def gelu(v):
    return 0.5 * v * (1.0 + jnp.tanh(ROOT * (v + 0.044715 * (v * v * v))))


def gelu_slope(v):
    t = jnp.tanh(ROOT * (v + 0.044715 * (v * v * v)))
    return 0.5 * (1.0 + t) + 0.5 * v * (1.0 - t * t) * (ROOT * (1.0 + 3 * 0.044715 * (v * v)))


def place_of():
    tile = lax.axis_index("tile")
    return tile, tile // 8, lax.rem(tile, 8), lax.axis_index("chan")


def x_peer(d):
    tile, _, _, x = place_of()
    return (tile, lax.rem(x + d, 4))


def z_peer(d):
    _, z, g, x = place_of()
    return (lax.rem(z + d, 8) * 8 + g, x)


def g_peer(d):
    _, z, g, x = place_of()
    return (z * 8 + lax.rem(g + d, 8), x)


def core_peer():
    tile, _, g, x = place_of()
    return (tile + 1 - 2 * lax.rem(g, 2), x)


def xy_peer(dx, dy):
    _, z, g, x = place_of()
    return (z * 8 + lax.rem(g + 2 * dy, 8), lax.rem(x + dx, 4))


AW, BW = 2048, 1536
XD = (2, 1, 3)
ZD = (4, 3, 5, 2, 6, 1, 7)
GD = (4, 3, 5, 2, 6, 1, 7)
FAR = (2, 1, 3, 0)
XYD = [(dx, dy) for dx in FAR for dy in FAR if dx or dy]
EDGE = (0, 31, 0, 31)


def side_by_side(weights, count):
    return jnp.concatenate([weights[t] for t in range(count)], axis=1)


def quarters(act):
    parts = act.reshape(8, 2, 2, 32, 128)
    return jnp.concatenate(
        [parts[:, a, b].reshape(256, 128) for a in range(2) for b in range(2)], axis=1
    )


def flip_map():
    rows = lax.broadcasted_iota(jnp.int32, (128, 128), 0)
    cols = lax.broadcasted_iota(jnp.int32, (128, 128), 1)
    return jnp.where(rows + cols == 127, 1.0, 0.0).astype(BF)


def level_kernel(*refs):
    names = INPUTS + ("out", "final_a", "final_b") + tuple(n for n, _ in SCRATCH)
    r = dict(zip(names, refs))
    tile, z, g, x = place_of()
    y, core = g // 2, lax.rem(g, 2)
    q = x
    mine = pl.ds(pl.multiple_of(x * 32, 32), 32)
    rounds = []

    def rows_of(n):
        return pl.ds(pl.multiple_of(n * 32, 32), 32)

    def local(n, src, dst):
        copy = pltpu.make_async_copy(src, dst, r["lsem"].at[n])
        copy.start()
        return copy

    def begin(whole):
        rounds.append(whole)
        return len(rounds) - 1

    def push(n, src, dst, peer):
        pltpu.make_async_remote_copy(
            src_ref=src, dst_ref=dst, send_sem=r["ss"].at[n], recv_sem=r["rs"].at[n],
            device_id=peer, device_id_type=MESH,
        ).start()

    def spread(whole, dirs, peer, src, dst):
        n = begin(whole)
        for d in dirs:
            push(n, src(d), dst(d), peer(d))
        return n

    def settle(n):
        pltpu.make_async_copy(rounds[n], rounds[n], r["rs"].at[n]).wait()

    barrier = pltpu.get_barrier_semaphore()
    peers = [x_peer(d) for d in XD] + [z_peer(d) for d in ZD] + [g_peer(d) for d in GD]
    peers += [xy_peer(dx, dy) for dx, dy in XYD if dx and dy]
    for peer in peers:
        pl.semaphore_signal(barrier, inc=1, device_id=peer, device_id_type=MESH)

    own_feat = local(0, r["feat"], r["fv"])
    own = {
        "pick": local(1, r["pick"], r["v_pick"]),
        "put": local(2, r["put"], r["v_put"]),
        "adj": local(3, r["adj"], r["s_adj"]),
    }
    adj = r["s_adj"]

    own["pick"].wait()
    own["put"].wait()
    own_feat.wait()
    fv, held = r["fv"], (r["held0"], r["held1"])
    stacked = jnp.concatenate([fv[:, s * 1024:(s + 1) * 1024] for s in range(4)], axis=0)
    cols = nn(stacked, r["v_pick"][...]).astype(BF)
    both = nn(cols[0:32], r["v_put"][0])
    for s in range(1, 4):
        both = both + nn(cols[32 * s:32 * s + 32], r["v_put"][s])
    flip = flip_map()
    rims = (
        fv[:, 3968:4096],
        both[:, 0:128].astype(BF),
        nn(fv[:, 0:128], flip).astype(BF),
        both[:, 128:256].astype(BF),
    )
    for s in range(4):
        held[0][z * 4 + s] = rims[s][0:16]
        held[1][g * 4 + s] = rims[s][16:32]
    pl.semaphore_wait(barrier, len(peers))
    ways = ((z, ZD, z_peer), (g, GD, g_peer))
    first = []
    for h in range(2):
        at, dirs, peer = ways[h]
        part = held[h].at[pl.ds(at * 4, 4)]
        first.append(spread(held[h].at[pl.ds(0, 28)], dirs, peer, lambda d: part, lambda d: part))

    own.update({
        "cmap": local(4, r["cmap"], r["v_cmap"]),
        "perm": local(5, r["perm"], r["v_perm"]),
        "fsel": local(6, r["fsel"], r["v_fsel"]),
        "place": local(7, r["place"], r["v_place"]),
        "rout": local(8, r["rout"].at[q], r["v_rout"]),
        "rin": local(9, r["rin"].at[q], r["v_rin"]),
    })

    def piece(n, j):
        if n == 0:
            start = pl.multiple_of(jnp.clip(j * 1024 - 128, 0, 2816), 128)
            return r["feat"].at[:, pl.ds(start, 1280)], r["strip"].at[mine, :]
        if n == 3:
            return r["ograd"].at[:, pl.ds(pl.multiple_of(j * 1024, 1024), 1024)], r["og"].at[mine, :]
        if n == 5:
            return r["up"], r["v_up"].at[mine, :]
        name = {1: "w1", 2: "wd", 4: "w2"}[n]
        return r[name], r["v_" + name].at[:, mine, :]

    bulk = {}

    def send_bulk(n):
        three = pl.ds(0, 96)
        into = r[("strip", "v_w1", "v_wd", "og", "v_w2", "v_up")[n]]
        whole = into.at[:, three, :] if n in (1, 2, 4) else into.at[three, :]
        m = begin(whole)
        for d in XD:
            src, dst = piece(n, lax.rem(x + d, 4))
            push(m, src, dst, x_peer(d))
        src, dst = piece(n, x)
        bulk[n] = (m, local(10 + n, src, dst))

    def take_bulk(n):
        m, copy = bulk[n]
        copy.wait()
        settle(m)

    for n in range(4):
        send_bulk(n)

    own["adj"].wait()

    def entry(t, k, h=0):
        p = adj[2 * k, t]
        s = lax.rem(adj[2 * k + 1, t] + TURNS[k], 4)
        if h:
            return jnp.logical_and(p >= 0, p // 8 == z), lax.rem(p, 8), s
        return jnp.logical_and(p >= 0, lax.rem(p, 8) == g), p // 8, s

    own["cmap"].wait()
    slots, landed = r["slots"], r["landed"]
    second = []
    for h in (1, 0):
        settle(first[h])
        _, dirs, peer = ways[1 - h]
        order = dirs + (0,)
        m = begin(landed.at[h, pl.ds(1, 7)])
        second.append(m)
        corners = [[] for _ in range(4)]
        for d in order:
            t = z * 8 + lax.rem(g + d, 8) if h == 0 else lax.rem(z + d, 8) * 8 + g
            for k in range(8):
                owned, n, s = entry(t, k, h)
                block = held[h][jnp.where(owned, n * 4 + s, 0)]
                block = jnp.where(owned, block, jnp.zeros_like(block))
                if k < 4:
                    slots[h, d, :, k * 128:(k + 1) * 128] = block
                else:
                    corners[k - 4].append(block)
        corner = nn(jnp.concatenate(corners[0], axis=0), r["v_cmap"][0])
        for k in range(1, 4):
            corner = corner + nn(jnp.concatenate(corners[k], axis=0), r["v_cmap"][k])
        for n, d in enumerate(order):
            slots[h, d, :, 512:640] = corner[16 * n:16 * n + 16].astype(BF)
            if d:
                push(m, slots.at[h, d], landed.at[h, d], peer(d))
    own["perm"].wait()
    take_bulk(0)
    perm, cb, strip = r["v_perm"], r["cb"], r["strip"]
    perms = perm[...].reshape(384, 128)
    shift = jnp.where(q == 0, -1, jnp.where(q == 3, 1, 0))

    def strip_block(n):
        at = jnp.clip(n + shift, 0, 9)
        return strip[:, pl.ds(pl.multiple_of(at * 128, 128), 128)]

    for n in range(1, 9):
        turned = nt(perms, strip_block(n))
        for b in range(3):
            cb[b, n * 128:(n + 1) * 128, :] = turned[b * 128:(b + 1) * 128].astype(BF)

    halves_of = []
    for m, h in zip(second, (1, 0)):
        settle(m)
        total = slots[h, 0].astype(F32)
        for d in range(1, 8):
            total = total + landed[h, d].astype(F32)
        halves_of.append(total)
    total = jnp.concatenate([halves_of[1], halves_of[0]], axis=0).astype(BF)

    own["fsel"].wait()
    picked, pout = r["picked"], r["pout"]
    ends = (total[:, 0:128], None, None, nn(total[:, 256:384], flip).astype(BF))
    for j in range(4):
        pout[j, :, 0:128] = nt(total, r["v_fsel"][j]).astype(BF)
        pout[j, :, 128:256] = jnp.zeros((32, 128), BF) if ends[j] is None else ends[j]
    c_x = spread(
        picked.at[pl.ds(0, 96), :], XD, x_peer, lambda d: pout.at[lax.rem(x + d, 4)], lambda d: picked.at[mine, :]
    )
    picked[mine, :] = pout[x]
    for n in (5, 4):
        send_bulk(n)
    own["place"].wait()
    take_bulk(1)
    take_bulk(2)
    w1c = side_by_side(r["v_w1"], 9)
    for n in (0, 9):
        block = strip_block(n)
        turned = nt(perms, jnp.where(q == n // 3, jnp.zeros_like(block), block))
        for b in range(3):
            cb[b, n * 128:(n + 1) * 128, :] = turned[b * 128:(b + 1) * 128].astype(BF)
    z1, act1 = r["z1"], r["act1"]
    w1 = r["v_w1"]

    def fine_taps(n):
        return jnp.concatenate(
            [cb[b, a * 128 + n * 256:a * 128 + n * 256 + 256, :] for a in range(3) for b in range(3)], axis=1
        )

    for n in range(4):
        z1[n * 256:(n + 1) * 256, :] = nt(fine_taps(n), w1c)
    w1_west = jnp.concatenate([w1[3 * a] for a in range(3)], axis=1)
    w1_east = jnp.concatenate([w1[3 * a + 2] for a in range(3)], axis=1)
    w1_end = jnp.where(q == 0, side_by_side(w1, 3), side_by_side(w1[6:9], 3))
    unit = jnp.where(
        lax.broadcasted_iota(jnp.int32, (128, 128), 0) == lax.broadcasted_iota(jnp.int32, (128, 128), 1), 1.0, 0.0
    ).astype(BF)
    settle(c_x)

    sides = picked[:, 0:128]
    side_rows = nt(unit, sides)
    end_rows = nt(perms, picked[:, 128:256])
    west = jnp.concatenate([side_rows[4 * a:4 * a + 32] for a in range(3)], axis=1).astype(BF)
    east = jnp.concatenate([side_rows[64 + 4 * a:96 + 4 * a] for a in range(3)], axis=1).astype(BF)
    ends = jnp.concatenate([end_rows[128 * b:128 * b + 128] for b in range(3)], axis=1).astype(BF)
    west, east, ends = nt(west, w1_west), nt(east, w1_east), nt(ends, w1_end)
    for n in range(8):
        rows = slice(n * 128, (n + 1) * 128)
        add = []
        cell = lax.broadcasted_iota(jnp.int32, (32, 128), 0)
        for m in range(4 * n, 4 * n + 4):
            add.append(
                jnp.where(cell == 0, west[m:m + 1], 0.0) + jnp.where(cell == 31, east[m:m + 1], 0.0)
            )
        pre = z1[rows, :] + jnp.concatenate(add, axis=0)
        if n in (0, 7):
            pre = pre + jnp.where(q == (0 if n == 0 else 3), ends, 0.0)
        z1[rows, :] = pre
        act1[rows, :] = gelu(pre).astype(BF)
    pre = nt(quarters(act1[...]), side_by_side(r["v_wd"], 4))
    r["z2"][...] = pre
    act2 = gelu(pre).astype(BF)
    r["act2"][...] = act2
    own["rout"].wait()
    rq = r["rq"]
    rq[...] = tn(act2, r["v_rout"][...]).astype(BF)

    x2in, halo = r["x2in"], r["halo"]
    c_x = spread(
        x2in.at[pl.ds(1, 3)], XD, x_peer, lambda d: rq.at[rows_of(lax.rem(x + d, 4)), :], lambda d: x2in.at[d]
    )
    c_h = begin(halo)
    push(c_h, r["act2"].at[pl.ds(224, 32), :], halo.at[0], x_peer(1))
    push(c_h, r["act2"].at[pl.ds(0, 32), :], halo.at[1], x_peer(3))
    total = rq[mine, :].astype(F32)
    settle(c_x)
    for d in XD:
        total = total + x2in[d].astype(F32)
    held2 = r["held2"]
    held2[z] = total.astype(BF)
    c_z = spread(held2.at[pl.ds(0, 7)], ZD, z_peer, lambda d: held2.at[z], lambda d: held2.at[z])

    take_bulk(3)
    take_bulk(5)
    og, ogt, up = r["og"], r["ogt"], r["v_up"]
    flat = perm[1]
    for n in range(8):
        ogt[n * 128:(n + 1) * 128, :] = nt(flat, og[:, n * 128:(n + 1) * 128]).astype(BF)
    cells = ogt[...].astype(F32).reshape(8, 4, 32, 128)
    pooled = (cells[:, 0] + cells[:, 1] + cells[:, 2] + cells[:, 3]).reshape(256, 128).astype(BF)
    back_up = nn(pooled, up[...])
    for n in (0, 9):
        for b in range(3):
            rows = slice(n * 128, (n + 1) * 128)
            new = jnp.where(q == n // 3, end_rows[b * 128:(b + 1) * 128], cb[b, rows, :].astype(F32))
            cb[b, rows, :] = new.astype(BF)
    for b in (0, 2):
        cb[b] = (cb[b].astype(F32) + nt(r["v_place"][b // 2], sides)).astype(BF)
    slope = gelu_slope(z1[...])
    r["slope"][...] = slope
    r["direct"][...] = slope * ogt[...].astype(F32)

    settle(c_z)
    rolled = r["rolled"]
    for n in range(8):
        block = held2[n].astype(F32)
        rolled[n * 4] = held2[n]
        for m in range(1, 4):
            rolled[n * 4 + m] = pltpu.roll(block, 32 * m, 1).astype(BF)
    lane = lax.broadcasted_iota(jnp.int32, (32, 128), 1)
    slots2, landed2 = r["slots2"], r["landed2"]
    c_g = begin(landed2.at[pl.ds(1, 7)])
    for d in GD + (0,):
        t = z * 8 + lax.rem(g + d, 8)
        both = [jnp.zeros((32, 128), F32), jnp.zeros((32, 128), F32)]
        for k in range(8):
            owned, n, s = entry(t, k)
            block = rolled[jnp.where(owned, n * 4 + lax.rem(k + 4 - s, 4), 0)].astype(F32)
            block = jnp.where(owned, block, 0.0)
            if k < 4:
                both[0] = jnp.where(lane // 32 == k, block, both[0])
            else:
                both[1] = jnp.where(lane == 32 * (k - 4) + EDGE[k - 4], block, both[1])
        slots2[d, :, 0:128] = both[0].astype(BF)
        slots2[d, :, 128:256] = both[1].astype(BF)
        if d:
            push(c_g, slots2.at[d], landed2.at[d], g_peer(d))
    settle(c_g)
    total = slots2[0].astype(F32)
    for d in range(1, 8):
        total = total + landed2[d].astype(F32)
    picked2 = r["picked2"]
    picked2[mine, :] = total.astype(BF)
    part2 = picked2.at[mine, :]
    c_x = spread(picked2.at[pl.ds(0, 96), :], XD, x_peer, lambda d: part2, lambda d: part2)
    own["rin"].wait()
    take_bulk(4)
    settle(c_h)
    settle(c_x)

    sel = r["v_rin"][...]
    rim = nt(sel, picked2[...])
    upper = jnp.where(q == 0, 0.0, halo[0].astype(F32))
    lower = jnp.where(q == 3, 0.0, halo[1].astype(F32))
    rows = jnp.concatenate([upper, act2.astype(F32), lower], axis=0) + rim[0:320]
    col = lax.rem(lax.broadcasted_iota(jnp.int32, (320, 128), 0), 32)
    west = jnp.where(col == 0, 0.0, pltpu.roll(rows, 1, 0)) + rim[320:640]
    east = jnp.where(col == 31, 0.0, pltpu.roll(rows, 319, 0)) + rim[640:960]
    blocks = [v.astype(BF) for v in (west, rows, east)]
    taps2 = jnp.concatenate([blocks[b][a * 32:a * 32 + 256] for a in range(3) for b in range(3)], axis=1)
    w2 = r["v_w2"]
    pre = nt(taps2, side_by_side(w2, 9))
    gz3 = (gelu_slope(pre) * back_up).astype(BF)
    none32, none64 = jnp.zeros((32, 128), F32), jnp.zeros((64, 128), F32)
    back = []
    for b in range(3):
        v0, v1, v2 = (nn(gz3, w2[3 * a + b]) for a in range(3))
        back.append(
            jnp.concatenate([v0, none64], axis=0)
            + jnp.concatenate([none32, v1, none32], axis=0)
            + jnp.concatenate([none64, v2], axis=0)
        )
    mid = (
        back[1]
        + jnp.where(col == 31, 0.0, pltpu.roll(back[0], 319, 0))
        + jnp.where(col == 0, 0.0, pltpu.roll(back[2], 1, 0))
    )
    cat = jnp.concatenate([mid.astype(BF), back[0].astype(BF), back[2].astype(BF)], axis=0)
    dq = r["dq"]
    dq[...] = tn(cat, sel).astype(BF)
    x4in, hout, hin = r["x4in"], r["hout"], r["hin"]
    c_x = spread(
        x4in.at[pl.ds(1, 3)], XD, x_peer, lambda d: dq.at[rows_of(lax.rem(x + d, 4)), :], lambda d: x4in.at[d]
    )
    hout[0] = mid[288:320]
    hout[1] = mid[0:32]
    c_h = begin(hin)
    push(c_h, hout.at[0], hin.at[0], x_peer(1))
    push(c_h, hout.at[1], hin.at[1], x_peer(3))

    other = 1 - core

    def halves(name, wide, parts):
        outs, ins = r[name + "c"], r[name + "ci"]
        for n in range(4):
            rows_n = pl.ds(pl.multiple_of(n * 32 + other * 16, 16), 16)
            at = 0
            for ref in parts:
                width = ref.shape[1]
                outs[n, :, at:at + width] = ref[rows_n, :].astype(BF)
                at += width
            outs[n, :, at:wide] = jnp.zeros((16, wide - at), BF)
        n = begin(ins)
        push(n, outs, ins, core_peer())
        return n

    def shares(name, wide, parts):
        outs, ins = r[name + "o"], r[name + "i"]
        share = wide // 4
        for n in range(4):
            rows_n = pl.ds(pl.multiple_of(n * 32 + core * 16, 16), 16)
            own_n = jnp.concatenate(
                [ref[rows_n, :] for ref in parts]
                + [jnp.zeros((16, wide - sum(ref.shape[1] for ref in parts)), F32)],
                axis=1,
            )
            summed = (own_n + r[name + "ci"][n].astype(F32)).astype(BF)
            for m in range(4):
                outs[n, m] = summed[:, m * share:(m + 1) * share]
        m = begin(ins.at[pl.ds(1, 15)])
        for dx, dy in XYD:
            push(m, outs.at[lax.rem(x + dx, 4), lax.rem(y + dy, 4)], ins.at[dx * 4 + dy], xy_peer(dx, dy))
        return m

    def along_z(name):
        total = r[name + "o"][x, y].astype(F32)
        for n in range(1, 16):
            total = total + r[name + "i"][n].astype(F32)
        zall = r[name + "z"]
        zall[z] = total.astype(BF)
        return spread(zall.at[pl.ds(0, 7)], ZD, z_peer, lambda d: zall.at[z], lambda d: zall.at[z])

    def whole(name):
        zall = r[name + "z"]
        total = zall[0].astype(F32)
        for n in range(1, 8):
            total = total + zall[n].astype(F32)
        return total.astype(BF)

    coarse = gelu(pre).astype(BF)
    lifted = nt(coarse, up[...])
    out, ostrip = r["out"], r["ostrip"]
    for n in range(8):
        row = lifted[n * 32:(n + 1) * 32]
        summed = act1[n * 128:(n + 1) * 128, :].astype(F32) + jnp.concatenate([row] * 4, axis=0)
        ostrip[:, n * 128:(n + 1) * 128] = tn(summed.astype(BF), flat).astype(BF)

    settle(c_x)
    total = dq[mine, :].astype(F32)
    for d in XD:
        total = total + x4in[d].astype(F32)
    held3 = r["held3"]
    held3[g] = total.astype(BF)
    c_g = spread(held3.at[pl.ds(0, 7)], GD, g_peer, lambda d: held3.at[g], lambda d: held3.at[g])
    lanes = pl.ds(pl.multiple_of(x * 1024, 1024), 1024)
    c_o = spread(
        out.at[:, pl.ds(0, 3072)], XD, x_peer,
        lambda d: ostrip.at[rows_of(lax.rem(x + d, 4)), :], lambda d: out.at[:, lanes],
    )
    own_out = local(16, ostrip.at[mine, :], out.at[:, lanes])

    r["gb_u"][...] = tn(pooled, coarse)
    r["gb_w"][...] = tn(gz3, taps2)
    parts_b = (r["gb_w"], r["gb_u"])
    c_bc = halves("b", BW, parts_b)
    settle(c_g)
    rolled3 = r["rolled3"]
    for j in range(8):
        for h in range(2):
            block = held3[j, :, 128 * h:128 * h + 128]
            rolled3[j * 8 + h * 4] = block
            for m in range(1, 4):
                rolled3[j * 8 + h * 4 + m] = pltpu.roll(block.astype(F32), 32 * m, 1).astype(BF)
    sums = [jnp.zeros((32, 128), F32) for _ in range(8)]
    for j in range(8):
        for k in range(8):
            owned, n, s = entry(z * 8 + j, k)
            block = rolled3[j * 8 + (k // 4) * 4 + lax.rem(s + 4 - k % 4, 4)].astype(F32)
            if k < 4:
                block = jnp.where(lane // 32 == s, block, 0.0)
            else:
                block = jnp.where(lane == 32 * s + EDGE[k - 4], block, 0.0)
            n = jnp.where(owned, n, -1)
            for m in range(8):
                sums[m] = sums[m] + jnp.where(n == m, block, 0.0)
    slots3, landed3 = r["slots3"], r["landed3"]
    for n in range(8):
        slots3[n] = sums[n].astype(BF)
    c_z = spread(
        landed3.at[pl.ds(1, 7)], ZD, z_peer, lambda d: slots3.at[lax.rem(z + d, 8)], lambda d: landed3.at[d]
    )
    settle(c_bc)
    c_b = shares("b", BW, parts_b)
    slope2 = gelu_slope(r["z2"][...])
    settle(c_z)
    total = slots3[z].astype(F32)
    for d in ZD:
        total = total + landed3[d].astype(F32)
    back_rim = r["back_rim"]
    back_rim[mine, :] = total.astype(BF)
    part3 = back_rim.at[mine, :]
    c_x = spread(back_rim.at[pl.ds(0, 96), :], XD, x_peer, lambda d: part3, lambda d: part3)
    settle(c_b)
    c_bz = along_z("b")
    settle(c_h)
    upper = jnp.where(q == 0, 0.0, hin[0])
    lower = jnp.where(q == 3, 0.0, hin[1])
    ga2 = mid[32:288] + jnp.concatenate([upper, jnp.zeros((192, 128), F32), lower], axis=0)
    settle(c_x)

    gz2 = (slope2 * (ga2 + nt(r["v_rout"][...], back_rim[...]))).astype(BF)
    wd = r["v_wd"]
    fine = [nn(gz2, wd[t]).reshape(8, 1, 32, 128) for t in range(4)]
    grown = jnp.concatenate(fine, axis=1).reshape(1024, 128)
    gz1 = (r["direct"][...] + r["slope"][...] * grown).astype(BF)
    r["ga_w"][...] = tn(
        gz1, jnp.concatenate([cb[b, a * 128:a * 128 + 1024, :] for a in range(3) for b in range(3)], axis=1)
    )
    r["ga_d"][...] = tn(gz2, quarters(act1[...]))
    parts_a = (r["ga_w"], r["ga_d"])
    c_ac = halves("a", AW, parts_a)

    def to_row(name, n):
        settle(n)
        final = r["final_" + name]
        final[g] = whole(name)
        return spread(final.at[pl.ds(0, 7)], GD, g_peer, lambda d: final.at[g], lambda d: final.at[g])

    c_bg = to_row("b", c_bz)
    settle(c_ac)
    c_a = shares("a", AW, parts_a)
    settle(c_a)
    c_az = along_z("a")
    settle(c_bg)
    settle(c_o)
    settle(to_row("a", c_az))
    own_out.wait()
    for n, whole in enumerate(rounds):
        pltpu.make_async_copy(whole, whole, r["ss"].at[n]).wait()


INPUTS = (
    "adj", "feat", "ograd", "w1", "wd", "w2", "up",
    "pick", "put", "perm", "cmap", "fsel", "place", "rout", "rin",
)


def buf(*shape, kind=BF):
    return pltpu.VMEM(shape, kind)


def sems(*shape):
    return pltpu.SemaphoreType.DMA(shape)


SCRATCH = [
    ("lsem", sems(17)), ("ss", sems(32)), ("rs", sems(32)), ("s_adj", pltpu.SMEM((16, 64), jnp.int32)),
    ("fv", buf(32, 4096)), ("v_pick", buf(1024, 128)), ("v_put", buf(4, 128, 256)), ("v_perm", buf(3, 128, 128)),
    ("v_cmap", buf(4, 128, 128)), ("v_fsel", buf(4, 128, 640)), ("v_place", buf(2, 1280, 128)),
    ("v_rout", buf(256, 128)), ("v_rin", buf(960, 256)),
    ("strip", buf(128, 1280)), ("og", buf(128, 1024)), ("v_w1", buf(9, 128, 128)), ("v_wd", buf(4, 128, 128)),
    ("v_w2", buf(9, 128, 128)), ("v_up", buf(128, 128)),
    ("held0", buf(32, 16, 128)), ("held1", buf(32, 16, 128)), ("slots", buf(2, 8, 16, 640)), ("landed", buf(2, 8, 16, 640)),
    ("pout", buf(4, 32, 256)), ("picked", buf(128, 256)),
    ("cb", buf(3, 1280, 128)), ("z1", buf(1024, 128, kind=F32)), ("act1", buf(1024, 128)),
    ("z2", buf(256, 128, kind=F32)), ("act2", buf(256, 128)), ("rq", buf(128, 128)), ("x2in", buf(4, 32, 128)),
    ("slope", buf(1024, 128, kind=F32)), ("direct", buf(1024, 128, kind=F32)),
    ("halo", buf(2, 32, 128)), ("held2", buf(8, 32, 128)), ("rolled", buf(32, 32, 128)), ("ogt", buf(1024, 128)),
    ("slots2", buf(8, 32, 256)), ("landed2", buf(8, 32, 256)), ("picked2", buf(128, 256)),
    ("dq", buf(128, 256)), ("x4in", buf(4, 32, 256)),
    ("hout", buf(2, 32, 128, kind=F32)), ("hin", buf(2, 32, 128, kind=F32)),
    ("held3", buf(8, 32, 256)), ("rolled3", buf(64, 32, 128)), ("ostrip", buf(128, 1024)),
    ("slots3", buf(8, 32, 128)), ("landed3", buf(8, 32, 128)), ("back_rim", buf(128, 128)),
    ("gb_u", buf(128, 128, kind=F32)), ("gb_w", buf(128, 1152, kind=F32)),
    ("ga_d", buf(128, 512, kind=F32)), ("ga_w", buf(128, 1152, kind=F32)),
    ("bc", buf(4, 16, BW)), ("bci", buf(4, 16, BW)), ("bo", buf(4, 4, 16, BW // 4)), ("bi", buf(16, 16, BW // 4)),
    ("bz", buf(8, 16, BW // 4)),
    ("ac", buf(4, 16, AW)), ("aci", buf(4, 16, AW)), ("ao", buf(4, 4, 16, AW // 4)), ("ai", buf(16, 16, AW // 4)),
    ("az", buf(8, 16, AW // 4)),
]


def level_call(*args):
    return pl.pallas_call(
        level_kernel,
        out_shape=(pltpu.VMEM((32, 4096), BF), pltpu.VMEM((8, 16, AW // 4), BF), pltpu.VMEM((8, 16, BW // 4), BF)),
        in_specs=[ANY] * 15,
        out_specs=[VM] * 3,
        scratch_shapes=[s for _, s in SCRATCH],
        compiler_params=pltpu.CompilerParams(collective_id=0, has_side_effects=True, vmem_limit_bytes=LIMIT),
    )(*args)


def result_kernel(out_in, final_a, final_b, out, g1, gd, g2, gu, *, scale):
    out[...] = out_in[...]
    for c in range(2):
        rows = pl.ds(c * 16, 16)
        for t in range(13):
            block = final_a[2 * (t // 4) + c, :, (t % 4) * 128:(t % 4 + 1) * 128].astype(F32) * scale
            if t < 9:
                g1[t, rows, :] = block
            else:
                gd[t - 9, rows, :] = block
        for t in range(10):
            at = (t % 3) * 128
            block = final_b[2 * (t // 3) + c, :, at:at + 128].astype(F32) * scale
            if t < 9:
                g2[t, rows, :] = block
            else:
                gu[rows, :] = block


def result_call(out_in, final_a, final_b, scale):
    return pl.pallas_call(
        functools.partial(result_kernel, scale=scale),
        out_shape=(
            jax.ShapeDtypeStruct((32, 4096), BF),
            jax.ShapeDtypeStruct((9, 32, 128), F32),
            jax.ShapeDtypeStruct((4, 32, 128), F32),
            jax.ShapeDtypeStruct((9, 32, 128), F32),
            jax.ShapeDtypeStruct((32, 128), F32),
        ),
        in_specs=[VM] * 3,
        out_specs=[VM] * 5,
        compiler_params=pltpu.CompilerParams(vmem_limit_bytes=16 * 1024 * 1024),
    )(out_in, final_a, final_b)


def per_device(features, conv1_weight, down_weight, conv2_weight, up_weight, out_grad, adjacency):
    pick, put = fine_rim_out()
    fine_sel, fine_place = fine_rim_maps()
    maps = [
        jnp.asarray(m, BF)
        for m in (pick, put, fine_perm(), corner_maps(), fine_sel, fine_place, coarse_rim_out(), coarse_rim_in())
    ]
    out, final_a, final_b = level_call(
        adjacency.transpose(1, 2, 0).reshape(16, 64), features, out_grad, conv1_weight, down_weight, conv2_weight, up_weight, *maps
    )
    return result_call(out, final_a, final_b, 262144 ** -0.5)


def solution(mesh):
    weights = P(None, "chan", None)
    return jax.shard_map(
        per_device,
        mesh=mesh,
        in_specs=(P("chan", "tile"), weights, weights, weights, P("chan", None), P("chan", "tile"), P()),
        out_specs=(P("chan", "tile"), weights, weights, weights, P("chan", None)),
        check_vma=False,
    )
```

```python
import functools

import jax
import jax.numpy as jnp
import numpy as np
from jax import lax
from jax.experimental import pallas as pl
from jax.experimental.pallas import tpu as pltpu
from jax.sharding import PartitionSpec as P

BF = jnp.bfloat16
F32 = jnp.float32
MESH = pl.DeviceIdType.MESH
TURNS = (0, 1, 2, 3, 0, 2, 2, 0)
VM = pl.BlockSpec(memory_space=pltpu.VMEM)
ANY = pl.BlockSpec(memory_space=pl.ANY)
LIMIT = 56 * 1024 * 1024


def fine_perm():
    out = np.zeros((3, 128, 128), np.float32)
    for b in range(3):
        for rr in range(2):
            for par in range(2):
                for k in range(32):
                    col = 2 * (k - 1 + b) + par
                    if 0 <= col < 64:
                        out[b, rr * 64 + par * 32 + k, rr * 64 + col] = 1
    return out


def corner_maps():
    out = np.zeros((4, 128, 128), np.float32)
    for i in range(2):
        for j in range(2):
            out[0, i * 64 + j, 2 * i + j] = 1
            out[1, (1 - i) * 64 + 63 - j, 4 + 2 * i + j] = 1
            out[2, (1 - i) * 64 + 1 - j, 8 + 2 * i + j] = 1
            out[3, i * 64 + 62 + j, 12 + 2 * i + j] = 1
    return out


def fine_rim_maps():
    sel = np.zeros((4, 128, 640), np.float32)
    for q in range(4):
        for r in range(20):
            ir = 16 * q - 2 + r
            for par in range(2):
                if 0 <= ir < 64:
                    west = 384 + par * 64 + 63 - ir
                    east = 128 + (1 - par) * 64 + ir
                elif ir < 0:
                    west = 512 + 12 + 2 * (ir + 2) + par
                    east = 512 + 0 + 2 * (ir + 2) + par
                else:
                    west = 512 + 8 + 2 * (ir - 64) + par
                    east = 512 + 4 + 2 * (ir - 64) + par
                sel[q, r * 2 + par, west] = 1
                sel[q, 64 + r * 2 + par, east] = 1
    place = np.zeros((2, 1280, 128), np.float32)
    for r in range(20):
        for par in range(2):
            place[0, r * 64 + par * 32, r * 2 + par] = 1
            place[1, r * 64 + par * 32 + 31, 64 + r * 2 + par] = 1
    return sel, place


def fine_rim_out():
    pick = np.zeros((1024, 128), np.float32)
    for r in range(16):
        for kind, col in enumerate((0, 1, 62, 63)):
            pick[r * 64 + col, kind * 16 + r] = 1
    put = np.zeros((4, 128, 256), np.float32)
    for s in range(4):
        for r16 in range(16):
            r = 16 * s + r16
            for kind, lane in enumerate((64 + r, r, 128 + 63 - r, 192 + 63 - r)):
                put[s, kind * 16 + r16, lane] = 1
    return pick, put


def coarse_rim_out():
    out = np.zeros((4, 256, 128), np.float32)
    for i in range(32):
        for s, (r, k) in enumerate(((31, i), (i, 0), (0, 31 - i), (31 - i, 31))):
            out[r // 8, (r % 8) * 32 + k, s * 32 + i] = 1
    return out


def coarse_rim_in():
    out = np.zeros((4, 960, 256), np.float32)
    for k in range(32):
        out[0, k, k] = 1
        out[3, 9 * 32 + k, 64 + 31 - k] = 1
    for q in range(4):
        for r in range(10):
            row = 8 * q - 1 + r
            if row < 0:
                west, east = 255, 128
            elif row >= 32:
                west, east = 192, 191
            else:
                west, east = 96 + 31 - row, 32 + row
            out[q, 320 + r * 32, west] = 1
            out[q, 640 + r * 32 + 31, east] = 1
    return out


def nt(a, b):
    return lax.dot_general(a, b, (((1,), (1,)), ((), ())), preferred_element_type=F32)


def tn(a, b):
    return lax.dot_general(a, b, (((0,), (0,)), ((), ())), preferred_element_type=F32)


def nn(a, b):
    return lax.dot_general(a, b, (((1,), (0,)), ((), ())), preferred_element_type=F32)


ROOT = 0.7978845608028654


def gelu(v):
    return 0.5 * v * (1.0 + jnp.tanh(ROOT * (v + 0.044715 * (v * v * v))))


def gelu_slope(v):
    t = jnp.tanh(ROOT * (v + 0.044715 * (v * v * v)))
    return 0.5 * (1.0 + t) + 0.5 * v * (1.0 - t * t) * (ROOT * (1.0 + 3 * 0.044715 * (v * v)))


AW, BW = 2048, 1536
XD = (2, 1, 3)
ZD = (4, 3, 5, 2, 6, 1, 7)
GD = (4, 3, 5, 2, 6, 1, 7)
FAR = (2, 1, 3, 0)
XYD = [(dx, dy) for dx in FAR for dy in FAR if dx or dy]
EDGE = (0, 31, 0, 31)


def side_by_side(weights, count):
    return jnp.concatenate([weights[t] for t in range(count)], axis=1)


def quarters(act):
    parts = act.reshape(8, 2, 2, 32, 128)
    return jnp.concatenate(
        [parts[:, a, b].reshape(256, 128) for a in range(2) for b in range(2)], axis=1
    )


def flip_map():
    rows = lax.broadcasted_iota(jnp.int32, (128, 128), 0)
    cols = lax.broadcasted_iota(jnp.int32, (128, 128), 1)
    return jnp.where(rows + cols == 127, 1.0, 0.0).astype(BF)


def level_kernel(*refs):
    names = INPUTS + ("out", "final_a", "final_b") + tuple(n for n, _ in SCRATCH)
    r = dict(zip(names, refs))
    tile, x = lax.axis_index("tile"), lax.axis_index("chan")
    z, g = tile // 8, lax.rem(tile, 8)
    y, core = g // 2, lax.rem(g, 2)
    q = x
    xs = [x] + [lax.rem(x + d, 4) for d in range(1, 4)]
    ys = [y] + [lax.rem(y + d, 4) for d in range(1, 4)]
    zs = [z] + [lax.rem(z + d, 8) for d in range(1, 8)]
    gs = [g] + [lax.rem(g + d, 8) for d in range(1, 8)]
    x_at = [(tile, xs[d]) for d in range(4)]
    z_at = [(zs[d] * 8 + g, x) for d in range(8)]
    g_at = [(z * 8 + gs[d], x) for d in range(8)]
    x_peer, z_peer, g_peer = x_at.__getitem__, z_at.__getitem__, g_at.__getitem__

    def xy_peer(dx, dy):
        return (g_at[2 * dy][0], xs[dx])

    mine = pl.ds(pl.multiple_of(x * 32, 32), 32)
    rounds = []

    def rows_of(n):
        return pl.ds(pl.multiple_of(n * 32, 32), 32)

    def local(n, src, dst):
        copy = pltpu.make_async_copy(src, dst, r["lsem"].at[n])
        copy.start()
        return copy

    def begin(whole):
        rounds.append(whole)
        return len(rounds) - 1

    def push(n, src, dst, peer):
        pltpu.make_async_remote_copy(
            src_ref=src, dst_ref=dst, send_sem=r["ss"].at[n], recv_sem=r["rs"].at[n],
            device_id=peer, device_id_type=MESH,
        ).start()

    def spread(whole, dirs, peer, src, dst):
        n = begin(whole)
        for d in dirs:
            push(n, src(d), dst(d), peer(d))
        return n

    def settle(n):
        pltpu.make_async_copy(rounds[n], rounds[n], r["rs"].at[n]).wait()

    barrier = pltpu.get_barrier_semaphore()
    peers = [x_peer(d) for d in XD] + [z_peer(d) for d in ZD] + [g_peer(d) for d in GD]
    peers += [xy_peer(dx, dy) for dx, dy in XYD if dx and dy]
    for peer in peers:
        pl.semaphore_signal(barrier, inc=1, device_id=peer, device_id_type=MESH)

    own_feat = local(0, r["feat"], r["fv"])
    own = {
        "pick": local(1, r["pick"], r["v_pick"]),
        "put": local(2, r["put"], r["v_put"]),
        "adj": local(3, r["adj"], r["s_adj"]),
    }
    adj = r["s_adj"]

    own["pick"].wait()
    own["put"].wait()
    own_feat.wait()
    fv, held = r["fv"], (r["held0"], r["held1"])
    stacked = jnp.concatenate([fv[:, s * 1024:(s + 1) * 1024] for s in range(4)], axis=0)
    cols = nn(stacked, r["v_pick"][...]).astype(BF)
    both = nn(cols[0:32], r["v_put"][0])
    for s in range(1, 4):
        both = both + nn(cols[32 * s:32 * s + 32], r["v_put"][s])
    flip = flip_map()
    rims = (
        fv[:, 3968:4096],
        both[:, 0:128].astype(BF),
        nn(fv[:, 0:128], flip).astype(BF),
        both[:, 128:256].astype(BF),
    )
    for s in range(4):
        held[0][z * 4 + s] = rims[s][0:16]
        held[1][g * 4 + s] = rims[s][16:32]
    pl.semaphore_wait(barrier, len(peers))
    ways = ((z, ZD, z_peer), (g, GD, g_peer))
    first = []
    for h in range(2):
        at, dirs, peer = ways[h]
        part = held[h].at[pl.ds(at * 4, 4)]
        first.append(spread(held[h].at[pl.ds(0, 28)], dirs, peer, lambda d: part, lambda d: part))

    own.update({
        "cmap": local(4, r["cmap"], r["v_cmap"]),
        "perm": local(5, r["perm"], r["v_perm"]),
        "fsel": local(6, r["fsel"], r["v_fsel"]),
        "place": local(7, r["place"], r["v_place"]),
        "rout": local(8, r["rout"].at[q], r["v_rout"]),
        "rin": local(9, r["rin"].at[q], r["v_rin"]),
    })

    def piece(n, j):
        if n == 0:
            start = pl.multiple_of(jnp.clip(j * 1024 - 128, 0, 2816), 128)
            return r["feat"].at[:, pl.ds(start, 1280)], r["strip"].at[mine, :]
        if n == 3:
            return r["ograd"].at[:, pl.ds(pl.multiple_of(j * 1024, 1024), 1024)], r["og"].at[mine, :]
        if n == 5:
            return r["up"], r["v_up"].at[mine, :]
        name = {1: "w1", 2: "wd", 4: "w2"}[n]
        return r[name], r["v_" + name].at[:, mine, :]

    bulk = {}

    def send_bulk(n):
        three = pl.ds(0, 96)
        into = r[("strip", "v_w1", "v_wd", "og", "v_w2", "v_up")[n]]
        whole = into.at[:, three, :] if n in (1, 2, 4) else into.at[three, :]
        m = begin(whole)
        for d in XD:
            src, dst = piece(n, xs[d])
            push(m, src, dst, x_peer(d))
        src, dst = piece(n, x)
        bulk[n] = (m, local(10 + n, src, dst))

    def take_bulk(n):
        m, copy = bulk[n]
        copy.wait()
        settle(m)

    for n in range(4):
        send_bulk(n)

    own["adj"].wait()

    table = r["table"]
    for n in range(8):
        for k in range(8):
            at = n * 8 + k
            for h in range(2):
                t = z * 8 + n if h == 0 else n * 8 + g
                p = adj[2 * k, t]
                s = lax.rem(adj[2 * k + 1, t] + TURNS[k], 4)
                owned = jnp.logical_and(p >= 0, (p // 8 == z) if h else (lax.rem(p, 8) == g))
                m = lax.rem(p, 8) if h else p // 8
                table[h, at] = jnp.where(owned, m * 4 + s, -1)
                if h == 0:
                    table[2, at] = jnp.where(owned, m * 4 + lax.rem(k + 4 - s, 4), -1)
                    table[3, at] = jnp.where(owned, m, -1)
                    table[4, at] = s
                    table[5, at] = n * 8 + (k // 4) * 4 + lax.rem(s + 4 - k % 4, 4)

    own["cmap"].wait()
    slots, landed = r["slots"], r["landed"]
    second = []
    for h in (1, 0):
        settle(first[h])
        _, dirs, peer = ways[1 - h]
        order = dirs + (0,)
        m = begin(landed.at[h, pl.ds(1, 7)])
        second.append(m)
        corners = [[] for _ in range(4)]
        for d in order:
            t = (gs[d] if h == 0 else zs[d]) * 8
            for k in range(8):
                n = table[h, t + k]
                block = held[h][jnp.maximum(n, 0)]
                block = jnp.where(n >= 0, block, jnp.zeros_like(block))
                if k < 4:
                    slots[h, d, :, k * 128:(k + 1) * 128] = block
                else:
                    corners[k - 4].append(block)
        corner = nn(jnp.concatenate(corners[0], axis=0), r["v_cmap"][0])
        for k in range(1, 4):
            corner = corner + nn(jnp.concatenate(corners[k], axis=0), r["v_cmap"][k])
        for n, d in enumerate(order):
            slots[h, d, :, 512:640] = corner[16 * n:16 * n + 16].astype(BF)
            if d:
                push(m, slots.at[h, d], landed.at[h, d], peer(d))
    own["perm"].wait()
    take_bulk(0)
    perm, cb, strip = r["v_perm"], r["cb"], r["strip"]
    perms = perm[...].reshape(384, 128)
    shift = jnp.where(q == 0, -1, jnp.where(q == 3, 1, 0))

    def strip_block(n):
        at = jnp.clip(n + shift, 0, 9)
        return strip[:, pl.ds(pl.multiple_of(at * 128, 128), 128)]

    for n in range(1, 9):
        turned = nt(perms, strip_block(n))
        for b in range(3):
            cb[b, n * 128:(n + 1) * 128, :] = turned[b * 128:(b + 1) * 128].astype(BF)

    halves_of = []
    for m, h in zip(second, (1, 0)):
        settle(m)
        total = slots[h, 0].astype(F32)
        for d in range(1, 8):
            total = total + landed[h, d].astype(F32)
        halves_of.append(total)
    total = jnp.concatenate([halves_of[1], halves_of[0]], axis=0).astype(BF)

    own["fsel"].wait()
    picked, pout = r["picked"], r["pout"]
    ends = (total[:, 0:128], None, None, nn(total[:, 256:384], flip).astype(BF))
    for j in range(4):
        pout[j, :, 0:128] = nt(total, r["v_fsel"][j]).astype(BF)
        pout[j, :, 128:256] = jnp.zeros((32, 128), BF) if ends[j] is None else ends[j]
    c_x = spread(
        picked.at[pl.ds(0, 96), :], XD, x_peer, lambda d: pout.at[xs[d]], lambda d: picked.at[mine, :]
    )
    picked[mine, :] = pout[x]
    for n in (5, 4):
        send_bulk(n)
    own["place"].wait()
    take_bulk(1)
    take_bulk(2)
    w1c = side_by_side(r["v_w1"], 9)
    for n in (0, 9):
        block = strip_block(n)
        turned = nt(perms, jnp.where(q == n // 3, jnp.zeros_like(block), block))
        for b in range(3):
            cb[b, n * 128:(n + 1) * 128, :] = turned[b * 128:(b + 1) * 128].astype(BF)
    z1, act1 = r["z1"], r["act1"]
    w1 = r["v_w1"]

    def fine_taps(n):
        return jnp.concatenate(
            [cb[b, a * 128 + n * 256:a * 128 + n * 256 + 256, :] for a in range(3) for b in range(3)], axis=1
        )

    for n in range(4):
        z1[n * 256:(n + 1) * 256, :] = nt(fine_taps(n), w1c)
    w1_west = jnp.concatenate([w1[3 * a] for a in range(3)], axis=1)
    w1_east = jnp.concatenate([w1[3 * a + 2] for a in range(3)], axis=1)
    w1_end = jnp.where(q == 0, side_by_side(w1, 3), side_by_side(w1[6:9], 3))
    unit = jnp.where(
        lax.broadcasted_iota(jnp.int32, (128, 128), 0) == lax.broadcasted_iota(jnp.int32, (128, 128), 1), 1.0, 0.0
    ).astype(BF)
    settle(c_x)

    sides = picked[:, 0:128]
    side_rows = nt(unit, sides)
    end_rows = nt(perms, picked[:, 128:256])
    west = jnp.concatenate([side_rows[4 * a:4 * a + 32] for a in range(3)], axis=1).astype(BF)
    east = jnp.concatenate([side_rows[64 + 4 * a:96 + 4 * a] for a in range(3)], axis=1).astype(BF)
    ends = jnp.concatenate([end_rows[128 * b:128 * b + 128] for b in range(3)], axis=1).astype(BF)
    west, east, ends = nt(west, w1_west), nt(east, w1_east), nt(ends, w1_end)
    for n in range(8):
        rows = slice(n * 128, (n + 1) * 128)
        add = []
        cell = lax.broadcasted_iota(jnp.int32, (32, 128), 0)
        for m in range(4 * n, 4 * n + 4):
            add.append(
                jnp.where(cell == 0, west[m:m + 1], 0.0) + jnp.where(cell == 31, east[m:m + 1], 0.0)
            )
        pre = z1[rows, :] + jnp.concatenate(add, axis=0)
        if n in (0, 7):
            pre = pre + jnp.where(q == (0 if n == 0 else 3), ends, 0.0)
        z1[rows, :] = pre
        act1[rows, :] = gelu(pre).astype(BF)
    pre = nt(quarters(act1[...]), side_by_side(r["v_wd"], 4))
    r["z2"][...] = pre
    act2 = gelu(pre).astype(BF)
    r["act2"][...] = act2
    own["rout"].wait()
    rq = r["rq"]
    rq[...] = tn(act2, r["v_rout"][...]).astype(BF)

    x2in, halo = r["x2in"], r["halo"]
    c_x = spread(
        x2in.at[pl.ds(1, 3)], XD, x_peer, lambda d: rq.at[rows_of(xs[d]), :], lambda d: x2in.at[d]
    )
    c_h = begin(halo)
    push(c_h, r["act2"].at[pl.ds(224, 32), :], halo.at[0], x_peer(1))
    push(c_h, r["act2"].at[pl.ds(0, 32), :], halo.at[1], x_peer(3))
    total = rq[mine, :].astype(F32)
    settle(c_x)
    for d in XD:
        total = total + x2in[d].astype(F32)
    held2 = r["held2"]
    held2[z] = total.astype(BF)
    c_z = spread(held2.at[pl.ds(0, 7)], ZD, z_peer, lambda d: held2.at[z], lambda d: held2.at[z])

    take_bulk(3)
    take_bulk(5)
    og, ogt, up = r["og"], r["ogt"], r["v_up"]
    flat = perm[1]
    for n in range(8):
        ogt[n * 128:(n + 1) * 128, :] = nt(flat, og[:, n * 128:(n + 1) * 128]).astype(BF)
    cells = ogt[...].astype(F32).reshape(8, 4, 32, 128)
    pooled = (cells[:, 0] + cells[:, 1] + cells[:, 2] + cells[:, 3]).reshape(256, 128).astype(BF)
    back_up = nn(pooled, up[...])
    for n in (0, 9):
        for b in range(3):
            rows = slice(n * 128, (n + 1) * 128)
            new = jnp.where(q == n // 3, end_rows[b * 128:(b + 1) * 128], cb[b, rows, :].astype(F32))
            cb[b, rows, :] = new.astype(BF)
    for b in (0, 2):
        cb[b] = (cb[b].astype(F32) + nt(r["v_place"][b // 2], sides)).astype(BF)
    slope = gelu_slope(z1[...])
    r["slope"][...] = slope
    r["direct"][...] = slope * ogt[...].astype(F32)

    settle(c_z)
    rolled = r["rolled"]
    for n in range(8):
        block = held2[n].astype(F32)
        rolled[n * 4] = held2[n]
        for m in range(1, 4):
            rolled[n * 4 + m] = pltpu.roll(block, 32 * m, 1).astype(BF)
    lane = lax.broadcasted_iota(jnp.int32, (32, 128), 1)
    slots2, landed2 = r["slots2"], r["landed2"]
    c_g = begin(landed2.at[pl.ds(1, 7)])
    for d in GD + (0,):
        t = gs[d] * 8
        both = [jnp.zeros((32, 128), F32), jnp.zeros((32, 128), F32)]
        for k in range(8):
            n = table[2, t + k]
            block = rolled[jnp.maximum(n, 0)].astype(F32)
            block = jnp.where(n >= 0, block, 0.0)
            if k < 4:
                both[0] = jnp.where(lane // 32 == k, block, both[0])
            else:
                both[1] = jnp.where(lane == 32 * (k - 4) + EDGE[k - 4], block, both[1])
        slots2[d, :, 0:128] = both[0].astype(BF)
        slots2[d, :, 128:256] = both[1].astype(BF)
        if d:
            push(c_g, slots2.at[d], landed2.at[d], g_peer(d))
    settle(c_g)
    total = slots2[0].astype(F32)
    for d in range(1, 8):
        total = total + landed2[d].astype(F32)
    picked2 = r["picked2"]
    picked2[mine, :] = total.astype(BF)
    part2 = picked2.at[mine, :]
    c_x = spread(picked2.at[pl.ds(0, 96), :], XD, x_peer, lambda d: part2, lambda d: part2)
    own["rin"].wait()
    take_bulk(4)
    settle(c_h)
    settle(c_x)

    sel = r["v_rin"][...]
    rim = nt(sel, picked2[...])
    upper = jnp.where(q == 0, 0.0, halo[0].astype(F32))
    lower = jnp.where(q == 3, 0.0, halo[1].astype(F32))
    rows = jnp.concatenate([upper, act2.astype(F32), lower], axis=0) + rim[0:320]
    col = lax.rem(lax.broadcasted_iota(jnp.int32, (320, 128), 0), 32)
    west = jnp.where(col == 0, 0.0, pltpu.roll(rows, 1, 0)) + rim[320:640]
    east = jnp.where(col == 31, 0.0, pltpu.roll(rows, 319, 0)) + rim[640:960]
    blocks = [v.astype(BF) for v in (west, rows, east)]
    taps2 = jnp.concatenate([blocks[b][a * 32:a * 32 + 256] for a in range(3) for b in range(3)], axis=1)
    w2 = r["v_w2"]
    pre = nt(taps2, side_by_side(w2, 9))
    gz3 = (gelu_slope(pre) * back_up).astype(BF)
    none32, none64 = jnp.zeros((32, 128), F32), jnp.zeros((64, 128), F32)
    back = []
    for b in range(3):
        v0, v1, v2 = (nn(gz3, w2[3 * a + b]) for a in range(3))
        back.append(
            jnp.concatenate([v0, none64], axis=0)
            + jnp.concatenate([none32, v1, none32], axis=0)
            + jnp.concatenate([none64, v2], axis=0)
        )
    mid = (
        back[1]
        + jnp.where(col == 31, 0.0, pltpu.roll(back[0], 319, 0))
        + jnp.where(col == 0, 0.0, pltpu.roll(back[2], 1, 0))
    )
    cat = jnp.concatenate([mid.astype(BF), back[0].astype(BF), back[2].astype(BF)], axis=0)
    dq = r["dq"]
    dq[...] = tn(cat, sel).astype(BF)
    x4in, hout, hin = r["x4in"], r["hout"], r["hin"]
    c_x = spread(
        x4in.at[pl.ds(1, 3)], XD, x_peer, lambda d: dq.at[rows_of(xs[d]), :], lambda d: x4in.at[d]
    )
    hout[0] = mid[288:320]
    hout[1] = mid[0:32]
    c_h = begin(hin)
    push(c_h, hout.at[0], hin.at[0], x_peer(1))
    push(c_h, hout.at[1], hin.at[1], x_peer(3))

    other = 1 - core

    def halves(name, wide, parts):
        outs, ins = r[name + "c"], r[name + "ci"]
        for n in range(4):
            rows_n = pl.ds(pl.multiple_of(n * 32 + other * 16, 16), 16)
            at = 0
            for ref in parts:
                width = ref.shape[1]
                outs[n, :, at:at + width] = ref[rows_n, :].astype(BF)
                at += width
            outs[n, :, at:wide] = jnp.zeros((16, wide - at), BF)
        n = begin(ins)
        push(n, outs, ins, (tile + 1 - 2 * core, x))
        return n

    def shares(name, wide, parts):
        outs, ins = r[name + "o"], r[name + "i"]
        share = wide // 4
        for n in range(4):
            rows_n = pl.ds(pl.multiple_of(n * 32 + core * 16, 16), 16)
            own_n = jnp.concatenate(
                [ref[rows_n, :] for ref in parts]
                + [jnp.zeros((16, wide - sum(ref.shape[1] for ref in parts)), F32)],
                axis=1,
            )
            summed = (own_n + r[name + "ci"][n].astype(F32)).astype(BF)
            for m in range(4):
                outs[n, m] = summed[:, m * share:(m + 1) * share]
        m = begin(ins.at[pl.ds(1, 15)])
        for dx, dy in XYD:
            push(m, outs.at[xs[dx], ys[dy]], ins.at[dx * 4 + dy], xy_peer(dx, dy))
        return m

    def along_z(name):
        total = r[name + "o"][x, y].astype(F32)
        for n in range(1, 16):
            total = total + r[name + "i"][n].astype(F32)
        zall = r[name + "z"]
        zall[z] = total.astype(BF)
        return spread(zall.at[pl.ds(0, 7)], ZD, z_peer, lambda d: zall.at[z], lambda d: zall.at[z])

    def whole(name):
        zall = r[name + "z"]
        total = zall[0].astype(F32)
        for n in range(1, 8):
            total = total + zall[n].astype(F32)
        return total.astype(BF)

    coarse = gelu(pre).astype(BF)
    lifted = nt(coarse, up[...])
    out, ostrip = r["out"], r["ostrip"]
    for n in range(8):
        row = lifted[n * 32:(n + 1) * 32]
        summed = act1[n * 128:(n + 1) * 128, :].astype(F32) + jnp.concatenate([row] * 4, axis=0)
        ostrip[:, n * 128:(n + 1) * 128] = tn(summed.astype(BF), flat).astype(BF)

    settle(c_x)
    total = dq[mine, :].astype(F32)
    for d in XD:
        total = total + x4in[d].astype(F32)
    held3 = r["held3"]
    held3[g] = total.astype(BF)
    c_g = spread(held3.at[pl.ds(0, 7)], GD, g_peer, lambda d: held3.at[g], lambda d: held3.at[g])
    lanes = pl.ds(pl.multiple_of(x * 1024, 1024), 1024)
    c_o = spread(
        out.at[:, pl.ds(0, 3072)], XD, x_peer,
        lambda d: ostrip.at[rows_of(xs[d]), :], lambda d: out.at[:, lanes],
    )
    own_out = local(16, ostrip.at[mine, :], out.at[:, lanes])

    r["gb_u"][...] = tn(pooled, coarse)
    r["gb_w"][...] = tn(gz3, taps2)
    parts_b = (r["gb_w"], r["gb_u"])
    c_bc = halves("b", BW, parts_b)
    settle(c_g)
    rolled3 = r["rolled3"]
    for j in range(8):
        for h in range(2):
            block = held3[j, :, 128 * h:128 * h + 128]
            rolled3[j * 8 + h * 4] = block
            for m in range(1, 4):
                rolled3[j * 8 + h * 4 + m] = pltpu.roll(block.astype(F32), 32 * m, 1).astype(BF)
    sums = [jnp.zeros((32, 128), F32) for _ in range(8)]
    for j in range(8):
        for k in range(8):
            at = j * 8 + k
            n, s = table[3, at], table[4, at]
            block = rolled3[table[5, at]].astype(F32)
            if k < 4:
                block = jnp.where(lane // 32 == s, block, 0.0)
            else:
                block = jnp.where(lane == 32 * s + EDGE[k - 4], block, 0.0)
            for m in range(8):
                sums[m] = sums[m] + jnp.where(n == m, block, 0.0)
    slots3, landed3 = r["slots3"], r["landed3"]
    for n in range(8):
        slots3[n] = sums[n].astype(BF)
    c_z = spread(
        landed3.at[pl.ds(1, 7)], ZD, z_peer, lambda d: slots3.at[zs[d]], lambda d: landed3.at[d]
    )
    settle(c_bc)
    c_b = shares("b", BW, parts_b)
    slope2 = gelu_slope(r["z2"][...])
    settle(c_z)
    total = slots3[z].astype(F32)
    for d in ZD:
        total = total + landed3[d].astype(F32)
    back_rim = r["back_rim"]
    back_rim[mine, :] = total.astype(BF)
    part3 = back_rim.at[mine, :]
    c_x = spread(back_rim.at[pl.ds(0, 96), :], XD, x_peer, lambda d: part3, lambda d: part3)
    settle(c_b)
    c_bz = along_z("b")
    settle(c_h)
    upper = jnp.where(q == 0, 0.0, hin[0])
    lower = jnp.where(q == 3, 0.0, hin[1])
    ga2 = mid[32:288] + jnp.concatenate([upper, jnp.zeros((192, 128), F32), lower], axis=0)
    settle(c_x)

    gz2 = (slope2 * (ga2 + nt(r["v_rout"][...], back_rim[...]))).astype(BF)
    wd = r["v_wd"]
    fine = [nn(gz2, wd[t]).reshape(8, 1, 32, 128) for t in range(4)]
    grown = jnp.concatenate(fine, axis=1).reshape(1024, 128)
    gz1 = (r["direct"][...] + r["slope"][...] * grown).astype(BF)
    r["ga_w"][...] = tn(
        gz1, jnp.concatenate([cb[b, a * 128:a * 128 + 1024, :] for a in range(3) for b in range(3)], axis=1)
    )
    r["ga_d"][...] = tn(gz2, quarters(act1[...]))
    parts_a = (r["ga_w"], r["ga_d"])
    c_ac = halves("a", AW, parts_a)

    def to_row(name, n):
        settle(n)
        final = r["final_" + name]
        final[g] = whole(name)
        return spread(final.at[pl.ds(0, 7)], GD, g_peer, lambda d: final.at[g], lambda d: final.at[g])

    c_bg = to_row("b", c_bz)
    settle(c_ac)
    c_a = shares("a", AW, parts_a)
    settle(c_a)
    c_az = along_z("a")
    settle(c_bg)
    settle(c_o)
    settle(to_row("a", c_az))
    own_out.wait()
    for n, whole in enumerate(rounds):
        pltpu.make_async_copy(whole, whole, r["ss"].at[n]).wait()


INPUTS = (
    "adj", "feat", "ograd", "w1", "wd", "w2", "up",
    "pick", "put", "perm", "cmap", "fsel", "place", "rout", "rin",
)


def buf(*shape, kind=BF):
    return pltpu.VMEM(shape, kind)


def sems(*shape):
    return pltpu.SemaphoreType.DMA(shape)


SCRATCH = [
    ("lsem", sems(17)), ("ss", sems(32)), ("rs", sems(32)), ("s_adj", pltpu.SMEM((16, 64), jnp.int32)),
    ("table", pltpu.SMEM((6, 64), jnp.int32)),
    ("fv", buf(32, 4096)), ("v_pick", buf(1024, 128)), ("v_put", buf(4, 128, 256)), ("v_perm", buf(3, 128, 128)),
    ("v_cmap", buf(4, 128, 128)), ("v_fsel", buf(4, 128, 640)), ("v_place", buf(2, 1280, 128)),
    ("v_rout", buf(256, 128)), ("v_rin", buf(960, 256)),
    ("strip", buf(128, 1280)), ("og", buf(128, 1024)), ("v_w1", buf(9, 128, 128)), ("v_wd", buf(4, 128, 128)),
    ("v_w2", buf(9, 128, 128)), ("v_up", buf(128, 128)),
    ("held0", buf(32, 16, 128)), ("held1", buf(32, 16, 128)), ("slots", buf(2, 8, 16, 640)), ("landed", buf(2, 8, 16, 640)),
    ("pout", buf(4, 32, 256)), ("picked", buf(128, 256)),
    ("cb", buf(3, 1280, 128)), ("z1", buf(1024, 128, kind=F32)), ("act1", buf(1024, 128)),
    ("z2", buf(256, 128, kind=F32)), ("act2", buf(256, 128)), ("rq", buf(128, 128)), ("x2in", buf(4, 32, 128)),
    ("slope", buf(1024, 128, kind=F32)), ("direct", buf(1024, 128, kind=F32)),
    ("halo", buf(2, 32, 128)), ("held2", buf(8, 32, 128)), ("rolled", buf(32, 32, 128)), ("ogt", buf(1024, 128)),
    ("slots2", buf(8, 32, 256)), ("landed2", buf(8, 32, 256)), ("picked2", buf(128, 256)),
    ("dq", buf(128, 256)), ("x4in", buf(4, 32, 256)),
    ("hout", buf(2, 32, 128, kind=F32)), ("hin", buf(2, 32, 128, kind=F32)),
    ("held3", buf(8, 32, 256)), ("rolled3", buf(64, 32, 128)), ("ostrip", buf(128, 1024)),
    ("slots3", buf(8, 32, 128)), ("landed3", buf(8, 32, 128)), ("back_rim", buf(128, 128)),
    ("gb_u", buf(128, 128, kind=F32)), ("gb_w", buf(128, 1152, kind=F32)),
    ("ga_d", buf(128, 512, kind=F32)), ("ga_w", buf(128, 1152, kind=F32)),
    ("bc", buf(4, 16, BW)), ("bci", buf(4, 16, BW)), ("bo", buf(4, 4, 16, BW // 4)), ("bi", buf(16, 16, BW // 4)),
    ("bz", buf(8, 16, BW // 4)),
    ("ac", buf(4, 16, AW)), ("aci", buf(4, 16, AW)), ("ao", buf(4, 4, 16, AW // 4)), ("ai", buf(16, 16, AW // 4)),
    ("az", buf(8, 16, AW // 4)),
]


def level_call(*args):
    return pl.pallas_call(
        level_kernel,
        out_shape=(pltpu.VMEM((32, 4096), BF), pltpu.VMEM((8, 16, AW // 4), BF), pltpu.VMEM((8, 16, BW // 4), BF)),
        in_specs=[ANY] * 15,
        out_specs=[VM] * 3,
        scratch_shapes=[s for _, s in SCRATCH],
        compiler_params=pltpu.CompilerParams(collective_id=0, has_side_effects=True, vmem_limit_bytes=LIMIT),
    )(*args)


def result_kernel(out_in, final_a, final_b, out, g1, gd, g2, gu, *, scale):
    out[...] = out_in[...]
    for c in range(2):
        rows = pl.ds(c * 16, 16)
        for t in range(13):
            block = final_a[2 * (t // 4) + c, :, (t % 4) * 128:(t % 4 + 1) * 128].astype(F32) * scale
            if t < 9:
                g1[t, rows, :] = block
            else:
                gd[t - 9, rows, :] = block
        for t in range(10):
            at = (t % 3) * 128
            block = final_b[2 * (t // 3) + c, :, at:at + 128].astype(F32) * scale
            if t < 9:
                g2[t, rows, :] = block
            else:
                gu[rows, :] = block


def result_call(out_in, final_a, final_b, scale):
    return pl.pallas_call(
        functools.partial(result_kernel, scale=scale),
        out_shape=(
            jax.ShapeDtypeStruct((32, 4096), BF),
            jax.ShapeDtypeStruct((9, 32, 128), F32),
            jax.ShapeDtypeStruct((4, 32, 128), F32),
            jax.ShapeDtypeStruct((9, 32, 128), F32),
            jax.ShapeDtypeStruct((32, 128), F32),
        ),
        in_specs=[VM] * 3,
        out_specs=[VM] * 5,
        compiler_params=pltpu.CompilerParams(vmem_limit_bytes=16 * 1024 * 1024),
    )(out_in, final_a, final_b)


def per_device(features, conv1_weight, down_weight, conv2_weight, up_weight, out_grad, adjacency):
    pick, put = fine_rim_out()
    fine_sel, fine_place = fine_rim_maps()
    maps = [
        jnp.asarray(m, BF)
        for m in (pick, put, fine_perm(), corner_maps(), fine_sel, fine_place, coarse_rim_out(), coarse_rim_in())
    ]
    out, final_a, final_b = level_call(
        adjacency.transpose(1, 2, 0).reshape(16, 64), features, out_grad, conv1_weight, down_weight, conv2_weight, up_weight, *maps
    )
    return result_call(out, final_a, final_b, 262144 ** -0.5)


def solution(mesh):
    weights = P(None, "chan", None)
    return jax.shard_map(
        per_device,
        mesh=mesh,
        in_specs=(P("chan", "tile"), weights, weights, weights, P("chan", None), P("chan", "tile"), P()),
        out_specs=(P("chan", "tile"), weights, weights, weights, P("chan", None)),
        check_vma=False,
    )
```

```python
import functools
import math

import jax
import jax.numpy as jnp
import numpy as np
from jax import lax
from jax.experimental import pallas as pl
from jax.experimental.pallas import tpu as pltpu
from jax.sharding import PartitionSpec as P

BF = jnp.bfloat16
F32 = jnp.float32
MESH = pl.DeviceIdType.MESH
TURNS = (0, 1, 2, 3, 0, 2, 2, 0)
VM = pl.BlockSpec(memory_space=pltpu.VMEM)
ANY = pl.BlockSpec(memory_space=pl.ANY)
LIMIT = 56 * 1024 * 1024


def fine_perm():
    out = np.zeros((3, 128, 128), np.float32)
    for b in range(3):
        for rr in range(2):
            for par in range(2):
                for k in range(32):
                    col = 2 * (k - 1 + b) + par
                    if 0 <= col < 64:
                        out[b, rr * 64 + par * 32 + k, rr * 64 + col] = 1
    return out


def corner_maps():
    out = np.zeros((4, 128, 128), np.float32)
    for i in range(2):
        for j in range(2):
            out[0, i * 64 + j, 2 * i + j] = 1
            out[1, (1 - i) * 64 + 63 - j, 4 + 2 * i + j] = 1
            out[2, (1 - i) * 64 + 1 - j, 8 + 2 * i + j] = 1
            out[3, i * 64 + 62 + j, 12 + 2 * i + j] = 1
    return out


def fine_rim_maps():
    sel = np.zeros((4, 128, 640), np.float32)
    for q in range(4):
        for r in range(20):
            ir = 16 * q - 2 + r
            for par in range(2):
                if 0 <= ir < 64:
                    west = 384 + par * 64 + 63 - ir
                    east = 128 + (1 - par) * 64 + ir
                elif ir < 0:
                    west = 512 + 12 + 2 * (ir + 2) + par
                    east = 512 + 0 + 2 * (ir + 2) + par
                else:
                    west = 512 + 8 + 2 * (ir - 64) + par
                    east = 512 + 4 + 2 * (ir - 64) + par
                sel[q, r * 2 + par, west] = 1
                sel[q, 64 + r * 2 + par, east] = 1
    place = np.zeros((2, 1280, 128), np.float32)
    for r in range(20):
        for par in range(2):
            place[0, r * 64 + par * 32, r * 2 + par] = 1
            place[1, r * 64 + par * 32 + 31, 64 + r * 2 + par] = 1
    return sel, place


def fine_rim_out():
    pick = np.zeros((1024, 128), np.float32)
    for r in range(16):
        for kind, col in enumerate((0, 1, 62, 63)):
            pick[r * 64 + col, kind * 16 + r] = 1
    put = np.zeros((4, 128, 256), np.float32)
    for s in range(4):
        for r16 in range(16):
            r = 16 * s + r16
            for kind, lane in enumerate((64 + r, r, 128 + 63 - r, 192 + 63 - r)):
                put[s, kind * 16 + r16, lane] = 1
    return pick, put


def coarse_rim_out():
    out = np.zeros((4, 256, 128), np.float32)
    for i in range(32):
        for s, (r, k) in enumerate(((31, i), (i, 0), (0, 31 - i), (31 - i, 31))):
            out[r // 8, (r % 8) * 32 + k, s * 32 + i] = 1
    return out


def coarse_rim_in():
    out = np.zeros((4, 960, 256), np.float32)
    for k in range(32):
        out[0, k, k] = 1
        out[3, 9 * 32 + k, 64 + 31 - k] = 1
    for q in range(4):
        for r in range(10):
            row = 8 * q - 1 + r
            if row < 0:
                west, east = 255, 128
            elif row >= 32:
                west, east = 192, 191
            else:
                west, east = 96 + 31 - row, 32 + row
            out[q, 320 + r * 32, west] = 1
            out[q, 640 + r * 32 + 31, east] = 1
    return out


def nt(a, b):
    return lax.dot_general(a, b, (((1,), (1,)), ((), ())), preferred_element_type=F32)


def tn(a, b):
    return lax.dot_general(a, b, (((0,), (0,)), ((), ())), preferred_element_type=F32)


def nn(a, b):
    return lax.dot_general(a, b, (((1,), (0,)), ((), ())), preferred_element_type=F32)


ROOT = 0.7978845608028654


def gelu(v):
    return 0.5 * v * (1.0 + jnp.tanh(ROOT * (v + 0.044715 * (v * v * v))))


def gelu_slope(v):
    t = jnp.tanh(ROOT * (v + 0.044715 * (v * v * v)))
    return 0.5 * (1.0 + t) + 0.5 * v * (1.0 - t * t) * (ROOT * (1.0 + 3 * 0.044715 * (v * v)))


AW, BW = 2048, 1536
XD = (2, 1, 3)
ZD = (4, 3, 5, 2, 6, 1, 7)
GD = (4, 3, 5, 2, 6, 1, 7)
FAR = (2, 1, 3, 0)
XYD = [(dx, dy) for dx in FAR for dy in FAR if dx or dy]
EDGE = (0, 31, 0, 31)


def side_by_side(weights, count):
    return jnp.concatenate([weights[t] for t in range(count)], axis=1)


def quarters(act):
    parts = act.reshape(8, 2, 2, 32, 128)
    return jnp.concatenate(
        [parts[:, a, b].reshape(256, 128) for a in range(2) for b in range(2)], axis=1
    )


def flip_map():
    rows = lax.broadcasted_iota(jnp.int32, (128, 128), 0)
    cols = lax.broadcasted_iota(jnp.int32, (128, 128), 1)
    return jnp.where(rows + cols == 127, 1.0, 0.0).astype(BF)


def level_kernel(*refs):
    names = INPUTS + ("out", "final_a", "final_b") + tuple(n for n, _ in SCRATCH)
    r = dict(zip(names, refs))
    tile, x = lax.axis_index("tile"), lax.axis_index("chan")
    z, g = tile // 8, lax.rem(tile, 8)
    y, core = g // 2, lax.rem(g, 2)
    q = x
    xs = [x] + [lax.rem(x + d, 4) for d in range(1, 4)]
    ys = [y] + [lax.rem(y + d, 4) for d in range(1, 4)]
    zs = [z] + [lax.rem(z + d, 8) for d in range(1, 8)]
    gs = [g] + [lax.rem(g + d, 8) for d in range(1, 8)]
    x_at = [(tile, xs[d]) for d in range(4)]
    z_at = [(zs[d] * 8 + g, x) for d in range(8)]
    g_at = [(z * 8 + gs[d], x) for d in range(8)]
    x_peer, z_peer, g_peer = x_at.__getitem__, z_at.__getitem__, g_at.__getitem__

    def xy_peer(dx, dy):
        return (g_at[2 * dy][0], xs[dx])

    mine = pl.ds(pl.multiple_of(x * 32, 32), 32)
    rounds, sent = [], []

    def rows_of(n):
        return pl.ds(pl.multiple_of(n * 32, 32), 32)

    def local(sem, src, dst):
        pltpu.make_async_copy(src, dst, sem).start()

    def wait(whole, sem):
        pltpu.make_async_copy(whole, whole, sem).wait()

    def begin(whole):
        rounds.append(whole)
        return len(rounds) - 1

    def push(n, src, dst, peer):
        pltpu.make_async_remote_copy(
            src_ref=src, dst_ref=dst, send_sem=r["ss"], recv_sem=r["rs"].at[n],
            device_id=peer, device_id_type=MESH,
        ).start()
        sent.append(math.prod(src.shape) * src.dtype.itemsize)

    def spread(whole, dirs, peer, src, dst):
        n = begin(whole)
        for d in dirs:
            push(n, src(d), dst(d), peer(d))
        return n

    def settle(n):
        wait(rounds[n], r["rs"].at[n])

    early = (("feat", "fv"), ("pick", "v_pick"), ("put", "v_put"))
    for src, dst in early:
        local(r["lsem"].at[0], r[src], r[dst])
    local(r["lsem"].at[1], r["adj"], r["s_adj"])
    barrier = pltpu.get_barrier_semaphore()
    peers = [x_peer(d) for d in XD] + [z_peer(d) for d in ZD] + [g_peer(d) for d in GD]
    peers += [xy_peer(dx, dy) for dx, dy in XYD if dx and dy]
    for peer in peers:
        pl.semaphore_signal(barrier, inc=1, device_id=peer, device_id_type=MESH)

    adj = r["s_adj"]

    wait(r["early"], r["lsem"].at[0])
    fv, held = r["fv"], (r["held0"], r["held1"])
    stacked = jnp.concatenate([fv[:, s * 1024:(s + 1) * 1024] for s in range(4)], axis=0)
    cols = nn(stacked, r["v_pick"][...]).astype(BF)
    both = nn(cols[0:32], r["v_put"][0])
    for s in range(1, 4):
        both = both + nn(cols[32 * s:32 * s + 32], r["v_put"][s])
    flip = flip_map()
    rims = (
        fv[:, 3968:4096],
        both[:, 0:128].astype(BF),
        nn(fv[:, 0:128], flip).astype(BF),
        both[:, 128:256].astype(BF),
    )
    for s in range(4):
        held[0][z * 4 + s] = rims[s][0:16]
        held[1][g * 4 + s] = rims[s][16:32]
    pl.semaphore_wait(barrier, len(peers))
    ways = ((z, ZD, z_peer), (g, GD, g_peer))
    first = []
    for h in range(2):
        at, dirs, peer = ways[h]
        part = held[h].at[pl.ds(at * 4, 4)]
        first.append(spread(held[h].at[pl.ds(0, 28)], dirs, peer, lambda d: part, lambda d: part))

    for name in ("cmap", "perm", "fsel", "place"):
        local(r["lsem"].at[2], r[name], r["v_" + name])
    for name in ("rout", "rin"):
        local(r["lsem"].at[2], r[name].at[q], r["v_" + name])

    def piece(n, j):
        if n == 0:
            start = pl.multiple_of(jnp.clip(j * 1024 - 128, 0, 2816), 128)
            return r["feat"].at[:, pl.ds(start, 1280)], r["strip"].at[mine, :]
        if n == 3:
            return r["ograd"].at[:, pl.ds(pl.multiple_of(j * 1024, 1024), 1024)], r["og"].at[mine, :]
        if n == 5:
            return r["up"], r["v_up"].at[mine, :]
        name = {1: "w1", 2: "wd", 4: "w2"}[n]
        return r[name], r["v_" + name].at[:, mine, :]

    bulk = {}

    def send_bulk(n):
        m = begin(r[("strip", "v_w1", "v_wd", "og", "v_w2", "v_up")[n]])
        for d in XD:
            src, dst = piece(n, xs[d])
            push(m, src, dst, x_peer(d))
        src, dst = piece(n, x)
        local(r["rs"].at[m], src, dst)
        bulk[n] = m

    def take_bulk(n):
        settle(bulk[n])

    for n in range(4):
        send_bulk(n)

    wait(r["s_adj"], r["lsem"].at[1])

    table = r["table"]
    for n in range(8):
        for k in range(8):
            at = n * 8 + k
            for h in range(2):
                t = z * 8 + n if h == 0 else n * 8 + g
                p = adj[2 * k, t]
                s = lax.rem(adj[2 * k + 1, t] + TURNS[k], 4)
                owned = jnp.logical_and(p >= 0, (p // 8 == z) if h else (lax.rem(p, 8) == g))
                m = lax.rem(p, 8) if h else p // 8
                table[h, at] = jnp.where(owned, m * 4 + s, -1)
                if h == 0:
                    table[2, at] = jnp.where(owned, m * 4 + lax.rem(k + 4 - s, 4), -1)
                    table[3, at] = jnp.where(owned, m, -1)
                    table[4, at] = s
                    table[5, at] = n * 8 + (k // 4) * 4 + lax.rem(s + 4 - k % 4, 4)

    wait(r["late"], r["lsem"].at[2])
    slots, landed = r["slots"], r["landed"]
    second = []
    for h in (1, 0):
        settle(first[h])
        _, dirs, peer = ways[1 - h]
        order = dirs + (0,)
        m = begin(landed.at[h, pl.ds(1, 7)])
        second.append(m)
        corners = [[] for _ in range(4)]
        for d in order:
            t = (gs[d] if h == 0 else zs[d]) * 8
            for k in range(8):
                n = table[h, t + k]
                block = held[h][jnp.maximum(n, 0)]
                block = jnp.where(n >= 0, block, jnp.zeros_like(block))
                if k < 4:
                    slots[h, d, :, k * 128:(k + 1) * 128] = block
                else:
                    corners[k - 4].append(block)
        corner = nn(jnp.concatenate(corners[0], axis=0), r["v_cmap"][0])
        for k in range(1, 4):
            corner = corner + nn(jnp.concatenate(corners[k], axis=0), r["v_cmap"][k])
        for n, d in enumerate(order):
            slots[h, d, :, 512:640] = corner[16 * n:16 * n + 16].astype(BF)
            if d:
                push(m, slots.at[h, d], landed.at[h, d], peer(d))
    take_bulk(0)
    perm, cb, strip = r["v_perm"], r["cb"], r["strip"]
    perms = perm[...].reshape(384, 128)
    shift = jnp.where(q == 0, -1, jnp.where(q == 3, 1, 0))

    def strip_block(n):
        at = jnp.clip(n + shift, 0, 9)
        return strip[:, pl.ds(pl.multiple_of(at * 128, 128), 128)]

    for n in range(1, 9):
        turned = nt(perms, strip_block(n))
        for b in range(3):
            cb[b, n * 128:(n + 1) * 128, :] = turned[b * 128:(b + 1) * 128].astype(BF)

    halves_of = []
    for m, h in zip(second, (1, 0)):
        settle(m)
        total = slots[h, 0].astype(F32)
        for d in range(1, 8):
            total = total + landed[h, d].astype(F32)
        halves_of.append(total)
    total = jnp.concatenate([halves_of[1], halves_of[0]], axis=0).astype(BF)

    picked, pout = r["picked"], r["pout"]
    ends = (total[:, 0:128], None, None, nn(total[:, 256:384], flip).astype(BF))
    for j in range(4):
        pout[j, :, 0:128] = nt(total, r["v_fsel"][j]).astype(BF)
        pout[j, :, 128:256] = jnp.zeros((32, 128), BF) if ends[j] is None else ends[j]
    c_x = spread(
        picked.at[pl.ds(0, 96), :], XD, x_peer, lambda d: pout.at[xs[d]], lambda d: picked.at[mine, :]
    )
    picked[mine, :] = pout[x]
    for n in (5, 4):
        send_bulk(n)
    take_bulk(1)
    take_bulk(2)
    w1c = side_by_side(r["v_w1"], 9)
    for n in (0, 9):
        block = strip_block(n)
        turned = nt(perms, jnp.where(q == n // 3, jnp.zeros_like(block), block))
        for b in range(3):
            cb[b, n * 128:(n + 1) * 128, :] = turned[b * 128:(b + 1) * 128].astype(BF)
    z1, act1 = r["z1"], r["act1"]
    w1 = r["v_w1"]

    def fine_taps(n):
        return jnp.concatenate(
            [cb[b, a * 128 + n * 256:a * 128 + n * 256 + 256, :] for a in range(3) for b in range(3)], axis=1
        )

    for n in range(4):
        z1[n * 256:(n + 1) * 256, :] = nt(fine_taps(n), w1c)
    w1_west = jnp.concatenate([w1[3 * a] for a in range(3)], axis=1)
    w1_east = jnp.concatenate([w1[3 * a + 2] for a in range(3)], axis=1)
    w1_end = jnp.where(q == 0, side_by_side(w1, 3), side_by_side(w1[6:9], 3))
    unit = jnp.where(
        lax.broadcasted_iota(jnp.int32, (128, 128), 0) == lax.broadcasted_iota(jnp.int32, (128, 128), 1), 1.0, 0.0
    ).astype(BF)
    settle(c_x)

    sides = picked[:, 0:128]
    side_rows = nt(unit, sides)
    end_rows = nt(perms, picked[:, 128:256])
    west = jnp.concatenate([side_rows[4 * a:4 * a + 32] for a in range(3)], axis=1).astype(BF)
    east = jnp.concatenate([side_rows[64 + 4 * a:96 + 4 * a] for a in range(3)], axis=1).astype(BF)
    ends = jnp.concatenate([end_rows[128 * b:128 * b + 128] for b in range(3)], axis=1).astype(BF)
    west, east, ends = nt(west, w1_west), nt(east, w1_east), nt(ends, w1_end)
    for n in range(8):
        rows = slice(n * 128, (n + 1) * 128)
        add = []
        cell = lax.broadcasted_iota(jnp.int32, (32, 128), 0)
        for m in range(4 * n, 4 * n + 4):
            add.append(
                jnp.where(cell == 0, west[m:m + 1], 0.0) + jnp.where(cell == 31, east[m:m + 1], 0.0)
            )
        pre = z1[rows, :] + jnp.concatenate(add, axis=0)
        if n in (0, 7):
            pre = pre + jnp.where(q == (0 if n == 0 else 3), ends, 0.0)
        z1[rows, :] = pre
        act1[rows, :] = gelu(pre).astype(BF)
    pre = nt(quarters(act1[...]), side_by_side(r["v_wd"], 4))
    r["z2"][...] = pre
    act2 = gelu(pre).astype(BF)
    r["act2"][...] = act2
    rq = r["rq"]
    rq[...] = tn(act2, r["v_rout"][...]).astype(BF)

    x2in, halo = r["x2in"], r["halo"]
    c_x = spread(
        x2in.at[pl.ds(1, 3)], XD, x_peer, lambda d: rq.at[rows_of(xs[d]), :], lambda d: x2in.at[d]
    )
    c_h = begin(halo)
    push(c_h, r["act2"].at[pl.ds(224, 32), :], halo.at[0], x_peer(1))
    push(c_h, r["act2"].at[pl.ds(0, 32), :], halo.at[1], x_peer(3))
    total = rq[mine, :].astype(F32)
    settle(c_x)
    for d in XD:
        total = total + x2in[d].astype(F32)
    held2 = r["held2"]
    held2[z] = total.astype(BF)
    c_z = spread(held2.at[pl.ds(0, 7)], ZD, z_peer, lambda d: held2.at[z], lambda d: held2.at[z])

    take_bulk(3)
    take_bulk(5)
    og, ogt, up = r["og"], r["ogt"], r["v_up"]
    flat = perm[1]
    for n in range(8):
        ogt[n * 128:(n + 1) * 128, :] = nt(flat, og[:, n * 128:(n + 1) * 128]).astype(BF)
    cells = ogt[...].astype(F32).reshape(8, 4, 32, 128)
    pooled = (cells[:, 0] + cells[:, 1] + cells[:, 2] + cells[:, 3]).reshape(256, 128).astype(BF)
    back_up = nn(pooled, up[...])
    for n in (0, 9):
        for b in range(3):
            rows = slice(n * 128, (n + 1) * 128)
            new = jnp.where(q == n // 3, end_rows[b * 128:(b + 1) * 128], cb[b, rows, :].astype(F32))
            cb[b, rows, :] = new.astype(BF)
    for b in (0, 2):
        cb[b] = (cb[b].astype(F32) + nt(r["v_place"][b // 2], sides)).astype(BF)
    slope = gelu_slope(z1[...])
    r["slope"][...] = slope
    r["direct"][...] = slope * ogt[...].astype(F32)

    settle(c_z)
    rolled = r["rolled"]
    for n in range(8):
        block = held2[n].astype(F32)
        rolled[n * 4] = held2[n]
        for m in range(1, 4):
            rolled[n * 4 + m] = pltpu.roll(block, 32 * m, 1).astype(BF)
    lane = lax.broadcasted_iota(jnp.int32, (32, 128), 1)
    slots2, landed2 = r["slots2"], r["landed2"]
    c_g = begin(landed2.at[pl.ds(1, 7)])
    for d in GD + (0,):
        t = gs[d] * 8
        both = [jnp.zeros((32, 128), F32), jnp.zeros((32, 128), F32)]
        for k in range(8):
            n = table[2, t + k]
            block = rolled[jnp.maximum(n, 0)].astype(F32)
            block = jnp.where(n >= 0, block, 0.0)
            if k < 4:
                both[0] = jnp.where(lane // 32 == k, block, both[0])
            else:
                both[1] = jnp.where(lane == 32 * (k - 4) + EDGE[k - 4], block, both[1])
        slots2[d, :, 0:128] = both[0].astype(BF)
        slots2[d, :, 128:256] = both[1].astype(BF)
        if d:
            push(c_g, slots2.at[d], landed2.at[d], g_peer(d))
    settle(c_g)
    total = slots2[0].astype(F32)
    for d in range(1, 8):
        total = total + landed2[d].astype(F32)
    picked2 = r["picked2"]
    picked2[mine, :] = total.astype(BF)
    part2 = picked2.at[mine, :]
    c_x = spread(picked2.at[pl.ds(0, 96), :], XD, x_peer, lambda d: part2, lambda d: part2)
    take_bulk(4)
    settle(c_h)
    settle(c_x)

    sel = r["v_rin"][...]
    rim = nt(sel, picked2[...])
    upper = jnp.where(q == 0, 0.0, halo[0].astype(F32))
    lower = jnp.where(q == 3, 0.0, halo[1].astype(F32))
    rows = jnp.concatenate([upper, act2.astype(F32), lower], axis=0) + rim[0:320]
    col = lax.rem(lax.broadcasted_iota(jnp.int32, (320, 128), 0), 32)
    west = jnp.where(col == 0, 0.0, pltpu.roll(rows, 1, 0)) + rim[320:640]
    east = jnp.where(col == 31, 0.0, pltpu.roll(rows, 319, 0)) + rim[640:960]
    blocks = [v.astype(BF) for v in (west, rows, east)]
    taps2 = jnp.concatenate([blocks[b][a * 32:a * 32 + 256] for a in range(3) for b in range(3)], axis=1)
    w2 = r["v_w2"]
    pre = nt(taps2, side_by_side(w2, 9))
    gz3 = (gelu_slope(pre) * back_up).astype(BF)
    none32, none64 = jnp.zeros((32, 128), F32), jnp.zeros((64, 128), F32)
    back = []
    for b in range(3):
        v0, v1, v2 = (nn(gz3, w2[3 * a + b]) for a in range(3))
        back.append(
            jnp.concatenate([v0, none64], axis=0)
            + jnp.concatenate([none32, v1, none32], axis=0)
            + jnp.concatenate([none64, v2], axis=0)
        )
    mid = (
        back[1]
        + jnp.where(col == 31, 0.0, pltpu.roll(back[0], 319, 0))
        + jnp.where(col == 0, 0.0, pltpu.roll(back[2], 1, 0))
    )
    cat = jnp.concatenate([mid.astype(BF), back[0].astype(BF), back[2].astype(BF)], axis=0)
    dq = r["dq"]
    dq[...] = tn(cat, sel).astype(BF)
    x4in, hout, hin = r["x4in"], r["hout"], r["hin"]
    c_x = spread(
        x4in.at[pl.ds(1, 3)], XD, x_peer, lambda d: dq.at[rows_of(xs[d]), :], lambda d: x4in.at[d]
    )
    hout[0] = mid[288:320]
    hout[1] = mid[0:32]
    c_h = begin(hin)
    push(c_h, hout.at[0], hin.at[0], x_peer(1))
    push(c_h, hout.at[1], hin.at[1], x_peer(3))

    other = 1 - core

    def halves(name, wide, parts):
        outs, ins = r[name + "c"], r[name + "ci"]
        for n in range(4):
            rows_n = pl.ds(pl.multiple_of(n * 32 + other * 16, 16), 16)
            at = 0
            for ref in parts:
                width = ref.shape[1]
                outs[n, :, at:at + width] = ref[rows_n, :].astype(BF)
                at += width
            outs[n, :, at:wide] = jnp.zeros((16, wide - at), BF)
        n = begin(ins)
        push(n, outs, ins, (tile + 1 - 2 * core, x))
        return n

    def shares(name, wide, parts):
        outs, ins = r[name + "o"], r[name + "i"]
        share = wide // 4
        for n in range(4):
            rows_n = pl.ds(pl.multiple_of(n * 32 + core * 16, 16), 16)
            own_n = jnp.concatenate(
                [ref[rows_n, :] for ref in parts]
                + [jnp.zeros((16, wide - sum(ref.shape[1] for ref in parts)), F32)],
                axis=1,
            )
            summed = (own_n + r[name + "ci"][n].astype(F32)).astype(BF)
            for m in range(4):
                outs[n, m] = summed[:, m * share:(m + 1) * share]
        m = begin(ins.at[pl.ds(1, 15)])
        for dx, dy in XYD:
            push(m, outs.at[xs[dx], ys[dy]], ins.at[dx * 4 + dy], xy_peer(dx, dy))
        return m

    def along_z(name):
        total = r[name + "o"][x, y].astype(F32)
        for n in range(1, 16):
            total = total + r[name + "i"][n].astype(F32)
        zall = r[name + "z"]
        zall[z] = total.astype(BF)
        return spread(zall.at[pl.ds(0, 7)], ZD, z_peer, lambda d: zall.at[z], lambda d: zall.at[z])

    def whole(name):
        zall = r[name + "z"]
        total = zall[0].astype(F32)
        for n in range(1, 8):
            total = total + zall[n].astype(F32)
        return total.astype(BF)

    coarse = gelu(pre).astype(BF)
    lifted = nt(coarse, up[...])
    out, ostrip = r["out"], r["ostrip"]
    for n in range(8):
        row = lifted[n * 32:(n + 1) * 32]
        summed = act1[n * 128:(n + 1) * 128, :].astype(F32) + jnp.concatenate([row] * 4, axis=0)
        ostrip[:, n * 128:(n + 1) * 128] = tn(summed.astype(BF), flat).astype(BF)

    settle(c_x)
    total = dq[mine, :].astype(F32)
    for d in XD:
        total = total + x4in[d].astype(F32)
    held3 = r["held3"]
    held3[g] = total.astype(BF)
    c_g = spread(held3.at[pl.ds(0, 7)], GD, g_peer, lambda d: held3.at[g], lambda d: held3.at[g])
    lanes = pl.ds(pl.multiple_of(x * 1024, 1024), 1024)
    c_o = spread(
        out, XD, x_peer,
        lambda d: ostrip.at[rows_of(xs[d]), :], lambda d: out.at[:, lanes],
    )
    local(r["rs"].at[c_o], ostrip.at[mine, :], out.at[:, lanes])

    r["gb_u"][...] = tn(pooled, coarse)
    r["gb_w"][...] = tn(gz3, taps2)
    parts_b = (r["gb_w"], r["gb_u"])
    c_bc = halves("b", BW, parts_b)
    settle(c_g)
    rolled3 = r["rolled3"]
    for j in range(8):
        for h in range(2):
            block = held3[j, :, 128 * h:128 * h + 128]
            rolled3[j * 8 + h * 4] = block
            for m in range(1, 4):
                rolled3[j * 8 + h * 4 + m] = pltpu.roll(block.astype(F32), 32 * m, 1).astype(BF)
    sums = [jnp.zeros((32, 128), F32) for _ in range(8)]
    for j in range(8):
        for k in range(8):
            at = j * 8 + k
            n, s = table[3, at], table[4, at]
            block = rolled3[table[5, at]].astype(F32)
            if k < 4:
                block = jnp.where(lane // 32 == s, block, 0.0)
            else:
                block = jnp.where(lane == 32 * s + EDGE[k - 4], block, 0.0)
            for m in range(8):
                sums[m] = sums[m] + jnp.where(n == m, block, 0.0)
    slots3, landed3 = r["slots3"], r["landed3"]
    for n in range(8):
        slots3[n] = sums[n].astype(BF)
    c_z = spread(
        landed3.at[pl.ds(1, 7)], ZD, z_peer, lambda d: slots3.at[zs[d]], lambda d: landed3.at[d]
    )
    settle(c_bc)
    c_b = shares("b", BW, parts_b)
    slope2 = gelu_slope(r["z2"][...])
    settle(c_z)
    total = slots3[z].astype(F32)
    for d in ZD:
        total = total + landed3[d].astype(F32)
    back_rim = r["back_rim"]
    back_rim[mine, :] = total.astype(BF)
    part3 = back_rim.at[mine, :]
    c_x = spread(back_rim.at[pl.ds(0, 96), :], XD, x_peer, lambda d: part3, lambda d: part3)
    settle(c_b)
    c_bz = along_z("b")
    settle(c_h)
    upper = jnp.where(q == 0, 0.0, hin[0])
    lower = jnp.where(q == 3, 0.0, hin[1])
    ga2 = mid[32:288] + jnp.concatenate([upper, jnp.zeros((192, 128), F32), lower], axis=0)
    settle(c_x)

    gz2 = (slope2 * (ga2 + nt(r["v_rout"][...], back_rim[...]))).astype(BF)
    wd = r["v_wd"]
    fine = [nn(gz2, wd[t]).reshape(8, 1, 32, 128) for t in range(4)]
    grown = jnp.concatenate(fine, axis=1).reshape(1024, 128)
    gz1 = (r["direct"][...] + r["slope"][...] * grown).astype(BF)
    r["ga_w"][...] = tn(
        gz1, jnp.concatenate([cb[b, a * 128:a * 128 + 1024, :] for a in range(3) for b in range(3)], axis=1)
    )
    r["ga_d"][...] = tn(gz2, quarters(act1[...]))
    parts_a = (r["ga_w"], r["ga_d"])
    c_ac = halves("a", AW, parts_a)

    def to_row(name, n):
        settle(n)
        final = r["final_" + name]
        final[g] = whole(name)
        return spread(final.at[pl.ds(0, 7)], GD, g_peer, lambda d: final.at[g], lambda d: final.at[g])

    c_bg = to_row("b", c_bz)
    settle(c_ac)
    c_a = shares("a", AW, parts_a)
    settle(c_a)
    c_az = along_z("a")
    settle(c_bg)
    settle(c_o)
    settle(to_row("a", c_az))
    assert sum(sent) == 256 * SENT, sum(sent) // 256
    wait(r["drain"], r["ss"])


INPUTS = (
    "adj", "feat", "ograd", "w1", "wd", "w2", "up",
    "pick", "put", "perm", "cmap", "fsel", "place", "rout", "rin",
)


def buf(*shape, kind=BF):
    return pltpu.VMEM(shape, kind)


def sems(*shape):
    return pltpu.SemaphoreType.DMA(shape)


SENT = 14064
SCRATCH = [
    ("early", buf(3072, 128)), ("late", buf(8192, 128)), ("drain", buf(SENT, 128)),
    ("lsem", sems(3)), ("ss", pltpu.SemaphoreType.DMA), ("rs", sems(30)), ("s_adj", pltpu.SMEM((16, 64), jnp.int32)),
    ("table", pltpu.SMEM((6, 64), jnp.int32)),
    ("fv", buf(32, 4096)), ("v_pick", buf(1024, 128)), ("v_put", buf(4, 128, 256)), ("v_perm", buf(3, 128, 128)),
    ("v_cmap", buf(4, 128, 128)), ("v_fsel", buf(4, 128, 640)), ("v_place", buf(2, 1280, 128)),
    ("v_rout", buf(256, 128)), ("v_rin", buf(960, 256)),
    ("strip", buf(128, 1280)), ("og", buf(128, 1024)), ("v_w1", buf(9, 128, 128)), ("v_wd", buf(4, 128, 128)),
    ("v_w2", buf(9, 128, 128)), ("v_up", buf(128, 128)),
    ("held0", buf(32, 16, 128)), ("held1", buf(32, 16, 128)), ("slots", buf(2, 8, 16, 640)), ("landed", buf(2, 8, 16, 640)),
    ("pout", buf(4, 32, 256)), ("picked", buf(128, 256)),
    ("cb", buf(3, 1280, 128)), ("z1", buf(1024, 128, kind=F32)), ("act1", buf(1024, 128)),
    ("z2", buf(256, 128, kind=F32)), ("act2", buf(256, 128)), ("rq", buf(128, 128)), ("x2in", buf(4, 32, 128)),
    ("slope", buf(1024, 128, kind=F32)), ("direct", buf(1024, 128, kind=F32)),
    ("halo", buf(2, 32, 128)), ("held2", buf(8, 32, 128)), ("rolled", buf(32, 32, 128)), ("ogt", buf(1024, 128)),
    ("slots2", buf(8, 32, 256)), ("landed2", buf(8, 32, 256)), ("picked2", buf(128, 256)),
    ("dq", buf(128, 256)), ("x4in", buf(4, 32, 256)),
    ("hout", buf(2, 32, 128, kind=F32)), ("hin", buf(2, 32, 128, kind=F32)),
    ("held3", buf(8, 32, 256)), ("rolled3", buf(64, 32, 128)), ("ostrip", buf(128, 1024)),
    ("slots3", buf(8, 32, 128)), ("landed3", buf(8, 32, 128)), ("back_rim", buf(128, 128)),
    ("gb_u", buf(128, 128, kind=F32)), ("gb_w", buf(128, 1152, kind=F32)),
    ("ga_d", buf(128, 512, kind=F32)), ("ga_w", buf(128, 1152, kind=F32)),
    ("bc", buf(4, 16, BW)), ("bci", buf(4, 16, BW)), ("bo", buf(4, 4, 16, BW // 4)), ("bi", buf(16, 16, BW // 4)),
    ("bz", buf(8, 16, BW // 4)),
    ("ac", buf(4, 16, AW)), ("aci", buf(4, 16, AW)), ("ao", buf(4, 4, 16, AW // 4)), ("ai", buf(16, 16, AW // 4)),
    ("az", buf(8, 16, AW // 4)),
]


def level_call(*args):
    return pl.pallas_call(
        level_kernel,
        out_shape=(pltpu.VMEM((32, 4096), BF), pltpu.VMEM((8, 16, AW // 4), BF), pltpu.VMEM((8, 16, BW // 4), BF)),
        in_specs=[ANY] * 15,
        out_specs=[VM] * 3,
        scratch_shapes=[s for _, s in SCRATCH],
        compiler_params=pltpu.CompilerParams(collective_id=0, has_side_effects=True, vmem_limit_bytes=LIMIT),
    )(*args)


def result_kernel(out_in, final_a, final_b, out, g1, gd, g2, gu, *, scale):
    out[...] = out_in[...]
    for c in range(2):
        rows = pl.ds(c * 16, 16)
        for t in range(13):
            block = final_a[2 * (t // 4) + c, :, (t % 4) * 128:(t % 4 + 1) * 128].astype(F32) * scale
            if t < 9:
                g1[t, rows, :] = block
            else:
                gd[t - 9, rows, :] = block
        for t in range(10):
            at = (t % 3) * 128
            block = final_b[2 * (t // 3) + c, :, at:at + 128].astype(F32) * scale
            if t < 9:
                g2[t, rows, :] = block
            else:
                gu[rows, :] = block


def result_call(out_in, final_a, final_b, scale):
    return pl.pallas_call(
        functools.partial(result_kernel, scale=scale),
        out_shape=(
            jax.ShapeDtypeStruct((32, 4096), BF),
            jax.ShapeDtypeStruct((9, 32, 128), F32),
            jax.ShapeDtypeStruct((4, 32, 128), F32),
            jax.ShapeDtypeStruct((9, 32, 128), F32),
            jax.ShapeDtypeStruct((32, 128), F32),
        ),
        in_specs=[VM] * 3,
        out_specs=[VM] * 5,
        compiler_params=pltpu.CompilerParams(vmem_limit_bytes=16 * 1024 * 1024),
    )(out_in, final_a, final_b)


def per_device(features, conv1_weight, down_weight, conv2_weight, up_weight, out_grad, adjacency):
    pick, put = fine_rim_out()
    fine_sel, fine_place = fine_rim_maps()
    maps = [
        jnp.asarray(m, BF)
        for m in (pick, put, fine_perm(), corner_maps(), fine_sel, fine_place, coarse_rim_out(), coarse_rim_in())
    ]
    out, final_a, final_b = level_call(
        adjacency.transpose(1, 2, 0).reshape(16, 64), features, out_grad, conv1_weight, down_weight, conv2_weight, up_weight, *maps
    )
    return result_call(out, final_a, final_b, 262144 ** -0.5)


def solution(mesh):
    weights = P(None, "chan", None)
    return jax.shard_map(
        per_device,
        mesh=mesh,
        in_specs=(P("chan", "tile"), weights, weights, weights, P("chan", None), P("chan", "tile"), P()),
        out_specs=(P("chan", "tile"), weights, weights, weights, P("chan", None)),
        check_vma=False,
    )
```

```python
import functools
import math

import jax
import jax.numpy as jnp
import numpy as np
from jax import lax
from jax.experimental import pallas as pl
from jax.experimental.pallas import tpu as pltpu
from jax.sharding import PartitionSpec as P

BF = jnp.bfloat16
F32 = jnp.float32
MESH = pl.DeviceIdType.MESH
TURNS = (0, 1, 2, 3, 0, 2, 2, 0)
VM = pl.BlockSpec(memory_space=pltpu.VMEM)
ANY = pl.BlockSpec(memory_space=pl.ANY)
LIMIT = 56 * 1024 * 1024


def fine_perm():
    out = np.zeros((3, 128, 128), np.float32)
    for b in range(3):
        for rr in range(2):
            for par in range(2):
                for k in range(32):
                    col = 2 * (k - 1 + b) + par
                    if 0 <= col < 64:
                        out[b, rr * 64 + par * 32 + k, rr * 64 + col] = 1
    return out


def corner_maps():
    out = np.zeros((4, 128, 128), np.float32)
    for i in range(2):
        for j in range(2):
            out[0, i * 64 + j, 2 * i + j] = 1
            out[1, (1 - i) * 64 + 63 - j, 4 + 2 * i + j] = 1
            out[2, (1 - i) * 64 + 1 - j, 8 + 2 * i + j] = 1
            out[3, i * 64 + 62 + j, 12 + 2 * i + j] = 1
    return out


def fine_rim_maps():
    sel = np.zeros((4, 128, 640), np.float32)
    for q in range(4):
        for r in range(20):
            ir = 16 * q - 2 + r
            for par in range(2):
                if 0 <= ir < 64:
                    west = 384 + par * 64 + 63 - ir
                    east = 128 + (1 - par) * 64 + ir
                elif ir < 0:
                    west = 512 + 12 + 2 * (ir + 2) + par
                    east = 512 + 0 + 2 * (ir + 2) + par
                else:
                    west = 512 + 8 + 2 * (ir - 64) + par
                    east = 512 + 4 + 2 * (ir - 64) + par
                sel[q, r * 2 + par, west] = 1
                sel[q, 64 + r * 2 + par, east] = 1
    place = np.zeros((2, 1280, 128), np.float32)
    for r in range(20):
        for par in range(2):
            place[0, r * 64 + par * 32, r * 2 + par] = 1
            place[1, r * 64 + par * 32 + 31, 64 + r * 2 + par] = 1
    return sel, place


def fine_rim_out():
    pick = np.zeros((1024, 128), np.float32)
    for r in range(16):
        for kind, col in enumerate((0, 1, 62, 63)):
            pick[r * 64 + col, kind * 16 + r] = 1
    put = np.zeros((4, 128, 256), np.float32)
    for s in range(4):
        for r16 in range(16):
            r = 16 * s + r16
            for kind, lane in enumerate((64 + r, r, 128 + 63 - r, 192 + 63 - r)):
                put[s, kind * 16 + r16, lane] = 1
    return pick, put


def coarse_rim_out():
    out = np.zeros((4, 256, 128), np.float32)
    for i in range(32):
        for s, (r, k) in enumerate(((31, i), (i, 0), (0, 31 - i), (31 - i, 31))):
            out[r // 8, (r % 8) * 32 + k, s * 32 + i] = 1
    return out


def coarse_rim_in():
    out = np.zeros((4, 960, 256), np.float32)
    for k in range(32):
        out[0, k, k] = 1
        out[3, 9 * 32 + k, 64 + 31 - k] = 1
    for q in range(4):
        for r in range(10):
            row = 8 * q - 1 + r
            if row < 0:
                west, east = 255, 128
            elif row >= 32:
                west, east = 192, 191
            else:
                west, east = 96 + 31 - row, 32 + row
            out[q, 320 + r * 32, west] = 1
            out[q, 640 + r * 32 + 31, east] = 1
    return out


def nt(a, b):
    return lax.dot_general(a, b, (((1,), (1,)), ((), ())), preferred_element_type=F32)


def tn(a, b):
    return lax.dot_general(a, b, (((0,), (0,)), ((), ())), preferred_element_type=F32)


def nn(a, b):
    return lax.dot_general(a, b, (((1,), (0,)), ((), ())), preferred_element_type=F32)


ROOT = 0.7978845608028654


def gelu(v):
    return 0.5 * v * (1.0 + jnp.tanh(ROOT * (v + 0.044715 * (v * v * v))))


def gelu_slope(v):
    t = jnp.tanh(ROOT * (v + 0.044715 * (v * v * v)))
    return 0.5 * (1.0 + t) + 0.5 * v * (1.0 - t * t) * (ROOT * (1.0 + 3 * 0.044715 * (v * v)))


AW, BW = 2048, 1536
XD = (2, 1, 3)
ZD = (4, 3, 5, 2, 6, 1, 7)
GD = (4, 3, 5, 2, 6, 1, 7)
FAR = (2, 1, 3, 0)
XYD = [(dx, dy) for dx in FAR for dy in FAR if dx or dy]
EDGE = (0, 31, 0, 31)


def side_by_side(weights, count):
    return jnp.concatenate([weights[t] for t in range(count)], axis=1)


def quarters(act):
    parts = act.reshape(8, 2, 2, 32, 128)
    return jnp.concatenate(
        [parts[:, a, b].reshape(256, 128) for a in range(2) for b in range(2)], axis=1
    )


def flip_map():
    rows = lax.broadcasted_iota(jnp.int32, (128, 128), 0)
    cols = lax.broadcasted_iota(jnp.int32, (128, 128), 1)
    return jnp.where(rows + cols == 127, 1.0, 0.0).astype(BF)


def level_kernel(*refs):
    names = INPUTS + ("out", "final_a", "final_b") + tuple(n for n, _ in SCRATCH)
    r = dict(zip(names, refs))
    tile, x = lax.axis_index("tile"), lax.axis_index("chan")
    z, g = tile // 8, lax.rem(tile, 8)
    y, core = g // 2, lax.rem(g, 2)
    q = x
    xs = [x] + [lax.rem(x + d, 4) for d in range(1, 4)]
    ys = [y] + [lax.rem(y + d, 4) for d in range(1, 4)]
    zs = [z] + [lax.rem(z + d, 8) for d in range(1, 8)]
    gs = [g] + [lax.rem(g + d, 8) for d in range(1, 8)]
    x_at = [(tile, xs[d]) for d in range(4)]
    z_at = [(zs[d] * 8 + g, x) for d in range(8)]
    g_at = [(z * 8 + gs[d], x) for d in range(8)]
    x_peer, z_peer, g_peer = x_at.__getitem__, z_at.__getitem__, g_at.__getitem__

    def xy_peer(dx, dy):
        return (g_at[2 * dy][0], xs[dx])

    mine = pl.ds(pl.multiple_of(x * 32, 32), 32)
    rounds, sent = [], []

    def rows_of(n):
        return pl.ds(pl.multiple_of(n * 32, 32), 32)

    def local(sem, src, dst):
        pltpu.make_async_copy(src, dst, sem).start()

    def wait(whole, sem):
        pltpu.make_async_copy(whole, whole, sem).wait()

    def begin(whole):
        rounds.append(whole)
        return len(rounds) - 1

    def push(n, src, dst, peer):
        pltpu.make_async_remote_copy(
            src_ref=src, dst_ref=dst, send_sem=r["ss"], recv_sem=r["rs"].at[n],
            device_id=peer, device_id_type=MESH,
        ).start()
        sent.append(math.prod(src.shape) * src.dtype.itemsize)

    def spread(whole, dirs, peer, src, dst):
        n = begin(whole)
        for d in dirs:
            push(n, src(d), dst(d), peer(d))
        return n

    def settle(n):
        wait(rounds[n], r["rs"].at[n])

    early = (("feat", "fv"), ("pick", "v_pick"), ("put", "v_put"))
    for src, dst in early:
        local(r["lsem"].at[0], r[src], r[dst])
    local(r["lsem"].at[1], r["adj"], r["s_adj"])
    barrier = pltpu.get_barrier_semaphore()
    peers = [x_peer(d) for d in XD] + [z_peer(d) for d in ZD] + [g_peer(d) for d in GD]
    peers += [xy_peer(dx, dy) for dx, dy in XYD if dx and dy]
    for peer in peers:
        pl.semaphore_signal(barrier, inc=1, device_id=peer, device_id_type=MESH)

    adj = r["s_adj"]

    wait(r["early"], r["lsem"].at[0])
    fv, held = r["fv"], (r["held0"], r["held1"])
    stacked = jnp.concatenate([fv[:, s * 1024:(s + 1) * 1024] for s in range(4)], axis=0)
    cols = nn(stacked, r["v_pick"][...]).astype(BF)
    both = nn(cols[0:32], r["v_put"][0])
    for s in range(1, 4):
        both = both + nn(cols[32 * s:32 * s + 32], r["v_put"][s])
    flip = flip_map()
    rims = (
        fv[:, 3968:4096],
        both[:, 0:128].astype(BF),
        nn(fv[:, 0:128], flip).astype(BF),
        both[:, 128:256].astype(BF),
    )
    for s in range(4):
        held[0][z * 4 + s] = rims[s][0:16]
        held[1][g * 4 + s] = rims[s][16:32]
    pl.semaphore_wait(barrier, len(peers))
    ways = ((z, ZD, z_peer), (g, GD, g_peer))
    first = []
    for h in range(2):
        at, dirs, peer = ways[h]
        part = held[h].at[pl.ds(at * 4, 4)]
        first.append(spread(held[h].at[pl.ds(0, 28)], dirs, peer, lambda d: part, lambda d: part))

    for name in ("cmap", "perm", "fsel", "place"):
        local(r["lsem"].at[2], r[name], r["v_" + name])
    for name in ("rout", "rin"):
        local(r["lsem"].at[2], r[name].at[q], r["v_" + name])

    def piece(n, j):
        if n == 0:
            start = pl.multiple_of(jnp.clip(j * 1024 - 128, 0, 2816), 128)
            return r["feat"].at[:, pl.ds(start, 1280)], r["strip"].at[mine, :]
        if n == 3:
            return r["ograd"].at[:, pl.ds(pl.multiple_of(j * 1024, 1024), 1024)], r["og"].at[mine, :]
        if n == 5:
            return r["up"], r["v_up"].at[mine, :]
        name = {1: "w1", 2: "wd", 4: "w2"}[n]
        return r[name].at[:, core], r["v_" + name].at[:, x, core]

    bulk = {}

    def send_bulk(n):
        into = r[("strip", "v_w1", "v_wd", "og", "v_w2", "v_up")[n]]
        m = begin(into.at[:, :, 0] if n in (1, 2, 4) else into)
        for d in XD:
            src, dst = piece(n, xs[d])
            push(m, src, dst, x_peer(d))
        src, dst = piece(n, x)
        local(r["rs"].at[m], src, dst)
        bulk[n] = m

    def share_bulk(n):
        settle(bulk[n])
        into = r[{1: "v_w1", 2: "v_wd", 4: "v_w2"}[n]]
        bulk[n] = begin(into.at[:, :, 0])
        push(bulk[n], into.at[:, :, core], into.at[:, :, core], (tile + 1 - 2 * core, x))

    def take_bulk(n):
        settle(bulk[n])

    for n in range(6):
        send_bulk(n)

    wait(r["s_adj"], r["lsem"].at[1])

    table = r["table"]
    for n in range(8):
        for k in range(8):
            at = n * 8 + k
            for h in range(2):
                t = z * 8 + n if h == 0 else n * 8 + g
                p = adj[2 * k, t]
                s = lax.rem(adj[2 * k + 1, t] + TURNS[k], 4)
                owned = jnp.logical_and(p >= 0, (p // 8 == z) if h else (lax.rem(p, 8) == g))
                m = lax.rem(p, 8) if h else p // 8
                table[h, at] = jnp.where(owned, m * 4 + s, -1)
                if h == 0:
                    table[2, at] = jnp.where(owned, m * 4 + lax.rem(k + 4 - s, 4), -1)
                    table[3, at] = jnp.where(owned, m, -1)
                    table[4, at] = s
                    table[5, at] = n * 8 + (k // 4) * 4 + lax.rem(s + 4 - k % 4, 4)

    wait(r["late"], r["lsem"].at[2])
    slots, landed = r["slots"], r["landed"]
    second = []
    for h in (1, 0):
        settle(first[h])
        _, dirs, peer = ways[1 - h]
        order = dirs + (0,)
        m = begin(landed.at[h, pl.ds(1, 7)])
        second.append(m)
        corners = [[] for _ in range(4)]
        for d in order:
            t = (gs[d] if h == 0 else zs[d]) * 8
            for k in range(8):
                n = table[h, t + k]
                block = held[h][jnp.maximum(n, 0)]
                block = jnp.where(n >= 0, block, jnp.zeros_like(block))
                if k < 4:
                    slots[h, d, :, k * 128:(k + 1) * 128] = block
                else:
                    corners[k - 4].append(block)
        corner = nn(jnp.concatenate(corners[0], axis=0), r["v_cmap"][0])
        for k in range(1, 4):
            corner = corner + nn(jnp.concatenate(corners[k], axis=0), r["v_cmap"][k])
        for n, d in enumerate(order):
            slots[h, d, :, 512:640] = corner[16 * n:16 * n + 16].astype(BF)
            if d:
                push(m, slots.at[h, d], landed.at[h, d], peer(d))
    take_bulk(0)
    perm, cb, strip = r["v_perm"], r["cb"], r["strip"]
    perms = perm[...].reshape(384, 128)
    shift = jnp.where(q == 0, -1, jnp.where(q == 3, 1, 0))

    def strip_block(n):
        at = jnp.clip(n + shift, 0, 9)
        return strip[:, pl.ds(pl.multiple_of(at * 128, 128), 128)]

    for n in range(1, 9):
        turned = nt(perms, strip_block(n))
        for b in range(3):
            cb[b, n * 128:(n + 1) * 128, :] = turned[b * 128:(b + 1) * 128].astype(BF)

    share_bulk(1)
    share_bulk(2)
    halves_of = []
    for m, h in zip(second, (1, 0)):
        settle(m)
        total = slots[h, 0].astype(F32)
        for d in range(1, 8):
            total = total + landed[h, d].astype(F32)
        halves_of.append(total)
    total = jnp.concatenate([halves_of[1], halves_of[0]], axis=0).astype(BF)

    picked, pout = r["picked"], r["pout"]
    ends = (total[:, 0:128], None, None, nn(total[:, 256:384], flip).astype(BF))
    for j in range(4):
        pout[j, :, 0:128] = nt(total, r["v_fsel"][j]).astype(BF)
        pout[j, :, 128:256] = jnp.zeros((32, 128), BF) if ends[j] is None else ends[j]
    c_x = spread(
        picked.at[pl.ds(0, 96), :], XD, x_peer, lambda d: pout.at[xs[d]], lambda d: picked.at[mine, :]
    )
    picked[mine, :] = pout[x]
    take_bulk(1)
    take_bulk(2)
    w1 = r["v_w1"][...].reshape(9, 128, 128)
    w1c = side_by_side(w1, 9)
    for n in (0, 9):
        block = strip_block(n)
        turned = nt(perms, jnp.where(q == n // 3, jnp.zeros_like(block), block))
        for b in range(3):
            cb[b, n * 128:(n + 1) * 128, :] = turned[b * 128:(b + 1) * 128].astype(BF)
    z1, act1 = r["z1"], r["act1"]

    def fine_taps(n):
        return jnp.concatenate(
            [cb[b, a * 128 + n * 256:a * 128 + n * 256 + 256, :] for a in range(3) for b in range(3)], axis=1
        )

    for n in range(4):
        z1[n * 256:(n + 1) * 256, :] = nt(fine_taps(n), w1c)
    w1_west = jnp.concatenate([w1[3 * a] for a in range(3)], axis=1)
    w1_east = jnp.concatenate([w1[3 * a + 2] for a in range(3)], axis=1)
    w1_end = jnp.where(q == 0, side_by_side(w1, 3), side_by_side(w1[6:9], 3))
    unit = jnp.where(
        lax.broadcasted_iota(jnp.int32, (128, 128), 0) == lax.broadcasted_iota(jnp.int32, (128, 128), 1), 1.0, 0.0
    ).astype(BF)
    settle(c_x)

    sides = picked[:, 0:128]
    side_rows = nt(unit, sides)
    end_rows = nt(perms, picked[:, 128:256])
    west = jnp.concatenate([side_rows[4 * a:4 * a + 32] for a in range(3)], axis=1).astype(BF)
    east = jnp.concatenate([side_rows[64 + 4 * a:96 + 4 * a] for a in range(3)], axis=1).astype(BF)
    ends = jnp.concatenate([end_rows[128 * b:128 * b + 128] for b in range(3)], axis=1).astype(BF)
    west, east, ends = nt(west, w1_west), nt(east, w1_east), nt(ends, w1_end)
    for n in range(8):
        rows = slice(n * 128, (n + 1) * 128)
        add = []
        cell = lax.broadcasted_iota(jnp.int32, (32, 128), 0)
        for m in range(4 * n, 4 * n + 4):
            add.append(
                jnp.where(cell == 0, west[m:m + 1], 0.0) + jnp.where(cell == 31, east[m:m + 1], 0.0)
            )
        pre = z1[rows, :] + jnp.concatenate(add, axis=0)
        if n in (0, 7):
            pre = pre + jnp.where(q == (0 if n == 0 else 3), ends, 0.0)
        z1[rows, :] = pre
        act1[rows, :] = gelu(pre).astype(BF)
    pre = nt(quarters(act1[...]), side_by_side(r["v_wd"][...].reshape(4, 128, 128), 4))
    r["z2"][...] = pre
    act2 = gelu(pre).astype(BF)
    r["act2"][...] = act2
    rq = r["rq"]
    rq[...] = tn(act2, r["v_rout"][...]).astype(BF)

    x2in, halo = r["x2in"], r["halo"]
    c_x = spread(
        x2in.at[pl.ds(1, 3)], XD, x_peer, lambda d: rq.at[rows_of(xs[d]), :], lambda d: x2in.at[d]
    )
    c_h = begin(halo)
    push(c_h, r["act2"].at[pl.ds(224, 32), :], halo.at[0], x_peer(1))
    push(c_h, r["act2"].at[pl.ds(0, 32), :], halo.at[1], x_peer(3))
    total = rq[mine, :].astype(F32)
    settle(c_x)
    for d in XD:
        total = total + x2in[d].astype(F32)
    held2 = r["held2"]
    held2[z] = total.astype(BF)
    c_z = spread(held2.at[pl.ds(0, 7)], ZD, z_peer, lambda d: held2.at[z], lambda d: held2.at[z])

    take_bulk(3)
    take_bulk(5)
    share_bulk(4)
    og, ogt, up = r["og"], r["ogt"], r["v_up"]
    flat = perm[1]
    for n in range(8):
        ogt[n * 128:(n + 1) * 128, :] = nt(flat, og[:, n * 128:(n + 1) * 128]).astype(BF)
    cells = ogt[...].astype(F32).reshape(8, 4, 32, 128)
    pooled = (cells[:, 0] + cells[:, 1] + cells[:, 2] + cells[:, 3]).reshape(256, 128).astype(BF)
    back_up = nn(pooled, up[...])
    for n in (0, 9):
        for b in range(3):
            rows = slice(n * 128, (n + 1) * 128)
            new = jnp.where(q == n // 3, end_rows[b * 128:(b + 1) * 128], cb[b, rows, :].astype(F32))
            cb[b, rows, :] = new.astype(BF)
    for b in (0, 2):
        cb[b] = (cb[b].astype(F32) + nt(r["v_place"][b // 2], sides)).astype(BF)
    slope = gelu_slope(z1[...])
    r["slope"][...] = slope
    r["direct"][...] = slope * ogt[...].astype(F32)

    settle(c_z)
    rolled = r["rolled"]
    for n in range(8):
        block = held2[n].astype(F32)
        rolled[n * 4] = held2[n]
        for m in range(1, 4):
            rolled[n * 4 + m] = pltpu.roll(block, 32 * m, 1).astype(BF)
    lane = lax.broadcasted_iota(jnp.int32, (32, 128), 1)
    slots2, landed2 = r["slots2"], r["landed2"]
    c_g = begin(landed2.at[pl.ds(1, 7)])
    for d in GD + (0,):
        t = gs[d] * 8
        both = [jnp.zeros((32, 128), F32), jnp.zeros((32, 128), F32)]
        for k in range(8):
            n = table[2, t + k]
            block = rolled[jnp.maximum(n, 0)].astype(F32)
            block = jnp.where(n >= 0, block, 0.0)
            if k < 4:
                both[0] = jnp.where(lane // 32 == k, block, both[0])
            else:
                both[1] = jnp.where(lane == 32 * (k - 4) + EDGE[k - 4], block, both[1])
        slots2[d, :, 0:128] = both[0].astype(BF)
        slots2[d, :, 128:256] = both[1].astype(BF)
        if d:
            push(c_g, slots2.at[d], landed2.at[d], g_peer(d))
    settle(c_g)
    total = slots2[0].astype(F32)
    for d in range(1, 8):
        total = total + landed2[d].astype(F32)
    picked2 = r["picked2"]
    picked2[mine, :] = total.astype(BF)
    part2 = picked2.at[mine, :]
    c_x = spread(picked2.at[pl.ds(0, 96), :], XD, x_peer, lambda d: part2, lambda d: part2)
    take_bulk(4)
    settle(c_h)
    settle(c_x)

    sel = r["v_rin"][...]
    rim = nt(sel, picked2[...])
    upper = jnp.where(q == 0, 0.0, halo[0].astype(F32))
    lower = jnp.where(q == 3, 0.0, halo[1].astype(F32))
    rows = jnp.concatenate([upper, act2.astype(F32), lower], axis=0) + rim[0:320]
    col = lax.rem(lax.broadcasted_iota(jnp.int32, (320, 128), 0), 32)
    west = jnp.where(col == 0, 0.0, pltpu.roll(rows, 1, 0)) + rim[320:640]
    east = jnp.where(col == 31, 0.0, pltpu.roll(rows, 319, 0)) + rim[640:960]
    blocks = [v.astype(BF) for v in (west, rows, east)]
    taps2 = jnp.concatenate([blocks[b][a * 32:a * 32 + 256] for a in range(3) for b in range(3)], axis=1)
    w2 = r["v_w2"][...].reshape(9, 128, 128)
    pre = nt(taps2, side_by_side(w2, 9))
    gz3 = (gelu_slope(pre) * back_up).astype(BF)
    none32, none64 = jnp.zeros((32, 128), F32), jnp.zeros((64, 128), F32)
    back = []
    for b in range(3):
        v0, v1, v2 = (nn(gz3, w2[3 * a + b]) for a in range(3))
        back.append(
            jnp.concatenate([v0, none64], axis=0)
            + jnp.concatenate([none32, v1, none32], axis=0)
            + jnp.concatenate([none64, v2], axis=0)
        )
    mid = (
        back[1]
        + jnp.where(col == 31, 0.0, pltpu.roll(back[0], 319, 0))
        + jnp.where(col == 0, 0.0, pltpu.roll(back[2], 1, 0))
    )
    cat = jnp.concatenate([mid.astype(BF), back[0].astype(BF), back[2].astype(BF)], axis=0)
    dq = r["dq"]
    dq[...] = tn(cat, sel).astype(BF)
    x4in, hout, hin = r["x4in"], r["hout"], r["hin"]
    c_x = spread(
        x4in.at[pl.ds(1, 3)], XD, x_peer, lambda d: dq.at[rows_of(xs[d]), :], lambda d: x4in.at[d]
    )
    hout[0] = mid[288:320]
    hout[1] = mid[0:32]
    c_h = begin(hin)
    push(c_h, hout.at[0], hin.at[0], x_peer(1))
    push(c_h, hout.at[1], hin.at[1], x_peer(3))

    other = 1 - core

    def halves(name, wide, parts):
        outs, ins = r[name + "c"], r[name + "ci"]
        for n in range(4):
            rows_n = pl.ds(pl.multiple_of(n * 32 + other * 16, 16), 16)
            at = 0
            for ref in parts:
                width = ref.shape[1]
                outs[n, :, at:at + width] = ref[rows_n, :].astype(BF)
                at += width
            outs[n, :, at:wide] = jnp.zeros((16, wide - at), BF)
        n = begin(ins)
        push(n, outs, ins, (tile + 1 - 2 * core, x))
        return n

    def shares(name, wide, parts):
        outs, ins = r[name + "o"], r[name + "i"]
        share = wide // 4
        for n in range(4):
            rows_n = pl.ds(pl.multiple_of(n * 32 + core * 16, 16), 16)
            own_n = jnp.concatenate(
                [ref[rows_n, :] for ref in parts]
                + [jnp.zeros((16, wide - sum(ref.shape[1] for ref in parts)), F32)],
                axis=1,
            )
            summed = (own_n + r[name + "ci"][n].astype(F32)).astype(BF)
            for m in range(4):
                outs[n, m] = summed[:, m * share:(m + 1) * share]
        m = begin(ins.at[pl.ds(1, 15)])
        for dx, dy in XYD:
            push(m, outs.at[xs[dx], ys[dy]], ins.at[dx * 4 + dy], xy_peer(dx, dy))
        return m

    def along_z(name):
        total = r[name + "o"][x, y].astype(F32)
        for n in range(1, 16):
            total = total + r[name + "i"][n].astype(F32)
        zall = r[name + "z"]
        zall[z] = total.astype(BF)
        return spread(zall.at[pl.ds(0, 7)], ZD, z_peer, lambda d: zall.at[z], lambda d: zall.at[z])

    def whole(name):
        zall = r[name + "z"]
        total = zall[0].astype(F32)
        for n in range(1, 8):
            total = total + zall[n].astype(F32)
        return total.astype(BF)

    coarse = gelu(pre).astype(BF)
    lifted = nt(coarse, up[...])
    out, ostrip = r["out"], r["ostrip"]
    for n in range(8):
        row = lifted[n * 32:(n + 1) * 32]
        summed = act1[n * 128:(n + 1) * 128, :].astype(F32) + jnp.concatenate([row] * 4, axis=0)
        ostrip[:, n * 128:(n + 1) * 128] = tn(summed.astype(BF), flat).astype(BF)

    settle(c_x)
    total = dq[mine, :].astype(F32)
    for d in XD:
        total = total + x4in[d].astype(F32)
    held3 = r["held3"]
    held3[g] = total.astype(BF)
    c_g = spread(held3.at[pl.ds(0, 7)], GD, g_peer, lambda d: held3.at[g], lambda d: held3.at[g])
    lanes = pl.ds(pl.multiple_of(x * 1024, 1024), 1024)
    c_o = spread(
        out, XD, x_peer,
        lambda d: ostrip.at[rows_of(xs[d]), :], lambda d: out.at[:, lanes],
    )
    local(r["rs"].at[c_o], ostrip.at[mine, :], out.at[:, lanes])

    r["gb_u"][...] = tn(pooled, coarse)
    r["gb_w"][...] = tn(gz3, taps2)
    parts_b = (r["gb_w"], r["gb_u"])
    c_bc = halves("b", BW, parts_b)
    settle(c_g)
    rolled3 = r["rolled3"]
    for j in range(8):
        for h in range(2):
            block = held3[j, :, 128 * h:128 * h + 128]
            rolled3[j * 8 + h * 4] = block
            for m in range(1, 4):
                rolled3[j * 8 + h * 4 + m] = pltpu.roll(block.astype(F32), 32 * m, 1).astype(BF)
    sums = [jnp.zeros((32, 128), F32) for _ in range(8)]
    for j in range(8):
        for k in range(8):
            at = j * 8 + k
            n, s = table[3, at], table[4, at]
            block = rolled3[table[5, at]].astype(F32)
            if k < 4:
                block = jnp.where(lane // 32 == s, block, 0.0)
            else:
                block = jnp.where(lane == 32 * s + EDGE[k - 4], block, 0.0)
            for m in range(8):
                sums[m] = sums[m] + jnp.where(n == m, block, 0.0)
    slots3, landed3 = r["slots3"], r["landed3"]
    for n in range(8):
        slots3[n] = sums[n].astype(BF)
    c_z = spread(
        landed3.at[pl.ds(1, 7)], ZD, z_peer, lambda d: slots3.at[zs[d]], lambda d: landed3.at[d]
    )
    settle(c_bc)
    c_b = shares("b", BW, parts_b)
    slope2 = gelu_slope(r["z2"][...])
    settle(c_z)
    total = slots3[z].astype(F32)
    for d in ZD:
        total = total + landed3[d].astype(F32)
    back_rim = r["back_rim"]
    back_rim[mine, :] = total.astype(BF)
    part3 = back_rim.at[mine, :]
    c_x = spread(back_rim.at[pl.ds(0, 96), :], XD, x_peer, lambda d: part3, lambda d: part3)
    settle(c_b)
    c_bz = along_z("b")
    settle(c_h)
    upper = jnp.where(q == 0, 0.0, hin[0])
    lower = jnp.where(q == 3, 0.0, hin[1])
    ga2 = mid[32:288] + jnp.concatenate([upper, jnp.zeros((192, 128), F32), lower], axis=0)
    settle(c_x)

    gz2 = (slope2 * (ga2 + nt(r["v_rout"][...], back_rim[...]))).astype(BF)
    wd = r["v_wd"][...].reshape(4, 128, 128)
    fine = [nn(gz2, wd[t]).reshape(8, 1, 32, 128) for t in range(4)]
    grown = jnp.concatenate(fine, axis=1).reshape(1024, 128)
    gz1 = (r["direct"][...] + r["slope"][...] * grown).astype(BF)
    r["ga_w"][...] = tn(
        gz1, jnp.concatenate([cb[b, a * 128:a * 128 + 1024, :] for a in range(3) for b in range(3)], axis=1)
    )
    r["ga_d"][...] = tn(gz2, quarters(act1[...]))
    parts_a = (r["ga_w"], r["ga_d"])
    c_ac = halves("a", AW, parts_a)

    def to_row(name, n):
        settle(n)
        final = r["final_" + name]
        final[g] = whole(name)
        return spread(final.at[pl.ds(0, 7)], GD, g_peer, lambda d: final.at[g], lambda d: final.at[g])

    settle(c_ac)
    c_a = shares("a", AW, parts_a)
    settle(c_a)
    c_az = along_z("a")
    c_bg = to_row("b", c_bz)
    settle(c_o)
    c_ag = to_row("a", c_az)
    settle(c_bg)
    settle(c_ag)
    assert sum(sent) == 256 * SENT, sum(sent) // 256
    wait(r["drain"], r["ss"])


INPUTS = (
    "adj", "feat", "ograd", "w1", "wd", "w2", "up",
    "pick", "put", "perm", "cmap", "fsel", "place", "rout", "rin",
)


def buf(*shape, kind=BF):
    return pltpu.VMEM(shape, kind)


def sems(*shape):
    return pltpu.SemaphoreType.DMA(shape)


SENT = 14416
SCRATCH = [
    ("early", buf(3072, 128)), ("late", buf(8192, 128)), ("drain", buf(SENT, 128)),
    ("lsem", sems(3)), ("ss", pltpu.SemaphoreType.DMA), ("rs", sems(33)), ("s_adj", pltpu.SMEM((16, 64), jnp.int32)),
    ("table", pltpu.SMEM((6, 64), jnp.int32)),
    ("fv", buf(32, 4096)), ("v_pick", buf(1024, 128)), ("v_put", buf(4, 128, 256)), ("v_perm", buf(3, 128, 128)),
    ("v_cmap", buf(4, 128, 128)), ("v_fsel", buf(4, 128, 640)), ("v_place", buf(2, 1280, 128)),
    ("v_rout", buf(256, 128)), ("v_rin", buf(960, 256)),
    ("strip", buf(128, 1280)), ("og", buf(128, 1024)), ("v_w1", buf(9, 4, 2, 16, 128)), ("v_wd", buf(4, 4, 2, 16, 128)),
    ("v_w2", buf(9, 4, 2, 16, 128)), ("v_up", buf(128, 128)),
    ("held0", buf(32, 16, 128)), ("held1", buf(32, 16, 128)), ("slots", buf(2, 8, 16, 640)), ("landed", buf(2, 8, 16, 640)),
    ("pout", buf(4, 32, 256)), ("picked", buf(128, 256)),
    ("cb", buf(3, 1280, 128)), ("z1", buf(1024, 128, kind=F32)), ("act1", buf(1024, 128)),
    ("z2", buf(256, 128, kind=F32)), ("act2", buf(256, 128)), ("rq", buf(128, 128)), ("x2in", buf(4, 32, 128)),
    ("slope", buf(1024, 128, kind=F32)), ("direct", buf(1024, 128, kind=F32)),
    ("halo", buf(2, 32, 128)), ("held2", buf(8, 32, 128)), ("rolled", buf(32, 32, 128)), ("ogt", buf(1024, 128)),
    ("slots2", buf(8, 32, 256)), ("landed2", buf(8, 32, 256)), ("picked2", buf(128, 256)),
    ("dq", buf(128, 256)), ("x4in", buf(4, 32, 256)),
    ("hout", buf(2, 32, 128, kind=F32)), ("hin", buf(2, 32, 128, kind=F32)),
    ("held3", buf(8, 32, 256)), ("rolled3", buf(64, 32, 128)), ("ostrip", buf(128, 1024)),
    ("slots3", buf(8, 32, 128)), ("landed3", buf(8, 32, 128)), ("back_rim", buf(128, 128)),
    ("gb_u", buf(128, 128, kind=F32)), ("gb_w", buf(128, 1152, kind=F32)),
    ("ga_d", buf(128, 512, kind=F32)), ("ga_w", buf(128, 1152, kind=F32)),
    ("bc", buf(4, 16, BW)), ("bci", buf(4, 16, BW)), ("bo", buf(4, 4, 16, BW // 4)), ("bi", buf(16, 16, BW // 4)),
    ("bz", buf(8, 16, BW // 4)),
    ("ac", buf(4, 16, AW)), ("aci", buf(4, 16, AW)), ("ao", buf(4, 4, 16, AW // 4)), ("ai", buf(16, 16, AW // 4)),
    ("az", buf(8, 16, AW // 4)),
]


def level_call(*args):
    return pl.pallas_call(
        level_kernel,
        out_shape=(pltpu.VMEM((32, 4096), BF), pltpu.VMEM((8, 16, AW // 4), BF), pltpu.VMEM((8, 16, BW // 4), BF)),
        in_specs=[ANY] * 15,
        out_specs=[VM] * 3,
        scratch_shapes=[s for _, s in SCRATCH],
        compiler_params=pltpu.CompilerParams(collective_id=0, has_side_effects=True, vmem_limit_bytes=LIMIT),
    )(*args)


def result_kernel(out_in, final_a, final_b, out, g1, gd, g2, gu, *, scale):
    out[...] = out_in[...]
    for c in range(2):
        rows = pl.ds(c * 16, 16)
        for t in range(13):
            block = final_a[2 * (t // 4) + c, :, (t % 4) * 128:(t % 4 + 1) * 128].astype(F32) * scale
            if t < 9:
                g1[t, rows, :] = block
            else:
                gd[t - 9, rows, :] = block
        for t in range(10):
            at = (t % 3) * 128
            block = final_b[2 * (t // 3) + c, :, at:at + 128].astype(F32) * scale
            if t < 9:
                g2[t, rows, :] = block
            else:
                gu[rows, :] = block


def result_call(out_in, final_a, final_b, scale):
    return pl.pallas_call(
        functools.partial(result_kernel, scale=scale),
        out_shape=(
            jax.ShapeDtypeStruct((32, 4096), BF),
            jax.ShapeDtypeStruct((9, 32, 128), F32),
            jax.ShapeDtypeStruct((4, 32, 128), F32),
            jax.ShapeDtypeStruct((9, 32, 128), F32),
            jax.ShapeDtypeStruct((32, 128), F32),
        ),
        in_specs=[VM] * 3,
        out_specs=[VM] * 5,
        compiler_params=pltpu.CompilerParams(vmem_limit_bytes=16 * 1024 * 1024),
    )(out_in, final_a, final_b)


def per_device(features, conv1_weight, down_weight, conv2_weight, up_weight, out_grad, adjacency):
    pick, put = fine_rim_out()
    fine_sel, fine_place = fine_rim_maps()
    maps = [
        jnp.asarray(m, BF)
        for m in (pick, put, fine_perm(), corner_maps(), fine_sel, fine_place, coarse_rim_out(), coarse_rim_in())
    ]
    out, final_a, final_b = level_call(
        adjacency.transpose(1, 2, 0).reshape(16, 64), features, out_grad,
        conv1_weight.reshape(9, 2, 16, 128), down_weight.reshape(4, 2, 16, 128), conv2_weight.reshape(9, 2, 16, 128),
        up_weight, *maps
    )
    return result_call(out, final_a, final_b, 262144 ** -0.5)


def solution(mesh):
    weights = P(None, "chan", None)
    return jax.shard_map(
        per_device,
        mesh=mesh,
        in_specs=(P("chan", "tile"), weights, weights, weights, P("chan", None), P("chan", "tile"), P()),
        out_specs=(P("chan", "tile"), weights, weights, weights, P("chan", None)),
        check_vma=False,
    )
```

```python
import functools
import math

import jax
import jax.numpy as jnp
import numpy as np
from jax import lax
from jax.experimental import pallas as pl
from jax.experimental.pallas import tpu as pltpu
from jax.sharding import PartitionSpec as P

BF = jnp.bfloat16
F32 = jnp.float32
MESH = pl.DeviceIdType.MESH
TURNS = (0, 1, 2, 3, 0, 2, 2, 0)
VM = pl.BlockSpec(memory_space=pltpu.VMEM)
ANY = pl.BlockSpec(memory_space=pl.ANY)
LIMIT = 56 * 1024 * 1024


def fine_perm():
    out = np.zeros((3, 128, 128), np.float32)
    for b in range(3):
        for rr in range(2):
            for par in range(2):
                for k in range(32):
                    col = 2 * (k - 1 + b) + par
                    if 0 <= col < 64:
                        out[b, rr * 64 + par * 32 + k, rr * 64 + col] = 1
    return out


def corner_maps():
    out = np.zeros((4, 128, 128), np.float32)
    for i in range(2):
        for j in range(2):
            out[0, i * 64 + j, 2 * i + j] = 1
            out[1, (1 - i) * 64 + 63 - j, 4 + 2 * i + j] = 1
            out[2, (1 - i) * 64 + 1 - j, 8 + 2 * i + j] = 1
            out[3, i * 64 + 62 + j, 12 + 2 * i + j] = 1
    return out


def fine_rim_maps():
    sel = np.zeros((4, 128, 640), np.float32)
    for q in range(4):
        for r in range(20):
            ir = 16 * q - 2 + r
            for par in range(2):
                if 0 <= ir < 64:
                    west = 384 + par * 64 + 63 - ir
                    east = 128 + (1 - par) * 64 + ir
                elif ir < 0:
                    west = 512 + 12 + 2 * (ir + 2) + par
                    east = 512 + 0 + 2 * (ir + 2) + par
                else:
                    west = 512 + 8 + 2 * (ir - 64) + par
                    east = 512 + 4 + 2 * (ir - 64) + par
                sel[q, r * 2 + par, west] = 1
                sel[q, 64 + r * 2 + par, east] = 1
    place = np.zeros((2, 1280, 128), np.float32)
    for r in range(20):
        for par in range(2):
            place[0, r * 64 + par * 32, r * 2 + par] = 1
            place[1, r * 64 + par * 32 + 31, 64 + r * 2 + par] = 1
    return sel, place


def fine_rim_out():
    pick = np.zeros((1024, 128), np.float32)
    for r in range(16):
        for kind, col in enumerate((0, 1, 62, 63)):
            pick[r * 64 + col, kind * 16 + r] = 1
    put = np.zeros((4, 128, 256), np.float32)
    for s in range(4):
        for r16 in range(16):
            r = 16 * s + r16
            for kind, lane in enumerate((64 + r, r, 128 + 63 - r, 192 + 63 - r)):
                put[s, kind * 16 + r16, lane] = 1
    return pick, put


def coarse_rim_out():
    out = np.zeros((4, 256, 128), np.float32)
    for i in range(32):
        for s, (r, k) in enumerate(((31, i), (i, 0), (0, 31 - i), (31 - i, 31))):
            out[r // 8, (r % 8) * 32 + k, s * 32 + i] = 1
    return out


def strip_rims():
    out = np.zeros((4, 48, 256), np.float32)
    for q in range(4):
        for r in range(8):
            out[q, r, r * 32] = 1
            out[q, 8 + r, r * 32 + 31] = 1
    for k in range(32):
        out[0, 16 + k, k] = 1
        out[3, 16 + k, 7 * 32 + k] = 1
    return out


def coarse_rim_in():
    out = np.zeros((4, 960, 256), np.float32)
    for k in range(32):
        out[0, k, k] = 1
        out[3, 9 * 32 + k, 64 + 31 - k] = 1
    for q in range(4):
        for r in range(10):
            row = 8 * q - 1 + r
            if row < 0:
                west, east = 255, 128
            elif row >= 32:
                west, east = 192, 191
            else:
                west, east = 96 + 31 - row, 32 + row
            out[q, 320 + r * 32, west] = 1
            out[q, 640 + r * 32 + 31, east] = 1
    return out


def nt(a, b):
    return lax.dot_general(a, b, (((1,), (1,)), ((), ())), preferred_element_type=F32)


def tn(a, b):
    return lax.dot_general(a, b, (((0,), (0,)), ((), ())), preferred_element_type=F32)


def nn(a, b):
    return lax.dot_general(a, b, (((1,), (0,)), ((), ())), preferred_element_type=F32)


ROOT = 0.7978845608028654


def gelu(v):
    return 0.5 * v * (1.0 + jnp.tanh(ROOT * (v + 0.044715 * (v * v * v))))


def gelu_slope(v):
    t = jnp.tanh(ROOT * (v + 0.044715 * (v * v * v)))
    return 0.5 * (1.0 + t) + 0.5 * v * (1.0 - t * t) * (ROOT * (1.0 + 3 * 0.044715 * (v * v)))


AW, BW = 2048, 1536
XD = (2, 1, 3)
ZD = (4, 3, 5, 2, 6, 1, 7)
GD = (4, 3, 5, 2, 6, 1, 7)
FAR = (2, 1, 3, 0)
GXD = sorted(
    ((dg, dx) for dg in range(8) for dx in range(4) if dg or dx),
    key=lambda d: -(min(d[0], 8 - d[0]) / 2 + min(d[1], 4 - d[1])),
)
XYD = [(dx, dy) for dx in FAR for dy in FAR if dx or dy]
EDGE = (0, 31, 0, 31)


def side_by_side(weights, count):
    return jnp.concatenate([weights[t] for t in range(count)], axis=1)


def quarters(act):
    parts = act.reshape(8, 2, 2, 32, 128)
    return jnp.concatenate(
        [parts[:, a, b].reshape(256, 128) for a in range(2) for b in range(2)], axis=1
    )


def flip_map():
    rows = lax.broadcasted_iota(jnp.int32, (128, 128), 0)
    cols = lax.broadcasted_iota(jnp.int32, (128, 128), 1)
    return jnp.where(rows + cols == 127, 1.0, 0.0).astype(BF)


def level_kernel(*refs):
    names = INPUTS + ("out", "final_a", "final_b") + tuple(n for n, _ in SCRATCH)
    r = dict(zip(names, refs))
    tile, x = lax.axis_index("tile"), lax.axis_index("chan")
    z, g = tile // 8, lax.rem(tile, 8)
    y, core = g // 2, lax.rem(g, 2)
    q = x
    xs = [x] + [lax.rem(x + d, 4) for d in range(1, 4)]
    ys = [y] + [lax.rem(y + d, 4) for d in range(1, 4)]
    zs = [z] + [lax.rem(z + d, 8) for d in range(1, 8)]
    gs = [g] + [lax.rem(g + d, 8) for d in range(1, 8)]
    x_at = [(tile, xs[d]) for d in range(4)]
    z_at = [(zs[d] * 8 + g, x) for d in range(8)]
    g_at = [(z * 8 + gs[d], x) for d in range(8)]
    x_peer, z_peer, g_peer = x_at.__getitem__, z_at.__getitem__, g_at.__getitem__

    def xy_peer(dx, dy):
        return (g_at[2 * dy][0], xs[dx])

    mine = pl.ds(pl.multiple_of(x * 32, 32), 32)
    def gx_peer(dg, dx):
        return (g_at[dg][0], xs[dx])

    rounds, sent = [], []

    def rows_of(n):
        return pl.ds(pl.multiple_of(n * 32, 32), 32)

    def local(sem, src, dst):
        pltpu.make_async_copy(src, dst, sem).start()

    def wait(whole, sem):
        pltpu.make_async_copy(whole, whole, sem).wait()

    def begin(whole):
        rounds.append(whole)
        return len(rounds) - 1

    def push(n, src, dst, peer):
        pltpu.make_async_remote_copy(
            src_ref=src, dst_ref=dst, send_sem=r["ss"], recv_sem=r["rs"].at[n],
            device_id=peer, device_id_type=MESH,
        ).start()
        sent.append(math.prod(src.shape) * src.dtype.itemsize)

    def spread(whole, dirs, peer, src, dst):
        n = begin(whole)
        for d in dirs:
            push(n, src(d), dst(d), peer(d))
        return n

    def settle(n):
        wait(rounds[n], r["rs"].at[n])

    early = (("feat", "fv"), ("pick", "v_pick"), ("put", "v_put"))
    for src, dst in early:
        local(r["lsem"].at[0], r[src], r[dst])
    local(r["lsem"].at[1], r["adj"], r["s_adj"])
    barrier = pltpu.get_barrier_semaphore()
    peers = [x_peer(d) for d in XD] + [z_peer(d) for d in ZD] + [g_peer(d) for d in GD]
    peers += [gx_peer(dg, dx) for dg, dx in GXD if dg and dx]
    for peer in peers:
        pl.semaphore_signal(barrier, inc=1, device_id=peer, device_id_type=MESH)

    adj = r["s_adj"]

    wait(r["early"], r["lsem"].at[0])
    fv, held = r["fv"], (r["held0"], r["held1"])
    stacked = jnp.concatenate([fv[:, s * 1024:(s + 1) * 1024] for s in range(4)], axis=0)
    cols = nn(stacked, r["v_pick"][...]).astype(BF)
    both = nn(cols[0:32], r["v_put"][0])
    for s in range(1, 4):
        both = both + nn(cols[32 * s:32 * s + 32], r["v_put"][s])
    flip = flip_map()
    rims = (
        fv[:, 3968:4096],
        both[:, 0:128].astype(BF),
        nn(fv[:, 0:128], flip).astype(BF),
        both[:, 128:256].astype(BF),
    )
    for s in range(4):
        held[0][z * 4 + s] = rims[s][0:16]
        held[1][g * 4 + s] = rims[s][16:32]
    pl.semaphore_wait(barrier, len(peers))
    ways = ((z, ZD, z_peer), (g, GD, g_peer))
    first = []
    for h in range(2):
        at, dirs, peer = ways[h]
        part = held[h].at[pl.ds(at * 4, 4)]
        first.append(spread(held[h].at[pl.ds(0, 28)], dirs, peer, lambda d: part, lambda d: part))

    for name in ("cmap", "perm", "fsel", "place"):
        local(r["lsem"].at[2], r[name], r["v_" + name])
    for name in ("rout", "rin", "src"):
        local(r["lsem"].at[2], r[name].at[q], r["v_" + name])

    def piece(n, j):
        if n == 0:
            start = pl.multiple_of(jnp.clip(j * 1024 - 128, 0, 2816), 128)
            return r["feat"].at[:, pl.ds(start, 1280)], r["strip"].at[mine, :]
        if n == 3:
            return r["ograd"].at[:, pl.ds(pl.multiple_of(j * 1024, 1024), 1024)], r["og"].at[mine, :]
        if n == 5:
            return r["up"], r["v_up"].at[mine, :]
        name = {1: "w1", 2: "wd", 4: "w2"}[n]
        return r[name].at[:, core], r["v_" + name].at[:, x, core]

    bulk = {}

    def send_bulk(n):
        into = r[("strip", "v_w1", "v_wd", "og", "v_w2", "v_up")[n]]
        m = begin(into.at[:, :, 0] if n in (1, 2, 4) else into)
        for d in XD:
            src, dst = piece(n, xs[d])
            push(m, src, dst, x_peer(d))
        src, dst = piece(n, x)
        local(r["rs"].at[m], src, dst)
        bulk[n] = m

    def share_bulk(n):
        settle(bulk[n])
        into = r[{1: "v_w1", 2: "v_wd", 4: "v_w2"}[n]]
        bulk[n] = begin(into.at[:, :, 0])
        push(bulk[n], into.at[:, :, core], into.at[:, :, core], (tile + 1 - 2 * core, x))

    def take_bulk(n):
        settle(bulk[n])

    for n in range(6):
        send_bulk(n)

    wait(r["s_adj"], r["lsem"].at[1])

    table = r["table"]
    for n in range(8):
        for k in range(8):
            at = n * 8 + k
            for h in range(2):
                t = z * 8 + n if h == 0 else n * 8 + g
                p = adj[2 * k, t]
                s = lax.rem(adj[2 * k + 1, t] + TURNS[k], 4)
                owned = jnp.logical_and(p >= 0, (p // 8 == z) if h else (lax.rem(p, 8) == g))
                m = lax.rem(p, 8) if h else p // 8
                table[h, at] = jnp.where(owned, m * 4 + s, -1)
                if h == 0:
                    table[3, at] = jnp.where(owned, m, -1)
                    table[4, at] = s
                    table[5, at] = n * 8 + (k // 4) * 4 + lax.rem(s + 4 - k % 4, 4)

    wait(r["late"], r["lsem"].at[2])
    slots, landed = r["slots"], r["landed"]
    second = []
    for h in (1, 0):
        settle(first[h])
        _, dirs, peer = ways[1 - h]
        order = dirs + (0,)
        m = begin(landed.at[h, pl.ds(1, 7)])
        second.append(m)
        corners = [[] for _ in range(4)]
        for d in order:
            t = (gs[d] if h == 0 else zs[d]) * 8
            for k in range(8):
                n = table[h, t + k]
                block = held[h][jnp.maximum(n, 0)]
                block = jnp.where(n >= 0, block, jnp.zeros_like(block))
                if k < 4:
                    slots[h, d, :, k * 128:(k + 1) * 128] = block
                else:
                    corners[k - 4].append(block)
        corner = nn(jnp.concatenate(corners[0], axis=0), r["v_cmap"][0])
        for k in range(1, 4):
            corner = corner + nn(jnp.concatenate(corners[k], axis=0), r["v_cmap"][k])
        for n, d in enumerate(order):
            slots[h, d, :, 512:640] = corner[16 * n:16 * n + 16].astype(BF)
            if d:
                push(m, slots.at[h, d], landed.at[h, d], peer(d))
    take_bulk(0)
    perm, cb, strip = r["v_perm"], r["cb"], r["strip"]
    perms = perm[...].reshape(384, 128)
    shift = jnp.where(q == 0, -1, jnp.where(q == 3, 1, 0))

    def strip_block(n):
        at = jnp.clip(n + shift, 0, 9)
        return strip[:, pl.ds(pl.multiple_of(at * 128, 128), 128)]

    for n in range(1, 9):
        turned = nt(perms, strip_block(n))
        for b in range(3):
            cb[b, n * 128:(n + 1) * 128, :] = turned[b * 128:(b + 1) * 128].astype(BF)

    share_bulk(1)
    share_bulk(2)

    spot = lax.broadcasted_iota(jnp.int32, (64, 128), 0)
    lane = lax.broadcasted_iota(jnp.int32, (64, 128), 1)
    in_west, in_side = spot < 16, spot < 32
    step = jnp.where(in_west, spot, spot - 16)
    for dg, dx in GXD + [(0, 0)]:
        at, xd = gs[dg] * 8, xs[dx]
        row = step + (8 * xd - 1)
        above, below = jnp.logical_and(in_side, row < 0), jnp.logical_and(in_side, row > 31)

        def by_spot(kind):
            v = [table[kind, at + k] for k in range(8)]
            end = jnp.where(xd == 0, v[0], v[2])
            side = jnp.where(in_west, v[3], jnp.where(in_side, v[1], end))
            side = jnp.where(above, jnp.where(in_west, v[7], v[4]), side)
            return jnp.where(below, jnp.where(in_west, v[6], v[5]), side)

        of, turn = by_spot(3), by_spot(4)
        cell = jnp.where(in_west, 31 - row, jnp.where(in_side, row, jnp.where(xd == 0, spot - 32, 63 - spot)))
        cell = jnp.where(above, jnp.where(in_west, 31, 0), cell)
        cell = jnp.where(below, jnp.where(in_west, 0, 31), cell)
        cell = jnp.where(turn <= 1, cell, 31 - cell)
        odd = jnp.logical_or(turn == 1, turn == 3)
        here = jnp.where(odd, jnp.logical_and(cell >= 8 * q, cell < 8 * q + 8).astype(jnp.int32),
                         jnp.where(turn == 0, jnp.where(q == 3, 1, 0), jnp.where(q == 0, 1, 0)))
        source = jnp.where(odd, cell - 8 * q + jnp.where(turn == 3, 8, 0), cell + 16)
        source = jnp.where(jnp.logical_and(of >= 0, here == 1), of * 48 + source, -1)
        for c in range(3):
            r["picks"][dg * 4 + dx, :, c * 128:(c + 1) * 128] = jnp.where(source == lane + 128 * c, 1.0, 0.0).astype(BF)

    halves_of = []
    for m, h in zip(second, (1, 0)):
        settle(m)
        total = slots[h, 0].astype(F32)
        for d in range(1, 8):
            total = total + landed[h, d].astype(F32)
        halves_of.append(total)
    total = jnp.concatenate([halves_of[1], halves_of[0]], axis=0).astype(BF)

    picked, pout = r["picked"], r["pout"]
    ends = (total[:, 0:128], None, None, nn(total[:, 256:384], flip).astype(BF))
    for j in range(4):
        pout[j, :, 0:128] = nt(total, r["v_fsel"][j]).astype(BF)
        pout[j, :, 128:256] = jnp.zeros((32, 128), BF) if ends[j] is None else ends[j]
    c_x = spread(
        picked.at[pl.ds(0, 96), :], XD, x_peer, lambda d: pout.at[xs[d]], lambda d: picked.at[mine, :]
    )
    picked[mine, :] = pout[x]
    take_bulk(1)
    take_bulk(2)
    w1 = r["v_w1"][...].reshape(9, 128, 128)
    w1c = side_by_side(w1, 9)
    for n in (0, 9):
        block = strip_block(n)
        turned = nt(perms, jnp.where(q == n // 3, jnp.zeros_like(block), block))
        for b in range(3):
            cb[b, n * 128:(n + 1) * 128, :] = turned[b * 128:(b + 1) * 128].astype(BF)
    z1, act1 = r["z1"], r["act1"]

    def fine_taps(n):
        return jnp.concatenate(
            [cb[b, a * 128 + n * 256:a * 128 + n * 256 + 256, :] for a in range(3) for b in range(3)], axis=1
        )

    for n in range(4):
        z1[n * 256:(n + 1) * 256, :] = nt(fine_taps(n), w1c)
    w1_west = jnp.concatenate([w1[3 * a] for a in range(3)], axis=1)
    w1_east = jnp.concatenate([w1[3 * a + 2] for a in range(3)], axis=1)
    w1_end = jnp.where(q == 0, side_by_side(w1, 3), side_by_side(w1[6:9], 3))
    unit = jnp.where(
        lax.broadcasted_iota(jnp.int32, (128, 128), 0) == lax.broadcasted_iota(jnp.int32, (128, 128), 1), 1.0, 0.0
    ).astype(BF)
    settle(c_x)

    sides = picked[:, 0:128]
    side_rows = nt(unit, sides)
    end_rows = nt(perms, picked[:, 128:256])
    west = jnp.concatenate([side_rows[4 * a:4 * a + 32] for a in range(3)], axis=1).astype(BF)
    east = jnp.concatenate([side_rows[64 + 4 * a:96 + 4 * a] for a in range(3)], axis=1).astype(BF)
    ends = jnp.concatenate([end_rows[128 * b:128 * b + 128] for b in range(3)], axis=1).astype(BF)
    west, east, ends = nt(west, w1_west), nt(east, w1_east), nt(ends, w1_end)
    for n in range(8):
        rows = slice(n * 128, (n + 1) * 128)
        add = []
        cell = lax.broadcasted_iota(jnp.int32, (32, 128), 0)
        for m in range(4 * n, 4 * n + 4):
            add.append(
                jnp.where(cell == 0, west[m:m + 1], 0.0) + jnp.where(cell == 31, east[m:m + 1], 0.0)
            )
        pre = z1[rows, :] + jnp.concatenate(add, axis=0)
        if n in (0, 7):
            pre = pre + jnp.where(q == (0 if n == 0 else 3), ends, 0.0)
        z1[rows, :] = pre
        act1[rows, :] = gelu(pre).astype(BF)
    pre = nt(quarters(act1[...]), side_by_side(r["v_wd"][...].reshape(4, 128, 128), 4))
    r["z2"][...] = pre
    act2 = gelu(pre).astype(BF)
    r["act2"][...] = act2
    held2 = r["held2"]
    held2[z] = nn(r["v_src"][...], act2).astype(BF)

    c_z = spread(held2.at[pl.ds(0, 7)], ZD, z_peer, lambda d: held2.at[z], lambda d: held2.at[z])
    halo = r["halo"]
    c_h = begin(halo)
    push(c_h, r["act2"].at[pl.ds(224, 32), :], halo.at[0], x_peer(1))
    push(c_h, r["act2"].at[pl.ds(0, 32), :], halo.at[1], x_peer(3))

    take_bulk(3)
    take_bulk(5)
    share_bulk(4)
    og, ogt, up = r["og"], r["ogt"], r["v_up"]
    flat = perm[1]
    for n in range(8):
        ogt[n * 128:(n + 1) * 128, :] = nt(flat, og[:, n * 128:(n + 1) * 128]).astype(BF)
    cells = ogt[...].astype(F32).reshape(8, 4, 32, 128)
    pooled = (cells[:, 0] + cells[:, 1] + cells[:, 2] + cells[:, 3]).reshape(256, 128).astype(BF)
    back_up = nn(pooled, up[...])
    for n in (0, 9):
        for b in range(3):
            rows = slice(n * 128, (n + 1) * 128)
            new = jnp.where(q == n // 3, end_rows[b * 128:(b + 1) * 128], cb[b, rows, :].astype(F32))
            cb[b, rows, :] = new.astype(BF)
    for b in (0, 2):
        cb[b] = (cb[b].astype(F32) + nt(r["v_place"][b // 2], sides)).astype(BF)
    slope = gelu_slope(z1[...])
    r["slope"][...] = slope
    r["direct"][...] = slope * ogt[...].astype(F32)

    settle(c_z)
    lane = lax.broadcasted_iota(jnp.int32, (32, 128), 1)
    slots2, landed2, picks = r["slots2"], r["landed2"], r["picks"]
    every = jnp.concatenate([held2[n] for n in range(8)], axis=0)
    c_g = begin(landed2)

    def at_end(n):
        return jnp.logical_or(n == 0, n == 3)

    for dg, dx in GXD + [(0, 0)]:
        d = dg * 4 + dx
        slots2[d] = nn(picks[d], every).astype(BF)
        if d:
            for size, ok in ((64, at_end(xs[dx])), (32, jnp.logical_not(at_end(xs[dx])))):

                @pl.when(ok)
                def _():
                    some = pl.ds(0, size)
                    pltpu.make_async_remote_copy(
                        src_ref=slots2.at[d, some], dst_ref=landed2.at[d, some],
                        send_sem=r["ss2"], recv_sem=r["rs"].at[c_g],
                        device_id=gx_peer(dg, dx), device_id_type=MESH,
                    ).start()

    @pl.when(at_end(x))
    def _():
        wait(landed2.at[pl.ds(1, 31)], r["rs"].at[c_g])

    @pl.when(jnp.logical_not(at_end(x)))
    def _():
        wait(landed2.at[pl.ds(1, 31), pl.ds(0, 32)], r["rs"].at[c_g])

    total = slots2[0, 0:32, :].astype(F32)
    for d in range(1, 32):
        total = total + landed2[d, 0:32, :].astype(F32)
    beyond = r["beyond"]
    beyond[...] = jnp.zeros((32, 128), F32)

    @pl.when(at_end(x))
    def _():
        row = slots2[0, 32:64, :].astype(F32)
        for d in range(1, 32):
            row = row + landed2[d, 32:64, :].astype(F32)
        beyond[...] = row

    take_bulk(4)
    settle(c_h)

    sel = r["v_rin"][...]
    upper = jnp.where(q == 0, beyond[...], halo[0].astype(F32))
    lower = jnp.where(q == 3, beyond[...], halo[1].astype(F32))
    rows = jnp.concatenate([upper, act2.astype(F32), lower], axis=0)
    col = lax.rem(lax.broadcasted_iota(jnp.int32, (320, 128), 0), 32)

    def along(first):
        return jnp.concatenate([jnp.broadcast_to(total[n:n + 1], (32, 128)) for n in range(first, first + 10)], axis=0)

    west = jnp.where(col == 0, along(0), pltpu.roll(rows, 1, 0))
    east = jnp.where(col == 31, along(16), pltpu.roll(rows, 319, 0))
    blocks = [v.astype(BF) for v in (west, rows, east)]
    taps2 = jnp.concatenate([blocks[b][a * 32:a * 32 + 256] for a in range(3) for b in range(3)], axis=1)
    w2 = r["v_w2"][...].reshape(9, 128, 128)
    pre = nt(taps2, side_by_side(w2, 9))
    gz3 = (gelu_slope(pre) * back_up).astype(BF)
    none32, none64 = jnp.zeros((32, 128), F32), jnp.zeros((64, 128), F32)
    back = []
    for b in range(3):
        v0, v1, v2 = (nn(gz3, w2[3 * a + b]) for a in range(3))
        back.append(
            jnp.concatenate([v0, none64], axis=0)
            + jnp.concatenate([none32, v1, none32], axis=0)
            + jnp.concatenate([none64, v2], axis=0)
        )
    mid = (
        back[1]
        + jnp.where(col == 31, 0.0, pltpu.roll(back[0], 319, 0))
        + jnp.where(col == 0, 0.0, pltpu.roll(back[2], 1, 0))
    )
    cat = jnp.concatenate([mid.astype(BF), back[0].astype(BF), back[2].astype(BF)], axis=0)
    dq = r["dq"]
    dq[...] = tn(cat, sel).astype(BF)
    x4in, hout, hin = r["x4in"], r["hout"], r["hin"]
    c_x = spread(
        x4in.at[pl.ds(1, 3)], XD, x_peer, lambda d: dq.at[rows_of(xs[d]), :], lambda d: x4in.at[d]
    )
    hout[0] = mid[288:320]
    hout[1] = mid[0:32]
    c_h = begin(hin)
    push(c_h, hout.at[0], hin.at[0], x_peer(1))
    push(c_h, hout.at[1], hin.at[1], x_peer(3))

    other = 1 - core

    def halves(name, wide, parts):
        outs, ins = r[name + "c"], r[name + "ci"]
        for n in range(4):
            rows_n = pl.ds(pl.multiple_of(n * 32 + other * 16, 16), 16)
            at = 0
            for ref in parts:
                width = ref.shape[1]
                outs[n, :, at:at + width] = ref[rows_n, :].astype(BF)
                at += width
            outs[n, :, at:wide] = jnp.zeros((16, wide - at), BF)
        n = begin(ins)
        push(n, outs, ins, (tile + 1 - 2 * core, x))
        return n

    def shares(name, wide, parts):
        outs, ins = r[name + "o"], r[name + "i"]
        share = wide // 4
        for n in range(4):
            rows_n = pl.ds(pl.multiple_of(n * 32 + core * 16, 16), 16)
            own_n = jnp.concatenate(
                [ref[rows_n, :] for ref in parts]
                + [jnp.zeros((16, wide - sum(ref.shape[1] for ref in parts)), F32)],
                axis=1,
            )
            summed = (own_n + r[name + "ci"][n].astype(F32)).astype(BF)
            for m in range(4):
                outs[n, m] = summed[:, m * share:(m + 1) * share]
        m = begin(ins.at[pl.ds(1, 15)])
        for dx, dy in XYD:
            push(m, outs.at[xs[dx], ys[dy]], ins.at[dx * 4 + dy], xy_peer(dx, dy))
        return m

    def along_z(name):
        total = r[name + "o"][x, y].astype(F32)
        for n in range(1, 16):
            total = total + r[name + "i"][n].astype(F32)
        zall = r[name + "z"]
        zall[z] = total.astype(BF)
        return spread(zall.at[pl.ds(0, 7)], ZD, z_peer, lambda d: zall.at[z], lambda d: zall.at[z])

    def whole(name):
        zall = r[name + "z"]
        total = zall[0].astype(F32)
        for n in range(1, 8):
            total = total + zall[n].astype(F32)
        return total.astype(BF)

    coarse = gelu(pre).astype(BF)
    lifted = nt(coarse, up[...])
    out, ostrip = r["out"], r["ostrip"]
    for n in range(8):
        row = lifted[n * 32:(n + 1) * 32]
        summed = act1[n * 128:(n + 1) * 128, :].astype(F32) + jnp.concatenate([row] * 4, axis=0)
        ostrip[:, n * 128:(n + 1) * 128] = tn(summed.astype(BF), flat).astype(BF)

    settle(c_x)
    total = dq[mine, :].astype(F32)
    for d in XD:
        total = total + x4in[d].astype(F32)
    held3 = r["held3"]
    held3[g] = total.astype(BF)
    c_g = spread(held3.at[pl.ds(0, 7)], GD, g_peer, lambda d: held3.at[g], lambda d: held3.at[g])
    lanes = pl.ds(pl.multiple_of(x * 1024, 1024), 1024)
    c_o = spread(
        out, XD, x_peer,
        lambda d: ostrip.at[rows_of(xs[d]), :], lambda d: out.at[:, lanes],
    )
    local(r["rs"].at[c_o], ostrip.at[mine, :], out.at[:, lanes])

    r["gb_u"][...] = tn(pooled, coarse)
    r["gb_w"][...] = tn(gz3, taps2)
    parts_b = (r["gb_w"], r["gb_u"])
    c_bc = halves("b", BW, parts_b)
    settle(c_g)
    rolled3 = r["rolled3"]
    for j in range(8):
        for h in range(2):
            block = held3[j, :, 128 * h:128 * h + 128]
            rolled3[j * 8 + h * 4] = block
            for m in range(1, 4):
                rolled3[j * 8 + h * 4 + m] = pltpu.roll(block.astype(F32), 32 * m, 1).astype(BF)
    sums = [jnp.zeros((32, 128), F32) for _ in range(8)]
    for j in range(8):
        for k in range(8):
            at = j * 8 + k
            n, s = table[3, at], table[4, at]
            block = rolled3[table[5, at]].astype(F32)
            if k < 4:
                block = jnp.where(lane // 32 == s, block, 0.0)
            else:
                block = jnp.where(lane == 32 * s + EDGE[k - 4], block, 0.0)
            for m in range(8):
                sums[m] = sums[m] + jnp.where(n == m, block, 0.0)
    slots3, landed3 = r["slots3"], r["landed3"]
    for n in range(8):
        slots3[n] = sums[n].astype(BF)
    c_z = spread(
        landed3.at[pl.ds(1, 7)], ZD, z_peer, lambda d: slots3.at[zs[d]], lambda d: landed3.at[d]
    )
    settle(c_bc)
    c_b = shares("b", BW, parts_b)
    slope2 = gelu_slope(r["z2"][...])
    settle(c_z)
    total = slots3[z].astype(F32)
    for d in ZD:
        total = total + landed3[d].astype(F32)
    back_rim = r["back_rim"]
    back_rim[mine, :] = total.astype(BF)
    part3 = back_rim.at[mine, :]
    c_x = spread(back_rim.at[pl.ds(0, 96), :], XD, x_peer, lambda d: part3, lambda d: part3)
    settle(c_b)
    c_bz = along_z("b")
    settle(c_h)
    upper = jnp.where(q == 0, 0.0, hin[0])
    lower = jnp.where(q == 3, 0.0, hin[1])
    ga2 = mid[32:288] + jnp.concatenate([upper, jnp.zeros((192, 128), F32), lower], axis=0)
    settle(c_x)

    gz2 = (slope2 * (ga2 + nt(r["v_rout"][...], back_rim[...]))).astype(BF)
    wd = r["v_wd"][...].reshape(4, 128, 128)
    fine = [nn(gz2, wd[t]).reshape(8, 1, 32, 128) for t in range(4)]
    grown = jnp.concatenate(fine, axis=1).reshape(1024, 128)
    gz1 = (r["direct"][...] + r["slope"][...] * grown).astype(BF)
    r["ga_w"][...] = tn(
        gz1, jnp.concatenate([cb[b, a * 128:a * 128 + 1024, :] for a in range(3) for b in range(3)], axis=1)
    )
    r["ga_d"][...] = tn(gz2, quarters(act1[...]))
    parts_a = (r["ga_w"], r["ga_d"])
    c_ac = halves("a", AW, parts_a)

    def to_row(name, n):
        settle(n)
        final = r["final_" + name]
        final[g] = whole(name)
        return spread(final.at[pl.ds(0, 7)], GD, g_peer, lambda d: final.at[g], lambda d: final.at[g])

    settle(c_ac)
    c_a = shares("a", AW, parts_a)
    settle(c_a)
    c_az = along_z("a")
    c_bg = to_row("b", c_bz)
    settle(c_o)
    c_ag = to_row("a", c_az)
    settle(c_bg)
    settle(c_ag)
    assert sum(sent) == 256 * SENT, sum(sent) // 256
    wait(r["drain"], r["ss"])

    @pl.when(at_end(x))
    def _():
        wait(r["drain"].at[pl.ds(0, 15 * 64 + 16 * 32)], r["ss2"])

    @pl.when(jnp.logical_not(at_end(x)))
    def _():
        wait(r["drain"].at[pl.ds(0, 16 * 64 + 15 * 32)], r["ss2"])


INPUTS = (
    "adj", "feat", "ograd", "w1", "wd", "w2", "up",
    "pick", "put", "perm", "cmap", "fsel", "place", "rout", "rin", "src",
)


def buf(*shape, kind=BF):
    return pltpu.VMEM(shape, kind)


def sems(*shape):
    return pltpu.SemaphoreType.DMA(shape)


SENT = 13792
SCRATCH = [
    ("early", buf(3072, 128)), ("late", buf(8288, 128)), ("drain", buf(SENT, 128)),
    ("lsem", sems(3)), ("ss", pltpu.SemaphoreType.DMA), ("ss2", pltpu.SemaphoreType.DMA), ("rs", sems(33)), ("s_adj", pltpu.SMEM((16, 64), jnp.int32)),
    ("table", pltpu.SMEM((6, 64), jnp.int32)),
    ("fv", buf(32, 4096)), ("v_pick", buf(1024, 128)), ("v_put", buf(4, 128, 256)), ("v_perm", buf(3, 128, 128)),
    ("v_cmap", buf(4, 128, 128)), ("v_fsel", buf(4, 128, 640)), ("v_place", buf(2, 1280, 128)),
    ("v_rout", buf(256, 128)), ("v_rin", buf(960, 256)), ("v_src", buf(48, 256)),
    ("strip", buf(128, 1280)), ("og", buf(128, 1024)), ("v_w1", buf(9, 4, 2, 16, 128)), ("v_wd", buf(4, 4, 2, 16, 128)),
    ("v_w2", buf(9, 4, 2, 16, 128)), ("v_up", buf(128, 128)),
    ("held0", buf(32, 16, 128)), ("held1", buf(32, 16, 128)), ("slots", buf(2, 8, 16, 640)), ("landed", buf(2, 8, 16, 640)),
    ("pout", buf(4, 32, 256)), ("picked", buf(128, 256)),
    ("cb", buf(3, 1280, 128)), ("z1", buf(1024, 128, kind=F32)), ("act1", buf(1024, 128)),
    ("z2", buf(256, 128, kind=F32)), ("act2", buf(256, 128)),
    ("slope", buf(1024, 128, kind=F32)), ("direct", buf(1024, 128, kind=F32)),
    ("halo", buf(2, 32, 128)), ("held2", buf(8, 48, 128)), ("picks", buf(32, 64, 384)), ("beyond", buf(32, 128, kind=F32)), ("ogt", buf(1024, 128)),
    ("slots2", buf(32, 64, 128)), ("landed2", buf(32, 64, 128)),
    ("dq", buf(128, 256)), ("x4in", buf(4, 32, 256)),
    ("hout", buf(2, 32, 128, kind=F32)), ("hin", buf(2, 32, 128, kind=F32)),
    ("held3", buf(8, 32, 256)), ("rolled3", buf(64, 32, 128)), ("ostrip", buf(128, 1024)),
    ("slots3", buf(8, 32, 128)), ("landed3", buf(8, 32, 128)), ("back_rim", buf(128, 128)),
    ("gb_u", buf(128, 128, kind=F32)), ("gb_w", buf(128, 1152, kind=F32)),
    ("ga_d", buf(128, 512, kind=F32)), ("ga_w", buf(128, 1152, kind=F32)),
    ("bc", buf(4, 16, BW)), ("bci", buf(4, 16, BW)), ("bo", buf(4, 4, 16, BW // 4)), ("bi", buf(16, 16, BW // 4)),
    ("bz", buf(8, 16, BW // 4)),
    ("ac", buf(4, 16, AW)), ("aci", buf(4, 16, AW)), ("ao", buf(4, 4, 16, AW // 4)), ("ai", buf(16, 16, AW // 4)),
    ("az", buf(8, 16, AW // 4)),
]


def level_call(*args):
    return pl.pallas_call(
        level_kernel,
        out_shape=(pltpu.VMEM((32, 4096), BF), pltpu.VMEM((8, 16, AW // 4), BF), pltpu.VMEM((8, 16, BW // 4), BF)),
        in_specs=[ANY] * 16,
        out_specs=[VM] * 3,
        scratch_shapes=[s for _, s in SCRATCH],
        compiler_params=pltpu.CompilerParams(collective_id=0, has_side_effects=True, vmem_limit_bytes=LIMIT),
    )(*args)


def result_kernel(out_in, final_a, final_b, out, g1, gd, g2, gu, *, scale):
    out[...] = out_in[...]
    for c in range(2):
        rows = pl.ds(c * 16, 16)
        for t in range(13):
            block = final_a[2 * (t // 4) + c, :, (t % 4) * 128:(t % 4 + 1) * 128].astype(F32) * scale
            if t < 9:
                g1[t, rows, :] = block
            else:
                gd[t - 9, rows, :] = block
        for t in range(10):
            at = (t % 3) * 128
            block = final_b[2 * (t // 3) + c, :, at:at + 128].astype(F32) * scale
            if t < 9:
                g2[t, rows, :] = block
            else:
                gu[rows, :] = block


def result_call(out_in, final_a, final_b, scale):
    return pl.pallas_call(
        functools.partial(result_kernel, scale=scale),
        out_shape=(
            jax.ShapeDtypeStruct((32, 4096), BF),
            jax.ShapeDtypeStruct((9, 32, 128), F32),
            jax.ShapeDtypeStruct((4, 32, 128), F32),
            jax.ShapeDtypeStruct((9, 32, 128), F32),
            jax.ShapeDtypeStruct((32, 128), F32),
        ),
        in_specs=[VM] * 3,
        out_specs=[VM] * 5,
        compiler_params=pltpu.CompilerParams(vmem_limit_bytes=16 * 1024 * 1024),
    )(out_in, final_a, final_b)


def per_device(features, conv1_weight, down_weight, conv2_weight, up_weight, out_grad, adjacency):
    pick, put = fine_rim_out()
    fine_sel, fine_place = fine_rim_maps()
    maps = [
        jnp.asarray(m, BF)
        for m in (pick, put, fine_perm(), corner_maps(), fine_sel, fine_place, coarse_rim_out(), coarse_rim_in(), strip_rims())
    ]
    out, final_a, final_b = level_call(
        adjacency.transpose(1, 2, 0).reshape(16, 64), features, out_grad,
        conv1_weight.reshape(9, 2, 16, 128), down_weight.reshape(4, 2, 16, 128), conv2_weight.reshape(9, 2, 16, 128),
        up_weight, *maps
    )
    return result_call(out, final_a, final_b, 262144 ** -0.5)


def solution(mesh):
    weights = P(None, "chan", None)
    return jax.shard_map(
        per_device,
        mesh=mesh,
        in_specs=(P("chan", "tile"), weights, weights, weights, P("chan", None), P("chan", "tile"), P()),
        out_specs=(P("chan", "tile"), weights, weights, weights, P("chan", None)),
        check_vma=False,
    )
```

```python
import functools
import math

import jax
import jax.numpy as jnp
import numpy as np
from jax import lax
from jax.experimental import pallas as pl
from jax.experimental.pallas import tpu as pltpu
from jax.sharding import PartitionSpec as P

BF = jnp.bfloat16
F32 = jnp.float32
MESH = pl.DeviceIdType.MESH
TURNS = (0, 1, 2, 3, 0, 2, 2, 0)
VM = pl.BlockSpec(memory_space=pltpu.VMEM)
ANY = pl.BlockSpec(memory_space=pl.ANY)
LIMIT = 56 * 1024 * 1024


def fine_perm():
    out = np.zeros((3, 128, 128), np.float32)
    for b in range(3):
        for rr in range(2):
            for par in range(2):
                for k in range(32):
                    col = 2 * (k - 1 + b) + par
                    if 0 <= col < 64:
                        out[b, rr * 64 + par * 32 + k, rr * 64 + col] = 1
    return out


def corner_maps():
    out = np.zeros((4, 128, 128), np.float32)
    for i in range(2):
        for j in range(2):
            out[0, i * 64 + j, 2 * i + j] = 1
            out[1, (1 - i) * 64 + 63 - j, 4 + 2 * i + j] = 1
            out[2, (1 - i) * 64 + 1 - j, 8 + 2 * i + j] = 1
            out[3, i * 64 + 62 + j, 12 + 2 * i + j] = 1
    return out


def fine_rim_maps():
    sel = np.zeros((4, 128, 640), np.float32)
    for q in range(4):
        for r in range(20):
            ir = 16 * q - 2 + r
            for par in range(2):
                if 0 <= ir < 64:
                    west = 384 + par * 64 + 63 - ir
                    east = 128 + (1 - par) * 64 + ir
                elif ir < 0:
                    west = 512 + 12 + 2 * (ir + 2) + par
                    east = 512 + 0 + 2 * (ir + 2) + par
                else:
                    west = 512 + 8 + 2 * (ir - 64) + par
                    east = 512 + 4 + 2 * (ir - 64) + par
                sel[q, r * 2 + par, west] = 1
                sel[q, 64 + r * 2 + par, east] = 1
    place = np.zeros((2, 1280, 128), np.float32)
    for r in range(20):
        for par in range(2):
            place[0, r * 64 + par * 32, r * 2 + par] = 1
            place[1, r * 64 + par * 32 + 31, 64 + r * 2 + par] = 1
    return sel, place


def fine_rim_out():
    pick = np.zeros((1024, 128), np.float32)
    for r in range(16):
        for kind, col in enumerate((0, 1, 62, 63)):
            pick[r * 64 + col, kind * 16 + r] = 1
    put = np.zeros((4, 128, 256), np.float32)
    for s in range(4):
        for r16 in range(16):
            r = 16 * s + r16
            for kind, lane in enumerate((64 + r, r, 128 + 63 - r, 192 + 63 - r)):
                put[s, kind * 16 + r16, lane] = 1
    return pick, put


def strip_rims():
    out = np.zeros((4, 48, 256), np.float32)
    for q in range(4):
        for r in range(8):
            out[q, r, r * 32] = 1
            out[q, 8 + r, r * 32 + 31] = 1
    for k in range(32):
        out[0, 16 + k, k] = 1
        out[3, 16 + k, 7 * 32 + k] = 1
    return out


def side_cells():
    out = np.zeros((4, 64, 1024), np.float32)
    for q in range(4):
        for r in range(10):
            out[q, r, 320 + r * 32] = 1
            out[q, 16 + r, 640 + r * 32 + 31] = 1
    for k in range(32):
        out[0, 32 + k, k] = 1
        out[3, 32 + k, 288 + k] = 1
    return out


def nt(a, b):
    return lax.dot_general(a, b, (((1,), (1,)), ((), ())), preferred_element_type=F32)


def tn(a, b):
    return lax.dot_general(a, b, (((0,), (0,)), ((), ())), preferred_element_type=F32)


def nn(a, b):
    return lax.dot_general(a, b, (((1,), (0,)), ((), ())), preferred_element_type=F32)


ROOT = 0.7978845608028654


def gelu(v):
    return 0.5 * v * (1.0 + jnp.tanh(ROOT * (v + 0.044715 * (v * v * v))))


def gelu_slope(v):
    t = jnp.tanh(ROOT * (v + 0.044715 * (v * v * v)))
    return 0.5 * (1.0 + t) + 0.5 * v * (1.0 - t * t) * (ROOT * (1.0 + 3 * 0.044715 * (v * v)))


AW, BW = 2048, 1536
XD = (2, 1, 3)
ZD = (4, 3, 5, 2, 6, 1, 7)
GD = (4, 3, 5, 2, 6, 1, 7)
FAR = (2, 1, 3, 0)
GXD = sorted(
    ((dg, dx) for dg in range(8) for dx in range(4) if dg or dx),
    key=lambda d: -(min(d[0], 8 - d[0]) / 2 + min(d[1], 4 - d[1])),
)
XYD = [(dx, dy) for dx in FAR for dy in FAR if dx or dy]


def side_by_side(weights, count):
    return jnp.concatenate([weights[t] for t in range(count)], axis=1)


def quarters(act):
    parts = act.reshape(8, 2, 2, 32, 128)
    return jnp.concatenate(
        [parts[:, a, b].reshape(256, 128) for a in range(2) for b in range(2)], axis=1
    )


def flip_map():
    rows = lax.broadcasted_iota(jnp.int32, (128, 128), 0)
    cols = lax.broadcasted_iota(jnp.int32, (128, 128), 1)
    return jnp.where(rows + cols == 127, 1.0, 0.0).astype(BF)


def level_kernel(*refs):
    names = INPUTS + ("out", "final_a", "final_b") + tuple(n for n, _ in SCRATCH)
    r = dict(zip(names, refs))
    tile, x = lax.axis_index("tile"), lax.axis_index("chan")
    z, g = tile // 8, lax.rem(tile, 8)
    y, core = g // 2, lax.rem(g, 2)
    q = x
    xs = [x] + [lax.rem(x + d, 4) for d in range(1, 4)]
    ys = [y] + [lax.rem(y + d, 4) for d in range(1, 4)]
    zs = [z] + [lax.rem(z + d, 8) for d in range(1, 8)]
    gs = [g] + [lax.rem(g + d, 8) for d in range(1, 8)]
    x_at = [(tile, xs[d]) for d in range(4)]
    z_at = [(zs[d] * 8 + g, x) for d in range(8)]
    g_at = [(z * 8 + gs[d], x) for d in range(8)]
    x_peer, z_peer, g_peer = x_at.__getitem__, z_at.__getitem__, g_at.__getitem__

    def xy_peer(dx, dy):
        return (g_at[2 * dy][0], xs[dx])

    mine = pl.ds(pl.multiple_of(x * 32, 32), 32)
    def gx_peer(dg, dx):
        return (g_at[dg][0], xs[dx])

    rounds, sent = [], []

    def rows_of(n):
        return pl.ds(pl.multiple_of(n * 32, 32), 32)

    def local(sem, src, dst):
        pltpu.make_async_copy(src, dst, sem).start()

    def wait(whole, sem):
        pltpu.make_async_copy(whole, whole, sem).wait()

    def begin(whole):
        rounds.append(whole)
        return len(rounds) - 1

    def push(n, src, dst, peer):
        pltpu.make_async_remote_copy(
            src_ref=src, dst_ref=dst, send_sem=r["ss"], recv_sem=r["rs"].at[n],
            device_id=peer, device_id_type=MESH,
        ).start()
        sent.append(math.prod(src.shape) * src.dtype.itemsize)

    def spread(whole, dirs, peer, src, dst):
        n = begin(whole)
        for d in dirs:
            push(n, src(d), dst(d), peer(d))
        return n

    def settle(n):
        wait(rounds[n], r["rs"].at[n])

    early = (("feat", "fv"), ("pick", "v_pick"), ("put", "v_put"))
    for src, dst in early:
        local(r["lsem"].at[0], r[src], r[dst])
    local(r["lsem"].at[1], r["adj"], r["s_adj"])
    r["landed3"][...] = jnp.zeros((32, 64, 128), BF)
    barrier = pltpu.get_barrier_semaphore()
    peers = [x_peer(d) for d in XD] + [z_peer(d) for d in ZD] + [g_peer(d) for d in GD]
    peers += [gx_peer(dg, dx) for dg, dx in GXD if dg and dx]
    for peer in peers:
        pl.semaphore_signal(barrier, inc=1, device_id=peer, device_id_type=MESH)

    adj = r["s_adj"]

    wait(r["early"], r["lsem"].at[0])
    fv, held = r["fv"], (r["held0"], r["held1"])
    stacked = jnp.concatenate([fv[:, s * 1024:(s + 1) * 1024] for s in range(4)], axis=0)
    cols = nn(stacked, r["v_pick"][...]).astype(BF)
    both = nn(cols[0:32], r["v_put"][0])
    for s in range(1, 4):
        both = both + nn(cols[32 * s:32 * s + 32], r["v_put"][s])
    flip = flip_map()
    rims = (
        fv[:, 3968:4096],
        both[:, 0:128].astype(BF),
        nn(fv[:, 0:128], flip).astype(BF),
        both[:, 128:256].astype(BF),
    )
    for s in range(4):
        held[0][z * 4 + s] = rims[s][0:16]
        held[1][g * 4 + s] = rims[s][16:32]
    pl.semaphore_wait(barrier, len(peers))
    ways = ((z, ZD, z_peer), (g, GD, g_peer))
    first = []
    for h in range(2):
        at, dirs, peer = ways[h]
        part = held[h].at[pl.ds(at * 4, 4)]
        first.append(spread(held[h].at[pl.ds(0, 28)], dirs, peer, lambda d: part, lambda d: part))

    for name in ("cmap", "perm", "fsel", "place"):
        local(r["lsem"].at[2], r[name], r["v_" + name])
    for name in ("rin", "src"):
        local(r["lsem"].at[2], r[name].at[q], r["v_" + name])

    def piece(n, j):
        if n == 0:
            start = pl.multiple_of(jnp.clip(j * 1024 - 128, 0, 2816), 128)
            return r["feat"].at[:, pl.ds(start, 1280)], r["strip"].at[mine, :]
        if n == 3:
            return r["ograd"].at[:, pl.ds(pl.multiple_of(j * 1024, 1024), 1024)], r["og"].at[mine, :]
        if n == 5:
            return r["up"], r["v_up"].at[mine, :]
        name = {1: "w1", 2: "wd", 4: "w2"}[n]
        return r[name].at[:, core], r["v_" + name].at[:, x, core]

    bulk = {}

    def send_bulk(n):
        into = r[("strip", "v_w1", "v_wd", "og", "v_w2", "v_up")[n]]
        m = begin(into.at[:, :, 0] if n in (1, 2, 4) else into)
        for d in XD:
            src, dst = piece(n, xs[d])
            push(m, src, dst, x_peer(d))
        src, dst = piece(n, x)
        local(r["rs"].at[m], src, dst)
        bulk[n] = m

    def share_bulk(n):
        settle(bulk[n])
        into = r[{1: "v_w1", 2: "v_wd", 4: "v_w2"}[n]]
        bulk[n] = begin(into.at[:, :, 0])
        push(bulk[n], into.at[:, :, core], into.at[:, :, core], (tile + 1 - 2 * core, x))

    def take_bulk(n):
        settle(bulk[n])

    for n in range(6):
        send_bulk(n)

    wait(r["s_adj"], r["lsem"].at[1])

    table = r["table"]
    for n in range(8):
        for k in range(8):
            at = n * 8 + k
            for h in range(2):
                t = z * 8 + n if h == 0 else n * 8 + g
                p = adj[2 * k, t]
                s = lax.rem(adj[2 * k + 1, t] + TURNS[k], 4)
                owned = jnp.logical_and(p >= 0, (p // 8 == z) if h else (lax.rem(p, 8) == g))
                m = lax.rem(p, 8) if h else p // 8
                table[h, at] = jnp.where(owned, m * 4 + s, -1)
                if h == 0:
                    table[3, at] = jnp.where(owned, m, -1)
                    table[4, at] = s

    wait(r["late"], r["lsem"].at[2])
    slots, landed = r["slots"], r["landed"]
    second = []
    for h in (1, 0):
        settle(first[h])
        _, dirs, peer = ways[1 - h]
        order = dirs + (0,)
        m = begin(landed.at[h, pl.ds(1, 7)])
        second.append(m)
        corners = [[] for _ in range(4)]
        for d in order:
            t = (gs[d] if h == 0 else zs[d]) * 8
            for k in range(8):
                n = table[h, t + k]
                block = held[h][jnp.maximum(n, 0)]
                block = jnp.where(n >= 0, block, jnp.zeros_like(block))
                if k < 4:
                    slots[h, d, :, k * 128:(k + 1) * 128] = block
                else:
                    corners[k - 4].append(block)
        corner = nn(jnp.concatenate(corners[0], axis=0), r["v_cmap"][0])
        for k in range(1, 4):
            corner = corner + nn(jnp.concatenate(corners[k], axis=0), r["v_cmap"][k])
        for n, d in enumerate(order):
            slots[h, d, :, 512:640] = corner[16 * n:16 * n + 16].astype(BF)
            if d:
                push(m, slots.at[h, d], landed.at[h, d], peer(d))
    take_bulk(0)
    perm, cb, strip = r["v_perm"], r["cb"], r["strip"]
    perms = perm[...].reshape(384, 128)
    shift = jnp.where(q == 0, -1, jnp.where(q == 3, 1, 0))

    def strip_block(n):
        at = jnp.clip(n + shift, 0, 9)
        return strip[:, pl.ds(pl.multiple_of(at * 128, 128), 128)]

    for n in range(1, 9):
        turned = nt(perms, strip_block(n))
        for b in range(3):
            cb[b, n * 128:(n + 1) * 128, :] = turned[b * 128:(b + 1) * 128].astype(BF)

    share_bulk(1)
    share_bulk(2)

    def sources(spot, at, xd):
        in_west, in_side = spot < 16, spot < 32
        row = jnp.where(in_west, spot, spot - 16) + (8 * xd - 1)
        above, below = jnp.logical_and(in_side, row < 0), jnp.logical_and(in_side, row > 31)

        def by_spot(kind):
            v = [table[kind, at + k] for k in range(8)]
            end = jnp.where(xd == 0, v[0], v[2])
            side = jnp.where(in_west, v[3], jnp.where(in_side, v[1], end))
            side = jnp.where(above, jnp.where(in_west, v[7], v[4]), side)
            return jnp.where(below, jnp.where(in_west, v[6], v[5]), side)

        of, turn = by_spot(3), by_spot(4)
        cell = jnp.where(in_west, 31 - row, jnp.where(in_side, row, jnp.where(xd == 0, spot - 32, 63 - spot)))
        cell = jnp.where(above, jnp.where(in_west, 31, 0), cell)
        cell = jnp.where(below, jnp.where(in_west, 0, 31), cell)
        cell = jnp.where(turn <= 1, cell, 31 - cell)
        odd = jnp.logical_or(turn == 1, turn == 3)
        here = jnp.where(odd, jnp.logical_and(cell >= 8 * q, cell < 8 * q + 8).astype(jnp.int32),
                         jnp.where(turn == 0, jnp.where(q == 3, 1, 0), jnp.where(q == 0, 1, 0)))
        source = jnp.where(odd, cell - 8 * q + jnp.where(turn == 3, 8, 0), cell + 16)
        return jnp.where(jnp.logical_and(of >= 0, here == 1), of * 48 + source, -1)

    spot = lax.broadcasted_iota(jnp.int32, (64, 128), 0)
    lane = lax.broadcasted_iota(jnp.int32, (64, 128), 1)
    for dg, dx in GXD + [(0, 0)]:
        source = sources(spot, gs[dg] * 8, xs[dx])
        for c in range(3):
            r["picks"][dg * 4 + dx, :, c * 128:(c + 1) * 128] = jnp.where(source == lane + 128 * c, 1.0, 0.0).astype(BF)

    halves_of = []
    for m, h in zip(second, (1, 0)):
        settle(m)
        total = slots[h, 0].astype(F32)
        for d in range(1, 8):
            total = total + landed[h, d].astype(F32)
        halves_of.append(total)
    total = jnp.concatenate([halves_of[1], halves_of[0]], axis=0).astype(BF)

    picked, pout = r["picked"], r["pout"]
    ends = (total[:, 0:128], None, None, nn(total[:, 256:384], flip).astype(BF))
    for j in range(4):
        pout[j, :, 0:128] = nt(total, r["v_fsel"][j]).astype(BF)
        pout[j, :, 128:256] = jnp.zeros((32, 128), BF) if ends[j] is None else ends[j]
    c_x = spread(
        picked.at[pl.ds(0, 96), :], XD, x_peer, lambda d: pout.at[xs[d]], lambda d: picked.at[mine, :]
    )
    picked[mine, :] = pout[x]
    take_bulk(1)
    take_bulk(2)
    w1 = r["v_w1"][...].reshape(9, 128, 128)
    w1c = side_by_side(w1, 9)
    for n in (0, 9):
        block = strip_block(n)
        turned = nt(perms, jnp.where(q == n // 3, jnp.zeros_like(block), block))
        for b in range(3):
            cb[b, n * 128:(n + 1) * 128, :] = turned[b * 128:(b + 1) * 128].astype(BF)
    z1, act1 = r["z1"], r["act1"]

    def fine_taps(n):
        return jnp.concatenate(
            [cb[b, a * 128 + n * 256:a * 128 + n * 256 + 256, :] for a in range(3) for b in range(3)], axis=1
        )

    for n in range(4):
        z1[n * 256:(n + 1) * 256, :] = nt(fine_taps(n), w1c)
    w1_west = jnp.concatenate([w1[3 * a] for a in range(3)], axis=1)
    w1_east = jnp.concatenate([w1[3 * a + 2] for a in range(3)], axis=1)
    w1_end = jnp.where(q == 0, side_by_side(w1, 3), side_by_side(w1[6:9], 3))
    unit = jnp.where(
        lax.broadcasted_iota(jnp.int32, (128, 128), 0) == lax.broadcasted_iota(jnp.int32, (128, 128), 1), 1.0, 0.0
    ).astype(BF)
    settle(c_x)

    sides = picked[:, 0:128]
    side_rows = nt(unit, sides)
    end_rows = nt(perms, picked[:, 128:256])
    west = jnp.concatenate([side_rows[4 * a:4 * a + 32] for a in range(3)], axis=1).astype(BF)
    east = jnp.concatenate([side_rows[64 + 4 * a:96 + 4 * a] for a in range(3)], axis=1).astype(BF)
    ends = jnp.concatenate([end_rows[128 * b:128 * b + 128] for b in range(3)], axis=1).astype(BF)
    west, east, ends = nt(west, w1_west), nt(east, w1_east), nt(ends, w1_end)
    for n in range(8):
        rows = slice(n * 128, (n + 1) * 128)
        add = []
        cell = lax.broadcasted_iota(jnp.int32, (32, 128), 0)
        for m in range(4 * n, 4 * n + 4):
            add.append(
                jnp.where(cell == 0, west[m:m + 1], 0.0) + jnp.where(cell == 31, east[m:m + 1], 0.0)
            )
        pre = z1[rows, :] + jnp.concatenate(add, axis=0)
        if n in (0, 7):
            pre = pre + jnp.where(q == (0 if n == 0 else 3), ends, 0.0)
        z1[rows, :] = pre
        act1[rows, :] = gelu(pre).astype(BF)
    pre = nt(quarters(act1[...]), side_by_side(r["v_wd"][...].reshape(4, 128, 128), 4))
    r["z2"][...] = pre
    act2 = gelu(pre).astype(BF)
    r["act2"][...] = act2
    held2 = r["held2"]
    held2[z] = nn(r["v_src"][...], act2).astype(BF)

    c_z = spread(held2.at[pl.ds(0, 7)], ZD, z_peer, lambda d: held2.at[z], lambda d: held2.at[z])
    halo = r["halo"]
    c_h = begin(halo)
    push(c_h, r["act2"].at[pl.ds(224, 32), :], halo.at[0], x_peer(1))
    push(c_h, r["act2"].at[pl.ds(0, 32), :], halo.at[1], x_peer(3))

    take_bulk(3)
    take_bulk(5)
    share_bulk(4)
    og, ogt, up = r["og"], r["ogt"], r["v_up"]
    flat = perm[1]
    for n in range(8):
        ogt[n * 128:(n + 1) * 128, :] = nt(flat, og[:, n * 128:(n + 1) * 128]).astype(BF)
    cells = ogt[...].astype(F32).reshape(8, 4, 32, 128)
    pooled = (cells[:, 0] + cells[:, 1] + cells[:, 2] + cells[:, 3]).reshape(256, 128).astype(BF)
    back_up = nn(pooled, up[...])
    for n in (0, 9):
        for b in range(3):
            rows = slice(n * 128, (n + 1) * 128)
            new = jnp.where(q == n // 3, end_rows[b * 128:(b + 1) * 128], cb[b, rows, :].astype(F32))
            cb[b, rows, :] = new.astype(BF)
    for b in (0, 2):
        cb[b] = (cb[b].astype(F32) + nt(r["v_place"][b // 2], sides)).astype(BF)
    slope = gelu_slope(z1[...])
    r["slope"][...] = slope
    r["direct"][...] = slope * ogt[...].astype(F32)

    lane = lax.broadcasted_iota(jnp.int32, (8, 128), 1)
    depth = lax.broadcasted_iota(jnp.int32, (384, 128), 0)
    for n in range(16):
        dg, dx = n // 2, 2 * (n % 2)
        left = lane < 64
        source = sources(jnp.where(left, lane, lane - 64), gs[dg] * 8, jnp.where(left, xs[dx], xs[dx + 1]))
        source = jnp.broadcast_to(source[0:1], (384, 128))
        r["adds"][:, n * 128:(n + 1) * 128] = jnp.where(source == depth, 1.0, 0.0).astype(BF)

    settle(c_z)
    slots2, landed2, picks = r["slots2"], r["landed2"], r["picks"]
    every = jnp.concatenate([held2[n] for n in range(8)], axis=0)
    c_g = begin(landed2)

    def at_end(n):
        return jnp.logical_or(n == 0, n == 3)

    for dg, dx in GXD + [(0, 0)]:
        d = dg * 4 + dx
        slots2[d] = nn(picks[d], every).astype(BF)
        if d:
            for size, ok in ((64, at_end(xs[dx])), (32, jnp.logical_not(at_end(xs[dx])))):

                @pl.when(ok)
                def _():
                    some = pl.ds(0, size)
                    pltpu.make_async_remote_copy(
                        src_ref=slots2.at[d, some], dst_ref=landed2.at[d, some],
                        send_sem=r["ss2"], recv_sem=r["rs"].at[c_g],
                        device_id=gx_peer(dg, dx), device_id_type=MESH,
                    ).start()

    @pl.when(at_end(x))
    def _():
        wait(landed2.at[pl.ds(1, 31)], r["rs"].at[c_g])

    @pl.when(jnp.logical_not(at_end(x)))
    def _():
        wait(landed2.at[pl.ds(1, 31), pl.ds(0, 32)], r["rs"].at[c_g])

    total = slots2[0, 0:32, :].astype(F32)
    for d in range(1, 32):
        total = total + landed2[d, 0:32, :].astype(F32)
    beyond = r["beyond"]
    beyond[...] = jnp.zeros((32, 128), F32)

    @pl.when(at_end(x))
    def _():
        row = slots2[0, 32:64, :].astype(F32)
        for d in range(1, 32):
            row = row + landed2[d, 32:64, :].astype(F32)
        beyond[...] = row

    take_bulk(4)
    settle(c_h)

    upper = jnp.where(q == 0, beyond[...], halo[0].astype(F32))
    lower = jnp.where(q == 3, beyond[...], halo[1].astype(F32))
    rows = jnp.concatenate([upper, act2.astype(F32), lower], axis=0)
    col = lax.rem(lax.broadcasted_iota(jnp.int32, (320, 128), 0), 32)

    def along(first):
        return jnp.concatenate([jnp.broadcast_to(total[n:n + 1], (32, 128)) for n in range(first, first + 10)], axis=0)

    west = jnp.where(col == 0, along(0), pltpu.roll(rows, 1, 0))
    east = jnp.where(col == 31, along(16), pltpu.roll(rows, 319, 0))
    blocks = [v.astype(BF) for v in (west, rows, east)]
    taps2 = jnp.concatenate([blocks[b][a * 32:a * 32 + 256] for a in range(3) for b in range(3)], axis=1)
    w2 = r["v_w2"][...].reshape(9, 128, 128)
    pre = nt(taps2, side_by_side(w2, 9))
    gz3 = (gelu_slope(pre) * back_up).astype(BF)
    none32, none64 = jnp.zeros((32, 128), F32), jnp.zeros((64, 128), F32)
    back = []
    for b in range(3):
        v0, v1, v2 = (nn(gz3, w2[3 * a + b]) for a in range(3))
        back.append(
            jnp.concatenate([v0, none64], axis=0)
            + jnp.concatenate([none32, v1, none32], axis=0)
            + jnp.concatenate([none64, v2], axis=0)
        )
    mid = (
        back[1]
        + jnp.where(col == 31, 0.0, pltpu.roll(back[0], 319, 0))
        + jnp.where(col == 0, 0.0, pltpu.roll(back[2], 1, 0))
    )
    cat = jnp.concatenate([mid, back[0], back[2], none64], axis=0).astype(BF)
    landed3 = r["landed3"]
    landed3[0] = nn(r["v_rin"][...], cat).astype(BF)
    hout, hin = r["hout"], r["hin"]
    c_g = begin(landed3)
    for size, ok in ((64, at_end(x)), (32, jnp.logical_not(at_end(x)))):

        @pl.when(ok)
        def _():
            some = pl.ds(0, size)
            for dg, dx in GXD:
                back_at = ((8 - dg) % 8) * 4 + (4 - dx) % 4
                pltpu.make_async_remote_copy(
                    src_ref=landed3.at[0, some], dst_ref=landed3.at[back_at, some],
                    send_sem=r["ss3"], recv_sem=r["rs"].at[c_g],
                    device_id=gx_peer(dg, dx), device_id_type=MESH,
                ).start()

    hout[0] = mid[288:320]
    hout[1] = mid[0:32]
    c_h = begin(hin)
    push(c_h, hout.at[0], hin.at[0], x_peer(1))
    push(c_h, hout.at[1], hin.at[1], x_peer(3))

    other = 1 - core

    def halves(name, wide, parts):
        outs, ins = r[name + "c"], r[name + "ci"]
        for n in range(4):
            rows_n = pl.ds(pl.multiple_of(n * 32 + other * 16, 16), 16)
            at = 0
            for ref in parts:
                width = ref.shape[1]
                outs[n, :, at:at + width] = ref[rows_n, :].astype(BF)
                at += width
            outs[n, :, at:wide] = jnp.zeros((16, wide - at), BF)
        n = begin(ins)
        push(n, outs, ins, (tile + 1 - 2 * core, x))
        return n

    def shares(name, wide, parts):
        outs, ins = r[name + "o"], r[name + "i"]
        share = wide // 4
        for n in range(4):
            rows_n = pl.ds(pl.multiple_of(n * 32 + core * 16, 16), 16)
            own_n = jnp.concatenate(
                [ref[rows_n, :] for ref in parts]
                + [jnp.zeros((16, wide - sum(ref.shape[1] for ref in parts)), F32)],
                axis=1,
            )
            summed = (own_n + r[name + "ci"][n].astype(F32)).astype(BF)
            for m in range(4):
                outs[n, m] = summed[:, m * share:(m + 1) * share]
        m = begin(ins.at[pl.ds(1, 15)])
        for dx, dy in XYD:
            push(m, outs.at[xs[dx], ys[dy]], ins.at[dx * 4 + dy], xy_peer(dx, dy))
        return m

    def along_z(name):
        total = r[name + "o"][x, y].astype(F32)
        for n in range(1, 16):
            total = total + r[name + "i"][n].astype(F32)
        zall = r[name + "z"]
        zall[z] = total.astype(BF)
        return spread(zall.at[pl.ds(0, 7)], ZD, z_peer, lambda d: zall.at[z], lambda d: zall.at[z])

    def whole(name):
        zall = r[name + "z"]
        total = zall[0].astype(F32)
        for n in range(1, 8):
            total = total + zall[n].astype(F32)
        return total.astype(BF)

    coarse = gelu(pre).astype(BF)
    lifted = nt(coarse, up[...])
    out, ostrip = r["out"], r["ostrip"]
    for n in range(8):
        row = lifted[n * 32:(n + 1) * 32]
        summed = act1[n * 128:(n + 1) * 128, :].astype(F32) + jnp.concatenate([row] * 4, axis=0)
        ostrip[:, n * 128:(n + 1) * 128] = tn(summed.astype(BF), flat).astype(BF)

    lanes = pl.ds(pl.multiple_of(x * 1024, 1024), 1024)
    c_o = spread(
        out, XD, x_peer,
        lambda d: ostrip.at[rows_of(xs[d]), :], lambda d: out.at[:, lanes],
    )
    local(r["rs"].at[c_o], ostrip.at[mine, :], out.at[:, lanes])

    r["gb_u"][...] = tn(pooled, coarse)
    r["gb_w"][...] = tn(gz3, taps2)
    parts_b = (r["gb_w"], r["gb_u"])
    c_bc = halves("b", BW, parts_b)
    some_rows, more_rows = pl.ds(0, 15 * 64 + 16 * 32), pl.ds(0, 16 * 64 + 15 * 32)

    @pl.when(at_end(x))
    def _():
        wait(r["drain"].at[some_rows], r["rs"].at[c_g])

    @pl.when(jnp.logical_not(at_end(x)))
    def _():
        wait(r["drain"].at[more_rows], r["rs"].at[c_g])

    total = nn(r["adds"][...], landed3[...].reshape(2048, 128))
    slots3, landed4 = r["slots3"], r["landed4"]
    for n in range(8):
        slots3[n] = total[n * 48:(n + 1) * 48].astype(BF)
    c_z = spread(
        landed4.at[pl.ds(1, 7)], ZD, z_peer, lambda d: slots3.at[zs[d]], lambda d: landed4.at[d]
    )
    settle(c_bc)
    c_b = shares("b", BW, parts_b)
    slope2 = gelu_slope(r["z2"][...])
    settle(c_h)
    upper = jnp.where(q == 0, 0.0, hin[0])
    lower = jnp.where(q == 3, 0.0, hin[1])
    ga2 = mid[32:288] + jnp.concatenate([upper, jnp.zeros((192, 128), F32), lower], axis=0)
    settle(c_z)
    total = slots3[z].astype(F32)
    for d in ZD:
        total = total + landed4[d].astype(F32)

    gz2 = (slope2 * (ga2 + tn(r["v_src"][...], total.astype(BF)))).astype(BF)
    wd = r["v_wd"][...].reshape(4, 128, 128)
    fine = [nn(gz2, wd[t]).reshape(8, 1, 32, 128) for t in range(4)]
    grown = jnp.concatenate(fine, axis=1).reshape(1024, 128)
    gz1 = (r["direct"][...] + r["slope"][...] * grown).astype(BF)
    r["ga_w"][...] = tn(
        gz1, jnp.concatenate([cb[b, a * 128:a * 128 + 1024, :] for a in range(3) for b in range(3)], axis=1)
    )
    r["ga_d"][...] = tn(gz2, quarters(act1[...]))
    parts_a = (r["ga_w"], r["ga_d"])
    c_ac = halves("a", AW, parts_a)
    settle(c_b)
    c_bz = along_z("b")

    def to_row(name, n):
        settle(n)
        final = r["final_" + name]
        final[g] = whole(name)
        return spread(final.at[pl.ds(0, 7)], GD, g_peer, lambda d: final.at[g], lambda d: final.at[g])

    settle(c_ac)
    c_a = shares("a", AW, parts_a)
    settle(c_a)
    c_az = along_z("a")
    c_bg = to_row("b", c_bz)
    settle(c_o)
    c_ag = to_row("a", c_az)
    settle(c_bg)
    settle(c_ag)
    assert sum(sent) == 256 * SENT, sum(sent) // 256
    wait(r["drain"], r["ss"])

    @pl.when(at_end(x))
    def _():
        wait(r["drain"].at[some_rows], r["ss2"])
        wait(r["drain"].at[pl.ds(0, 31 * 64)], r["ss3"])

    @pl.when(jnp.logical_not(at_end(x)))
    def _():
        wait(r["drain"].at[more_rows], r["ss2"])
        wait(r["drain"].at[pl.ds(0, 31 * 32)], r["ss3"])


INPUTS = (
    "adj", "feat", "ograd", "w1", "wd", "w2", "up",
    "pick", "put", "perm", "cmap", "fsel", "place", "rin", "src",
)


def buf(*shape, kind=BF):
    return pltpu.VMEM(shape, kind)


def sems(*shape):
    return pltpu.SemaphoreType.DMA(shape)


SENT = 13168
SCRATCH = [
    ("early", buf(3072, 128)), ("late", buf(6624, 128)), ("drain", buf(SENT, 128)),
    ("lsem", sems(3)), ("ss", pltpu.SemaphoreType.DMA), ("ss2", pltpu.SemaphoreType.DMA), ("ss3", pltpu.SemaphoreType.DMA), ("rs", sems(33)), ("s_adj", pltpu.SMEM((16, 64), jnp.int32)),
    ("table", pltpu.SMEM((6, 64), jnp.int32)),
    ("fv", buf(32, 4096)), ("v_pick", buf(1024, 128)), ("v_put", buf(4, 128, 256)), ("v_perm", buf(3, 128, 128)),
    ("v_cmap", buf(4, 128, 128)), ("v_fsel", buf(4, 128, 640)), ("v_place", buf(2, 1280, 128)),
    ("v_rin", buf(64, 1024)), ("v_src", buf(48, 256)),
    ("strip", buf(128, 1280)), ("og", buf(128, 1024)), ("v_w1", buf(9, 4, 2, 16, 128)), ("v_wd", buf(4, 4, 2, 16, 128)),
    ("v_w2", buf(9, 4, 2, 16, 128)), ("v_up", buf(128, 128)),
    ("held0", buf(32, 16, 128)), ("held1", buf(32, 16, 128)), ("slots", buf(2, 8, 16, 640)), ("landed", buf(2, 8, 16, 640)),
    ("pout", buf(4, 32, 256)), ("picked", buf(128, 256)),
    ("cb", buf(3, 1280, 128)), ("z1", buf(1024, 128, kind=F32)), ("act1", buf(1024, 128)),
    ("z2", buf(256, 128, kind=F32)), ("act2", buf(256, 128)),
    ("slope", buf(1024, 128, kind=F32)), ("direct", buf(1024, 128, kind=F32)),
    ("halo", buf(2, 32, 128)), ("held2", buf(8, 48, 128)), ("picks", buf(32, 64, 384)), ("beyond", buf(32, 128, kind=F32)), ("ogt", buf(1024, 128)),
    ("slots2", buf(32, 64, 128)), ("landed2", buf(32, 64, 128)),
    ("adds", buf(384, 2048)), ("landed3", buf(32, 64, 128)), ("slots3", buf(8, 48, 128)), ("landed4", buf(8, 48, 128)),
    ("hout", buf(2, 32, 128, kind=F32)), ("hin", buf(2, 32, 128, kind=F32)), ("ostrip", buf(128, 1024)),
    ("gb_u", buf(128, 128, kind=F32)), ("gb_w", buf(128, 1152, kind=F32)),
    ("ga_d", buf(128, 512, kind=F32)), ("ga_w", buf(128, 1152, kind=F32)),
    ("bc", buf(4, 16, BW)), ("bci", buf(4, 16, BW)), ("bo", buf(4, 4, 16, BW // 4)), ("bi", buf(16, 16, BW // 4)),
    ("bz", buf(8, 16, BW // 4)),
    ("ac", buf(4, 16, AW)), ("aci", buf(4, 16, AW)), ("ao", buf(4, 4, 16, AW // 4)), ("ai", buf(16, 16, AW // 4)),
    ("az", buf(8, 16, AW // 4)),
]


def level_call(*args):
    return pl.pallas_call(
        level_kernel,
        out_shape=(pltpu.VMEM((32, 4096), BF), pltpu.VMEM((8, 16, AW // 4), BF), pltpu.VMEM((8, 16, BW // 4), BF)),
        in_specs=[ANY] * 15,
        out_specs=[VM] * 3,
        scratch_shapes=[s for _, s in SCRATCH],
        compiler_params=pltpu.CompilerParams(collective_id=0, has_side_effects=True, vmem_limit_bytes=LIMIT),
    )(*args)


def result_kernel(out_in, final_a, final_b, out, g1, gd, g2, gu, *, scale):
    out[...] = out_in[...]
    for c in range(2):
        rows = pl.ds(c * 16, 16)
        for t in range(13):
            block = final_a[2 * (t // 4) + c, :, (t % 4) * 128:(t % 4 + 1) * 128].astype(F32) * scale
            if t < 9:
                g1[t, rows, :] = block
            else:
                gd[t - 9, rows, :] = block
        for t in range(10):
            at = (t % 3) * 128
            block = final_b[2 * (t // 3) + c, :, at:at + 128].astype(F32) * scale
            if t < 9:
                g2[t, rows, :] = block
            else:
                gu[rows, :] = block


def result_call(out_in, final_a, final_b, scale):
    return pl.pallas_call(
        functools.partial(result_kernel, scale=scale),
        out_shape=(
            jax.ShapeDtypeStruct((32, 4096), BF),
            jax.ShapeDtypeStruct((9, 32, 128), F32),
            jax.ShapeDtypeStruct((4, 32, 128), F32),
            jax.ShapeDtypeStruct((9, 32, 128), F32),
            jax.ShapeDtypeStruct((32, 128), F32),
        ),
        in_specs=[VM] * 3,
        out_specs=[VM] * 5,
        compiler_params=pltpu.CompilerParams(vmem_limit_bytes=16 * 1024 * 1024),
    )(out_in, final_a, final_b)


def per_device(features, conv1_weight, down_weight, conv2_weight, up_weight, out_grad, adjacency):
    pick, put = fine_rim_out()
    fine_sel, fine_place = fine_rim_maps()
    maps = [
        jnp.asarray(m, BF)
        for m in (pick, put, fine_perm(), corner_maps(), fine_sel, fine_place, side_cells(), strip_rims())
    ]
    out, final_a, final_b = level_call(
        adjacency.transpose(1, 2, 0).reshape(16, 64), features, out_grad,
        conv1_weight.reshape(9, 2, 16, 128), down_weight.reshape(4, 2, 16, 128), conv2_weight.reshape(9, 2, 16, 128),
        up_weight, *maps
    )
    return result_call(out, final_a, final_b, 262144 ** -0.5)


def solution(mesh):
    weights = P(None, "chan", None)
    return jax.shard_map(
        per_device,
        mesh=mesh,
        in_specs=(P("chan", "tile"), weights, weights, weights, P("chan", None), P("chan", "tile"), P()),
        out_specs=(P("chan", "tile"), weights, weights, weights, P("chan", None)),
        check_vma=False,
    )
```

```python
import functools
import math

import jax
import jax.numpy as jnp
import numpy as np
from jax import lax
from jax.experimental import pallas as pl
from jax.experimental.pallas import tpu as pltpu
from jax.sharding import PartitionSpec as P

BF = jnp.bfloat16
F32 = jnp.float32
MESH = pl.DeviceIdType.MESH
TURNS = (0, 1, 2, 3, 0, 2, 2, 0)
VM = pl.BlockSpec(memory_space=pltpu.VMEM)
ANY = pl.BlockSpec(memory_space=pl.ANY)
LIMIT = 56 * 1024 * 1024


def fine_perm():
    out = np.zeros((3, 128, 128), np.float32)
    for b in range(3):
        for rr in range(2):
            for par in range(2):
                for k in range(32):
                    col = 2 * (k - 1 + b) + par
                    if 0 <= col < 64:
                        out[b, rr * 64 + par * 32 + k, rr * 64 + col] = 1
    return out


def corner_maps():
    out = np.zeros((4, 128, 128), np.float32)
    for i in range(2):
        for j in range(2):
            out[0, i * 64 + j, 2 * i + j] = 1
            out[1, (1 - i) * 64 + 63 - j, 4 + 2 * i + j] = 1
            out[2, (1 - i) * 64 + 1 - j, 8 + 2 * i + j] = 1
            out[3, i * 64 + 62 + j, 12 + 2 * i + j] = 1
    return out


def fine_rim_maps():
    sel = np.zeros((4, 128, 640), np.float32)
    for q in range(4):
        for r in range(20):
            ir = 16 * q - 2 + r
            for par in range(2):
                if 0 <= ir < 64:
                    west = 384 + par * 64 + 63 - ir
                    east = 128 + (1 - par) * 64 + ir
                elif ir < 0:
                    west = 512 + 12 + 2 * (ir + 2) + par
                    east = 512 + 0 + 2 * (ir + 2) + par
                else:
                    west = 512 + 8 + 2 * (ir - 64) + par
                    east = 512 + 4 + 2 * (ir - 64) + par
                sel[q, r * 2 + par, west] = 1
                sel[q, 64 + r * 2 + par, east] = 1
    place = np.zeros((2, 1280, 128), np.float32)
    for r in range(20):
        for par in range(2):
            place[0, r * 64 + par * 32, r * 2 + par] = 1
            place[1, r * 64 + par * 32 + 31, 64 + r * 2 + par] = 1
    return sel, place


def fine_rim_out():
    pick = np.zeros((1024, 128), np.float32)
    for r in range(16):
        for kind, col in enumerate((0, 1, 62, 63)):
            pick[r * 64 + col, kind * 16 + r] = 1
    put = np.zeros((4, 128, 256), np.float32)
    for s in range(4):
        for r16 in range(16):
            r = 16 * s + r16
            for kind, lane in enumerate((64 + r, r, 128 + 63 - r, 192 + 63 - r)):
                put[s, kind * 16 + r16, lane] = 1
    return pick, put


def strip_rims():
    out = np.zeros((4, 48, 256), np.float32)
    for q in range(4):
        for r in range(8):
            out[q, r, r * 32] = 1
            out[q, 8 + r, r * 32 + 31] = 1
    for k in range(32):
        out[0, 16 + k, k] = 1
        out[3, 16 + k, 7 * 32 + k] = 1
    return out


def side_cells():
    out = np.zeros((4, 64, 1024), np.float32)
    for q in range(4):
        for r in range(10):
            out[q, r, 320 + r * 32] = 1
            out[q, 16 + r, 640 + r * 32 + 31] = 1
    for k in range(32):
        out[0, 32 + k, k] = 1
        out[3, 32 + k, 288 + k] = 1
    return out


def nt(a, b):
    return lax.dot_general(a, b, (((1,), (1,)), ((), ())), preferred_element_type=F32)


def tn(a, b):
    return lax.dot_general(a, b, (((0,), (0,)), ((), ())), preferred_element_type=F32)


def nn(a, b):
    return lax.dot_general(a, b, (((1,), (0,)), ((), ())), preferred_element_type=F32)


ROOT = 0.7978845608028654


def gelu(v):
    return 0.5 * v * (1.0 + jnp.tanh(ROOT * (v + 0.044715 * (v * v * v))))


def gelu_slope(v):
    t = jnp.tanh(ROOT * (v + 0.044715 * (v * v * v)))
    return 0.5 * (1.0 + t) + 0.5 * v * (1.0 - t * t) * (ROOT * (1.0 + 3 * 0.044715 * (v * v)))


AW, BW = 2048, 1536
XD = (2, 1, 3)
ZD = (4, 3, 5, 2, 6, 1, 7)
GD = (4, 3, 5, 2, 6, 1, 7)
FAR = (2, 1, 3, 0)
GXD = sorted(
    ((dg, dx) for dg in range(8) for dx in range(4) if dg or dx),
    key=lambda d: -(min(d[0], 8 - d[0]) / 2 + min(d[1], 4 - d[1])),
)
XYD = [(dx, dy) for dx in FAR for dy in FAR if dx or dy]


def side_by_side(weights, count):
    return jnp.concatenate([weights[t] for t in range(count)], axis=1)


def quarters(act):
    parts = act.reshape(8, 2, 2, 32, 128)
    return jnp.concatenate(
        [parts[:, a, b].reshape(256, 128) for a in range(2) for b in range(2)], axis=1
    )


def flip_map():
    rows = lax.broadcasted_iota(jnp.int32, (128, 128), 0)
    cols = lax.broadcasted_iota(jnp.int32, (128, 128), 1)
    return jnp.where(rows + cols == 127, 1.0, 0.0).astype(BF)


def level_kernel(*refs):
    names = INPUTS + ("out", "final_a", "final_b") + tuple(n for n, _ in SCRATCH)
    r = dict(zip(names, refs))
    tile, x = lax.axis_index("tile"), lax.axis_index("chan")
    z, g = tile // 8, lax.rem(tile, 8)
    y, core = g // 2, lax.rem(g, 2)
    q = x
    xs = [x] + [lax.rem(x + d, 4) for d in range(1, 4)]
    ys = [y] + [lax.rem(y + d, 4) for d in range(1, 4)]
    zs = [z] + [lax.rem(z + d, 8) for d in range(1, 8)]
    gs = [g] + [lax.rem(g + d, 8) for d in range(1, 8)]
    x_at = [(tile, xs[d]) for d in range(4)]
    z_at = [(zs[d] * 8 + g, x) for d in range(8)]
    g_at = [(z * 8 + gs[d], x) for d in range(8)]
    x_peer, z_peer, g_peer = x_at.__getitem__, z_at.__getitem__, g_at.__getitem__

    def xy_peer(dx, dy):
        return (g_at[2 * dy][0], xs[dx])

    mine = pl.ds(pl.multiple_of(x * 32, 32), 32)
    def gx_peer(dg, dx):
        return (g_at[dg][0], xs[dx])

    rounds, sent = [], []

    def rows_of(n):
        return pl.ds(pl.multiple_of(n * 32, 32), 32)

    def local(sem, src, dst):
        pltpu.make_async_copy(src, dst, sem).start()

    def wait(whole, sem):
        pltpu.make_async_copy(whole, whole, sem).wait()

    def begin(whole):
        rounds.append(whole)
        return len(rounds) - 1

    def push(n, src, dst, peer):
        pltpu.make_async_remote_copy(
            src_ref=src, dst_ref=dst, send_sem=r["ss"], recv_sem=r["rs"].at[n],
            device_id=peer, device_id_type=MESH,
        ).start()
        sent.append(math.prod(src.shape) * src.dtype.itemsize)

    def spread(whole, dirs, peer, src, dst):
        n = begin(whole)
        for d in dirs:
            push(n, src(d), dst(d), peer(d))
        return n

    def settle(n):
        wait(rounds[n], r["rs"].at[n])

    early = (("feat", "fv"), ("pick", "v_pick"), ("put", "v_put"))
    for src, dst in early:
        local(r["lsem"].at[0], r[src], r[dst])
    local(r["lsem"].at[1], r["adj"], r["s_adj"])
    r["landed3"][...] = jnp.zeros((32, 64, 128), BF)
    barrier = pltpu.get_barrier_semaphore()
    peers = [x_peer(d) for d in XD] + [z_peer(d) for d in ZD] + [g_peer(d) for d in GD]
    peers += [gx_peer(dg, dx) for dg, dx in GXD if dg and dx]
    for peer in peers:
        pl.semaphore_signal(barrier, inc=1, device_id=peer, device_id_type=MESH)

    adj = r["s_adj"]

    wait(r["early"], r["lsem"].at[0])
    fv, held = r["fv"], (r["held0"], r["held1"])
    stacked = jnp.concatenate([fv[:, s * 1024:(s + 1) * 1024] for s in range(4)], axis=0)
    cols = nn(stacked, r["v_pick"][...]).astype(BF)
    both = nn(cols[0:32], r["v_put"][0])
    for s in range(1, 4):
        both = both + nn(cols[32 * s:32 * s + 32], r["v_put"][s])
    flip = flip_map()
    rims = (
        fv[:, 3968:4096],
        both[:, 0:128].astype(BF),
        nn(fv[:, 0:128], flip).astype(BF),
        both[:, 128:256].astype(BF),
    )
    for s in range(4):
        held[0][z * 4 + s] = rims[s][0:16]
        held[1][g * 4 + s] = rims[s][16:32]
    pl.semaphore_wait(barrier, len(peers))
    ways = ((z, ZD, z_peer), (g, GD, g_peer))
    first = []
    for h in range(2):
        at, dirs, peer = ways[h]
        part = held[h].at[pl.ds(at * 4, 4)]
        first.append(spread(held[h].at[pl.ds(0, 28)], dirs, peer, lambda d: part, lambda d: part))

    for name in ("cmap", "perm", "fsel", "place"):
        local(r["lsem"].at[2], r[name], r["v_" + name])
    for name in ("rin", "src"):
        local(r["lsem"].at[2], r[name].at[q], r["v_" + name])

    def piece(n, j):
        if n == 0:
            start = pl.multiple_of(jnp.clip(j * 1024 - 128, 0, 2816), 128)
            return r["feat"].at[:, pl.ds(start, 1280)], r["strip"].at[mine, :]
        if n == 3:
            return r["ograd"].at[:, pl.ds(pl.multiple_of(j * 1024, 1024), 1024)], r["og"].at[mine, :]
        if n == 5:
            return r["up"], r["v_up"].at[mine, :]
        name = {1: "w1", 2: "wd", 4: "w2"}[n]
        return r[name].at[:, core], r["v_" + name].at[:, x, core]

    bulk = {}

    def send_bulk(n):
        into = r[("strip", "v_w1", "v_wd", "og", "v_w2", "v_up")[n]]
        m = begin(into.at[:, :, 0] if n in (1, 2, 4) else into)
        for d in XD:
            src, dst = piece(n, xs[d])
            push(m, src, dst, x_peer(d))
        src, dst = piece(n, x)
        local(r["rs"].at[m], src, dst)
        bulk[n] = m

    def share_bulk(n):
        settle(bulk[n])
        into = r[{1: "v_w1", 2: "v_wd", 4: "v_w2"}[n]]
        bulk[n] = begin(into.at[:, :, 0])
        push(bulk[n], into.at[:, :, core], into.at[:, :, core], (tile + 1 - 2 * core, x))

    def take_bulk(n):
        settle(bulk[n])

    for n in range(6):
        send_bulk(n)

    wait(r["s_adj"], r["lsem"].at[1])

    table = r["table"]
    for n in range(8):
        for k in range(8):
            at = n * 8 + k
            for h in range(2):
                t = z * 8 + n if h == 0 else n * 8 + g
                p = adj[2 * k, t]
                s = lax.rem(adj[2 * k + 1, t] + TURNS[k], 4)
                owned = jnp.logical_and(p >= 0, (p // 8 == z) if h else (lax.rem(p, 8) == g))
                m = lax.rem(p, 8) if h else p // 8
                table[h, at] = jnp.where(owned, m * 4 + s, -1)
                if h == 0:
                    table[3, at] = jnp.where(owned, m, -1)
                    table[4, at] = s

    wait(r["late"], r["lsem"].at[2])
    slots, landed = r["slots"], r["landed"]
    second = []
    for h in (1, 0):
        settle(first[h])
        _, dirs, peer = ways[1 - h]
        order = dirs + (0,)
        m = begin(landed.at[h, pl.ds(1, 7)])
        second.append(m)
        corners = [[] for _ in range(4)]
        for d in order:
            t = (gs[d] if h == 0 else zs[d]) * 8
            for k in range(8):
                n = table[h, t + k]
                block = held[h][jnp.maximum(n, 0)]
                block = jnp.where(n >= 0, block, jnp.zeros_like(block))
                if k < 4:
                    slots[h, d, :, k * 128:(k + 1) * 128] = block
                else:
                    corners[k - 4].append(block)
        corner = nn(jnp.concatenate(corners[0], axis=0), r["v_cmap"][0])
        for k in range(1, 4):
            corner = corner + nn(jnp.concatenate(corners[k], axis=0), r["v_cmap"][k])
        for n, d in enumerate(order):
            slots[h, d, :, 512:640] = corner[16 * n:16 * n + 16].astype(BF)
            if d:
                push(m, slots.at[h, d], landed.at[h, d], peer(d))
    take_bulk(0)
    perm, cb, strip = r["v_perm"], r["cb"], r["strip"]
    perms = perm[...].reshape(384, 128)
    shift = jnp.where(q == 0, -1, jnp.where(q == 3, 1, 0))

    def strip_block(n):
        at = jnp.clip(n + shift, 0, 9)
        return strip[:, pl.ds(pl.multiple_of(at * 128, 128), 128)]

    for n in range(1, 9):
        turned = nt(perms, strip_block(n))
        for b in range(3):
            cb[b, n * 128:(n + 1) * 128, :] = turned[b * 128:(b + 1) * 128].astype(BF)

    share_bulk(1)
    share_bulk(2)

    def sources(spot, at, xd):
        in_west, in_side = spot < 16, spot < 32
        row = jnp.where(in_west, spot, spot - 16) + (8 * xd - 1)
        above, below = jnp.logical_and(in_side, row < 0), jnp.logical_and(in_side, row > 31)

        def by_spot(kind):
            v = [table[kind, at + k] for k in range(8)]
            end = jnp.where(xd == 0, v[0], v[2])
            side = jnp.where(in_west, v[3], jnp.where(in_side, v[1], end))
            side = jnp.where(above, jnp.where(in_west, v[7], v[4]), side)
            return jnp.where(below, jnp.where(in_west, v[6], v[5]), side)

        of, turn = by_spot(3), by_spot(4)
        cell = jnp.where(in_west, 31 - row, jnp.where(in_side, row, jnp.where(xd == 0, spot - 32, 63 - spot)))
        cell = jnp.where(above, jnp.where(in_west, 31, 0), cell)
        cell = jnp.where(below, jnp.where(in_west, 0, 31), cell)
        cell = jnp.where(turn <= 1, cell, 31 - cell)
        odd = jnp.logical_or(turn == 1, turn == 3)
        here = jnp.where(odd, jnp.logical_and(cell >= 8 * q, cell < 8 * q + 8).astype(jnp.int32),
                         jnp.where(turn == 0, jnp.where(q == 3, 1, 0), jnp.where(q == 0, 1, 0)))
        source = jnp.where(odd, cell - 8 * q + jnp.where(turn == 3, 8, 0), cell + 16)
        return jnp.where(jnp.logical_and(of >= 0, here == 1), of * 48 + source, -1)

    spot = lax.broadcasted_iota(jnp.int32, (64, 128), 0)
    lane = lax.broadcasted_iota(jnp.int32, (64, 128), 1)
    for dg, dx in GXD + [(0, 0)]:
        source = sources(spot, gs[dg] * 8, xs[dx])
        for c in range(3):
            r["picks"][dg * 4 + dx, :, c * 128:(c + 1) * 128] = jnp.where(source == lane + 128 * c, 1.0, 0.0).astype(BF)

    halves_of = []
    for m, h in zip(second, (1, 0)):
        settle(m)
        total = slots[h, 0].astype(F32)
        for d in range(1, 8):
            total = total + landed[h, d].astype(F32)
        halves_of.append(total)
    total = jnp.concatenate([halves_of[1], halves_of[0]], axis=0).astype(BF)

    picked, pout = r["picked"], r["pout"]
    ends = (total[:, 0:128], None, None, nn(total[:, 256:384], flip).astype(BF))
    for j in range(4):
        pout[j, :, 0:128] = nt(total, r["v_fsel"][j]).astype(BF)
        pout[j, :, 128:256] = jnp.zeros((32, 128), BF) if ends[j] is None else ends[j]
    c_x = spread(
        picked.at[pl.ds(0, 96), :], XD, x_peer, lambda d: pout.at[xs[d]], lambda d: picked.at[mine, :]
    )
    picked[mine, :] = pout[x]
    take_bulk(1)
    take_bulk(2)
    w1 = r["v_w1"][...].reshape(9, 128, 128)
    w1c = side_by_side(w1, 9)
    for n in (0, 9):
        block = strip_block(n)
        turned = nt(perms, jnp.where(q == n // 3, jnp.zeros_like(block), block))
        for b in range(3):
            cb[b, n * 128:(n + 1) * 128, :] = turned[b * 128:(b + 1) * 128].astype(BF)
    z1, act1 = r["z1"], r["act1"]

    def fine_taps(n):
        return jnp.concatenate(
            [cb[b, a * 128 + n * 256:a * 128 + n * 256 + 256, :] for a in range(3) for b in range(3)], axis=1
        )

    for n in range(4):
        z1[n * 256:(n + 1) * 256, :] = nt(fine_taps(n), w1c)
    w1_west = jnp.concatenate([w1[3 * a] for a in range(3)], axis=1)
    w1_east = jnp.concatenate([w1[3 * a + 2] for a in range(3)], axis=1)
    w1_end = jnp.where(q == 0, side_by_side(w1, 3), side_by_side(w1[6:9], 3))
    unit = jnp.where(
        lax.broadcasted_iota(jnp.int32, (128, 128), 0) == lax.broadcasted_iota(jnp.int32, (128, 128), 1), 1.0, 0.0
    ).astype(BF)
    settle(c_x)

    sides = picked[:, 0:128]
    side_rows = nt(unit, sides)
    end_rows = nt(perms, picked[:, 128:256])
    west = jnp.concatenate([side_rows[4 * a:4 * a + 32] for a in range(3)], axis=1).astype(BF)
    east = jnp.concatenate([side_rows[64 + 4 * a:96 + 4 * a] for a in range(3)], axis=1).astype(BF)
    ends = jnp.concatenate([end_rows[128 * b:128 * b + 128] for b in range(3)], axis=1).astype(BF)
    west, east, ends = nt(west, w1_west), nt(east, w1_east), nt(ends, w1_end)
    for n in range(8):
        rows = slice(n * 128, (n + 1) * 128)
        add = []
        cell = lax.broadcasted_iota(jnp.int32, (32, 128), 0)
        for m in range(4 * n, 4 * n + 4):
            add.append(
                jnp.where(cell == 0, west[m:m + 1], 0.0) + jnp.where(cell == 31, east[m:m + 1], 0.0)
            )
        pre = z1[rows, :] + jnp.concatenate(add, axis=0)
        if n in (0, 7):
            pre = pre + jnp.where(q == (0 if n == 0 else 3), ends, 0.0)
        z1[rows, :] = pre
        act1[rows, :] = gelu(pre).astype(BF)
    pre = nt(quarters(act1[...]), side_by_side(r["v_wd"][...].reshape(4, 128, 128), 4))
    r["z2"][...] = pre
    act2 = gelu(pre).astype(BF)
    r["act2"][...] = act2
    held2 = r["held2"]
    held2[z] = nn(r["v_src"][...], act2).astype(BF)

    c_z = spread(held2.at[pl.ds(0, 7)], ZD, z_peer, lambda d: held2.at[z], lambda d: held2.at[z])
    halo = r["halo"]
    c_h = begin(halo)
    push(c_h, r["act2"].at[pl.ds(224, 32), :], halo.at[0], x_peer(1))
    push(c_h, r["act2"].at[pl.ds(0, 32), :], halo.at[1], x_peer(3))

    take_bulk(3)
    take_bulk(5)
    share_bulk(4)
    og, ogt, up = r["og"], r["ogt"], r["v_up"]
    flat = perm[1]
    for n in range(8):
        ogt[n * 128:(n + 1) * 128, :] = nt(flat, og[:, n * 128:(n + 1) * 128]).astype(BF)
    cells = ogt[...].astype(F32).reshape(8, 4, 32, 128)
    pooled = (cells[:, 0] + cells[:, 1] + cells[:, 2] + cells[:, 3]).reshape(256, 128).astype(BF)
    back_up = nn(pooled, up[...])
    for n in (0, 9):
        for b in range(3):
            rows = slice(n * 128, (n + 1) * 128)
            new = jnp.where(q == n // 3, end_rows[b * 128:(b + 1) * 128], cb[b, rows, :].astype(F32))
            cb[b, rows, :] = new.astype(BF)
    for b in (0, 2):
        cb[b] = (cb[b].astype(F32) + nt(r["v_place"][b // 2], sides)).astype(BF)
    slope = gelu_slope(z1[...])
    r["slope"][...] = slope
    r["direct"][...] = slope * ogt[...].astype(F32)

    lane = lax.broadcasted_iota(jnp.int32, (8, 128), 1)
    depth = lax.broadcasted_iota(jnp.int32, (384, 128), 0)
    for n in range(16):
        dg, dx = n // 2, 2 * (n % 2)
        left = lane < 64
        source = sources(jnp.where(left, lane, lane - 64), gs[dg] * 8, jnp.where(left, xs[dx], xs[dx + 1]))
        source = jnp.broadcast_to(source[0:1], (384, 128))
        r["adds"][:, n * 128:(n + 1) * 128] = jnp.where(source == depth, 1.0, 0.0).astype(BF)

    settle(c_z)
    slots2, landed2, picks = r["slots2"], r["landed2"], r["picks"]
    every = jnp.concatenate([held2[n] for n in range(8)], axis=0)
    c_g = begin(landed2)

    def at_end(n):
        return jnp.logical_or(n == 0, n == 3)

    for dx in FAR:
        for dg in GD + (0,):
            slots2[dg * 4 + dx] = nn(picks[dg * 4 + dx], every).astype(BF)
        for size, ok in ((64, at_end(xs[dx])), (32, jnp.logical_not(at_end(xs[dx])))):

            @pl.when(ok)
            def _():
                some = pl.ds(0, size)
                for dg in GD + (0,):
                    if dg or dx:
                        pltpu.make_async_remote_copy(
                            src_ref=slots2.at[dg * 4 + dx, some], dst_ref=landed2.at[dg * 4 + dx, some],
                            send_sem=r["ss2"], recv_sem=r["rs"].at[c_g],
                            device_id=gx_peer(dg, dx), device_id_type=MESH,
                        ).start()

    @pl.when(at_end(x))
    def _():
        wait(landed2.at[pl.ds(1, 31)], r["rs"].at[c_g])

    @pl.when(jnp.logical_not(at_end(x)))
    def _():
        wait(landed2.at[pl.ds(1, 31), pl.ds(0, 32)], r["rs"].at[c_g])

    total = slots2[0, 0:32, :].astype(F32)
    for d in range(1, 32):
        total = total + landed2[d, 0:32, :].astype(F32)
    beyond = r["beyond"]
    beyond[...] = jnp.zeros((32, 128), F32)

    @pl.when(at_end(x))
    def _():
        row = slots2[0, 32:64, :].astype(F32)
        for d in range(1, 32):
            row = row + landed2[d, 32:64, :].astype(F32)
        beyond[...] = row

    take_bulk(4)
    settle(c_h)

    upper = jnp.where(q == 0, beyond[...], halo[0].astype(F32))
    lower = jnp.where(q == 3, beyond[...], halo[1].astype(F32))
    rows = jnp.concatenate([upper, act2.astype(F32), lower], axis=0)
    col = lax.rem(lax.broadcasted_iota(jnp.int32, (320, 128), 0), 32)

    def along(first):
        return jnp.concatenate([jnp.broadcast_to(total[n:n + 1], (32, 128)) for n in range(first, first + 10)], axis=0)

    west = jnp.where(col == 0, along(0), pltpu.roll(rows, 1, 0))
    east = jnp.where(col == 31, along(16), pltpu.roll(rows, 319, 0))
    blocks = [v.astype(BF) for v in (west, rows, east)]
    taps2 = jnp.concatenate([blocks[b][a * 32:a * 32 + 256] for a in range(3) for b in range(3)], axis=1)
    w2 = r["v_w2"][...].reshape(9, 128, 128)
    pre = nt(taps2, side_by_side(w2, 9))
    gz3 = (gelu_slope(pre) * back_up).astype(BF)
    none32, none64 = jnp.zeros((32, 128), F32), jnp.zeros((64, 128), F32)
    back = []
    for b in range(3):
        v0, v1, v2 = (nn(gz3, w2[3 * a + b]) for a in range(3))
        back.append(
            jnp.concatenate([v0, none64], axis=0)
            + jnp.concatenate([none32, v1, none32], axis=0)
            + jnp.concatenate([none64, v2], axis=0)
        )
    mid = (
        back[1]
        + jnp.where(col == 31, 0.0, pltpu.roll(back[0], 319, 0))
        + jnp.where(col == 0, 0.0, pltpu.roll(back[2], 1, 0))
    )
    cat = jnp.concatenate([mid, back[0], back[2], none64], axis=0).astype(BF)
    landed3 = r["landed3"]
    landed3[0] = nn(r["v_rin"][...], cat).astype(BF)
    hout, hin = r["hout"], r["hin"]
    c_g = begin(landed3)
    for size, ok in ((64, at_end(x)), (32, jnp.logical_not(at_end(x)))):

        @pl.when(ok)
        def _():
            some = pl.ds(0, size)
            for dg, dx in GXD:
                back_at = ((8 - dg) % 8) * 4 + (4 - dx) % 4
                pltpu.make_async_remote_copy(
                    src_ref=landed3.at[0, some], dst_ref=landed3.at[back_at, some],
                    send_sem=r["ss3"], recv_sem=r["rs"].at[c_g],
                    device_id=gx_peer(dg, dx), device_id_type=MESH,
                ).start()

    hout[0] = mid[288:320]
    hout[1] = mid[0:32]
    c_h = begin(hin)
    push(c_h, hout.at[0], hin.at[0], x_peer(1))
    push(c_h, hout.at[1], hin.at[1], x_peer(3))

    other = 1 - core

    def halves(name, wide, parts):
        outs, ins = r[name + "c"], r[name + "ci"]
        for n in range(4):
            rows_n = pl.ds(pl.multiple_of(n * 32 + other * 16, 16), 16)
            at = 0
            for ref in parts:
                width = ref.shape[1]
                outs[n, :, at:at + width] = ref[rows_n, :].astype(BF)
                at += width
            outs[n, :, at:wide] = jnp.zeros((16, wide - at), BF)
        n = begin(ins)
        push(n, outs, ins, (tile + 1 - 2 * core, x))
        return n

    def shares(name, wide, parts):
        outs, ins = r[name + "o"], r[name + "i"]
        share = wide // 4
        for n in range(4):
            rows_n = pl.ds(pl.multiple_of(n * 32 + core * 16, 16), 16)
            own_n = jnp.concatenate(
                [ref[rows_n, :] for ref in parts]
                + [jnp.zeros((16, wide - sum(ref.shape[1] for ref in parts)), F32)],
                axis=1,
            )
            summed = (own_n + r[name + "ci"][n].astype(F32)).astype(BF)
            for m in range(4):
                outs[n, m] = summed[:, m * share:(m + 1) * share]
        m = begin(ins.at[pl.ds(1, 15)])
        for dx, dy in XYD:
            push(m, outs.at[xs[dx], ys[dy]], ins.at[dx * 4 + dy], xy_peer(dx, dy))
        return m

    def along_z(name):
        total = r[name + "o"][x, y].astype(F32)
        for n in range(1, 16):
            total = total + r[name + "i"][n].astype(F32)
        zall = r[name + "z"]
        zall[z] = total.astype(BF)
        return spread(zall.at[pl.ds(0, 7)], ZD, z_peer, lambda d: zall.at[z], lambda d: zall.at[z])

    def whole(name):
        zall = r[name + "z"]
        total = zall[0].astype(F32)
        for n in range(1, 8):
            total = total + zall[n].astype(F32)
        return total.astype(BF)

    coarse = gelu(pre).astype(BF)
    lifted = nt(coarse, up[...])
    out, ostrip = r["out"], r["ostrip"]
    for n in range(8):
        row = lifted[n * 32:(n + 1) * 32]
        summed = act1[n * 128:(n + 1) * 128, :].astype(F32) + jnp.concatenate([row] * 4, axis=0)
        ostrip[:, n * 128:(n + 1) * 128] = tn(summed.astype(BF), flat).astype(BF)

    lanes = pl.ds(pl.multiple_of(x * 1024, 1024), 1024)
    c_o = spread(
        out, XD, x_peer,
        lambda d: ostrip.at[rows_of(xs[d]), :], lambda d: out.at[:, lanes],
    )
    local(r["rs"].at[c_o], ostrip.at[mine, :], out.at[:, lanes])

    r["gb_u"][...] = tn(pooled, coarse)
    r["gb_w"][...] = tn(gz3, taps2)
    parts_b = (r["gb_w"], r["gb_u"])
    c_bc = halves("b", BW, parts_b)
    some_rows, more_rows = pl.ds(0, 15 * 64 + 16 * 32), pl.ds(0, 16 * 64 + 15 * 32)

    @pl.when(at_end(x))
    def _():
        wait(r["drain"].at[some_rows], r["rs"].at[c_g])

    @pl.when(jnp.logical_not(at_end(x)))
    def _():
        wait(r["drain"].at[more_rows], r["rs"].at[c_g])

    total = nn(r["adds"][...], landed3[...].reshape(2048, 128))
    slots3, landed4 = r["slots3"], r["landed4"]
    for n in range(8):
        slots3[n] = total[n * 48:(n + 1) * 48].astype(BF)
    c_z = spread(
        landed4.at[pl.ds(1, 7)], ZD, z_peer, lambda d: slots3.at[zs[d]], lambda d: landed4.at[d]
    )
    settle(c_bc)
    c_b = shares("b", BW, parts_b)
    slope2 = gelu_slope(r["z2"][...])
    settle(c_h)
    upper = jnp.where(q == 0, 0.0, hin[0])
    lower = jnp.where(q == 3, 0.0, hin[1])
    ga2 = mid[32:288] + jnp.concatenate([upper, jnp.zeros((192, 128), F32), lower], axis=0)
    settle(c_z)
    total = slots3[z].astype(F32)
    for d in ZD:
        total = total + landed4[d].astype(F32)

    gz2 = (slope2 * (ga2 + tn(r["v_src"][...], total.astype(BF)))).astype(BF)
    wd = r["v_wd"][...].reshape(4, 128, 128)
    fine = [nn(gz2, wd[t]).reshape(8, 1, 32, 128) for t in range(4)]
    grown = jnp.concatenate(fine, axis=1).reshape(1024, 128)
    gz1 = (r["direct"][...] + r["slope"][...] * grown).astype(BF)
    r["ga_w"][...] = tn(
        gz1, jnp.concatenate([cb[b, a * 128:a * 128 + 1024, :] for a in range(3) for b in range(3)], axis=1)
    )
    r["ga_d"][...] = tn(gz2, quarters(act1[...]))
    parts_a = (r["ga_w"], r["ga_d"])
    c_ac = halves("a", AW, parts_a)
    settle(c_b)
    c_bz = along_z("b")

    def to_row(name, n):
        settle(n)
        final = r["final_" + name]
        final[g] = whole(name)
        return spread(final.at[pl.ds(0, 7)], GD, g_peer, lambda d: final.at[g], lambda d: final.at[g])

    settle(c_ac)
    c_a = shares("a", AW, parts_a)
    settle(c_a)
    c_az = along_z("a")
    c_bg = to_row("b", c_bz)
    settle(c_o)
    c_ag = to_row("a", c_az)
    settle(c_bg)
    settle(c_ag)
    assert sum(sent) == 256 * SENT, sum(sent) // 256
    wait(r["drain"], r["ss"])

    @pl.when(at_end(x))
    def _():
        wait(r["drain"].at[some_rows], r["ss2"])
        wait(r["drain"].at[pl.ds(0, 31 * 64)], r["ss3"])

    @pl.when(jnp.logical_not(at_end(x)))
    def _():
        wait(r["drain"].at[more_rows], r["ss2"])
        wait(r["drain"].at[pl.ds(0, 31 * 32)], r["ss3"])


INPUTS = (
    "adj", "feat", "ograd", "w1", "wd", "w2", "up",
    "pick", "put", "perm", "cmap", "fsel", "place", "rin", "src",
)


def buf(*shape, kind=BF):
    return pltpu.VMEM(shape, kind)


def sems(*shape):
    return pltpu.SemaphoreType.DMA(shape)


SENT = 13168
SCRATCH = [
    ("early", buf(3072, 128)), ("late", buf(6624, 128)), ("drain", buf(SENT, 128)),
    ("lsem", sems(3)), ("ss", pltpu.SemaphoreType.DMA), ("ss2", pltpu.SemaphoreType.DMA), ("ss3", pltpu.SemaphoreType.DMA), ("rs", sems(33)), ("s_adj", pltpu.SMEM((16, 64), jnp.int32)),
    ("table", pltpu.SMEM((6, 64), jnp.int32)),
    ("fv", buf(32, 4096)), ("v_pick", buf(1024, 128)), ("v_put", buf(4, 128, 256)), ("v_perm", buf(3, 128, 128)),
    ("v_cmap", buf(4, 128, 128)), ("v_fsel", buf(4, 128, 640)), ("v_place", buf(2, 1280, 128)),
    ("v_rin", buf(64, 1024)), ("v_src", buf(48, 256)),
    ("strip", buf(128, 1280)), ("og", buf(128, 1024)), ("v_w1", buf(9, 4, 2, 16, 128)), ("v_wd", buf(4, 4, 2, 16, 128)),
    ("v_w2", buf(9, 4, 2, 16, 128)), ("v_up", buf(128, 128)),
    ("held0", buf(32, 16, 128)), ("held1", buf(32, 16, 128)), ("slots", buf(2, 8, 16, 640)), ("landed", buf(2, 8, 16, 640)),
    ("pout", buf(4, 32, 256)), ("picked", buf(128, 256)),
    ("cb", buf(3, 1280, 128)), ("z1", buf(1024, 128, kind=F32)), ("act1", buf(1024, 128)),
    ("z2", buf(256, 128, kind=F32)), ("act2", buf(256, 128)),
    ("slope", buf(1024, 128, kind=F32)), ("direct", buf(1024, 128, kind=F32)),
    ("halo", buf(2, 32, 128)), ("held2", buf(8, 48, 128)), ("picks", buf(32, 64, 384)), ("beyond", buf(32, 128, kind=F32)), ("ogt", buf(1024, 128)),
    ("slots2", buf(32, 64, 128)), ("landed2", buf(32, 64, 128)),
    ("adds", buf(384, 2048)), ("landed3", buf(32, 64, 128)), ("slots3", buf(8, 48, 128)), ("landed4", buf(8, 48, 128)),
    ("hout", buf(2, 32, 128, kind=F32)), ("hin", buf(2, 32, 128, kind=F32)), ("ostrip", buf(128, 1024)),
    ("gb_u", buf(128, 128, kind=F32)), ("gb_w", buf(128, 1152, kind=F32)),
    ("ga_d", buf(128, 512, kind=F32)), ("ga_w", buf(128, 1152, kind=F32)),
    ("bc", buf(4, 16, BW)), ("bci", buf(4, 16, BW)), ("bo", buf(4, 4, 16, BW // 4)), ("bi", buf(16, 16, BW // 4)),
    ("bz", buf(8, 16, BW // 4)),
    ("ac", buf(4, 16, AW)), ("aci", buf(4, 16, AW)), ("ao", buf(4, 4, 16, AW // 4)), ("ai", buf(16, 16, AW // 4)),
    ("az", buf(8, 16, AW // 4)),
]


def level_call(*args):
    return pl.pallas_call(
        level_kernel,
        out_shape=(pltpu.VMEM((32, 4096), BF), pltpu.VMEM((8, 16, AW // 4), BF), pltpu.VMEM((8, 16, BW // 4), BF)),
        in_specs=[ANY] * 15,
        out_specs=[VM] * 3,
        scratch_shapes=[s for _, s in SCRATCH],
        compiler_params=pltpu.CompilerParams(collective_id=0, has_side_effects=True, vmem_limit_bytes=LIMIT),
    )(*args)


def result_kernel(out_in, final_a, final_b, out, g1, gd, g2, gu, *, scale):
    out[...] = out_in[...]
    for c in range(2):
        rows = pl.ds(c * 16, 16)
        for t in range(13):
            block = final_a[2 * (t // 4) + c, :, (t % 4) * 128:(t % 4 + 1) * 128].astype(F32) * scale
            if t < 9:
                g1[t, rows, :] = block
            else:
                gd[t - 9, rows, :] = block
        for t in range(10):
            at = (t % 3) * 128
            block = final_b[2 * (t // 3) + c, :, at:at + 128].astype(F32) * scale
            if t < 9:
                g2[t, rows, :] = block
            else:
                gu[rows, :] = block


def result_call(out_in, final_a, final_b, scale):
    return pl.pallas_call(
        functools.partial(result_kernel, scale=scale),
        out_shape=(
            jax.ShapeDtypeStruct((32, 4096), BF),
            jax.ShapeDtypeStruct((9, 32, 128), F32),
            jax.ShapeDtypeStruct((4, 32, 128), F32),
            jax.ShapeDtypeStruct((9, 32, 128), F32),
            jax.ShapeDtypeStruct((32, 128), F32),
        ),
        in_specs=[VM] * 3,
        out_specs=[VM] * 5,
        compiler_params=pltpu.CompilerParams(vmem_limit_bytes=16 * 1024 * 1024),
    )(out_in, final_a, final_b)


def per_device(features, conv1_weight, down_weight, conv2_weight, up_weight, out_grad, adjacency):
    pick, put = fine_rim_out()
    fine_sel, fine_place = fine_rim_maps()
    maps = [
        jnp.asarray(m, BF)
        for m in (pick, put, fine_perm(), corner_maps(), fine_sel, fine_place, side_cells(), strip_rims())
    ]
    out, final_a, final_b = level_call(
        adjacency.transpose(1, 2, 0).reshape(16, 64), features, out_grad,
        conv1_weight.reshape(9, 2, 16, 128), down_weight.reshape(4, 2, 16, 128), conv2_weight.reshape(9, 2, 16, 128),
        up_weight, *maps
    )
    return result_call(out, final_a, final_b, 262144 ** -0.5)


def solution(mesh):
    weights = P(None, "chan", None)
    return jax.shard_map(
        per_device,
        mesh=mesh,
        in_specs=(P("chan", "tile"), weights, weights, weights, P("chan", None), P("chan", "tile"), P()),
        out_specs=(P("chan", "tile"), weights, weights, weights, P("chan", None)),
        check_vma=False,
    )
```
